32 devices in a mesh: seq: 8 (over z, x), batch: 4 (over y, core).
Axes of the slice: x: 2, y: 2, z: 4, core: 2. Of those that a mesh axis runs over, the one named last changes fastest.
Arguments:
- inputs: bfloat16 [2, 4, 2048, 768], P(None, 'batch', 'seq'), may hold values from -6 to 6
- cotangent: bfloat16 [2, 4, 2048, 768], P(None, 'batch', 'seq'), may hold values from -6 to 6
- doc_lengths: int32 [2, 4, 4], P(None, 'batch'), may hold values from 0 to 2048, as said below
- random_blocks: int32 [2, 4, 32, 3], P(None, 'batch'), may hold values from 0 to 31, as said below
- w_query: bfloat16 [768, 768], P(('seq', 'batch')), may hold values from -0.21875 to 0.21875
- w_key: bfloat16 [768, 768], P(('seq', 'batch')), may hold values from -0.21875 to 0.21875
- w_value: bfloat16 [768, 768], P(('seq', 'batch')), may hold values from -0.21875 to 0.21875
- w_out: bfloat16 [768, 768], P(('seq', 'batch')), may hold values from -0.875 to 0.875
- w_up: bfloat16 [768, 3072], P(('seq', 'batch')), may hold values from -0.21875 to 0.21875
- w_down: bfloat16 [3072, 768], P(('seq', 'batch')), may hold values from -0.109375 to 0.109375
- b_query: bfloat16 [768], P(('seq', 'batch')), may hold values from -3 to 3
- b_value: bfloat16 [768], P(('seq', 'batch')), may hold values from -3 to 3
- b_out: bfloat16 [768], P(('seq', 'batch')), may hold values from -3 to 3
- b_up: bfloat16 [3072], P(('seq', 'batch')), may hold values from -3 to 3
- b_down: bfloat16 [768], P(('seq', 'batch')), may hold values from -3 to 3
- gain_attn: bfloat16 [768], P(('seq', 'batch')), may hold values from 0.5 to 1.5
- bias_attn: bfloat16 [768], P(('seq', 'batch')), may hold values from -3 to 3
- gain_ffn: bfloat16 [768], P(('seq', 'batch')), may hold values from 0.5 to 1.5
- bias_ffn: bfloat16 [768], P(('seq', 'batch')), may hold values from -3 to 3
Outputs:
- outputs: bfloat16 [2, 4, 2048, 768], P(None, 'batch', 'seq')
- grad_inputs: float32 [2, 4, 2048, 768], P(None, 'batch', 'seq')
- grad_w_query: float32 [768, 768], P(('seq', 'batch'))
- grad_w_key: float32 [768, 768], P(('seq', 'batch'))
- grad_w_value: float32 [768, 768], P(('seq', 'batch'))
- grad_w_out: float32 [768, 768], P(('seq', 'batch'))
- grad_w_up: float32 [768, 3072], P(('seq', 'batch'))
- grad_w_down: float32 [3072, 768], P(('seq', 'batch'))
- grad_b_query: float32 [768], P(('seq', 'batch'))
- grad_b_value: float32 [768], P(('seq', 'batch'))
- grad_b_out: float32 [768], P(('seq', 'batch'))
- grad_b_up: float32 [3072], P(('seq', 'batch'))
- grad_b_down: float32 [768], P(('seq', 'batch'))
- grad_gain_attn: float32 [768], P(('seq', 'batch'))
- grad_bias_attn: float32 [768], P(('seq', 'batch'))
- grad_gain_ffn: float32 [768], P(('seq', 'batch'))
- grad_bias_ffn: float32 [768], P(('seq', 'batch'))
The draws below stay inside these ranges and needn't reach their ends.
Inputs may be any that keep to these rules, and one draw needn't show every extreme that they name: `doc_lengths`: every entry is a multiple of 128 and the 4 entries of a sequence add up to 2048. For each sequence index s, in one micro-batch drawn from the seed sequence s is a single document: first entry 2048, the others 0; elsewhere all entries are positive. `random_blocks`: entry [m, s, d * 4 + j, r] names a block of sequence (m, s). With t = (m * 3 + r) * 4 + j, the device along seq that holds the named block (entry // 4) depends only on s, d and t modulo the number of devices along seq, and different residues give different devices. The 3 entries of one block differ.
All inputs are finite; a program needn't handle non-finite values.
Results may differ from the reference program's by a relative error of at most 0.014.
Values may be sent and summed in bfloat16 or wider, within the bound.
A program may use at most 320 MiB of HBM per device.

```python
import jax
import jax.numpy as jnp
from jax import lax

D = 768
HD = 64
FF = 3072
BLK = 64
WIN = 8
GLB = 2
RAND = 3
NDOC = 4
SEQ_DEV = 256
MB = 2
SEQS = 4
LEN = 2048
BLOCKS = 32
BLK_DEV = 4


def draw_doc_lengths(key, part):
    key = jax.random.fold_in(key, 11)
    unit_count = LEN // (GLB * BLK)
    row_keys = jax.random.split(key, MB * SEQS + 1)

    def ragged_row(row_key):
        shuffled = jax.random.permutation(row_key, unit_count - 1)[:NDOC - 1] + 1
        cut_points = jnp.sort(shuffled).astype(jnp.int32)
        edge_list = jnp.concatenate([jnp.zeros((1,), jnp.int32), cut_points, jnp.full((1,), unit_count, jnp.int32)])
        return ((edge_list[1:] - edge_list[:-1]) * (GLB * BLK)).astype(jnp.int32)
    ragged = jax.vmap(ragged_row)(row_keys[1:]).reshape(MB, SEQS, NDOC)
    chosen = jax.random.randint(row_keys[0], (SEQS,), 0, MB)
    single_doc = jnp.zeros((NDOC,), jnp.int32).at[0].set(LEN)
    spanning = jnp.arange(MB)[:, None] == chosen[None, :]
    return jnp.where(spanning[:, :, None], single_doc[None, None, :], ragged).astype(jnp.int32)


def draw_random_blocks(key, part):
    key = jax.random.fold_in(key, 23)
    dev_count = BLOCKS // BLK_DEV
    perm_key, base_key = jax.random.split(key)
    perm_keys = jax.random.split(perm_key, SEQS * dev_count)
    shuffles = jax.vmap(lambda row_key: jax.random.permutation(row_key, dev_count))(perm_keys).reshape(SEQS, dev_count, dev_count)
    base_slot = jax.random.randint(base_key, (MB, SEQS, dev_count, BLK_DEV, 1), 0, BLK_DEV)
    micro_idx = jnp.arange(MB).reshape(MB, 1, 1, 1, 1)
    seq_idx = jnp.arange(SEQS).reshape(1, SEQS, 1, 1, 1)
    dev_idx = jnp.arange(dev_count).reshape(1, 1, dev_count, 1, 1)
    block_idx = jnp.arange(BLK_DEV).reshape(1, 1, 1, BLK_DEV, 1)
    rand_idx = jnp.arange(RAND).reshape(1, 1, 1, 1, RAND)
    slot_number = (micro_idx * RAND + rand_idx) * BLK_DEV + block_idx
    residue = slot_number % dev_count
    offset = shuffles[seq_idx, dev_idx, residue]
    source = (dev_idx + offset) % dev_count
    within = (base_slot + rand_idx) % BLK_DEV
    named = source * BLK_DEV + within
    return named.reshape(MB, SEQS, BLOCKS, RAND).astype(jnp.int32)


def steps_of(rng, shape, cuts, low, top_value):
    def one(dim, blocks):
        heights = jax.random.uniform(jax.random.fold_in(jax.random.fold_in(rng, 6), dim), (blocks,), jnp.float32, low / len(cuts), top_value / len(cuts))
        return jnp.repeat(jnp.exp(heights), shape[dim] // blocks).reshape((-1,) + (1,) * (len(shape) - dim - 1))

    level = one(*cuts[0])
    for cut in cuts[1:]:
        level = level * one(*cut)
    return level


def gaussian(key, shape, spread, limit, shards=(), kind=jnp.bfloat16):
    loudness = steps_of(key, shape, shards, -0.22, 0.18) if shards else 1.0
    array = jax.random.normal(key, shape, jnp.float32) * spread * loudness
    return jnp.minimum(jnp.maximum(array, -limit), limit).astype(kind)


def setup_inputs(seed: int = 0) -> dict:
    arg_keys = jax.random.split(jax.random.key(seed), 20)
    inputs = gaussian(arg_keys[0], (MB, SEQS, LEN, D), 1.0, 6.0, ((1, 4), (2, 8)))
    cotangent = gaussian(arg_keys[1], (MB, SEQS, LEN, D), 1.0, 6.0, ((1, 4), (2, 8)))
    doc_lengths = draw_doc_lengths(jax.random.fold_in(arg_keys[19], 71), 0)
    random_blocks = draw_random_blocks(jax.random.fold_in(arg_keys[19], 71), 0)
    w_query = gaussian(arg_keys[4], (D, D), D ** -0.5, 0.21875, ((0, 32),))
    w_key = gaussian(arg_keys[5], (D, D), D ** -0.5, 0.21875, ((0, 32),))
    w_value = gaussian(arg_keys[6], (D, D), D ** -0.5, 0.21875, ((0, 32),))
    w_out = gaussian(arg_keys[7], (D, D), (D // 16) ** -0.5, 0.875, ((0, 32),))
    w_up = gaussian(arg_keys[8], (D, FF), D ** -0.5, 0.21875, ((0, 32),))
    w_down = gaussian(arg_keys[9], (FF, D), FF ** -0.5, 0.109375, ((0, 32),))
    b_query = gaussian(arg_keys[10], (D,), 0.5, 3.0, ((0, 32),))
    b_value = gaussian(arg_keys[11], (D,), 0.5, 3.0, ((0, 32),))
    b_out = gaussian(arg_keys[12], (D,), 0.5, 3.0, ((0, 32),))
    b_up = gaussian(arg_keys[13], (FF,), 0.5, 3.0, ((0, 32),))
    b_down = gaussian(arg_keys[14], (D,), 0.5, 3.0, ((0, 32),))
    gain_attn = jnp.clip(1.0 + 0.1 * jax.random.normal(arg_keys[15], (D,), jnp.float32), 0.5, 1.5).astype(jnp.bfloat16)
    bias_attn = gaussian(arg_keys[16], (D,), 0.5, 3.0, ((0, 32),))
    gain_ffn = jnp.clip(1.0 + 0.1 * jax.random.normal(arg_keys[17], (D,), jnp.float32), 0.5, 1.5).astype(jnp.bfloat16)
    bias_ffn = gaussian(arg_keys[18], (D,), 0.5, 3.0, ((0, 32),))
    return {"inputs": inputs, "cotangent": cotangent, "doc_lengths": doc_lengths, "random_blocks": random_blocks, "w_query": w_query, "w_key": w_key, "w_value": w_value, "w_out": w_out, "w_up": w_up, "w_down": w_down, "b_query": b_query, "b_value": b_value, "b_out": b_out, "b_up": b_up, "b_down": b_down, "gain_attn": gain_attn, "bias_attn": bias_attn, "gain_ffn": gain_ffn, "bias_ffn": bias_ffn}


masked_value = -1e+30
norm_epsilon = 1e-06

@jax.custom_vjp
def low(v):
    return lax.optimization_barrier(v.astype(jnp.bfloat16)).astype(jnp.float32)

@jax.custom_vjp
def low_back(v):
    return v

def low_keep(v):
    return (low(v), None)

def low_pass(kept, grad):
    return (grad,)

def back_keep(v):
    return (v, None)

def back_low(kept, grad):
    return (low(grad),)
low.defvjp(low_keep, low_pass)
low_back.defvjp(back_keep, back_low)

def doc_tables(lengths, positions):
    doc_ends = jnp.cumsum(lengths).astype(jnp.int32)
    starts = doc_ends - lengths
    counted = (doc_ends[None, :] <= positions[:, None]).astype(jnp.int32)
    doc_index = jnp.minimum(lax.optimization_barrier(jnp.sum(counted, axis=1)).astype(jnp.int32), lengths.shape[0] - 1)
    picked = jnp.arange(lengths.shape[0], dtype=jnp.int32)[None, :] == doc_index[:, None]
    doc_first = lax.optimization_barrier(jnp.sum(jnp.where(picked, starts[None, :], 0), axis=1)).astype(jnp.int32)
    return (doc_index, doc_first)

def mask_parts(lengths, query_pos, key_pos, query_block, rand_mine, seq_len):
    glob_rows = GLB * BLK
    key_clip = jnp.clip(key_pos, 0, seq_len - 1)
    doc_query, first_query = doc_tables(lengths, query_pos)
    doc_key, first_key = doc_tables(lengths, key_clip)
    nearby = jnp.abs(jnp.floor_divide(key_pos, BLK)[None, :] - jnp.floor_divide(query_pos, BLK)[:, None]) <= WIN
    inside = (key_pos >= 0) & (key_pos < seq_len) & (key_clip - first_key >= glob_rows)
    window_mask = nearby & inside[None, :] & (doc_key[None, :] == doc_query[:, None])
    glob_doc = jnp.repeat(jnp.arange(lengths.shape[0], dtype=jnp.int32), glob_rows)
    glob_mask = glob_doc[None, :] == doc_query[:, None]
    doc_block = doc_tables(lengths, query_block * BLK)[0]
    rand_flat = rand_mine.reshape(-1) * BLK
    doc_rand, first_rand = doc_tables(lengths, rand_flat)
    rand_shape = rand_mine.shape
    rand_mask = (doc_rand.reshape(rand_shape) == doc_block[:, None]) & (jnp.abs(rand_mine - query_block[:, None]) > WIN) & ((rand_flat - first_rand).reshape(rand_shape) >= glob_rows)
    rand_mask = jnp.repeat(rand_mask, BLK, axis=1)
    return (window_mask, glob_mask, rand_mask, doc_query, first_query)

def attention(queries, key_rows, values, lengths, rand_table):
    highest = lax.Precision.HIGHEST
    seq_len = queries.shape[0]
    model_width = queries.shape[1]
    head_count = model_width // HD
    halo_rows = WIN * BLK
    glob_rows = GLB * BLK
    row_count = 2 * SEQ_DEV
    blk_rows = row_count // BLK
    score_scale = HD ** (-0.5)
    padded_keys = jnp.pad(key_rows, ((halo_rows, halo_rows), (0, 0)))
    padded_values = jnp.pad(values, ((halo_rows, halo_rows), (0, 0)))
    doc_ends = jnp.cumsum(lengths).astype(jnp.int32)
    starts = doc_ends - lengths
    glob_pos = jnp.clip(starts[:, None] + jnp.arange(glob_rows, dtype=jnp.int32)[None, :], 0, seq_len - 1).reshape(-1)
    glob_keys = key_rows[glob_pos].reshape(-1, head_count, HD)
    glob_values = values[glob_pos].reshape(-1, head_count, HD)

    def one_block(block_index):
        row_start = block_index * row_count
        query_heads = lax.dynamic_slice_in_dim(queries, row_start, row_count, 0).reshape(row_count, head_count, HD)
        window_keys = lax.dynamic_slice_in_dim(padded_keys, row_start, row_count + 2 * halo_rows, 0).reshape(-1, head_count, HD)
        window_values = lax.dynamic_slice_in_dim(padded_values, row_start, row_count + 2 * halo_rows, 0).reshape(-1, head_count, HD)
        query_pos = row_start + jnp.arange(row_count, dtype=jnp.int32)
        key_pos = row_start - halo_rows + jnp.arange(row_count + 2 * halo_rows, dtype=jnp.int32)
        query_block = block_index * blk_rows + jnp.arange(blk_rows, dtype=jnp.int32)
        rand_mine = lax.dynamic_slice_in_dim(rand_table, block_index * blk_rows, blk_rows, 0)
        window_mask, glob_mask, rand_mask, doc_query, first_query = mask_parts(lengths, query_pos, key_pos, query_block, rand_mine, seq_len)
        rand_pos = (rand_mine[:, :, None] * BLK + jnp.arange(BLK, dtype=jnp.int32)[None, None, :]).reshape(blk_rows, RAND * BLK)
        rand_keys = key_rows[rand_pos].reshape(blk_rows, RAND * BLK, head_count, HD)
        rand_values = values[rand_pos].reshape(blk_rows, RAND * BLK, head_count, HD)
        block_heads = query_heads.reshape(blk_rows, BLK, head_count, HD)
        window_scores = low_back(jnp.einsum('qhd,khd->hqk', query_heads, window_keys, precision=highest) * score_scale)
        window_scores = jnp.where(window_mask[None], window_scores, masked_value)
        glob_scores = low_back(jnp.einsum('qhd,khd->hqk', query_heads, glob_keys, precision=highest) * score_scale)
        glob_scores = jnp.where(glob_mask[None], glob_scores, masked_value)
        rand_scores = low_back(jnp.einsum('jqhd,jkhd->hjqk', block_heads, rand_keys, precision=highest) * score_scale)
        rand_scores = jnp.where(rand_mask[None, :, None, :], rand_scores, masked_value)
        rand_flat = rand_scores.reshape(head_count, row_count, -1)
        top_score = jnp.maximum(jnp.maximum(lax.optimization_barrier(jnp.max(window_scores, axis=-1)), lax.optimization_barrier(jnp.max(glob_scores, axis=-1))), lax.optimization_barrier(jnp.max(rand_flat, axis=-1)))
        row_total = lax.optimization_barrier(jnp.sum(jnp.exp(window_scores - top_score[..., None]), axis=-1))
        row_total = row_total + lax.optimization_barrier(jnp.sum(jnp.exp(glob_scores - top_score[..., None]), axis=-1))
        row_total = row_total + lax.optimization_barrier(jnp.sum(jnp.exp(rand_flat - top_score[..., None]), axis=-1))
        log_norm = top_score + jnp.log(row_total)
        prob_window = jnp.exp(window_scores - log_norm[..., None])
        prob_glob = jnp.exp(glob_scores - log_norm[..., None])
        prob_rand = jnp.exp(rand_scores - log_norm.reshape(head_count, blk_rows, BLK)[..., None])
        summed = jnp.einsum('hqk,khd->qhd', low(prob_window), window_values, precision=highest)
        summed = summed + jnp.einsum('hqk,khd->qhd', low(prob_glob), glob_values, precision=highest)
        summed = summed + jnp.einsum('hjqk,jkhd->jqhd', low(prob_rand), rand_values, precision=highest).reshape(row_count, head_count, HD)
        return summed.reshape(row_count, model_width)
    blocks_out = lax.map(jax.checkpoint(one_block), jnp.arange(seq_len // row_count, dtype=jnp.int32))
    return blocks_out.reshape(seq_len, model_width)

def normalize(values_in, norm_gain, norm_shift):
    average = lax.optimization_barrier(jnp.mean(values_in, axis=-1, keepdims=True))
    centred = values_in - average
    inverse = lax.rsqrt(lax.optimization_barrier(jnp.mean(centred * centred, axis=-1, keepdims=True)) + norm_epsilon)
    return centred * inverse * norm_gain + norm_shift

def layer_forward(tokens, weights, lengths, rand_table):
    w_query, w_key, w_value, w_out, w_up, w_down, b_query, b_value, b_out, b_up, b_down, gain_attn, bias_attn, gain_ffn, bias_ffn = weights
    highest = lax.Precision.HIGHEST
    queries = low_back(low(jnp.dot(tokens, w_query, precision=highest) + b_query))
    key_rows = low_back(low(jnp.dot(tokens, w_key, precision=highest)))
    values = low_back(low(jnp.dot(tokens, w_value, precision=highest) + b_value))
    attended = low_back(low(attention(queries, key_rows, values, lengths, rand_table)))
    branch = low_back(jnp.dot(attended, w_out, precision=highest) + b_out)
    middle = normalize(tokens + branch, gain_attn, bias_attn)
    hidden_pre = low_back(jnp.dot(low(middle), w_up, precision=highest) + b_up)
    hidden = low(jax.nn.gelu(hidden_pre, approximate=True))
    ffn_out = low_back(jnp.dot(hidden, w_down, precision=highest) + b_down)
    return normalize(middle + ffn_out, gain_ffn, bias_ffn)

def reference(inputs, cotangent, doc_lengths, random_blocks, w_query, w_key, w_value, w_out, w_up, w_down, b_query, b_value, b_out, b_up, b_down, gain_attn, bias_attn, gain_ffn, bias_ffn):
    weights = tuple((parameter.astype(jnp.float32) for parameter in (w_query, w_key, w_value, w_out, w_up, w_down, b_query, b_value, b_out, b_up, b_down, gain_attn, bias_attn, gain_ffn, bias_ffn)))
    seq_count = MB * SEQS
    flat_inputs = inputs.reshape(seq_count, LEN, D)
    flat_cot = cotangent.reshape(seq_count, LEN, D)
    flat_lengths = doc_lengths.reshape(seq_count, NDOC)
    flat_rand = random_blocks.reshape(seq_count, BLOCKS, RAND)

    def one_sequence(running, pieces):
        seq_in, seq_cot, lengths, rand_table = pieces

        def forward(tokens, params):
            return layer_forward(tokens, params, lengths, rand_table)
        result, pullback = jax.vjp(forward, seq_in.astype(jnp.float32), weights)
        grad_tokens, grad_params = pullback(seq_cot.astype(jnp.float32))
        running = tuple((summed + addend for summed, addend in zip(running, grad_params)))
        return (running, (result.astype(jnp.bfloat16), grad_tokens))
    initial = tuple((jnp.zeros(parameter.shape, jnp.float32) for parameter in weights))
    totals, (result_all, grad_all) = lax.scan(one_sequence, initial, (flat_inputs, flat_cot, flat_lengths, flat_rand))
    return (result_all.reshape(MB, SEQS, LEN, D), grad_all.reshape(MB, SEQS, LEN, D), totals[0], totals[1], totals[2], totals[3], totals[4], totals[5], totals[6], totals[7], totals[8], totals[9], totals[10], totals[11], totals[12], totals[13], totals[14])
```

```python
import functools

import jax
import jax.numpy as jnp
from jax import lax
from jax.experimental import pallas as pl
from jax.experimental.pallas import tpu as pltpu
from jax.sharding import PartitionSpec as P

F32 = jnp.float32
BF = jnp.bfloat16

MESH = pl.DeviceIdType.MESH
PIECE = 592
ROWS = 304


def place():
    s, b = lax.axis_index("seq"), lax.axis_index("batch")
    return s // 2, s % 2, b // 2, b % 2


def device(z, x, y, c):
    return (2 * z + x, 2 * y + c)


def greet(z, x, y, c):
    barrier = pltpu.get_barrier_semaphore()

    def tell(to):
        pl.semaphore_signal(barrier, inc=1, device_id=to, device_id_type=MESH)

    tell(device(z, 1 - x, y, c))
    tell(device(z, x, 1 - y, c))
    tell(device(z, x, y, 1 - c))
    pl.when(z > 0)(lambda: tell(device(z - 1, x, y, c)))
    pl.when(z < 3)(lambda: tell(device(z + 1, x, y, c)))
    pl.semaphore_wait(barrier, 3 + (z > 0).astype(jnp.int32) + (z < 3).astype(jnp.int32))


def lanes(c):
    return pl.ds(pl.multiple_of(c * 384, 128), 384)


def remote(src, dst, send, recv, to):
    return pltpu.make_async_remote_copy(
        src_ref=src, dst_ref=dst, send_sem=send, recv_sem=recv, device_id=to, device_id_type=MESH
    )


def gather_kernel(x_ref, own_ref, xall, wall, mate, merged, mate_sem, local_sem,
                  wsend, wrecv, crecv, xsend, xrecv):
    z, x, y, c = place()
    UP, DOWN, XX, YY, CC = range(5)
    to = {
        UP: device(z + 1, x, y, c),
        DOWN: device(z - 1, x, y, c),
        XX: device(z, 1 - x, y, c),
        YY: device(z, x, 1 - y, c),
        CC: device(z, x, y, 1 - c),
    }
    can = {UP: z < 3, DOWN: z > 0, XX: None, YY: None, CC: None}
    mine, theirs = lanes(c), lanes(1 - c)

    def x_piece(zz, xx):
        return pl.ds(pl.multiple_of((2 * zz + xx) * 256, 256), 256)

    def x_copy(zz, xx, way, src=None):
        i = 2 * zz + xx
        ref = xall.at[:, x_piece(zz, xx), :]
        return remote(ref if src is None else src, ref, xsend.at[i, way], xrecv.at[i], to[way])

    def w_copy(zz, xx, yy, way, src=None):
        i = (2 * zz + xx) * 2 + yy
        ref = wall.at[i, :, mine]
        return remote(ref if src is None else src, ref, wsend.at[i, way],
                      crecv.at[i] if way == CC else wrecv.at[i], to[way])

    def guarded(way, act):
        if can[way] is None:
            act()
        else:
            pl.when(can[way])(act)

    greet(z, x, y, c)
    swap = remote(own_ref.at[:, theirs], mate, mate_sem.at[0], mate_sem.at[1], to[CC])
    swap.start()
    keep_x = pltpu.make_async_copy(x_ref, xall.at[:, x_piece(z, x), :], local_sem.at[0])
    keep_x.start()
    for way in (UP, DOWN, XX):
        guarded(way, lambda way=way: x_copy(z, x, way, x_ref).start())
    swap.wait()
    for seg in range(8):
        here = own_ref[24 * seg:24 * seg + 24, mine]
        there = mate[24 * seg:24 * seg + 24, :]
        pair = jnp.where(c == 0, jnp.concatenate([here, there], 0), jnp.concatenate([there, here], 0))
        merged[48 * seg:48 * seg + 48, :] = pair.astype(BF)
    here, there = own_ref[192:288, mine], mate[192:288, :]
    merged[384:576, :] = jnp.where(
        c == 0, jnp.concatenate([here, there], 0), jnp.concatenate([there, here], 0)
    ).astype(BF)
    merged[576:592, :] = (own_ref[288:304, mine] + mate[288:304, :]).astype(BF)
    keep_w = pltpu.make_async_copy(merged, wall.at[(2 * z + x) * 2 + y, :, mine], local_sem.at[1])
    keep_w.start()
    for way in (UP, DOWN, XX, YY, CC):
        guarded(way, lambda way=way: w_copy(z, x, y, way, merged).start())

    for k in range(1, 4):
        def from_below(k=k):
            x_copy(z - k, x, UP).wait_recv()
            pl.when(z < 3)(lambda: x_copy(z - k, x, UP).start())
            x_copy(z - k, x, XX).start()
            w_copy(z - k, x, y, UP).wait_recv()
            pl.when(z < 3)(lambda: w_copy(z - k, x, y, UP).start())
            for way in (XX, YY, CC):
                w_copy(z - k, x, y, way).start()

        def from_above(k=k):
            x_copy(z + k, x, DOWN).wait_recv()
            pl.when(z > 0)(lambda: x_copy(z + k, x, DOWN).start())
            x_copy(z + k, x, XX).start()
            w_copy(z + k, x, y, DOWN).wait_recv()
            pl.when(z > 0)(lambda: w_copy(z + k, x, y, DOWN).start())
            for way in (XX, YY, CC):
                w_copy(z + k, x, y, way).start()

        pl.when(z >= k)(from_below)
        pl.when(z + k <= 3)(from_above)

    def around(act):
        act(z)
        for k in range(1, 4):
            pl.when(z >= k)(lambda k=k: act(z - k))
            pl.when(z + k <= 3)(lambda k=k: act(z + k))

    def from_x(zz):
        w_copy(zz, 1 - x, y, XX).wait_recv()
        w_copy(zz, 1 - x, y, YY).start()
        w_copy(zz, 1 - x, y, CC).start()

    around(from_x)
    for xx in (x, 1 - x):
        def from_y(zz, xx=xx):
            w_copy(zz, xx, 1 - y, YY).wait_recv()
            w_copy(zz, xx, 1 - y, CC).start()

        around(from_y)
    around(lambda zz: x_copy(zz, 1 - x, XX).wait_recv())

    def from_mate(i, _):
        remote(wall.at[i, :, theirs], wall.at[i, :, theirs], wsend.at[i, CC], crecv.at[i], to[CC]).wait_recv()
        return 0

    lax.fori_loop(0, 16, from_mate, 0)
    keep_x.wait()
    keep_w.wait()
    for k in range(4):
        def z_line(zz, k=k):
            x_copy(zz, x, XX).wait_send()
            for way in (XX, YY, CC):
                w_copy(zz, x, y, way).wait_send()
            w_copy(zz, 1 - x, y, YY).wait_send()
            w_copy(zz, 1 - x, y, CC).wait_send()
            w_copy(zz, x, 1 - y, CC).wait_send()
            w_copy(zz, 1 - x, 1 - y, CC).wait_send()

        z_line(k)
        def ups(k=k):
            x_copy(k, x, UP).wait_send()
            w_copy(k, x, y, UP).wait_send()

        def downs(k=k):
            x_copy(k, x, DOWN).wait_send()
            w_copy(k, x, y, DOWN).wait_send()

        pl.when((k <= z) & (z < 3))(ups)
        pl.when((k >= z) & (z > 0))(downs)


def gather_all(x, own):
    dma = pltpu.SemaphoreType.DMA
    return pl.pallas_call(
        gather_kernel,
        out_shape=[
            jax.ShapeDtypeStruct((x.shape[0], 8 * x.shape[1], x.shape[2]), BF),
            jax.ShapeDtypeStruct((16, PIECE, 768), BF),
        ],
        in_specs=[pl.BlockSpec(memory_space=pl.ANY), pl.BlockSpec(memory_space=pltpu.VMEM)],
        out_specs=[pl.BlockSpec(memory_space=pl.ANY)] * 2,
        scratch_shapes=[
            pltpu.VMEM((ROWS, 384), F32), pltpu.VMEM((PIECE, 384), BF),
            dma((2,)), dma((2,)), dma((16, 5)), dma((16,)), dma((16,)), dma((8, 3)), dma((8,)),
        ],
        compiler_params=pltpu.CompilerParams(
            collective_id=0, has_side_effects=True, vmem_limit_bytes=48 * 2**20
        ),
    )(x, own)


def scatter_kernel(gq, gk, gv, go, gu, gd, gb, dxp, dxo_in,
                   oq, ok, ov, oo, ou, od, ob, odx,
                   acc, mate, yr, xr, zr, dacc, dxr, dzr, fin, snd, rcv, own_dx,
                   lsem, msend, mrecv, ysem, xsem, zsem, dlsem, dxsem, dzsem, fsem):
    z, x, y, c = place()
    mine, theirs = lanes(c), lanes(1 - c)
    near_x, near_y, near_c = device(z, 1 - x, y, c), device(z, x, 1 - y, c), device(z, x, y, 1 - c)
    above, below = device(z + 1, x, y, c), device(z - 1, x, y, c)

    def parts(yy, cc):
        off = pl.multiple_of(cc * 384, 128)
        for i, (ref, start, rows) in enumerate(
            ((gq, 0, 48), (gk, 48, 48), (gv, 96, 48), (go, 144, 48), (gd, 384, 192), (gb, 576, 16))
        ):
            yield i, ref.at[:, yy, :, pl.ds(off, 384)], pl.ds(start, rows)
        for j in range(4):
            col = pl.multiple_of(j * 768 + cc * 384, 128)
            yield 6 + j, gu.at[:, yy, :, pl.ds(col, 384)], pl.ds(192 + 48 * j, 48)

    def far(i):
        return jnp.where(z < 2, 3 - i, i)

    def dx_send(zz):
        return remote(dxp.at[:, pl.ds(pl.multiple_of((2 * zz + 1 - x) * 256, 256), 256), :], dxr.at[zz],
                      dxsem.at[0, zz], dxsem.at[1, zz], near_x)

    greet(z, x, y, c)
    for i in range(4):
        dx_send(far(i)).start()
    locals_, swaps = {}, {}
    for t, yy in enumerate((1 - y, y)):
        for i, src, rows in parts(yy, 1 - c):
            swaps[t, i] = remote(src, mate.at[:, yy, rows, :], msend.at[t, i], mrecv.at[t, i], near_c)
            swaps[t, i].start()
        for i, src, rows in parts(yy, c):
            locals_[t, i] = pltpu.make_async_copy(src, acc.at[:, yy, rows, :], lsem.at[t, i])
            locals_[t, i].start()
    dx_local = []
    for zz in range(4):
        cp = pltpu.make_async_copy(
            dxp.at[:, pl.ds(pl.multiple_of((2 * zz + x) * 256, 256), 256), :], dacc.at[zz], dlsem.at[zz])
        cp.start()
        dx_local.append(cp)
    own_cp = pltpu.make_async_copy(dxo_in, own_dx, dlsem.at[4])
    own_cp.start()

    def y_copy(s):
        return remote(acc.at[s, 1 - y], yr.at[s], ysem.at[0, s], ysem.at[1, s], near_y)

    def x_copy(zz):
        return remote(acc.at[2 * zz + 1 - x, y], xr.at[zz], xsem.at[0, zz], xsem.at[1, zz], near_x)

    def z_copy(zz, way):
        return remote(acc.at[2 * zz + x, y], zr.at[way, zz], zsem.at[0, way, zz], zsem.at[1, way, zz],
                      above if way == 0 else below)

    def dz_copy(zz, way):
        return remote(dacc.at[zz], dzr.at[way, zz], dzsem.at[0, way, zz], dzsem.at[1, way, zz],
                      above if way == 0 else below)

    for i in range(10):
        locals_[0, i].wait()
        swaps[0, i].wait_recv()

    def y_step(i, _):
        s = 2 * far(i % 4) + jnp.where(i < 4, 1 - x, x)
        acc[s, 1 - y] = (acc[s, 1 - y].astype(F32) + mate[s, 1 - y].astype(F32)).astype(BF)
        y_copy(s).start()
        return 0

    lax.fori_loop(0, 8, y_step, 0)
    for i in range(10):
        locals_[1, i].wait()
        swaps[1, i].wait_recv()

    def x_step(i, _):
        zz = far(i)
        s = 2 * zz + 1 - x
        y_copy(s).wait_recv()
        acc[s, y] = (acc[s, y].astype(F32) + mate[s, y].astype(F32) + yr[s].astype(F32)).astype(BF)
        x_copy(zz).start()
        return 0

    lax.fori_loop(0, 4, x_step, 0)
    for cp in dx_local:
        cp.wait()

    def z_step(zz, way, has_more):
        s = 2 * zz + x
        dx_send(zz).wait_recv()
        dacc[zz] = (dacc[zz].astype(F32) + dxr[zz].astype(F32)).astype(BF)

        def more_dx():
            dz_copy(zz, way).wait_recv()
            dacc[zz] = (dacc[zz].astype(F32) + dzr[way, zz].astype(F32)).astype(BF)

        pl.when(has_more)(more_dx)
        dz_copy(zz, way).start()
        y_copy(s).wait_recv()
        x_copy(zz).wait_recv()
        acc[s, y] = (acc[s, y].astype(F32) + mate[s, y].astype(F32) + yr[s].astype(F32)
                     + xr[zz].astype(F32)).astype(BF)

        def more():
            z_copy(zz, way).wait_recv()
            acc[s, y] = (acc[s, y].astype(F32) + zr[way, zz].astype(F32)).astype(BF)

        pl.when(has_more)(more)
        z_copy(zz, way).start()

    for i in range(3):
        pl.when(3 - i > z)(lambda i=i: z_step(3 - i, 0, z > 0))
        pl.when(i < z)(lambda i=i: z_step(i, 1, z < 3))
    s = 2 * z + x
    dx_send(z).wait_recv()
    own_cp.wait()
    odx[...] = own_dx[...] + dacc[z].astype(F32) + dxr[z].astype(F32)
    for way, cond in ((0, z > 0), (1, z < 3)):
        def last_dx(way=way):
            dz_copy(z, way).wait_recv()
            odx[...] += dzr[way, z].astype(F32)

        pl.when(cond)(last_dx)
    y_copy(s).wait_recv()
    x_copy(z).wait_recv()
    fin[...] = acc[s, y].astype(F32) + mate[s, y].astype(F32) + yr[s].astype(F32) + xr[z].astype(F32)
    for way, cond in ((0, z > 0), (1, z < 3)):
        def last(way=way):
            z_copy(z, way).wait_recv()
            fin[...] += zr[way, z].astype(F32)

        pl.when(cond)(last)

    def rows_of(cc):
        for seg in range(8):
            yield 24 * seg, pl.multiple_of(48 * seg + 24 * cc, 8), 24
        yield 192, pl.multiple_of(384 + 96 * cc, 8), 96
        yield 288, 576, 16

    for dst, src, n in rows_of(1 - c):
        snd[pl.ds(dst, n), :] = fin[pl.ds(src, n), :]
    last_swap = remote(snd, rcv, fsem.at[0], fsem.at[1], near_c)
    last_swap.start()
    outs = (oq, ok, ov, oo)

    def put(cols, get):
        for i, out in enumerate(outs):
            out[:, cols] = get(24 * i, 24)

    for (dst, src, n), slot in zip(rows_of(c), range(10)):
        value = fin[pl.ds(src, n), :]
        if slot < 4:
            outs[slot][:, mine] = value
        elif slot < 8:
            ou[:, pl.ds(pl.multiple_of((slot - 4) * 768 + c * 384, 128), 384)] = value
        elif slot == 8:
            od[:, mine] = value
        else:
            ob[:, mine] = value
    last_swap.wait()
    for (dst, src, n), slot in zip(rows_of(c), range(10)):
        value = rcv[pl.ds(dst, n), :]
        if slot < 4:
            outs[slot][:, theirs] = value
        elif slot < 8:
            ou[:, pl.ds(pl.multiple_of((slot - 4) * 768 + (1 - c) * 384, 128), 384)] = value
        elif slot == 8:
            od[:, theirs] = value
        else:
            ob[:, theirs] = value
    for i in range(10):
        swaps[0, i].wait_send()
        swaps[1, i].wait_send()
    for i in range(8):
        y_copy(i).wait_send()
    for i in range(4):
        x_copy(i).wait_send()
        dx_send(i).wait_send()

        def ups(i=i):
            z_copy(i, 0).wait_send()
            dz_copy(i, 0).wait_send()

        def downs(i=i):
            z_copy(i, 1).wait_send()
            dz_copy(i, 1).wait_send()

        pl.when(i > z)(ups)
        pl.when(i < z)(downs)


def scatter_all(gq, gk, gv, go, gu, gd, gb, dxp, own):
    dma = pltpu.SemaphoreType.DMA
    sd = jax.ShapeDtypeStruct
    views = [g.reshape(8, 2, 48, g.shape[-1]) for g in (gq, gk, gv, go, gu)]
    views += [gd.reshape(8, 2, 192, 768), jnp.broadcast_to(gb.astype(BF), (8, 2, 16, 768)), dxp, own]
    mb = own.shape[0]
    v = pltpu.VMEM
    return pl.pallas_call(
        scatter_kernel,
        out_shape=[sd((24, 768), F32)] * 4 + [sd((24, 3072), F32), sd((96, 768), F32), sd((16, 768), F32),
                                              sd(own.shape, F32)],
        in_specs=[pl.BlockSpec(memory_space=pl.ANY)] * 9,
        out_specs=[pl.BlockSpec(memory_space=pltpu.VMEM)] * 8,
        scratch_shapes=[
            v((8, 2, PIECE, 384), BF), v((8, 2, PIECE, 384), BF), v((8, PIECE, 384), BF), v((4, PIECE, 384), BF),
            v((2, 4, PIECE, 384), BF), v((4, mb, 256, 768), BF), v((4, mb, 256, 768), BF),
            v((2, 4, mb, 256, 768), BF), v((PIECE, 384), F32), v((ROWS, 384), F32), v((ROWS, 384), F32),
            v((mb, 256, 768), F32),
            dma((2, 10)), dma((2, 10)), dma((2, 10)), dma((2, 8)), dma((2, 4)), dma((2, 2, 4)), dma((5,)),
            dma((2, 4)), dma((2, 2, 4)), dma((2,)),
        ],
        compiler_params=pltpu.CompilerParams(
            collective_id=1, has_side_effects=True, vmem_limit_bytes=58 * 2**20
        ),
    )(*views)

NS = 2304
CHUNKS = 9


def dot(a, b):
    return lax.dot_general(a, b, (((1,), (0,)), ((), ())), preferred_element_type=F32)


def dot_nt(a, b):
    return lax.dot_general(a, b, (((1,), (1,)), ((), ())), preferred_element_type=F32)


def dot_tn(a, b):
    return lax.dot_general(a, b, (((0,), (0,)), ((), ())), preferred_element_type=F32)


def project_kernel(idx, xall, wall, bias, xs_ref, k_ref, v_ref, q_ref, xs, w, sems, wsem):
    m, i = pl.program_id(0), pl.program_id(1)

    @pl.when((m == 0) & (i == 0))
    def _():
        copy = pltpu.make_async_copy(wall.at[:, pl.ds(0, 144), :], w, wsem)
        copy.start()
        for mm in range(2):
            for cc in range(CHUNKS):
                pieces = [(0, 256)] if cc < 5 else [(0, 128), (128, 128)] if cc == 5 else [(64 * t, 64) for t in range(4)]
                base = cc if cc < 5 else 5 if cc == 5 else 7 + 4 * (cc - 6)
                for t, (off, n) in enumerate(pieces):
                    start = pl.multiple_of(idx[mm, base + t], 64)
                    pltpu.make_async_copy(xall.at[mm, pl.ds(start, n), :], xs.at[mm, cc, pl.ds(off, n), :],
                                          sems.at[mm, cc]).start()
        copy.wait()

    pltpu.make_async_copy(xall.at[0, pl.ds(0, 256), :], xs.at[m, i], sems.at[m, i]).wait()
    rows = xs[m, i]
    xs_ref[0] = rows
    k_ref[0] = dot(rows, w[:, 48:96, :].reshape(768, 768)).astype(BF)
    v_ref[0] = (dot(rows, w[:, 96:144, :].reshape(768, 768)) + bias[1:2, :]).astype(BF)

    @pl.when(i == 2)
    def _():
        q = (dot(rows, w[:, 0:48, :].reshape(768, 768)) + bias[0:1, :]).astype(BF)
        q_ref[0] = q * jnp.asarray(0.125, BF)


def project(idx, xall, wall, bias):
    mb = xall.shape[0]
    sd = jax.ShapeDtypeStruct
    chunk = pl.BlockSpec((1, 256, 768), lambda m, i, t: (m, i, 0))
    return pl.pallas_call(
        project_kernel,
        grid_spec=pltpu.PrefetchScalarGridSpec(
            num_scalar_prefetch=1,
            grid=(mb, CHUNKS),
            in_specs=[pl.BlockSpec(memory_space=pl.ANY)] * 2 + [pl.BlockSpec((16, 768), lambda m, i, t: (0, 0))],
            out_specs=[chunk, chunk, chunk, pl.BlockSpec((1, 256, 768), lambda m, i, t: (m, 0, 0))],
            scratch_shapes=[
                pltpu.VMEM((mb, CHUNKS, 256, 768), BF), pltpu.VMEM((16, 144, 768), BF),
                pltpu.SemaphoreType.DMA((mb, CHUNKS)), pltpu.SemaphoreType.DMA,
            ],
        ),
        out_shape=[sd((mb, NS, 768), BF)] * 3 + [sd((mb, 256, 768), BF)],
        compiler_params=pltpu.CompilerParams(vmem_limit_bytes=48 * 2**20),
    )(idx, xall, wall, bias)


EPS = 1e-6
G0, G1 = 0.7978845608, 0.044715


def norm(v):
    mean = jnp.mean(v, axis=-1, keepdims=True)
    centred = v - mean
    inverse = lax.rsqrt(jnp.mean(centred * centred, axis=-1, keepdims=True) + EPS)
    return centred * inverse, inverse


def norm_back(g, normed, inverse, gain):
    c = g * gain
    return inverse * (c - jnp.mean(c, axis=-1, keepdims=True)
                      - normed * jnp.mean(c * normed, axis=-1, keepdims=True))


def middle_kernel(att, x, cot, wall, bias, out_ref, datt_ref, done_ref, go_ref, gu_ref, gd_ref, gb_ref,
                  w, wsem, pre, hid, mid, low, n1, r1, ffn):
    rows = x.shape[0]
    copies = [
        pltpu.make_async_copy(wall.at[:, pl.ds(144, 48), :], w.at[:, pl.ds(0, 48), :], wsem.at[0]),
        pltpu.make_async_copy(wall.at[:, pl.ds(192, 192), :], w.at[:, pl.ds(48, 192), :], wsem.at[1]),
        pltpu.make_async_copy(wall.at[:, pl.ds(384, 192), :], w.at[:, pl.ds(240, 192), :], wsem.at[2]),
    ]
    for cp in copies:
        cp.start()
    half = rows // 2
    copies[0].wait()
    w_out = w[:, 0:48, :].reshape(768, 768)
    for h in range(2):
        r = pl.ds(h * half, half)
        t = x[r, :].astype(F32) + dot(att[r, :], w_out) + bias[2:3, :]
        normed, inverse = norm(t)
        n1[r, :] = normed
        r1[r, :] = jnp.broadcast_to(inverse, (half, 128))
        value = normed * bias[4:5, :] + bias[5:6, :]
        mid[r, :] = value
        low[r, :] = value.astype(BF)
    ffn[...] = jnp.broadcast_to(bias[3:4, :], ffn.shape)
    copies[1].wait()
    copies[2].wait()

    def up_block(j):
        return w[:, pl.ds(pl.multiple_of(48 + 48 * j, 16), 48), :].reshape(768, 768)

    def down_block(j):
        return w[pl.ds(4 * j, 4), 240:432, :].reshape(768, 768)

    def forward(j, _):
        wu, wd = up_block(j), down_block(j)
        for h in range(2):
            r = pl.ds(h * half, half)
            u = dot(low[r, :], wu) + bias[pl.ds(8 + j, 1), :]
            pre[j, r, :] = u
            g = (0.5 * u * (1.0 + jnp.tanh(G0 * (u + G1 * u * u * u)))).astype(BF)
            hid[j, r, :] = g
            ffn[r, :] += dot(g, wd)
        return 0

    lax.fori_loop(0, 4, forward, 0)
    gb_ref[...] = jnp.zeros_like(gb_ref)
    for h in range(2):
        r = pl.ds(h * half, half)
        normed, inverse = norm(mid[r, :] + ffn[r, :])
        out_ref[r, :] = (normed * bias[6:7, :] + bias[7:8, :]).astype(BF)
        g = cot[r, :].astype(F32)
        gb_ref[6:7, :] += jnp.sum(g * normed, axis=0, keepdims=True)
        gb_ref[7:8, :] += jnp.sum(g, axis=0, keepdims=True)
        d_two = norm_back(g, normed, inverse, bias[6:7, :])
        mid[r, :] = d_two
        d_ffn = d_two.astype(BF)
        datt_ref[r, :] = d_ffn
        gb_ref[3:4, :] += jnp.sum(d_ffn.astype(F32), axis=0, keepdims=True)

    def backward(j, _):
        wu, wd = up_block(j), down_block(j)
        d_ffn = datt_ref[...]
        gd_ref[pl.ds(pl.multiple_of(j * 768, 768), 768), :] = dot_tn(hid[j], d_ffn).astype(BF)
        for h in range(2):
            r = pl.ds(h * half, half)
            u = pre[j, r, :]
            th = jnp.tanh(G0 * (u + G1 * u * u * u))
            slope = 0.5 * (1.0 + th) + 0.5 * u * (1.0 - th * th) * (G0 * (1.0 + 3.0 * G1 * u * u))
            d_pre = (dot_nt(datt_ref[r, :], wd) * slope).astype(BF)
            hid[j, r, :] = d_pre
            gb_ref[pl.ds(8 + j, 1), :] += jnp.sum(d_pre.astype(F32), axis=0, keepdims=True)
            mid[r, :] += dot_nt(d_pre, wu)
        gu_ref[:, pl.ds(pl.multiple_of(j * 768, 768), 768)] = dot_tn(low[...], hid[j]).astype(BF)
        return 0

    lax.fori_loop(0, 4, backward, 0)
    for h in range(2):
        r = pl.ds(h * half, half)
        d_mid, normed = mid[r, :], n1[r, :]
        gb_ref[4:5, :] += jnp.sum(d_mid * normed, axis=0, keepdims=True)
        gb_ref[5:6, :] += jnp.sum(d_mid, axis=0, keepdims=True)
        d_one = norm_back(d_mid, normed, r1[r, 0:1], bias[4:5, :])
        done_ref[r, :] = d_one
        d_branch = d_one.astype(BF)
        low[r, :] = d_branch
        gb_ref[2:3, :] += jnp.sum(d_branch.astype(F32), axis=0, keepdims=True)
        datt_ref[r, :] = dot_nt(d_branch, w_out).astype(BF)
    go_ref[...] = dot_tn(att[...], low[...]).astype(BF)


def middle(att, x, cot, wall, bias):
    rows = x.shape[0]
    sd = jax.ShapeDtypeStruct
    vm = pl.BlockSpec(memory_space=pltpu.VMEM)
    return pl.pallas_call(
        middle_kernel,
        in_specs=[vm, vm, vm, pl.BlockSpec(memory_space=pl.ANY), vm],
        out_specs=[vm] * 7,
        out_shape=[sd((rows, 768), BF), sd((rows, 768), BF), sd((rows, 768), F32), sd((768, 768), BF),
                   sd((768, 3072), BF), sd((3072, 768), BF), sd((16, 768), F32)],
        scratch_shapes=[
            pltpu.VMEM((16, 432, 768), BF), pltpu.SemaphoreType.DMA((3,)),
            pltpu.VMEM((4, rows, 768), F32), pltpu.VMEM((4, rows, 768), BF),
            pltpu.VMEM((rows, 768), F32), pltpu.VMEM((rows, 768), BF), pltpu.VMEM((rows, 768), F32),
            pltpu.VMEM((rows, 128), F32), pltpu.VMEM((rows, 768), F32),
        ],
        compiler_params=pltpu.CompilerParams(vmem_limit_bytes=60 * 2**20),
    )(att, x, cot, wall, bias)


def back_kernel(scattered, idx, xs_ref, dk_ref, dv_ref, dq_ref, done_ref, wall, gb_in, dx_ref, own_ref, gq_ref, gk_ref, gv_ref, gb_ref,
                w, wsem, acc, aq, ak, av):
    m, i = pl.program_id(0), pl.program_id(1)

    @pl.when((m == 0) & (i == 0))
    def _():
        copy = pltpu.make_async_copy(wall.at[:, pl.ds(0, 144), :], w, wsem)
        copy.start()
        acc[...] = jnp.zeros_like(acc)
        aq[...] = jnp.zeros_like(aq)
        ak[...] = jnp.zeros_like(ak)
        av[...] = jnp.zeros_like(av)
        gb_ref[...] = gb_in[...]
        copy.wait()

    rows, dk, dv = xs_ref[0], dk_ref[0], dv_ref[0]
    ak[...] += dot_tn(rows, dk)
    av[...] += dot_tn(rows, dv)
    gb_ref[1:2, :] += jnp.sum(dv.astype(F32), axis=0, keepdims=True)
    dx = dot_nt(dk, w[:, 48:96, :].reshape(768, 768)) + dot_nt(dv, w[:, 96:144, :].reshape(768, 768))

    def add(slot, off, n):
        start = pl.multiple_of(idx[m, slot], 64)
        acc[m, pl.ds(start, n), :] += dx[off:off + n]

    if not scattered:
        dx_ref[0] = jnp.where(i == 2, jnp.zeros_like(dx), dx).astype(BF)

    @pl.when((i < 5) & (i != 2) & scattered)
    def _():
        add(jnp.minimum(i, 4), 0, 256)

    @pl.when((i == 5) & scattered)
    def _():
        add(5, 0, 128)
        add(6, 128, 128)

    @pl.when((i > 5) & scattered)
    def _():
        for t in range(4):
            add(7 + 4 * (i - 6) + t, 64 * t, 64)

    @pl.when(i == 2)
    def _():
        dq = dq_ref[0]
        aq[...] += dot_tn(rows, dq)
        gb_ref[0:1, :] += jnp.sum(dq.astype(F32), axis=0, keepdims=True)
        own_ref[0] = dx + done_ref[0] + dot_nt(dq, w[:, 0:48, :].reshape(768, 768))

    @pl.when((i == CHUNKS - 1) & scattered)
    def _():
        dx_ref[m if scattered else 0] = acc[m].astype(BF)

    @pl.when((m == 1) & (i == CHUNKS - 1))
    def _():
        gq_ref[...] = aq[...].astype(BF)
        gk_ref[...] = ak[...].astype(BF)
        gv_ref[...] = av[...].astype(BF)


def back(idx, xs, dk, dv, dq, done, wall, gb, seq_len):
    mb = xs.shape[0]
    sd = jax.ShapeDtypeStruct
    chunk = pl.BlockSpec((1, 256, 768), lambda m, i, t: (m, i, 0))
    one = pl.BlockSpec((1, 256, 768), lambda m, i, t: (m, 0, 0))
    whole = lambda *s: pl.BlockSpec(s, lambda m, i, t: (0,) * len(s))
    scattered = seq_len > 0
    held = seq_len if scattered else 256
    return pl.pallas_call(
        functools.partial(back_kernel, scattered),
        grid_spec=pltpu.PrefetchScalarGridSpec(
            num_scalar_prefetch=1,
            grid=(mb, CHUNKS),
            in_specs=[chunk, chunk, chunk, one, one, pl.BlockSpec(memory_space=pl.ANY), whole(16, 768)],
            out_specs=[whole(mb, seq_len, 768) if scattered else chunk, one, whole(768, 768), whole(768, 768), whole(768, 768), whole(16, 768)],
            scratch_shapes=[
                pltpu.VMEM((16, 144, 768), BF), pltpu.SemaphoreType.DMA, pltpu.VMEM((mb, held, 768), F32),
                pltpu.VMEM((768, 768), F32), pltpu.VMEM((768, 768), F32), pltpu.VMEM((768, 768), F32),
            ],
        ),
        out_shape=[sd((mb, seq_len if scattered else NS, 768), BF), sd((mb, 256, 768), F32), sd((768, 768), BF), sd((768, 768), BF),
                   sd((768, 768), BF), sd((16, 768), F32)],
        compiler_params=pltpu.CompilerParams(vmem_limit_bytes=60 * 2**20),
    )(idx, xs, dk, dv, dq, done, wall, gb)
HALF=128; WK=1152; NW=1280; NK=1664; NS=2304
def key_rows(h):
    return ((HALF*h,WK),(NW+HALF*h,HALF),(NW+2*HALF+384*h,384))
def cat_rows(ref,h):
    return jnp.concatenate([ref[0,pl.ds(a,n),:] for a,n in key_rows(h)],axis=0)
def split_heads(v):
    lane=lax.broadcasted_iota(jnp.int32,v.shape,1)
    z=jnp.zeros_like(v)
    return jnp.concatenate([jnp.where(lane<64,v,z),jnp.where(lane>=64,v,z)],axis=0)
def merge_heads(v):
    n=v.shape[0]//2
    lane=lax.broadcasted_iota(jnp.int32,(n,v.shape[1]),1)
    return jnp.where(lane<64,v[:n],v[n:])
def ind_ext(n):
    r=lax.broadcasted_iota(jnp.int32,(2*n,128),0); l=lax.broadcasted_iota(jnp.int32,(2*n,128),1)
    first=(r%n)<64
    return jnp.where(((l==0)&first)|((l==1)&jnp.logical_not(first)),1.0,0.0)
def ext3(base,col):
    l=lax.broadcasted_iota(jnp.int32,base.shape,1)
    hi=col.astype(BF).astype(F32); r=col-hi; mi=r.astype(BF).astype(F32); lo=r-mi
    return jnp.where(l==2,hi,jnp.where(l==3,mi,jnp.where(l==4,lo,base))).astype(BF)
def fwd_kernel(q_ref,k_ref,v_ref,me_ref,o_ref,l_ref):
    p=pl.program_id(1)
    ind=ind_ext(HALF).astype(BF)
    for h in range(2):
        me=me_ref[0,h]
        qe=jnp.concatenate([split_heads(q_ref[0,pl.ds(h*HALF,HALF),:]),ind],axis=1)
        ke=jnp.concatenate([cat_rows(k_ref,h),me],axis=1)
        s=dot_nt(qe,ke)
        top=jnp.max(s,axis=1,keepdims=True)
        e=jnp.exp(s-top).astype(BF)
        ve=jnp.concatenate([cat_rows(v_ref,h),me],axis=1)
        o=dot(e,ve)
        tot=o[:,130:131]
        o_ref[0,pl.ds(h*HALF,HALF),:]=merge_heads(o[:,:128]/tot).astype(BF)
        l_ref[0,0,pl.ds(h*256,256),:]=jnp.broadcast_to(top+jnp.log(tot),(256,128))
def attn_fwd(q,k,v,me):
    mb=q.shape[0]; npair=q.shape[2]//128
    return pl.pallas_call(fwd_kernel,grid=(mb,npair),
      in_specs=[pl.BlockSpec((1,256,128),lambda m,p:(m,0,p)),pl.BlockSpec((1,NS,128),lambda m,p:(m,0,p)),pl.BlockSpec((1,NS,128),lambda m,p:(m,0,p)),
        pl.BlockSpec((1,2,NK,128),lambda m,p:(m,0,0,0))],
      out_specs=[pl.BlockSpec((1,256,128),lambda m,p:(m,0,p)),pl.BlockSpec((1,1,512,128),lambda m,p:(m,p,0,0))],
      out_shape=[jax.ShapeDtypeStruct(q.shape,BF),jax.ShapeDtypeStruct((mb,npair,512,128),F32)],
      compiler_params=pltpu.CompilerParams(vmem_limit_bytes=56*2**20))(q,k,v,me)
def bwd_kernel(CH,q_ref,k_ref,v_ref,me_ref,o_ref,do_ref,l_ref,dq_ref,dk_ref,dv_ref,dka,dva):
    ind=ind_ext(HALF)
    zero=jnp.zeros_like(ind)
    dka[...]=jnp.zeros_like(dka); dva[...]=jnp.zeros_like(dva)
    for h in range(2):
        rows=pl.ds(h*HALF,HALF)
        qs=split_heads(q_ref[0,rows,:])
        do2=do_ref[0,rows,:]
        dos=split_heads(do2)
        o2=o_ref[0,rows,:].astype(F32)
        delta=jnp.sum(dos.astype(F32)*jnp.concatenate([o2,o2],axis=0),axis=1,keepdims=True)
        lse=l_ref[0,0,pl.ds(h*256,256),0:1]
        qe=jnp.concatenate([qs,ext3(ind,-lse)],axis=1)
        doe=jnp.concatenate([dos,ext3(zero,-delta)],axis=1)
        dqt=jnp.zeros((128,256),F32)
        off=0
        for a,n in key_rows(h):
            c0=0
            while c0<n:
                c=min(CH,n-c0)
                kr=pl.ds(a+c0,c)
                k2=k_ref[0,kr,:]; v2=v_ref[0,kr,:]; me=me_ref[0,h,pl.ds(off+c0,c),:]
                st=dot_nt(jnp.concatenate([k2,me],axis=1),qe)
                pt=jnp.exp(st)
                dpt=dot_nt(jnp.concatenate([v2,me],axis=1),doe)
                ds=(pt*dpt).astype(BF)
                dva[kr,:]+=dot(pt.astype(BF),dos)
                dka[kr,:]+=dot(ds,qs)
                dqt=dqt+dot(k2.T,ds)
                c0+=c
            off+=n
        dq_ref[0,rows,:]=(merge_heads(dqt.T)*0.125).astype(BF)
    dk_ref[0]=dka[...].astype(BF); dv_ref[0]=dva[...].astype(BF)
def attn_bwd(q,k,v,me,o,do,l,CH=384):
    mb=q.shape[0]; npair=q.shape[2]//128
    qs=pl.BlockSpec((1,256,128),lambda m,p:(m,0,p)); ks=pl.BlockSpec((1,NS,128),lambda m,p:(m,0,p))
    return pl.pallas_call(functools.partial(bwd_kernel,CH),grid=(mb,npair),
      in_specs=[qs,ks,ks,pl.BlockSpec((1,2,NK,128),lambda m,p:(m,0,0,0)),qs,qs,pl.BlockSpec((1,1,512,128),lambda m,p:(m,p,0,0))],
      out_specs=[qs,ks,ks],
      out_shape=[jax.ShapeDtypeStruct(q.shape,BF),jax.ShapeDtypeStruct(k.shape,BF),jax.ShapeDtypeStruct(k.shape,BF)],
      scratch_shapes=[pltpu.VMEM((NS,128),F32)]*2,
      compiler_params=pltpu.CompilerParams(vmem_limit_bytes=56*2**20))(q,k,v,me,o,do,l)


BLK = 64
WIN = 8
RAND = 3
ALL = ("seq", "batch")


def own_rows(wq, wk, wv, wo, wu, wd, vectors, b_up, owner, owners):
    width = wq.shape[1]
    lane = jnp.arange(width, dtype=jnp.int32)
    n = vectors[0].shape[0]
    table = jnp.stack(vectors).astype(F32)
    table = jnp.where(lane // n == owner, jnp.tile(table, (1, width // n)), 0.0)
    m = b_up.shape[0]
    flat = jnp.arange(4 * width, dtype=jnp.int32)
    ups = jnp.where(flat // m == owner, jnp.tile(b_up.astype(F32), 4 * width // m), 0.0).reshape(4, width)
    up = wu.reshape(wu.shape[0], 4, width).transpose(1, 0, 2).reshape(-1, width)
    rows = jnp.concatenate([wq, wk, wv, wo, up, wd], axis=0).astype(F32)
    return rows, jnp.concatenate([table, ups, jnp.zeros((4, width), F32)], axis=0)


def block_plan(lengths, randoms, device, blocks):
    ends = jnp.cumsum(lengths, axis=1)
    starts = ends - lengths

    def doc_of(block):
        at = block * BLK
        shape = (lengths.shape[0],) + (1,) * (block.ndim - 1) + (lengths.shape[1],)
        doc = jnp.sum((ends.reshape(shape) <= at[..., None]).astype(jnp.int32), axis=-1)
        doc = jnp.minimum(doc, lengths.shape[1] - 1)
        hit = jnp.arange(lengths.shape[1], dtype=jnp.int32) == doc[..., None]
        return doc, jnp.sum(jnp.where(hit, starts.reshape(shape), 0), axis=-1)

    mb = lengths.shape[0]
    half = jnp.arange(2, dtype=jnp.int32)
    query = device * 4 + 2 * half[:, None] + half[None, :]
    query = jnp.broadcast_to(query[None], (mb, 2, 2))
    q_doc, q_first = doc_of(query)
    window = device * 4 + 2 * half[:, None] - WIN + jnp.arange(2 * WIN + 2, dtype=jnp.int32)[None, :]
    window = jnp.broadcast_to(window[None], (mb, 2, 2 * WIN + 2))
    w_doc, w_first = doc_of(jnp.clip(window, 0, blocks - 1))
    w_good = (window >= 0) & (window < blocks) & (window * BLK - w_first >= 2 * BLK)
    see_window = (
        w_good[:, :, None, :]
        & (w_doc[:, :, None, :] == q_doc[..., None])
        & (jnp.abs(window[:, :, None, :] - query[..., None]) <= WIN)
    )
    see_glob = jnp.ones((mb, 2, 2, 2), bool)
    named = lax.dynamic_slice_in_dim(randoms, device * 4, 4, 1).reshape(mb, 2, 2, RAND)
    r_doc, r_first = doc_of(named)
    r_good = (
        (r_doc == q_doc[..., None])
        & (jnp.abs(named - query[..., None]) > WIN)
        & (named * BLK - r_first >= 2 * BLK)
    )
    see_random = (r_good[:, :, None] & jnp.eye(2, dtype=bool)[None, None, :, :, None]).reshape(mb, 2, 2, 2 * RAND)
    see = jnp.concatenate([see_window, see_glob, see_random], axis=3)
    bias = jnp.where(see, 0.0, -1e30).astype(BF)
    bias = jnp.broadcast_to(bias[..., None], bias.shape + (BLK,)).reshape(mb, 2, 2, -1, 1)
    lane = jnp.arange(128, dtype=jnp.int32)
    extra = jnp.where(
        lane == 0, bias[:, :, 0], jnp.where(lane == 1, bias[:, :, 1], jnp.where(lane < 5, 1.0, 0.0).astype(BF))
    )
    chunk = jnp.clip(device + jnp.arange(-2, 3, dtype=jnp.int32), 0, blocks // 4 - 1) * (4 * BLK)
    where = jnp.concatenate(
        [jnp.broadcast_to(chunk[None], (mb, 5)), q_first[:, :, 0], named.reshape(mb, -1) * BLK], axis=1
    )
    return where.astype(jnp.int32), extra


def on_device(inputs, cotangent, doc_lengths, random_blocks, wq, wk, wv, wo, wu, wd, b_query, b_value, b_out,
              b_up, b_down, gain_attn, bias_attn, gain_ffn, bias_ffn):
    mb, _, rows, width = inputs.shape
    devices, owners = lax.axis_size("seq"), lax.axis_size("seq") * lax.axis_size("batch")
    device = lax.axis_index("seq")
    owner = device * lax.axis_size("batch") + lax.axis_index("batch")
    linked = devices == 8 and owners == 32
    seq_len = devices * rows
    x, cot = inputs[:, 0], cotangent[:, 0]
    where, extra = block_plan(doc_lengths[:, 0], random_blocks[:, 0], device, seq_len // BLK)
    vectors = (b_query, b_value, b_out, b_down, gain_attn, bias_attn, gain_ffn, bias_ffn)
    packed, table = own_rows(wq, wk, wv, wo, wu, wd, vectors, b_up, owner, owners)
    if linked:
        xall, wall = gather_all(x, jnp.concatenate([packed, table], axis=0))
        bias = jnp.sum(wall[:, 576:592, :].astype(F32), axis=0)
    else:
        xall = lax.all_gather(x, "seq", axis=1, tiled=True)
        bias = lax.psum(table, ALL)
        full = [lax.all_gather(w, ALL, axis=0, tiled=True) for w in (wq, wk, wv, wo, wu, wd)]
        up = full[4].reshape(16, 48, 4, width).transpose(0, 2, 1, 3).reshape(16, 192, width)
        wall = jnp.concatenate(
            [w.reshape(16, 48, width) for w in full[:4]] + [up, full[5].reshape(16, 192, width),
                                                           jnp.zeros((16, 16, width), BF)], axis=1)
    xs, k, v, q = project(where, xall, wall, bias)
    att, lse = attn_fwd(q, k, v, extra)
    flat = lambda t: t.reshape(-1, t.shape[-1])
    out, datt, done, go, gu, gd, gb = middle(flat(att), flat(x), flat(cot), wall, bias)
    dq, dk, dv = attn_bwd(q, k, v, extra, att, datt.reshape(att.shape), lse, 640)
    done = done.reshape(mb, rows, width)
    if linked:
        dxp, own, gq, gk, gv, gb = back(where, xs, dk, dv, dq, done, wall, gb, seq_len)
        *grads, gb, dx = scatter_all(gq, gk, gv, go, gu, gd, gb, dxp, own)
    else:
        dxs, own, gq, gk, gv, gb = back(where, xs, dk, dv, dq, done, wall, gb, 0)
        start = jnp.concatenate([where[:, :5, None] + jnp.arange(0, 256, BLK), ], axis=1).reshape(mb, -1)
        glob = (where[:, 5:7, None] + jnp.arange(0, 128, BLK)).reshape(mb, -1)
        to = jnp.concatenate([start, glob, where[:, 7:]], axis=1) // BLK
        parts = dxs.reshape(mb, -1, BLK, width)
        total = jnp.zeros((mb, seq_len // BLK, BLK, width), F32)
        total = jax.vmap(lambda t, i, p: t.at[i].add(p))(total, to, parts.astype(F32))
        dx = own + lax.psum_scatter(total.reshape(mb, seq_len, width), "seq", scatter_dimension=1, tiled=True)
        grads = [lax.psum_scatter(g.astype(F32), ALL, scatter_dimension=0, tiled=True) for g in (gq, gk, gv, go, gu, gd)]
        gb = lax.psum(gb, ALL)
    n, m = b_query.shape[0], b_up.shape[0]
    small = lax.dynamic_slice_in_dim(gb[:8], owner * n, n, 1)
    ups = lax.dynamic_slice_in_dim(gb[8:12].reshape(-1), owner * m, m, 0)
    return (
        out.reshape(inputs.shape), dx[:, None], *grads,
        small[0], small[1], small[2], ups, small[3], small[4], small[5], small[6], small[7],
    )


def solution(mesh):
    tokens = P(None, "batch", "seq", None)
    mat, vec = P(ALL, None), P(ALL)
    in_specs = (tokens, tokens, P(None, "batch", None), P(None, "batch", None, None)) + (mat,) * 6 + (vec,) * 9
    out_specs = (tokens, tokens) + (mat,) * 6 + (vec,) * 9
    return jax.shard_map(on_device, mesh=mesh, in_specs=in_specs, out_specs=out_specs, check_vma=False)
```

```python
import functools

import jax
import jax.numpy as jnp
from jax import lax
from jax.experimental import pallas as pl
from jax.experimental.pallas import tpu as pltpu
from jax.sharding import PartitionSpec as P

F32 = jnp.float32
BF = jnp.bfloat16


HALF, WK, NW, NK, NS = 128, 1152, 1280, 1664, 2304
TOP, REST = 160, 432
MESH = pl.DeviceIdType.MESH
UP, DOWN, XX, YY, CC = range(5)
WAYS = (UP, DOWN, XX, YY, CC)


def dot(a, b):
    return lax.dot_general(a, b, (((1,), (0,)), ((), ())), preferred_element_type=F32)


def dot_nt(a, b):
    return lax.dot_general(a, b, (((1,), (1,)), ((), ())), preferred_element_type=F32)


def dot_tn(a, b):
    return lax.dot_general(a, b, (((0,), (0,)), ((), ())), preferred_element_type=F32)


def place():
    s, b = lax.axis_index("seq"), lax.axis_index("batch")
    return s // 2, s % 2, b // 2, b % 2


def device(z, x, y, c):
    return (2 * z + x, 2 * y + c)


def greet(z, x, y, c):
    barrier = pltpu.get_barrier_semaphore()

    def tell(to):
        pl.semaphore_signal(barrier, inc=1, device_id=to, device_id_type=MESH)

    tell(device(z, 1 - x, y, c))
    tell(device(z, x, 1 - y, c))
    tell(device(z, x, y, 1 - c))
    pl.when(z > 0)(lambda: tell(device(z - 1, x, y, c)))
    pl.when(z < 3)(lambda: tell(device(z + 1, x, y, c)))
    pl.semaphore_wait(barrier, 3 + (z > 0).astype(jnp.int32) + (z < 3).astype(jnp.int32))


def lanes(c):
    return pl.ds(pl.multiple_of(c * 384, 128), 384)


def rows_at(i, n):
    return pl.ds(pl.multiple_of(i * n, n), n)


def remote(src, dst, send, recv, to):
    return pltpu.make_async_remote_copy(
        src_ref=src, dst_ref=dst, send_sem=send, recv_sem=recv, device_id=to, device_id_type=MESH
    )


def key_rows(h):
    return ((HALF * h, WK), (NW + HALF * h, HALF), (NW + 2 * HALF + 384 * h, 384))


def split_heads(v):
    lane = lax.broadcasted_iota(jnp.int32, v.shape, 1)
    z = jnp.zeros_like(v)
    return jnp.concatenate([jnp.where(lane < 64, v, z), jnp.where(lane >= 64, v, z)], axis=0)


def merge_heads(v):
    n = v.shape[0] // 2
    lane = lax.broadcasted_iota(jnp.int32, (n, v.shape[1]), 1)
    return jnp.where(lane < 64, v[:n], v[n:])


def block_columns():
    r = lax.broadcasted_iota(jnp.int32, (2 * HALF, 128), 0)
    lane = lax.broadcasted_iota(jnp.int32, (2 * HALF, 128), 1)
    first = (r % HALF) < 64
    return jnp.where(((lane == 0) & first) | ((lane == 1) & jnp.logical_not(first)), 1.0, 0.0)


def with_column(base, col):
    lane = lax.broadcasted_iota(jnp.int32, base.shape, 1)
    hi = col.astype(BF).astype(F32)
    rest = col - hi
    mid = rest.astype(BF).astype(F32)
    return jnp.where(lane == 2, hi, jnp.where(lane == 3, mid, jnp.where(lane == 4, rest - mid, base))).astype(BF)


def write_extra(see, extra):
    lane = lax.broadcasted_iota(jnp.int32, (64, 128), 1)
    ones = jnp.where((lane >= 2) & (lane < 5), 1.0, 0.0)

    def one(i, _):
        m, h, t = i // 52, (i // 26) % 2, i % 26
        value = jnp.where(lane == 0, see[m, h, 0, t], jnp.where(lane == 1, see[m, h, 1, t], ones))
        extra[m, h, rows_at(t, 64), :] = value.astype(BF)
        return 0

    lax.fori_loop(0, 104, one, 0)


def forward_kernel(idx, see, x_ref, wq, wk, wv, wo, wu, wd, table,
                   att, lse, q_out, xs_out, k_out, v_out, wall, top_out, bias,
                   own, mate, merged, merged_b, xall0, xall1, xs, ks, vs, wa, extra,
                   mate_sem, lsem, osem, asend, arecv, acrecv, bsend, brecv, bcrecv, xsend, xrecv):
    z, x, y, c = place()
    s = 2 * z + x
    to = {UP: device(z + 1, x, y, c), DOWN: device(z - 1, x, y, c), XX: device(z, 1 - x, y, c),
          YY: device(z, x, 1 - y, c), CC: device(z, x, y, 1 - c)}
    mine, theirs = lanes(c), lanes(1 - c)
    xall = (xall0, xall1)

    def guarded(way, act):
        if way == UP:
            pl.when(z < 3)(act)
        elif way == DOWN:
            pl.when(z > 0)(act)
        else:
            act()

    def x_copy(m, zz, xx, way, own_rows=False):
        i = 2 * zz + xx
        ref = xall[m].at[pl.ds(4 * i, 4)]
        return remote(x_ref.at[m] if own_rows else ref, ref, xsend.at[m, i, way], xrecv.at[m, i], to[way])

    def a_copy(zz, xx, yy, way, src=None):
        i = (2 * zz + xx) * 2 + yy
        ref = wa.at[i, :, mine]
        return remote(ref if src is None else src, ref, asend.at[i, way],
                      acrecv.at[i] if way == CC else arecv.at[i], to[way])

    def b_copy(zz, xx, yy, way, src=None):
        i = (2 * zz + xx) * 2 + yy
        ref = wall.at[i, :, mine]
        return remote(ref if src is None else src, ref, bsend.at[i, way],
                      bcrecv.at[i] if way == CC else brecv.at[i], to[way])

    greet(z, x, y, c)
    for way in (UP, DOWN, XX):
        guarded(way, lambda way=way: x_copy(0, z, x, way, True).start())
    for m in range(2):
        pltpu.make_async_copy(x_ref.at[m], xall[m].at[pl.ds(4 * s, 4)], lsem.at[m]).start()
    own[0:16, :] = table[...]
    for i, ref in enumerate((wq, wk, wv, wo)):
        own[16 + 24 * i:40 + 24 * i, :] = ref[...].astype(F32)
    for j in range(4):
        own[112 + 24 * j:136 + 24 * j, :] = wu[:, 768 * j:768 * j + 768].astype(F32)
    own[208:304, :] = wd[...].astype(F32)
    swap = remote(own.at[:, theirs], mate, mate_sem.at[0], mate_sem.at[1], to[CC])
    swap.start()
    swap.wait()

    def paired(start, n):
        here, there = own[start:start + n, mine], mate[start:start + n, :]
        return jnp.where(c == 0, jnp.concatenate([here, there], 0), jnp.concatenate([there, here], 0)).astype(BF)

    merged[0:16, :] = (own[0:16, mine] + mate[0:16, :]).astype(BF)
    for i in range(3):
        merged[16 + 48 * i:64 + 48 * i, :] = paired(16 + 24 * i, 24)
    keep_a = pltpu.make_async_copy(merged, wa.at[s * 2 + y, :, mine], lsem.at[2])
    keep_a.start()
    for way in WAYS:
        guarded(way, lambda way=way: a_copy(z, x, y, way, merged).start())
    for i in range(5):
        merged_b[48 * i:48 * i + 48, :] = paired(88 + 24 * i, 24)
    merged_b[240:432, :] = paired(208, 96)
    b_copy(z, x, y, YY, merged_b).start()
    b_copy(z, x, y, CC, merged_b).start()
    keep_b = pltpu.make_async_copy(merged_b, wall.at[s * 2 + y, :, mine], lsem.at[3])
    keep_b.start()
    write_extra(see, extra)

    def x_line(m, k, a=True):
        def below():
            x_copy(m, z - k, x, UP).wait_recv()
            pl.when(z < 3)(lambda: x_copy(m, z - k, x, UP).start())
            x_copy(m, z - k, x, XX).start()

        def above():
            x_copy(m, z + k, x, DOWN).wait_recv()
            pl.when(z > 0)(lambda: x_copy(m, z + k, x, DOWN).start())
            x_copy(m, z + k, x, XX).start()

        pl.when((z >= k) & (k <= 3))(below)
        pl.when(z + k <= 3)(above)

    def w_line(copy, k):
        def below():
            copy(z - k, x, y, UP).wait_recv()
            pl.when(z < 3)(lambda: copy(z - k, x, y, UP).start())
            for way in (XX, YY, CC):
                copy(z - k, x, y, way).start()

        def above():
            copy(z + k, x, y, DOWN).wait_recv()
            pl.when(z > 0)(lambda: copy(z + k, x, y, DOWN).start())
            for way in (XX, YY, CC):
                copy(z + k, x, y, way).start()

        pl.when((z >= k) & (k <= 3))(below)
        pl.when(z + k <= 3)(above)

    def at_distance(act, k):
        pl.when((k >= 0) & (k <= z))(lambda: act(z - k))
        pl.when((k > 0) & (z + k <= 3))(lambda: act(z + k))

    def w_from_x(copy, k):
        def act(zz):
            copy(zz, 1 - x, y, XX).wait_recv()
            copy(zz, 1 - x, y, YY).start()
            copy(zz, 1 - x, y, CC).start()

        at_distance(act, k)

    def w_from_y(copy, xx, k):
        def act(zz):
            copy(zz, xx, 1 - y, YY).wait_recv()
            copy(zz, xx, 1 - y, CC).start()

        at_distance(act, k)

    zfirst = c == 0

    def b_own_column(k):
        def passed(zz, way, more):
            b_copy(zz, x, y, way).wait_recv()
            pl.when(more)(lambda: b_copy(zz, x, y, way).start())
            b_copy(zz, x, y, YY).start()
            b_copy(zz, x, y, CC).start()

        pl.when((z >= k) & (k <= 3))(lambda: passed(z - k, UP, z < 3))
        pl.when(z + k <= 3)(lambda: passed(z + k, DOWN, z > 0))

    def b_to_x(k):
        def across(zz):
            b_copy(zz, x, y, XX).start()

        pl.when(zfirst)(lambda: at_distance(across, k))

    def b_other_column(k):
        def shared(zz):
            b_copy(zz, 1 - x, y, YY).start()
            b_copy(zz, 1 - x, y, CC).start()

        def crossed(zz):
            b_copy(zz, 1 - x, y, XX).wait_recv()
            shared(zz)

        def passed(zz, way, more):
            b_copy(zz, 1 - x, y, way).wait_recv()
            pl.when(more)(lambda: b_copy(zz, 1 - x, y, way).start())
            shared(zz)

        def first():
            crossed(z)
            pl.when(jnp.logical_not(zfirst) & (z < 3))(lambda: b_copy(z, 1 - x, y, UP).start())
            pl.when(jnp.logical_not(zfirst) & (z > 0))(lambda: b_copy(z, 1 - x, y, DOWN).start())

        def later():
            pl.when(zfirst)(lambda: at_distance(crossed, k))
            pl.when(jnp.logical_not(zfirst) & (z >= k))(lambda: passed(z - k, UP, z < 3))
            pl.when(jnp.logical_not(zfirst) & (z + k <= 3))(lambda: passed(z + k, DOWN, z > 0))

        pl.when(k == 0)(first)
        pl.when((k > 0) & (k <= 3))(later)

    def start_x1(way):
        guarded(way, lambda: x_copy(1, z, x, way, True).start())

    def start_relay(k, _):
        x_line(0, k)
        w_line(a_copy, k)
        w_from_x(a_copy, k - 1)

        @pl.when(k == 2)
        def _():
            start_x1(UP)
            start_x1(DOWN)
            for way in (UP, DOWN):
                guarded(way, lambda way=way: b_copy(z, x, y, way, merged_b).start())

        return 0

    lax.fori_loop(1, 4, start_relay, 0)
    start_x1(XX)
    w_from_x(a_copy, 3)
    x_line(1, 1)
    b_copy(z, x, y, XX, merged_b).start()
    for xx in (x, 1 - x):
        lax.fori_loop(0, 4, lambda k, _, xx=xx: (w_from_y(a_copy, xx, k), 0)[1], 0)
    keep_a.wait()

    def arrived(i, _):
        ref = wa.at[i, :, theirs]
        remote(ref, ref, asend.at[i, CC], acrecv.at[i], to[CC]).wait_recv()
        return 0

    lax.fori_loop(0, 16, arrived, 0)
    bias[...] = jnp.sum(wa[:, 0:16, :].astype(F32), axis=0)
    top_copy = pltpu.make_async_copy(wa, top_out, lsem.at[4])
    top_copy.start()
    lane = lax.broadcasted_iota(jnp.int32, (2 * HALF, 128), 1)
    ind = block_columns().astype(BF)
    lse[...] = jnp.zeros_like(lse)

    def out_copy(m, t):
        src, dst = ((xs, xs_out), (ks, k_out), (vs, v_out))[t]
        return pltpu.make_async_copy(src.at[m], dst.at[m], osem.at[m, t])

    def gather(m):
        def x_here(zz):
            x_copy(m, zz, 1 - x, XX).wait_recv()

        for k in range(4):
            at_distance(x_here, k)
        pltpu.make_async_copy(x_ref.at[m], xall[m].at[pl.ds(4 * s, 4)], lsem.at[m]).wait()
        for t in range(5):
            chunk = xall[m][pl.ds(4 * jnp.clip(s - 2 + t, 0, 7), 4)]
            xs[m, 256 * t:256 * t + 256, :] = chunk.reshape(256, chunk.shape[-1])

        def named(t, _):
            xs[m, pl.ds(pl.multiple_of(NW + 64 * t, 64), 64), :] = xall[m][idx[m, t]]
            return 0

        lax.fori_loop(0, 16, named, 0)
        out_copy(m, 0).start()
        q = (dot(xs[m, 512:768, :], wa[:, 16:64, :].reshape(768, 768)) + bias[0:1, :]).astype(BF)
        q_out[m] = q * jnp.asarray(0.125, BF)

    def project(m, i):
        r = rows_at(i, 768)
        rows = xs[m, r, :]
        ks[m, r, :] = dot(rows, wa[:, 64:112, :].reshape(768, 768)).astype(BF)
        vs[m, r, :] = (dot(rows, wa[:, 112:160, :].reshape(768, 768)) + bias[1:2, :]).astype(BF)

    def pair(m, p):
        col = pl.ds(pl.multiple_of(p * 128, 128), 128)
        for h in range(2):
            r = pl.ds(h * HALF, HALF)
            more = extra[m, h]
            keys = jnp.concatenate([ks[m, a:a + n, col] for a, n in key_rows(h)], axis=0)
            vals = jnp.concatenate([vs[m, a:a + n, col] for a, n in key_rows(h)], axis=0)
            scores = dot_nt(jnp.concatenate([split_heads(q_out[m, r, col]), ind], axis=1),
                            jnp.concatenate([keys, more], axis=1))
            top = jnp.max(scores, axis=1, keepdims=True)
            e = jnp.exp(scores - top).astype(BF)
            o = dot(e, jnp.concatenate([vals, more], axis=1))
            total = o[:, 130:131]
            att[m, r, col] = merge_heads(o[:, :128] / total).astype(BF)
            rr = pl.ds(h * 2 * HALF, 2 * HALF)
            lse[m, rr, :] = jnp.where(lane == p, top + jnp.log(total), lse[m, rr, :])

    def picked(g, plan):
        k = jnp.full((), 9, jnp.int32)
        for at, value in plan:
            k = jnp.where(g == at, value, k)
        return k

    def pump(g):
        x_line(1, picked(g, PUMP_X))
        b_own_column(picked(g, PUMP_OWN))
        b_other_column(picked(g, PUMP_OTHER))
        b_to_x(picked(g, PUMP_CROSS))
        w_from_y(b_copy, x, picked(g, PUMP_Y0))
        w_from_y(b_copy, 1 - x, picked(g, PUMP_Y1))

    def step(g, _):
        m, i = g // 9, g % 9
        pl.when(g == 0)(lambda: gather(0))
        pl.when(g == 9)(lambda: gather(1))
        pl.when(i < 3)(lambda: project(m, i))

        @pl.when(i == 3)
        def _():
            out_copy(m, 1).start()
            out_copy(m, 2).start()

        pl.when(i >= 3)(lambda: pair(m, i - 3))
        pump(g)
        return 0

    lax.fori_loop(0, 18, step, 0)

    lax.fori_loop(18, 26, lambda g, _: (pump(g), 0)[1], 0)

    def b_arrived(i, _):
        ref = wall.at[i, :, theirs]
        remote(ref, ref, bsend.at[i, CC], bcrecv.at[i], to[CC]).wait_recv()
        return 0

    lax.fori_loop(0, 16, b_arrived, 0)
    keep_b.wait()
    top_copy.wait()
    for m in range(2):
        for t in range(3):
            out_copy(m, t).wait()

    def sent(k, _):
        for m in range(2):
            x_copy(m, k, x, XX).wait_send()
        for copy in (a_copy, b_copy):
            for way in (YY, CC):
                copy(k, x, y, way).wait_send()
                copy(k, 1 - x, y, way).wait_send()
            copy(k, x, 1 - y, CC).wait_send()
            copy(k, 1 - x, 1 - y, CC).wait_send()
        a_copy(k, x, y, XX).wait_send()
        pl.when(zfirst | (k == z))(lambda: b_copy(k, x, y, XX).wait_send())

        def line(way):
            x_copy(0, k, x, way).wait_send()
            x_copy(1, k, x, way).wait_send()
            a_copy(k, x, y, way).wait_send()
            b_copy(k, x, y, way).wait_send()
            pl.when(jnp.logical_not(zfirst))(lambda: b_copy(k, 1 - x, y, way).wait_send())

        pl.when((k <= z) & (z < 3))(lambda: line(UP))
        pl.when((k >= z) & (z > 0))(lambda: line(DOWN))
        return 0

    lax.fori_loop(0, 4, sent, 0)


PUMP_X = ((1, 2), (6, 3))
PUMP_OWN = ((0, 1), (4, 2), (8, 3))
PUMP_OTHER = ((3, 0), (8, 1), (12, 2), (15, 3))
PUMP_CROSS = ((6, 1), (8, 2), (9, 3))
PUMP_Y0 = ((1, 0), (3, 1), (7, 2), (10, 3))
PUMP_Y1 = ((7, 0), (12, 1), (15, 2), (18, 3))


def forward_all(idx, see, x, weights, table):
    dma = pltpu.SemaphoreType.DMA
    sd = jax.ShapeDtypeStruct
    vm, anywhere, sm = (pl.BlockSpec(memory_space=m) for m in (pltpu.VMEM, pl.ANY, pltpu.SMEM))
    mb, rows, width = x.shape
    v = pltpu.VMEM
    return pl.pallas_call(
        forward_kernel,
        out_shape=[
            sd((mb, rows, width), BF), sd((mb, 2 * rows, 128), F32), sd((mb, rows, width), BF),
            sd((mb, NS, width), BF), sd((mb, NS, width), BF), sd((mb, NS, width), BF),
            sd((16, REST, width), BF), sd((16, TOP, width), BF), sd((16, width), F32),
        ],
        in_specs=[sm, sm, anywhere] + [vm] * 7,
        out_specs=[vm, vm, vm, anywhere, anywhere, anywhere, anywhere, anywhere, vm],
        scratch_shapes=[
            v((304, width), F32), v((304, 384), F32), v((TOP, 384), BF), v((REST, 384), BF),
            v((8 * rows // 64, 64, width), BF), v((8 * rows // 64, 64, width), BF),
            v((mb, NS, width), BF), v((mb, NS, width), BF), v((mb, NS, width), BF),
            v((16, TOP, width), BF), v((mb, 2, NK, 128), BF),
            dma((2,)), dma((5,)), dma((mb, 3)),
            dma((16, 5)), dma((16,)), dma((16,)), dma((16, 5)), dma((16,)), dma((16,)),
            dma((mb, 8, 3)), dma((mb, 8)),
        ],
        compiler_params=pltpu.CompilerParams(
            collective_id=0, has_side_effects=True, vmem_limit_bytes=60 * 2**20
        ),
    )(idx, see, x.reshape(mb, rows // 64, 64, width), *weights, table)


def backward_kernel(see, q, att, datt, lse, x_in, tgt, gb_in, done, k_in, v_in, xs_in, top_in, go, gu, gd,
                    oq, ok, ov, oo, ou, od, ob, odx,
                    kb, vb, xsb, wa, extra, dka, dva, dq, gk, gv, gb,
                    acc, mate, yr, xr, zr, dxp, dxr, dzr, fin, snd, rcv,
                    ksem, lsem, msem, msem2, asem, ysem, xsem, zsem, ysem2, xsem2, zsem2, dxsem, dzsem, fsem, ready):
    z, x, y, c = place()
    s = 2 * z + x
    mine, theirs = lanes(c), lanes(1 - c)
    near_x, near_y, near_c = device(z, 1 - x, y, c), device(z, x, 1 - y, c), device(z, x, y, 1 - c)
    above, below = device(z + 1, x, y, c), device(z - 1, x, y, c)

    def far(i):
        inner = jnp.where(i == 0, 3, jnp.where(i == 1, 0, jnp.where(i == 2, 2, 1)))
        low = jnp.where(z == 0, 3 - i, jnp.where(z == 1, inner, i))
        return jnp.where(z == 2, 3 - inner, low)

    def column(p):
        return pl.ds(pl.multiple_of(p * 128, 128), 128)

    def load_keys(m, p):
        return (pltpu.make_async_copy(k_in.at[m, :, column(p)], kb.at[:, column(p)], ksem.at[0, p]),
                pltpu.make_async_copy(v_in.at[m, :, column(p)], vb.at[:, column(p)], ksem.at[1, p]))

    def start_keys(m):
        def one(p, _):
            for cp in load_keys(m, p):
                cp.start()
            return 0

        lax.fori_loop(0, 6, one, 0)

    start_keys(0)
    top_copy = pltpu.make_async_copy(top_in, wa, lsem.at[0])
    top_copy.start()
    done_copy = pltpu.make_async_copy(done, odx, lsem.at[1])
    done_copy.start()
    greet(z, x, y, c)

    def parts(yy, cc):
        off = pl.multiple_of(cc * 384, 128)
        yield 0, go.at[:, yy, :, pl.ds(off, 384)], pl.ds(0, 48)
        yield 1, gd.at[:, yy, :, pl.ds(off, 384)], pl.ds(240, 192)
        for j in range(4):
            col = pl.multiple_of(j * 768 + cc * 384, 128)
            yield 2 + j, gu.at[:, yy, :, pl.ds(col, 384)], pl.ds(48 + 48 * j, 48)

    swaps, loads = {}, {}
    for t, yy in enumerate((1 - y, y)):
        for i, src, rows in parts(yy, 1 - c):
            swaps[t, i] = remote(src, mate.at[:, yy, rows, :], msem.at[0, t, i], msem.at[1, t, i], near_c)
            swaps[t, i].start()
        for i, src, rows in parts(yy, c):
            loads[t, i] = pltpu.make_async_copy(src, acc.at[:, yy, rows, :], asem.at[t, i])
            loads[t, i].start()
    write_extra(see, extra)
    gb[...] = gb_in[...]
    gk[...] = jnp.zeros_like(gk)
    gv[...] = jnp.zeros_like(gv)

    class Reduce:
        def __init__(self, rows, ys, xs_, zs):
            self.rows, self.ys, self.xs, self.zs = rows, ys, xs_, zs

        def a(self, s_, yy):
            return acc.at[s_, yy, pl.ds(0, self.rows), :]

        def y_copy(self, s_):
            return remote(self.a(s_, 1 - y), yr.at[s_, pl.ds(0, self.rows), :], self.ys.at[0, s_], self.ys.at[1, s_], near_y)

        def x_copy(self, zz):
            return remote(self.a(2 * zz + 1 - x, y), xr.at[zz, pl.ds(0, self.rows), :], self.xs.at[0, zz],
                          self.xs.at[1, zz], near_x)

        def z_copy(self, zz, slot, to):
            return remote(self.a(2 * zz + x, y), zr.at[slot, pl.ds(0, self.rows), :], self.zs.at[0, zz],
                          self.zs.at[1, slot], to)

        def add(self, s_, yy, others):
            r = pl.ds(0, self.rows)
            total = acc[s_, yy, r, :].astype(F32)
            for ref, index in others:
                total = total + ref[(*index, r, slice(None))].astype(F32)
            return total

        def y_step(self, i):
            s_ = 2 * far(i % 4) + jnp.where(i < 4, 1 - x, x)
            acc[s_, 1 - y, pl.ds(0, self.rows), :] = self.add(s_, 1 - y, [(mate, (s_, 1 - y))]).astype(BF)
            self.y_copy(s_).start()

        def x_step(self, i):
            zz = far(i)
            s_ = 2 * zz + 1 - x
            self.y_copy(s_).wait_recv()
            acc[s_, y, pl.ds(0, self.rows), :] = self.add(s_, y, [(mate, (s_, y)), (yr, (s_,))]).astype(BF)
            self.x_copy(zz).start()

        def along(self, zz, up):
            s_ = 2 * zz + x
            self.y_copy(s_).wait_recv()
            self.x_copy(zz).wait_recv()
            others = [(mate, (s_, y)), (yr, (s_,)), (xr, (zz,))]
            r = pl.ds(0, self.rows)
            more = z > 0 if up else z < 3

            @pl.when(more)
            def _():
                self.z_copy(zz, zz, above).wait_recv()
                acc[s_, y, r, :] = self.add(s_, y, others + [(zr, (zz,))]).astype(BF)

            @pl.when(jnp.logical_not(more))
            def _():
                acc[s_, y, r, :] = self.add(s_, y, others).astype(BF)

            if up:
                self.z_copy(zz, zz, above).start()
            else:
                self.z_copy(zz, jnp.where(zz == z - 1, 4, zz), below).start()

        def z_step(self, i):
            pl.when(3 - i > z)(lambda: self.along(3 - i, True))
            pl.when(i < z)(lambda: self.along(i, False))

        def finish(self):
            self.y_copy(s).wait_recv()
            self.x_copy(z).wait_recv()
            r = pl.ds(0, self.rows)
            fin[r, :] = self.add(s, y, [(mate, (s, y)), (yr, (s,)), (xr, (z,))])
            for slot, cond in ((z, z > 0), (4, z < 3)):
                @pl.when(cond)
                def _(slot=slot):
                    self.z_copy(z, slot, above).wait_recv()
                    fin[r, :] += zr[slot, r, :].astype(F32)

        def drain(self):
            def one(i, _):
                self.y_copy(i).wait_send()
                return 0

            lax.fori_loop(0, 8, one, 0)

            def two(i, _):
                self.x_copy(i).wait_send()
                pl.when(i != z)(lambda: self.z_copy(i, i, above).wait_send())
                return 0

            lax.fori_loop(0, 4, two, 0)

    rest = Reduce(REST, ysem, xsem, zsem)
    top = Reduce(TOP, ysem2, xsem2, zsem2)

    def dx_x(m, zz):
        return remote(dxp.at[2 * zz + 1 - x], dxr.at[m, zz], dxsem.at[0, m, zz], dxsem.at[1, m, zz], near_x)

    def dx_z(m, zz, slot, to):
        return remote(dxp.at[2 * zz + x], dzr.at[m, slot], dzsem.at[0, m, zz], dzsem.at[1, m, slot], to)

    def dx_along(m, zz, up):
        s_ = 2 * zz + x
        dx_x(m, zz).wait_recv()
        more = z > 0 if up else z < 3

        @pl.when(more)
        def _():
            dx_z(m, zz, zz, above).wait_recv()
            dxp[s_] = (dxp[s_].astype(F32) + dxr[m, zz].astype(F32) + dzr[m, zz].astype(F32)).astype(BF)

        @pl.when(jnp.logical_not(more))
        def _():
            dxp[s_] = (dxp[s_].astype(F32) + dxr[m, zz].astype(F32)).astype(BF)

        if up:
            dx_z(m, zz, zz, above).start()
        else:
            dx_z(m, zz, jnp.where(zz == z - 1, 4, zz), below).start()

    def dx_step(m, i):
        pl.when(3 - i > z)(lambda: dx_along(m, 3 - i, True))
        pl.when(i < z)(lambda: dx_along(m, i, False))

    def dx_finish(m):
        dx_x(m, z).wait_recv()
        odx[m] += dxr[m, z].astype(F32)
        for slot, cond in ((z, z > 0), (4, z < 3)):
            @pl.when(cond)
            def _(slot=slot):
                dx_z(m, z, slot, above).wait_recv()
                odx[m] += dzr[m, slot].astype(F32)

    def dx_sent(m):
        def one(i, _):
            dx_x(m, i).wait_send()
            pl.when(i != z)(lambda: dx_z(m, i, i, above).wait_send())
            return 0

        lax.fori_loop(0, 4, one, 0)

    ind = block_columns()

    def pair(m, p):
        col = column(p)
        for cp in load_keys(m, p):
            cp.wait()
        dka[...] = jnp.zeros_like(dka)
        dva[...] = jnp.zeros_like(dva)
        for h in range(2):
            rows = pl.ds(h * HALF, HALF)
            qs = split_heads(q[m, rows, col])
            dos = split_heads(datt[m, rows, col])
            o2 = att[m, rows, col].astype(F32)
            delta = jnp.sum(dos.astype(F32) * jnp.concatenate([o2, o2], axis=0), axis=1, keepdims=True)
            stats = lse[m, pl.ds(h * 2 * HALF, 2 * HALF), :]
            lane = lax.broadcasted_iota(jnp.int32, stats.shape, 1)
            log_norm = jnp.sum(jnp.where(lane == p, stats, 0.0), axis=1, keepdims=True)
            qe = jnp.concatenate([qs, with_column(ind, -log_norm)], axis=1)
            doe = jnp.concatenate([dos, with_column(jnp.zeros_like(ind), -delta)], axis=1)
            dqt = jnp.zeros((128, 2 * HALF), F32)
            (wa_, wn), (ga, gn), (ra, rn) = key_rows(h)
            off = 0
            for pieces in (((wa_, 576),), ((wa_ + 576, 576),), ((ga, gn), (ra, rn))):
                n = sum(t for _, t in pieces)
                k2 = jnp.concatenate([kb[a:a + t, col] for a, t in pieces], axis=0)
                v2 = jnp.concatenate([vb[a:a + t, col] for a, t in pieces], axis=0)
                more = extra[m, h, off:off + n, :]
                pt = jnp.exp(dot_nt(jnp.concatenate([k2, more], axis=1), qe))
                ds = (pt * dot_nt(jnp.concatenate([v2, more], axis=1), doe)).astype(BF)
                dv_ = dot(pt.astype(BF), dos)
                dk_ = dot(ds, qs)
                dqt = dqt + dot(k2.T, ds)
                if off < WK:
                    a, t = pieces[0]
                    dka[a:a + t, :] += dk_
                    dva[a:a + t, :] += dv_
                else:
                    at = 0
                    for a, t in pieces:
                        kb[a:a + t, col] = dk_[at:at + t].astype(BF)
                        vb[a:a + t, col] = dv_[at:at + t].astype(BF)
                        at += t
                off += n
            dq[m, rows, col] = (merge_heads(dqt.T) * 0.125).astype(BF)
        kb[0:NW, col] = dka[...].astype(BF)
        vb[0:NW, col] = dva[...].astype(BF)

    def weight(i):
        return wa[:, :, 16 + 48 * i:64 + 48 * i, :].reshape(768, 768)

    def dx_rows(m, i):
        r = rows_at(i, 768)
        value = dot_nt(kb[r, :], weight(1)) + dot_nt(vb[r, :], weight(2))
        xsb[r, :] = value.astype(BF)

        @pl.when(i == 0)
        def _():
            odx[m] += value[512:768] + dot_nt(dq[m], weight(0))

    def dx_piece(m, i):
        t = 2 * far(i % 4) + jnp.where(i < 4, 1 - x, x)
        row = lax.broadcasted_iota(jnp.int32, (256, 1024), 0) + 256 * t
        chosen = jnp.where(row == tgt[m], 1.0, 0.0).astype(BF)
        value = dot(chosen, xsb[NW:NS, :])
        w = t - s + 2

        @pl.when(t == s)
        def _():
            odx[m] += value

        @pl.when(t != s)
        def _():
            near = xsb[rows_at(jnp.clip(w, 0, 4), 256), :].astype(F32)
            dxp[t] = (value + jnp.where((w >= 0) & (w < 5), near, 0.0)).astype(BF)

        pl.when(i < 4)(lambda: dx_x(m, far(i % 4)).start())

    def weight_grads(m, i):
        r = rows_at(i, 768)
        rows = xsb[r, :]
        dvr = vb[r, :]
        gk[...] += dot_tn(rows, kb[r, :])
        gv[...] += dot_tn(rows, dvr)
        gb[1:2, :] += jnp.sum(dvr.astype(F32), axis=0, keepdims=True)

    def picked(g, plan):
        k = jnp.full((), 9, jnp.int32)
        for at, value in plan:
            k = jnp.where(g == at, value, k)
        return k

    def pump(g):
        k = picked(g, PLAN_Y)
        pl.when(k < 9)(lambda: rest.y_step(k))
        k2 = picked(g, PLAN_X)
        pl.when(k2 < 9)(lambda: rest.x_step(k2))
        k3 = picked(g, PLAN_D)
        pl.when(k3 < 3)(lambda: dx_step(0, k3))
        pl.when(k3 == 3)(lambda: dx_finish(0))
        k4 = picked(g, PLAN_Z)
        pl.when(k4 < 3)(lambda: rest.z_step(k4))
        pl.when(k4 == 3)(rest.finish)

    for i in range(6):
        loads[0, i].wait()
        swaps[0, i].wait_recv()
    rest.y_step(0)
    done_copy.wait()

    def micro(m, _):
        pl.when(m == 1)(lambda: start_keys(1))

        def pairs(p, _):
            pair(m, p)

            @pl.when((m == 0) & (p == 4))
            def _():
                for i in range(6):
                    loads[1, i].wait()
                    swaps[1, i].wait_recv()
                top_copy.wait()

            pump(12 * m + p)
            return 0

        lax.fori_loop(0, 6, pairs, 0)

        def rows(i, _):
            dx_rows(m, i)
            pump(12 * m + 6 + i)
            return 0

        lax.fori_loop(0, 3, rows, 0)
        pl.when(m == 1)(lambda: dx_sent(0))
        lax.fori_loop(0, 8, lambda i, _: (dx_piece(m, i), 0)[1], 0)
        xs_copy = pltpu.make_async_copy(xs_in.at[m], xsb, lsem.at[2])
        xs_copy.start()
        xs_copy.wait()

        def grads(i, _):
            weight_grads(m, i)
            pump(12 * m + 9 + i)
            return 0

        lax.fori_loop(0, 3, grads, 0)
        return 0

    lax.fori_loop(0, 2, micro, 0)
    lax.fori_loop(24, 30, lambda g, _: (pump(g), 0)[1], 0)

    rest.drain()
    for t in range(2):
        for i in range(6):
            swaps[t, i].wait_send()

    def put(kept, start, n, cc, ref, col0, first):
        ref[:, pl.ds(pl.multiple_of(col0 + cc * 384, 128), 384)] = kept

    def rest_rows(cc):
        yield oo, 0, pl.multiple_of(24 * cc, 8), 24, 0
        for j in range(4):
            yield ou, 24 + 24 * j, pl.multiple_of(48 + 48 * j + 24 * cc, 8), 24, 768 * j
        yield od, 120, pl.multiple_of(240 + 96 * cc, 8), 96, 0

    def top_rows(cc):
        yield ob, 216, 0, 16, 0
        for i, ref in enumerate((oq, ok, ov)):
            yield ref, 232 + 24 * i, pl.multiple_of(16 + 48 * i + 24 * cc, 8), 24, 0

    def hand_over(rows_of):
        for ref, at, start, n, col in rows_of(1 - c):
            snd[at:at + n, :] = fin[pl.ds(start, n), :]
        for ref, at, start, n, col in rows_of(c):
            ref[:, pl.ds(pl.multiple_of(col + c * 384, 128), 384)] = fin[pl.ds(start, n), :]

    def take_over(rows_of):
        for ref, at, start, n, col in rows_of(c):
            ref[:, pl.ds(pl.multiple_of(col + (1 - c) * 384, 128), 384)] = rcv[at:at + n, :]

    hand_over(rest_rows)
    last0 = remote(snd.at[0:216, :], rcv.at[0:216, :], fsem.at[0, 0], fsem.at[1, 0], near_c)
    last0.start()

    def tell(to):
        pl.semaphore_signal(ready, inc=1, device_id=to, device_id_type=MESH)

    for to in (near_x, near_y, near_c):
        tell(to)
    pl.when(z > 0)(lambda: tell(below))
    pl.when(z < 3)(lambda: tell(above))
    gb[0:1, :] += jnp.sum(dq[0].astype(F32) + dq[1].astype(F32), axis=0, keepdims=True)
    gq = dot_tn(x_in[0], dq[0]) + dot_tn(x_in[1], dq[1])
    wa[:, :, 16:64, :] = gq.astype(BF).reshape(8, 2, 48, 768)
    wa[:, :, 64:112, :] = gk[...].astype(BF).reshape(8, 2, 48, 768)
    wa[:, :, 112:160, :] = gv[...].astype(BF).reshape(8, 2, 48, 768)
    low = gb[...].astype(BF)

    def spread(i, _):
        wa[i // 2, i % 2, 0:16, :] = low
        return 0

    lax.fori_loop(0, 16, spread, 0)
    pl.semaphore_wait(ready, 3 + (z > 0).astype(jnp.int32) + (z < 3).astype(jnp.int32))
    swap2 = [remote(wa.at[:, yy, :, theirs], mate.at[:, yy, pl.ds(0, TOP), :], msem2.at[0, t], msem2.at[1, t], near_c)
             for t, yy in enumerate((1 - y, y))]
    own2 = [pltpu.make_async_copy(wa.at[:, yy, :, mine], acc.at[:, yy, pl.ds(0, TOP), :], lsem.at[3 + t])
            for t, yy in enumerate((1 - y, y))]
    for cp in swap2 + own2:
        cp.start()
    swap2[0].wait_recv()
    own2[0].wait()
    lax.fori_loop(0, 8, lambda i, _: (top.y_step(i), 0)[1], 0)
    dx_step(1, 0)
    swap2[1].wait_recv()
    own2[1].wait()

    def cross(i, _):
        top.x_step(i)
        return 0

    lax.fori_loop(0, 4, cross, 0)
    dx_step(1, 1)
    top.z_step(0)
    dx_step(1, 2)
    top.z_step(1)
    top.z_step(2)
    dx_finish(1)
    last0.wait()
    top.finish()
    hand_over(top_rows)
    last1 = remote(snd.at[216:304, :], rcv.at[216:304, :], fsem.at[0, 1], fsem.at[1, 1], near_c)
    last1.start()
    take_over(rest_rows)
    last1.wait()
    take_over(top_rows)
    top.drain()
    dx_sent(1)
    for cp in swap2:
        cp.wait_send()


PLAN_Y = ((0, 1), (1, 2), (2, 3), (3, 4), (4, 5), (5, 6), (6, 7))
PLAN_X = ((5, 0), (6, 1), (7, 2), (8, 3))
PLAN_D = ((14, 0), (16, 1), (18, 2), (20, 3))
PLAN_Z = ((13, 0), (15, 1), (17, 2), (19, 3))


def backward_all(see, q, att, datt, lse, x, tgt, gb, done, k, v, xs, top, go, gu, gd):
    dma = pltpu.SemaphoreType.DMA
    sd = jax.ShapeDtypeStruct
    vm, anywhere, sm = (pl.BlockSpec(memory_space=m) for m in (pltpu.VMEM, pl.ANY, pltpu.SMEM))
    mb, rows, width = x.shape
    s = pltpu.VMEM
    views = [top.reshape(8, 2, TOP, width), go.reshape(8, 2, 48, width), gu.reshape(8, 2, 48, 4 * width),
             gd.reshape(8, 2, 192, width)]
    return pl.pallas_call(
        backward_kernel,
        out_shape=[sd((24, width), F32)] * 4 + [sd((24, 4 * width), F32), sd((96, width), F32), sd((16, width), F32),
                                                sd(x.shape, F32)],
        in_specs=[sm] + [vm] * 7 + [anywhere] * 8,
        out_specs=[vm] * 8,
        scratch_shapes=[
            s((NS, width), BF), s((NS, width), BF), s((NS, width), BF), s((8, 2, TOP, width), BF),
            s((mb, 2, NK, 128), BF), s((NW, 128), F32), s((NW, 128), F32), s((mb, rows, width), BF),
            s((width, width), F32), s((width, width), F32), s((16, width), F32),
            s((8, 2, REST, 384), BF), s((8, 2, REST, 384), BF), s((8, REST, 384), BF), s((4, REST, 384), BF),
            s((5, REST, 384), BF),
            s((8, rows, width), BF), s((mb, 4, rows, width), BF), s((mb, 5, rows, width), BF),
            s((REST, 384), F32), s((304, 384), F32), s((304, 384), F32),
            dma((2, 6)), dma((5,)), dma((2, 2, 6)), dma((2, 2)), dma((2, 6)),
            dma((2, 8)), dma((2, 4)), dma((2, 5)), dma((2, 8)), dma((2, 4)), dma((2, 5)),
            dma((2, mb, 4)), dma((2, mb, 5)), dma((2, 2)), pltpu.SemaphoreType.REGULAR,
        ],
        compiler_params=pltpu.CompilerParams(
            collective_id=1, has_side_effects=True, vmem_limit_bytes=62 * 2**20
        ),
    )(see, q, att, datt, lse, x, tgt, gb, done, k, v, xs, *views)


CHUNKS = 9


def project_kernel(idx, xall, wall, bias, xs_ref, k_ref, v_ref, q_ref, xs, w, sems, wsem):
    m, i = pl.program_id(0), pl.program_id(1)

    @pl.when((m == 0) & (i == 0))
    def _():
        copy = pltpu.make_async_copy(wall.at[:, pl.ds(16, 144), :], w, wsem)
        copy.start()
        for mm in range(2):
            for cc in range(CHUNKS):
                pieces = [(0, 256)] if cc < 5 else [(0, 128), (128, 128)] if cc == 5 else [(64 * t, 64) for t in range(4)]
                base = cc if cc < 5 else 5 if cc == 5 else 7 + 4 * (cc - 6)
                for t, (off, n) in enumerate(pieces):
                    start = pl.multiple_of(idx[mm, base + t], 64)
                    pltpu.make_async_copy(xall.at[mm, pl.ds(start, n), :], xs.at[mm, cc, pl.ds(off, n), :],
                                          sems.at[mm, cc]).start()
        copy.wait()

    pltpu.make_async_copy(xall.at[0, pl.ds(0, 256), :], xs.at[m, i], sems.at[m, i]).wait()
    rows = xs[m, i]
    xs_ref[0] = rows
    k_ref[0] = dot(rows, w[:, 48:96, :].reshape(768, 768)).astype(BF)
    v_ref[0] = (dot(rows, w[:, 96:144, :].reshape(768, 768)) + bias[1:2, :]).astype(BF)

    @pl.when(i == 2)
    def _():
        q = (dot(rows, w[:, 0:48, :].reshape(768, 768)) + bias[0:1, :]).astype(BF)
        q_ref[0] = q * jnp.asarray(0.125, BF)


def project(idx, xall, wall, bias):
    mb = xall.shape[0]
    sd = jax.ShapeDtypeStruct
    chunk = pl.BlockSpec((1, 256, 768), lambda m, i, t: (m, i, 0))
    return pl.pallas_call(
        project_kernel,
        grid_spec=pltpu.PrefetchScalarGridSpec(
            num_scalar_prefetch=1,
            grid=(mb, CHUNKS),
            in_specs=[pl.BlockSpec(memory_space=pl.ANY)] * 2 + [pl.BlockSpec((16, 768), lambda m, i, t: (0, 0))],
            out_specs=[chunk, chunk, chunk, pl.BlockSpec((1, 256, 768), lambda m, i, t: (m, 0, 0))],
            scratch_shapes=[
                pltpu.VMEM((mb, CHUNKS, 256, 768), BF), pltpu.VMEM((16, 144, 768), BF),
                pltpu.SemaphoreType.DMA((mb, CHUNKS)), pltpu.SemaphoreType.DMA,
            ],
        ),
        out_shape=[sd((mb, NS, 768), BF)] * 3 + [sd((mb, 256, 768), BF)],
        compiler_params=pltpu.CompilerParams(vmem_limit_bytes=48 * 2**20),
    )(idx, xall, wall, bias)


EPS = 1e-6
G0, G1 = 0.7978845608, 0.044715


def norm(v):
    mean = jnp.mean(v, axis=-1, keepdims=True)
    centred = v - mean
    inverse = lax.rsqrt(jnp.mean(centred * centred, axis=-1, keepdims=True) + EPS)
    return centred * inverse, inverse


def norm_back(g, normed, inverse, gain):
    c = g * gain
    return inverse * (c - jnp.mean(c, axis=-1, keepdims=True)
                      - normed * jnp.mean(c * normed, axis=-1, keepdims=True))


def middle_kernel(att, x, cot, wall, bias, out_ref, datt_ref, done_ref, go_ref, gu_ref, gd_ref, gb_ref,
                  w, wsem, pre, hid, mid, low, n1, r1, ffn):
    rows = x.shape[0]
    copies = [
        pltpu.make_async_copy(wall.at[:, pl.ds(0, 48), :], w.at[:, pl.ds(0, 48), :], wsem.at[0]),
        pltpu.make_async_copy(wall.at[:, pl.ds(48, 192), :], w.at[:, pl.ds(48, 192), :], wsem.at[1]),
        pltpu.make_async_copy(wall.at[:, pl.ds(240, 192), :], w.at[:, pl.ds(240, 192), :], wsem.at[2]),
    ]
    for cp in copies:
        cp.start()
    half = rows // 2
    copies[0].wait()
    w_out = w[:, 0:48, :].reshape(768, 768)
    for h in range(2):
        r = pl.ds(h * half, half)
        t = x[r, :].astype(F32) + dot(att[r, :], w_out) + bias[2:3, :]
        normed, inverse = norm(t)
        n1[r, :] = normed
        r1[r, :] = jnp.broadcast_to(inverse, (half, 128))
        value = normed * bias[4:5, :] + bias[5:6, :]
        mid[r, :] = value
        low[r, :] = value.astype(BF)
    ffn[...] = jnp.broadcast_to(bias[3:4, :], ffn.shape)
    copies[1].wait()
    copies[2].wait()

    def up_block(j):
        return w[:, pl.ds(pl.multiple_of(48 + 48 * j, 16), 48), :].reshape(768, 768)

    def down_block(j):
        return w[pl.ds(4 * j, 4), 240:432, :].reshape(768, 768)

    def forward(j, _):
        wu, wd = up_block(j), down_block(j)
        for h in range(2):
            r = pl.ds(h * half, half)
            u = dot(low[r, :], wu) + bias[pl.ds(8 + j, 1), :]
            pre[j, r, :] = u
            g = (0.5 * u * (1.0 + jnp.tanh(G0 * (u + G1 * u * u * u)))).astype(BF)
            hid[j, r, :] = g
            ffn[r, :] += dot(g, wd)
        return 0

    lax.fori_loop(0, 4, forward, 0)
    gb_ref[...] = jnp.zeros_like(gb_ref)
    for h in range(2):
        r = pl.ds(h * half, half)
        normed, inverse = norm(mid[r, :] + ffn[r, :])
        out_ref[r, :] = (normed * bias[6:7, :] + bias[7:8, :]).astype(BF)
        g = cot[r, :].astype(F32)
        gb_ref[6:7, :] += jnp.sum(g * normed, axis=0, keepdims=True)
        gb_ref[7:8, :] += jnp.sum(g, axis=0, keepdims=True)
        d_two = norm_back(g, normed, inverse, bias[6:7, :])
        mid[r, :] = d_two
        d_ffn = d_two.astype(BF)
        datt_ref[r, :] = d_ffn
        gb_ref[3:4, :] += jnp.sum(d_ffn.astype(F32), axis=0, keepdims=True)

    def backward(j, _):
        wu, wd = up_block(j), down_block(j)
        d_ffn = datt_ref[...]
        gd_ref[pl.ds(pl.multiple_of(j * 768, 768), 768), :] = dot_tn(hid[j], d_ffn).astype(BF)
        for h in range(2):
            r = pl.ds(h * half, half)
            u = pre[j, r, :]
            th = jnp.tanh(G0 * (u + G1 * u * u * u))
            slope = 0.5 * (1.0 + th) + 0.5 * u * (1.0 - th * th) * (G0 * (1.0 + 3.0 * G1 * u * u))
            d_pre = (dot_nt(datt_ref[r, :], wd) * slope).astype(BF)
            hid[j, r, :] = d_pre
            gb_ref[pl.ds(8 + j, 1), :] += jnp.sum(d_pre.astype(F32), axis=0, keepdims=True)
            mid[r, :] += dot_nt(d_pre, wu)
        gu_ref[:, pl.ds(pl.multiple_of(j * 768, 768), 768)] = dot_tn(low[...], hid[j]).astype(BF)
        return 0

    lax.fori_loop(0, 4, backward, 0)
    for h in range(2):
        r = pl.ds(h * half, half)
        d_mid, normed = mid[r, :], n1[r, :]
        gb_ref[4:5, :] += jnp.sum(d_mid * normed, axis=0, keepdims=True)
        gb_ref[5:6, :] += jnp.sum(d_mid, axis=0, keepdims=True)
        d_one = norm_back(d_mid, normed, r1[r, 0:1], bias[4:5, :])
        done_ref[r, :] = d_one
        d_branch = d_one.astype(BF)
        low[r, :] = d_branch
        gb_ref[2:3, :] += jnp.sum(d_branch.astype(F32), axis=0, keepdims=True)
        datt_ref[r, :] = dot_nt(d_branch, w_out).astype(BF)
    go_ref[...] = dot_tn(att[...], low[...]).astype(BF)


def middle(att, x, cot, wall, bias):
    rows = x.shape[0]
    sd = jax.ShapeDtypeStruct
    vm = pl.BlockSpec(memory_space=pltpu.VMEM)
    return pl.pallas_call(
        middle_kernel,
        in_specs=[vm, vm, vm, pl.BlockSpec(memory_space=pl.ANY), vm],
        out_specs=[vm] * 7,
        out_shape=[sd((rows, 768), BF), sd((rows, 768), BF), sd((rows, 768), F32), sd((768, 768), BF),
                   sd((768, 3072), BF), sd((3072, 768), BF), sd((16, 768), F32)],
        scratch_shapes=[
            pltpu.VMEM((16, 432, 768), BF), pltpu.SemaphoreType.DMA((3,)),
            pltpu.VMEM((4, rows, 768), F32), pltpu.VMEM((4, rows, 768), BF),
            pltpu.VMEM((rows, 768), F32), pltpu.VMEM((rows, 768), BF), pltpu.VMEM((rows, 768), F32),
            pltpu.VMEM((rows, 128), F32), pltpu.VMEM((rows, 768), F32),
        ],
        compiler_params=pltpu.CompilerParams(vmem_limit_bytes=60 * 2**20),
    )(att, x, cot, wall, bias)


def back_kernel(scattered, idx, xs_ref, dk_ref, dv_ref, dq_ref, done_ref, wall, gb_in, dx_ref, own_ref, gq_ref, gk_ref, gv_ref, gb_ref,
                w, wsem, acc, aq, ak, av):
    m, i = pl.program_id(0), pl.program_id(1)

    @pl.when((m == 0) & (i == 0))
    def _():
        copy = pltpu.make_async_copy(wall.at[:, pl.ds(16, 144), :], w, wsem)
        copy.start()
        acc[...] = jnp.zeros_like(acc)
        aq[...] = jnp.zeros_like(aq)
        ak[...] = jnp.zeros_like(ak)
        av[...] = jnp.zeros_like(av)
        gb_ref[...] = gb_in[...]
        copy.wait()

    rows, dk, dv = xs_ref[0], dk_ref[0], dv_ref[0]
    ak[...] += dot_tn(rows, dk)
    av[...] += dot_tn(rows, dv)
    gb_ref[1:2, :] += jnp.sum(dv.astype(F32), axis=0, keepdims=True)
    dx = dot_nt(dk, w[:, 48:96, :].reshape(768, 768)) + dot_nt(dv, w[:, 96:144, :].reshape(768, 768))

    def add(slot, off, n):
        start = pl.multiple_of(idx[m, slot], 64)
        acc[m, pl.ds(start, n), :] += dx[off:off + n]

    if not scattered:
        dx_ref[0] = jnp.where(i == 2, jnp.zeros_like(dx), dx).astype(BF)

    @pl.when((i < 5) & (i != 2) & scattered)
    def _():
        add(jnp.minimum(i, 4), 0, 256)

    @pl.when((i == 5) & scattered)
    def _():
        add(5, 0, 128)
        add(6, 128, 128)

    @pl.when((i > 5) & scattered)
    def _():
        for t in range(4):
            add(7 + 4 * (i - 6) + t, 64 * t, 64)

    @pl.when(i == 2)
    def _():
        dq = dq_ref[0]
        aq[...] += dot_tn(rows, dq)
        gb_ref[0:1, :] += jnp.sum(dq.astype(F32), axis=0, keepdims=True)
        own_ref[0] = dx + done_ref[0] + dot_nt(dq, w[:, 0:48, :].reshape(768, 768))

    @pl.when((i == CHUNKS - 1) & scattered)
    def _():
        dx_ref[m if scattered else 0] = acc[m].astype(BF)

    @pl.when((m == 1) & (i == CHUNKS - 1))
    def _():
        gq_ref[...] = aq[...].astype(BF)
        gk_ref[...] = ak[...].astype(BF)
        gv_ref[...] = av[...].astype(BF)


def back(idx, xs, dk, dv, dq, done, wall, gb, seq_len):
    mb = xs.shape[0]
    sd = jax.ShapeDtypeStruct
    chunk = pl.BlockSpec((1, 256, 768), lambda m, i, t: (m, i, 0))
    one = pl.BlockSpec((1, 256, 768), lambda m, i, t: (m, 0, 0))
    whole = lambda *s: pl.BlockSpec(s, lambda m, i, t: (0,) * len(s))
    scattered = seq_len > 0
    held = seq_len if scattered else 256
    return pl.pallas_call(
        functools.partial(back_kernel, scattered),
        grid_spec=pltpu.PrefetchScalarGridSpec(
            num_scalar_prefetch=1,
            grid=(mb, CHUNKS),
            in_specs=[chunk, chunk, chunk, one, one, pl.BlockSpec(memory_space=pl.ANY), whole(16, 768)],
            out_specs=[whole(mb, seq_len, 768) if scattered else chunk, one, whole(768, 768), whole(768, 768), whole(768, 768), whole(16, 768)],
            scratch_shapes=[
                pltpu.VMEM((16, 144, 768), BF), pltpu.SemaphoreType.DMA, pltpu.VMEM((mb, held, 768), F32),
                pltpu.VMEM((768, 768), F32), pltpu.VMEM((768, 768), F32), pltpu.VMEM((768, 768), F32),
            ],
        ),
        out_shape=[sd((mb, seq_len if scattered else NS, 768), BF), sd((mb, 256, 768), F32), sd((768, 768), BF), sd((768, 768), BF),
                   sd((768, 768), BF), sd((16, 768), F32)],
        compiler_params=pltpu.CompilerParams(vmem_limit_bytes=60 * 2**20),
    )(idx, xs, dk, dv, dq, done, wall, gb)

def cat_rows(ref, h):
    return jnp.concatenate([ref[0, pl.ds(a, n), :] for a, n in key_rows(h)], axis=0)


def fwd_kernel(q_ref,k_ref,v_ref,me_ref,o_ref,l_ref):
    p=pl.program_id(1)
    ind=block_columns().astype(BF)
    for h in range(2):
        me=me_ref[0,h]
        qe=jnp.concatenate([split_heads(q_ref[0,pl.ds(h*HALF,HALF),:]),ind],axis=1)
        ke=jnp.concatenate([cat_rows(k_ref, h),me],axis=1)
        s=dot_nt(qe,ke)
        top=jnp.max(s,axis=1,keepdims=True)
        e=jnp.exp(s-top).astype(BF)
        ve=jnp.concatenate([cat_rows(v_ref,h),me],axis=1)
        o=dot(e,ve)
        tot=o[:,130:131]
        o_ref[0,pl.ds(h*HALF,HALF),:]=merge_heads(o[:,:128]/tot).astype(BF)
        l_ref[0,0,pl.ds(h*256,256),:]=jnp.broadcast_to(top+jnp.log(tot),(256,128))
def attn_fwd(q,k,v,me):
    mb=q.shape[0]; npair=q.shape[2]//128
    return pl.pallas_call(fwd_kernel,grid=(mb,npair),
      in_specs=[pl.BlockSpec((1,256,128),lambda m,p:(m,0,p)),pl.BlockSpec((1,NS,128),lambda m,p:(m,0,p)),pl.BlockSpec((1,NS,128),lambda m,p:(m,0,p)),
        pl.BlockSpec((1,2,NK,128),lambda m,p:(m,0,0,0))],
      out_specs=[pl.BlockSpec((1,256,128),lambda m,p:(m,0,p)),pl.BlockSpec((1,1,512,128),lambda m,p:(m,p,0,0))],
      out_shape=[jax.ShapeDtypeStruct(q.shape,BF),jax.ShapeDtypeStruct((mb,npair,512,128),F32)],
      compiler_params=pltpu.CompilerParams(vmem_limit_bytes=56*2**20))(q,k,v,me)
def bwd_kernel(CH,q_ref,k_ref,v_ref,me_ref,o_ref,do_ref,l_ref,dq_ref,dk_ref,dv_ref,dka,dva):
    ind=block_columns()
    zero=jnp.zeros_like(ind)
    dka[...]=jnp.zeros_like(dka); dva[...]=jnp.zeros_like(dva)
    for h in range(2):
        rows=pl.ds(h*HALF,HALF)
        qs=split_heads(q_ref[0,rows,:])
        do2=do_ref[0,rows,:]
        dos=split_heads(do2)
        o2=o_ref[0,rows,:].astype(F32)
        delta=jnp.sum(dos.astype(F32)*jnp.concatenate([o2,o2],axis=0),axis=1,keepdims=True)
        lse=l_ref[0,0,pl.ds(h*256,256),0:1]
        qe=jnp.concatenate([qs,with_column(ind,-lse)],axis=1)
        doe=jnp.concatenate([dos,with_column(zero,-delta)],axis=1)
        dqt=jnp.zeros((128,256),F32)
        off=0
        for a,n in key_rows(h):
            c0=0
            while c0<n:
                c=min(CH,n-c0)
                kr=pl.ds(a+c0,c)
                k2=k_ref[0,kr,:]; v2=v_ref[0,kr,:]; me=me_ref[0,h,pl.ds(off+c0,c),:]
                st=dot_nt(jnp.concatenate([k2,me],axis=1),qe)
                pt=jnp.exp(st)
                dpt=dot_nt(jnp.concatenate([v2,me],axis=1),doe)
                ds=(pt*dpt).astype(BF)
                dva[kr,:]+=dot(pt.astype(BF),dos)
                dka[kr,:]+=dot(ds,qs)
                dqt=dqt+dot(k2.T,ds)
                c0+=c
            off+=n
        dq_ref[0,rows,:]=(merge_heads(dqt.T)*0.125).astype(BF)
    dk_ref[0]=dka[...].astype(BF); dv_ref[0]=dva[...].astype(BF)
def attn_bwd(q,k,v,me,o,do,l,CH=384):
    mb=q.shape[0]; npair=q.shape[2]//128
    qs=pl.BlockSpec((1,256,128),lambda m,p:(m,0,p)); ks=pl.BlockSpec((1,NS,128),lambda m,p:(m,0,p))
    return pl.pallas_call(functools.partial(bwd_kernel,CH),grid=(mb,npair),
      in_specs=[qs,ks,ks,pl.BlockSpec((1,2,NK,128),lambda m,p:(m,0,0,0)),qs,qs,pl.BlockSpec((1,1,512,128),lambda m,p:(m,p,0,0))],
      out_specs=[qs,ks,ks],
      out_shape=[jax.ShapeDtypeStruct(q.shape,BF),jax.ShapeDtypeStruct(k.shape,BF),jax.ShapeDtypeStruct(k.shape,BF)],
      scratch_shapes=[pltpu.VMEM((NS,128),F32)]*2,
      compiler_params=pltpu.CompilerParams(vmem_limit_bytes=56*2**20))(q,k,v,me,o,do,l)


BLK = 64
WIN = 8
RAND = 3
ALL = ("seq", "batch")


def vector_table(vectors, b_up, owner, width):
    lane = jnp.arange(width, dtype=jnp.int32)
    n, m = vectors[0].shape[0], b_up.shape[0]
    table = jnp.where(lane // n == owner, jnp.tile(jnp.stack(vectors).astype(F32), (1, width // n)), 0.0)
    flat = jnp.arange(4 * width, dtype=jnp.int32)
    ups = jnp.where(flat // m == owner, jnp.tile(b_up.astype(F32), 4 * width // m), 0.0).reshape(4, width)
    return jnp.concatenate([table, ups, jnp.zeros((4, width), F32)], axis=0)


def block_plan(lengths, randoms, device, blocks):
    ends = jnp.cumsum(lengths, axis=1)
    starts = ends - lengths

    def doc_of(block):
        at = block * BLK
        shape = (lengths.shape[0],) + (1,) * (block.ndim - 1) + (lengths.shape[1],)
        doc = jnp.sum((ends.reshape(shape) <= at[..., None]).astype(jnp.int32), axis=-1)
        doc = jnp.minimum(doc, lengths.shape[1] - 1)
        hit = jnp.arange(lengths.shape[1], dtype=jnp.int32) == doc[..., None]
        return doc, jnp.sum(jnp.where(hit, starts.reshape(shape), 0), axis=-1)

    mb = lengths.shape[0]
    half = jnp.arange(2, dtype=jnp.int32)
    query = device * 4 + 2 * half[:, None] + half[None, :]
    query = jnp.broadcast_to(query[None], (mb, 2, 2))
    q_doc, q_first = doc_of(query)
    window = device * 4 + 2 * half[:, None] - WIN + jnp.arange(2 * WIN + 2, dtype=jnp.int32)[None, :]
    window = jnp.broadcast_to(window[None], (mb, 2, 2 * WIN + 2))
    w_doc, w_first = doc_of(jnp.clip(window, 0, blocks - 1))
    w_good = (window >= 0) & (window < blocks) & (window * BLK - w_first >= 2 * BLK)
    see_window = (
        w_good[:, :, None, :]
        & (w_doc[:, :, None, :] == q_doc[..., None])
        & (jnp.abs(window[:, :, None, :] - query[..., None]) <= WIN)
    )
    see_glob = jnp.ones((mb, 2, 2, 2), bool)
    named = lax.dynamic_slice_in_dim(randoms, device * 4, 4, 1).reshape(mb, 2, 2, RAND)
    r_doc, r_first = doc_of(named)
    r_good = (
        (r_doc == q_doc[..., None])
        & (jnp.abs(named - query[..., None]) > WIN)
        & (named * BLK - r_first >= 2 * BLK)
    )
    see_random = (r_good[:, :, None] & jnp.eye(2, dtype=bool)[None, None, :, :, None]).reshape(mb, 2, 2, 2 * RAND)
    see = jnp.concatenate([see_window, see_glob, see_random], axis=3)
    chunk = jnp.clip(device + jnp.arange(-2, 3, dtype=jnp.int32), 0, blocks // 4 - 1) * (4 * BLK)
    where = jnp.concatenate(
        [jnp.broadcast_to(chunk[None], (mb, 5)), q_first[:, :, 0], named.reshape(mb, -1) * BLK], axis=1
    )
    rest = jnp.concatenate(
        [(where[:, 5:7, None] + jnp.arange(2 * BLK, dtype=jnp.int32)).reshape(mb, -1),
         (where[:, 7:, None] + jnp.arange(BLK, dtype=jnp.int32)).reshape(mb, -1)], axis=1
    )
    return where, jnp.where(see, 0.0, -1e30), rest[:, None]


def mask_columns(see):
    bias = jnp.broadcast_to(see[..., None], see.shape + (BLK,)).reshape(see.shape[:3] + (-1, 1))
    lane = jnp.arange(128, dtype=jnp.int32)
    ones = jnp.where((lane >= 2) & (lane < 5), 1.0, 0.0)
    return jnp.where(lane == 0, bias[:, :, 0], jnp.where(lane == 1, bias[:, :, 1], ones)).astype(BF)


def on_device(inputs, cotangent, doc_lengths, random_blocks, wq, wk, wv, wo, wu, wd, b_query, b_value, b_out,
              b_up, b_down, gain_attn, bias_attn, gain_ffn, bias_ffn):
    mb, _, rows, width = inputs.shape
    devices, owners = lax.axis_size("seq"), lax.axis_size("seq") * lax.axis_size("batch")
    device = lax.axis_index("seq")
    owner = device * lax.axis_size("batch") + lax.axis_index("batch")
    linked = devices == 8 and owners == 32
    seq_len = devices * rows
    x, cot = inputs[:, 0], cotangent[:, 0]
    where, see, rest = block_plan(doc_lengths[:, 0], random_blocks[:, 0], device, seq_len // BLK)
    vectors = (b_query, b_value, b_out, b_down, gain_attn, bias_attn, gain_ffn, bias_ffn)
    table = vector_table(vectors, b_up, owner, width)
    flat = lambda t: t.reshape(-1, t.shape[-1])
    if linked:
        att, lse, q, xs, k, v, wall, top, bias = forward_all(rest[:, 0, ::BLK] // BLK, see, x, (wq, wk, wv, wo, wu, wd), table)
    else:
        extra = mask_columns(see)
        xall = lax.all_gather(x, "seq", axis=1, tiled=True)
        bias = lax.psum(table, ALL)
        full = [lax.all_gather(w, ALL, axis=0, tiled=True) for w in (wq, wk, wv, wo, wu, wd)]
        fold = lambda w: w.reshape(16, -1, width)
        up = full[4].reshape(16, 48, 4, width).transpose(0, 2, 1, 3).reshape(16, 192, width)
        wall = jnp.concatenate([fold(full[3]), up, fold(full[5])], axis=1)
        top = jnp.concatenate([jnp.zeros((16, 16, width), BF)] + [fold(w) for w in full[:3]], axis=1)
        xs, k, v, q = project(where, xall, top, bias)
        att, lse = attn_fwd(q, k, v, extra)
    out, datt, done, go, gu, gd, gb = middle(flat(att), flat(x), flat(cot), wall, bias)
    datt, done = datt.reshape(att.shape), done.reshape(mb, rows, width)
    if linked:
        *grads, gb, dx = backward_all(see, q, att, datt, lse, x, rest, gb, done, k, v, xs, top, go, gu, gd)
    else:
        dq, dk, dv = attn_bwd(q, k, v, extra, att, datt, lse, 640)
        dxs, own, gq, gk, gv, gb = back(where, xs, dk, dv, dq, done, top, gb, 0)
        start = (where[:, :5, None] + jnp.arange(0, 256, BLK)).reshape(mb, -1)
        glob = (where[:, 5:7, None] + jnp.arange(0, 128, BLK)).reshape(mb, -1)
        to = jnp.concatenate([start, glob, where[:, 7:]], axis=1) // BLK
        parts = dxs.reshape(mb, -1, BLK, width)
        total = jnp.zeros((mb, seq_len // BLK, BLK, width), F32)
        total = jax.vmap(lambda t, i, p: t.at[i].add(p))(total, to, parts.astype(F32))
        dx = own + lax.psum_scatter(total.reshape(mb, seq_len, width), "seq", scatter_dimension=1, tiled=True)
        grads = [lax.psum_scatter(g.astype(F32), ALL, scatter_dimension=0, tiled=True) for g in (gq, gk, gv, go, gu, gd)]
        gb = lax.psum(gb, ALL)
    n, m = b_query.shape[0], b_up.shape[0]
    small = lax.dynamic_slice_in_dim(gb[:8], owner * n, n, 1)
    ups = lax.dynamic_slice_in_dim(gb[8:12].reshape(-1), owner * m, m, 0)
    return (
        out.reshape(inputs.shape), dx[:, None], *grads,
        small[0], small[1], small[2], ups, small[3], small[4], small[5], small[6], small[7],
    )


def solution(mesh):
    tokens = P(None, "batch", "seq", None)
    mat, vec = P(ALL, None), P(ALL)
    in_specs = (tokens, tokens, P(None, "batch", None), P(None, "batch", None, None)) + (mat,) * 6 + (vec,) * 9
    out_specs = (tokens, tokens) + (mat,) * 6 + (vec,) * 9
    return jax.shard_map(on_device, mesh=mesh, in_specs=in_specs, out_specs=out_specs, check_vma=False)
```

```python
import functools

import jax
import jax.numpy as jnp
from jax import lax
from jax.experimental import pallas as pl
from jax.experimental.pallas import tpu as pltpu
from jax.sharding import PartitionSpec as P

F32 = jnp.float32
BF = jnp.bfloat16


HALF, WK, NW, NK, NS = 128, 1152, 1280, 1664, 2304
TOP, REST = 160, 432
MESH = pl.DeviceIdType.MESH
UP, DOWN, XX, YY, CC = range(5)
WAYS = (UP, DOWN, XX, YY, CC)


def dot(a, b):
    return lax.dot_general(a, b, (((1,), (0,)), ((), ())), preferred_element_type=F32)


def dot_nt(a, b):
    return lax.dot_general(a, b, (((1,), (1,)), ((), ())), preferred_element_type=F32)


def dot_tn(a, b):
    return lax.dot_general(a, b, (((0,), (0,)), ((), ())), preferred_element_type=F32)


def place():
    s, b = lax.axis_index("seq"), lax.axis_index("batch")
    return s // 2, s % 2, b // 2, b % 2


def device(z, x, y, c):
    return (2 * z + x, 2 * y + c)


def greet(z, x, y, c):
    barrier = pltpu.get_barrier_semaphore()

    def tell(to):
        pl.semaphore_signal(barrier, inc=1, device_id=to, device_id_type=MESH)

    tell(device(z, 1 - x, y, c))
    tell(device(z, x, 1 - y, c))
    tell(device(z, x, y, 1 - c))
    pl.when(z > 0)(lambda: tell(device(z - 1, x, y, c)))
    pl.when(z < 3)(lambda: tell(device(z + 1, x, y, c)))
    pl.semaphore_wait(barrier, 3 + (z > 0).astype(jnp.int32) + (z < 3).astype(jnp.int32))


def lanes(c):
    return pl.ds(pl.multiple_of(c * 384, 128), 384)


def rows_at(i, n):
    return pl.ds(pl.multiple_of(i * n, n), n)


def remote(src, dst, send, recv, to):
    return pltpu.make_async_remote_copy(
        src_ref=src, dst_ref=dst, send_sem=send, recv_sem=recv, device_id=to, device_id_type=MESH
    )


def key_rows(h):
    return ((HALF * h, WK), (NW + HALF * h, HALF), (NW + 2 * HALF + 384 * h, 384))


def split_heads(v):
    lane = lax.broadcasted_iota(jnp.int32, v.shape, 1)
    z = jnp.zeros_like(v)
    return jnp.concatenate([jnp.where(lane < 64, v, z), jnp.where(lane >= 64, v, z)], axis=0)


def merge_heads(v):
    n = v.shape[0] // 2
    lane = lax.broadcasted_iota(jnp.int32, (n, v.shape[1]), 1)
    return jnp.where(lane < 64, v[:n], v[n:])


def block_columns():
    r = lax.broadcasted_iota(jnp.int32, (2 * HALF, 128), 0)
    lane = lax.broadcasted_iota(jnp.int32, (2 * HALF, 128), 1)
    first = (r % HALF) < 64
    return jnp.where(((lane == 0) & first) | ((lane == 1) & jnp.logical_not(first)), 1.0, 0.0)


def with_column(base, col):
    lane = lax.broadcasted_iota(jnp.int32, base.shape, 1)
    hi = col.astype(BF).astype(F32)
    rest = col - hi
    mid = rest.astype(BF).astype(F32)
    return jnp.where(lane == 2, hi, jnp.where(lane == 3, mid, jnp.where(lane == 4, rest - mid, base))).astype(BF)


def doc_of(lengths, m, block):
    at = block * 64
    doc, first, end = jnp.int32(0), jnp.int32(0), jnp.int32(0)
    for i in range(3):
        end = end + lengths[m, i]
        doc = doc + (end <= at).astype(jnp.int32)
        first = jnp.where(end <= at, end, first)
    return doc, first


def write_extra(lengths, randoms, s, extra):
    lane = lax.broadcasted_iota(jnp.int32, (64, 128), 1)
    ones = jnp.where((lane >= 2) & (lane < 5), 1.0, 0.0)

    def one(i, _):
        m, h, t = i // 52, (i // 26) % 2, i % 26
        r = jnp.maximum(t - 20, 0)
        named = randoms[m, 4 * s + 2 * h + r // 3, r % 3]
        block = jnp.where(t < 18, 4 * s + 2 * h - 8 + t, named)
        inside = (block >= 0) & (block < 32)
        doc, first = doc_of(lengths, m, jnp.clip(block, 0, 31))
        good = inside & (block * 64 - first >= 128)
        terms = []
        for k in range(2):
            query = 4 * s + 2 * h + k
            q_doc, _ = doc_of(lengths, m, query)
            near = jnp.abs(block - query) <= 8
            window = (t < 18) & near
            named_here = (t >= 20) & (r // 3 == k) & jnp.logical_not(near)
            seen = ((t >= 18) & (t < 20)) | (good & (doc == q_doc) & (window | named_here))
            terms.append(jnp.where(seen, 0.0, -1e30))
        value = jnp.where(lane == 0, terms[0], jnp.where(lane == 1, terms[1], ones))
        extra[m, h, rows_at(t, 64), :] = value.astype(BF)
        return 0

    lax.fori_loop(0, 104, one, 0)


def rest_block(lengths, randoms, s, m, t):
    r = jnp.maximum(t - 4, 0)
    named = randoms[m, 4 * s + r // 3, r % 3]
    _, first = doc_of(lengths, m, 4 * s + 2 * jnp.minimum(t // 2, 1))
    return jnp.where(t < 4, first // 64 + t % 2, named)


def forward_kernel(lengths, randoms, x_ref, wq, wk, wv, wo, wu, wd, vectors, b_up,
                   att, lse, q_out, xs_out, k_out, v_out, wall, top_out, bias, extra, targets,
                   own, mate, merged, merged_b, xall0, xall1, xs, ks, vs, wa,
                   mate_sem, lsem, osem, asend, arecv, acrecv, bsend, brecv, bcrecv, xsend, xrecv):
    z, x, y, c = place()
    s = 2 * z + x
    to = {UP: device(z + 1, x, y, c), DOWN: device(z - 1, x, y, c), XX: device(z, 1 - x, y, c),
          YY: device(z, x, 1 - y, c), CC: device(z, x, y, 1 - c)}
    mine, theirs = lanes(c), lanes(1 - c)
    xall = (xall0, xall1)

    def guarded(way, act):
        if way == UP:
            pl.when(z < 3)(act)
        elif way == DOWN:
            pl.when(z > 0)(act)
        else:
            act()

    def x_copy(m, zz, xx, way, own_rows=False):
        i = 2 * zz + xx
        ref = xall[m].at[pl.ds(4 * i, 4)]
        return remote(x_ref.at[m] if own_rows else ref, ref, xsend.at[m, i, way], xrecv.at[m, i], to[way])

    def a_copy(zz, xx, yy, way, src=None):
        i = (2 * zz + xx) * 2 + yy
        ref = wa.at[i, :, mine]
        return remote(ref if src is None else src, ref, asend.at[i, way],
                      acrecv.at[i] if way == CC else arecv.at[i], to[way])

    def b_copy(zz, xx, yy, way, src=None):
        i = (2 * zz + xx) * 2 + yy
        ref = wall.at[i, :, mine]
        return remote(ref if src is None else src, ref, bsend.at[i, way],
                      bcrecv.at[i] if way == CC else brecv.at[i], to[way])

    greet(z, x, y, c)
    for way in (UP, DOWN, XX):
        guarded(way, lambda way=way: x_copy(0, z, x, way, True).start())
    for m in range(2):
        pltpu.make_async_copy(x_ref.at[m], xall[m].at[pl.ds(4 * s, 4)], lsem.at[m]).start()
    owner = 4 * s + 2 * y + c
    small = vectors[...].astype(F32)
    n = small.shape[1]
    own[0:8, :] = pltpu.roll(jnp.concatenate([small, jnp.zeros((8, 768 - n), F32)], axis=1), owner * n, axis=1)
    ups = b_up[...].astype(F32)
    n = ups.shape[1]
    ups = jnp.concatenate([ups, jnp.zeros((1, 768 - n), F32)], axis=1)
    ups = pltpu.roll(jnp.broadcast_to(ups, (8, 768)), (owner % 8) * n, axis=1)
    row = lax.broadcasted_iota(jnp.int32, (8, 768), 0)
    own[8:16, :] = jnp.where(row == owner // 8, ups, 0.0)
    for i, ref in enumerate((wq, wk, wv, wo)):
        own[16 + 24 * i:40 + 24 * i, :] = ref[...].astype(F32)
    for j in range(4):
        own[112 + 24 * j:136 + 24 * j, :] = wu[:, 768 * j:768 * j + 768].astype(F32)
    own[208:304, :] = wd[...].astype(F32)
    swap = remote(own.at[:, theirs], mate, mate_sem.at[0], mate_sem.at[1], to[CC])
    swap.start()
    swap.wait()

    def paired(start, n):
        here, there = own[start:start + n, mine], mate[start:start + n, :]
        return jnp.where(c == 0, jnp.concatenate([here, there], 0), jnp.concatenate([there, here], 0)).astype(BF)

    merged[0:16, :] = (own[0:16, mine] + mate[0:16, :]).astype(BF)
    for i in range(3):
        merged[16 + 48 * i:64 + 48 * i, :] = paired(16 + 24 * i, 24)
    keep_a = pltpu.make_async_copy(merged, wa.at[s * 2 + y, :, mine], lsem.at[2])
    keep_a.start()
    for way in WAYS:
        guarded(way, lambda way=way: a_copy(z, x, y, way, merged).start())
    for i in range(5):
        merged_b[48 * i:48 * i + 48, :] = paired(88 + 24 * i, 24)
    merged_b[240:432, :] = paired(208, 96)
    b_copy(z, x, y, YY, merged_b).start()
    b_copy(z, x, y, CC, merged_b).start()
    keep_b = pltpu.make_async_copy(merged_b, wall.at[s * 2 + y, :, mine], lsem.at[3])
    keep_b.start()
    write_extra(lengths, randoms, s, extra)

    lane = lax.broadcasted_iota(jnp.int32, (1, 1024), 1)
    for m in range(2):
        targets[m] = lax.fori_loop(
            0, 16, lambda t, v, m=m: jnp.where(
                lane // 64 == t, rest_block(lengths, randoms, s, m, t) * 64 + lane % 64, v), jnp.zeros_like(lane))

    def x_line(m, k, a=True):
        def below():
            x_copy(m, z - k, x, UP).wait_recv()
            pl.when(z < 3)(lambda: x_copy(m, z - k, x, UP).start())
            x_copy(m, z - k, x, XX).start()

        def above():
            x_copy(m, z + k, x, DOWN).wait_recv()
            pl.when(z > 0)(lambda: x_copy(m, z + k, x, DOWN).start())
            x_copy(m, z + k, x, XX).start()

        pl.when((z >= k) & (k <= 3))(below)
        pl.when(z + k <= 3)(above)

    def w_line(copy, k):
        def below():
            copy(z - k, x, y, UP).wait_recv()
            pl.when(z < 3)(lambda: copy(z - k, x, y, UP).start())
            for way in (XX, YY, CC):
                copy(z - k, x, y, way).start()

        def above():
            copy(z + k, x, y, DOWN).wait_recv()
            pl.when(z > 0)(lambda: copy(z + k, x, y, DOWN).start())
            for way in (XX, YY, CC):
                copy(z + k, x, y, way).start()

        pl.when((z >= k) & (k <= 3))(below)
        pl.when(z + k <= 3)(above)

    def at_distance(act, k):
        pl.when((k >= 0) & (k <= z))(lambda: act(z - k))
        pl.when((k > 0) & (z + k <= 3))(lambda: act(z + k))

    def w_from_x(copy, k):
        def act(zz):
            copy(zz, 1 - x, y, XX).wait_recv()
            copy(zz, 1 - x, y, YY).start()
            copy(zz, 1 - x, y, CC).start()

        at_distance(act, k)

    def w_from_y(copy, xx, k):
        def act(zz):
            copy(zz, xx, 1 - y, YY).wait_recv()
            copy(zz, xx, 1 - y, CC).start()

        at_distance(act, k)

    zfirst = c == 0

    def b_own_column(k):
        def passed(zz, way, more):
            b_copy(zz, x, y, way).wait_recv()
            pl.when(more)(lambda: b_copy(zz, x, y, way).start())
            b_copy(zz, x, y, YY).start()
            b_copy(zz, x, y, CC).start()

        pl.when((z >= k) & (k <= 3))(lambda: passed(z - k, UP, z < 3))
        pl.when(z + k <= 3)(lambda: passed(z + k, DOWN, z > 0))

    def b_to_x(k):
        def across(zz):
            b_copy(zz, x, y, XX).start()

        pl.when(zfirst)(lambda: at_distance(across, k))

    def b_other_column(k):
        def shared(zz):
            b_copy(zz, 1 - x, y, YY).start()
            b_copy(zz, 1 - x, y, CC).start()

        def crossed(zz):
            b_copy(zz, 1 - x, y, XX).wait_recv()
            shared(zz)

        def passed(zz, way, more):
            b_copy(zz, 1 - x, y, way).wait_recv()
            pl.when(more)(lambda: b_copy(zz, 1 - x, y, way).start())
            shared(zz)

        def first():
            crossed(z)
            pl.when(jnp.logical_not(zfirst) & (z < 3))(lambda: b_copy(z, 1 - x, y, UP).start())
            pl.when(jnp.logical_not(zfirst) & (z > 0))(lambda: b_copy(z, 1 - x, y, DOWN).start())

        def later():
            pl.when(zfirst)(lambda: at_distance(crossed, k))
            pl.when(jnp.logical_not(zfirst) & (z >= k))(lambda: passed(z - k, UP, z < 3))
            pl.when(jnp.logical_not(zfirst) & (z + k <= 3))(lambda: passed(z + k, DOWN, z > 0))

        pl.when(k == 0)(first)
        pl.when((k > 0) & (k <= 3))(later)

    def start_x1(way):
        guarded(way, lambda: x_copy(1, z, x, way, True).start())

    def start_relay(k, _):
        x_line(0, k)
        w_line(a_copy, k)
        w_from_x(a_copy, k - 1)

        @pl.when(k == 2)
        def _():
            start_x1(UP)
            start_x1(DOWN)
            for way in (UP, DOWN):
                guarded(way, lambda way=way: b_copy(z, x, y, way, merged_b).start())

        return 0

    lax.fori_loop(1, 4, start_relay, 0)
    start_x1(XX)
    w_from_x(a_copy, 3)
    x_line(1, 1)
    b_copy(z, x, y, XX, merged_b).start()
    for xx in (x, 1 - x):
        lax.fori_loop(0, 4, lambda k, _, xx=xx: (w_from_y(a_copy, xx, k), 0)[1], 0)
    keep_a.wait()

    def arrived(i, _):
        ref = wa.at[i, :, theirs]
        remote(ref, ref, asend.at[i, CC], acrecv.at[i], to[CC]).wait_recv()
        return 0

    lax.fori_loop(0, 16, arrived, 0)
    bias[...] = jnp.sum(wa[:, 0:16, :].astype(F32), axis=0)
    top_copy = pltpu.make_async_copy(wa, top_out, lsem.at[4])
    top_copy.start()
    lane = lax.broadcasted_iota(jnp.int32, (HALF, 128), 1)
    ind = block_columns().astype(BF)
    lse[...] = jnp.zeros_like(lse)

    def out_copy(m, t):
        src, dst = ((xs, xs_out), (ks, k_out), (vs, v_out))[t]
        return pltpu.make_async_copy(src.at[m], dst.at[m], osem.at[m, t])

    def gather(m):
        def x_here(zz):
            x_copy(m, zz, 1 - x, XX).wait_recv()

        for k in range(4):
            at_distance(x_here, k)
        pltpu.make_async_copy(x_ref.at[m], xall[m].at[pl.ds(4 * s, 4)], lsem.at[m]).wait()
        for t in range(5):
            chunk = xall[m][pl.ds(4 * jnp.clip(s - 2 + t, 0, 7), 4)]
            xs[m, 256 * t:256 * t + 256, :] = chunk.reshape(256, chunk.shape[-1])

        def named(t, _):
            xs[m, pl.ds(pl.multiple_of(NW + 64 * t, 64), 64), :] = xall[m][rest_block(lengths, randoms, s, m, t)]
            return 0

        lax.fori_loop(0, 16, named, 0)
        out_copy(m, 0).start()
        q = (dot(xs[m, 512:768, :], wa[:, 16:64, :].reshape(768, 768)) + bias[0:1, :]).astype(BF)
        q_out[m] = q * jnp.asarray(0.125, BF)

    def project(m, i):
        r = rows_at(i, 768)
        rows = xs[m, r, :]
        ks[m, r, :] = dot(rows, wa[:, 64:112, :].reshape(768, 768)).astype(BF)
        vs[m, r, :] = (dot(rows, wa[:, 112:160, :].reshape(768, 768)) + bias[1:2, :]).astype(BF)

    def pair(m, p):
        col = pl.ds(pl.multiple_of(p * 128, 128), 128)
        for h in range(2):
            r = pl.ds(h * HALF, HALF)
            more = extra[m, h]
            keys = jnp.concatenate([ks[m, a:a + n, col] for a, n in key_rows(h)], axis=0)
            vals = jnp.concatenate([vs[m, a:a + n, col] for a, n in key_rows(h)], axis=0)
            scores = dot_nt(jnp.concatenate([split_heads(q_out[m, r, col]), ind], axis=1),
                            jnp.concatenate([keys, more], axis=1))
            top = jnp.max(scores, axis=1, keepdims=True)
            e = jnp.exp(scores - top).astype(BF)
            o = dot(e, jnp.concatenate([vals, more], axis=1))
            total = o[:, 130:131]
            att[m, r, col] = merge_heads(o[:, :128] / total).astype(BF)
            norm = top + jnp.log(total)
            lse[m, r, :] = jnp.where(lane == 2 * p, norm[:HALF], jnp.where(lane == 2 * p + 1, norm[HALF:], lse[m, r, :]))

    def picked(g, plan):
        k = jnp.full((), 9, jnp.int32)
        for at, value in plan:
            k = jnp.where(g == at, value, k)
        return k

    def pump(g):
        x_line(1, picked(g, PUMP_X))
        b_own_column(picked(g, PUMP_OWN))
        b_other_column(picked(g, PUMP_OTHER))
        b_to_x(picked(g, PUMP_CROSS))
        w_from_y(b_copy, x, picked(g, PUMP_Y0))
        w_from_y(b_copy, 1 - x, picked(g, PUMP_Y1))

    def step(g, _):
        m, i = g // 9, g % 9
        pl.when(g == 0)(lambda: gather(0))
        pl.when(g == 9)(lambda: gather(1))
        pl.when(i < 3)(lambda: project(m, i))

        @pl.when(i == 3)
        def _():
            out_copy(m, 1).start()
            out_copy(m, 2).start()

        pl.when(i >= 3)(lambda: pair(m, i - 3))
        pump(g)
        return 0

    lax.fori_loop(0, 18, step, 0)

    lax.fori_loop(18, 26, lambda g, _: (pump(g), 0)[1], 0)

    def b_arrived(i, _):
        ref = wall.at[i, :, theirs]
        remote(ref, ref, bsend.at[i, CC], bcrecv.at[i], to[CC]).wait_recv()
        return 0

    lax.fori_loop(0, 16, b_arrived, 0)
    keep_b.wait()
    top_copy.wait()
    for m in range(2):
        for t in range(3):
            out_copy(m, t).wait()

    def sent(k, _):
        for m in range(2):
            x_copy(m, k, x, XX).wait_send()
        for copy in (a_copy, b_copy):
            for way in (YY, CC):
                copy(k, x, y, way).wait_send()
                copy(k, 1 - x, y, way).wait_send()
            copy(k, x, 1 - y, CC).wait_send()
            copy(k, 1 - x, 1 - y, CC).wait_send()
        a_copy(k, x, y, XX).wait_send()
        pl.when(zfirst | (k == z))(lambda: b_copy(k, x, y, XX).wait_send())

        def line(way):
            x_copy(0, k, x, way).wait_send()
            x_copy(1, k, x, way).wait_send()
            a_copy(k, x, y, way).wait_send()
            b_copy(k, x, y, way).wait_send()
            pl.when(jnp.logical_not(zfirst))(lambda: b_copy(k, 1 - x, y, way).wait_send())

        pl.when((k <= z) & (z < 3))(lambda: line(UP))
        pl.when((k >= z) & (z > 0))(lambda: line(DOWN))
        return 0

    lax.fori_loop(0, 4, sent, 0)


PUMP_X = ((1, 2), (6, 3))
PUMP_OWN = ((0, 1), (4, 2), (8, 3))
PUMP_OTHER = ((3, 0), (8, 1), (12, 2), (15, 3))
PUMP_CROSS = ((6, 1), (8, 2), (9, 3))
PUMP_Y0 = ((1, 0), (3, 1), (7, 2), (10, 3))
PUMP_Y1 = ((7, 0), (12, 1), (15, 2), (18, 3))


def forward_all(lengths, randoms, x, weights, vectors, b_up):
    dma = pltpu.SemaphoreType.DMA
    sd = jax.ShapeDtypeStruct
    vm, anywhere, sm = (pl.BlockSpec(memory_space=m) for m in (pltpu.VMEM, pl.ANY, pltpu.SMEM))
    mb, rows, width = x.shape
    v = pltpu.VMEM
    return pl.pallas_call(
        forward_kernel,
        out_shape=[
            sd((mb, rows, width), BF), sd((mb, rows, 128), F32), sd((mb, rows, width), BF),
            sd((mb, NS, width), BF), sd((mb, NS, width), BF), sd((mb, NS, width), BF),
            sd((16, REST, width), BF), sd((16, TOP, width), BF), sd((16, width), F32),
            sd((mb, 2, NK, 128), BF), sd((mb, 1, 1024), jnp.int32),
        ],
        in_specs=[sm, sm, anywhere] + [vm] * 8,
        out_specs=[vm, vm, vm, anywhere, anywhere, anywhere, anywhere, anywhere, vm, vm, vm],
        scratch_shapes=[
            v((304, width), F32), v((304, 384), F32), v((TOP, 384), BF), v((REST, 384), BF),
            v((8 * rows // 64, 64, width), BF), v((8 * rows // 64, 64, width), BF),
            v((mb, NS, width), BF), v((mb, NS, width), BF), v((mb, NS, width), BF),
            v((16, TOP, width), BF),
            dma((2,)), dma((5,)), dma((mb, 3)),
            dma((16, 5)), dma((16,)), dma((16,)), dma((16, 5)), dma((16,)), dma((16,)),
            dma((mb, 8, 3)), dma((mb, 8)),
        ],
        compiler_params=pltpu.CompilerParams(
            collective_id=0, has_side_effects=True, vmem_limit_bytes=60 * 2**20
        ),
    )(lengths, randoms, x.reshape(mb, rows // 64, 64, width), *weights, vectors, b_up)


def backward_kernel(datt, stats, tgt, gb_in, extra_in, q_in, done, k_in, v_in, xs_in, top_in, go, gu, gd,
                    oq, ok, ov, oo, ou, od, ob, odx,
                    kb, vb, xsb, wa, extra, dka, dva, q, ga, gb,
                    acc, mate, yr, mate2, yr2, xr, zr, dxp, dxr, dzr, fin, rcv,
                    ksem, lsem, msem, msem2, asem, ysem, xsem, zsem, ysem2, xsem2, zsem2, dxsem, dzsem, fsem, ready):
    z, x, y, c = place()
    s = 2 * z + x
    mine, theirs = lanes(c), lanes(1 - c)
    near_x, near_y, near_c = device(z, 1 - x, y, c), device(z, x, 1 - y, c), device(z, x, y, 1 - c)
    above, below = device(z + 1, x, y, c), device(z - 1, x, y, c)

    def far(i):
        inner = jnp.where(i == 0, 3, jnp.where(i == 1, 0, jnp.where(i == 2, 2, 1)))
        low = jnp.where(z == 0, 3 - i, jnp.where(z == 1, inner, i))
        return jnp.where(z == 2, 3 - inner, low)

    def slot_of(i, zz):
        zt = jnp.where(zz == 0, 3 - i, jnp.where((zz == 1) & (i == 2), 2, 3))
        return zt, (zz == 0) | ((zz == 1) & (i >= 1)) | ((zz == 2) & (i == 2))

    def at_slot(act, i):
        up, sends_up = slot_of(i, z)
        down, sends_down = slot_of(i, 3 - z)
        pl.when(sends_up)(lambda: act(up, True))
        pl.when(sends_down)(lambda: act(3 - down, False))

    def column(p):
        return pl.ds(pl.multiple_of(p * 128, 128), 128)

    def load_keys(m, p):
        return (pltpu.make_async_copy(k_in.at[m, :, column(p)], kb.at[:, column(p)], ksem.at[0, p]),
                pltpu.make_async_copy(v_in.at[m, :, column(p)], vb.at[:, column(p)], ksem.at[1, p]))

    def start_keys(m):
        def one(p, _):
            for cp in load_keys(m, p):
                cp.start()
            return 0

        lax.fori_loop(0, 6, one, 0)

    start_keys(0)
    extra_copy = pltpu.make_async_copy(extra_in, extra, lsem.at[4])
    extra_copy.start()
    q_copy = pltpu.make_async_copy(q_in, q, lsem.at[3])
    q_copy.start()
    top_copy = pltpu.make_async_copy(top_in.at[:, :, pl.ds(16, 144), :], wa, lsem.at[0])
    top_copy.start()
    done_copy = pltpu.make_async_copy(done, odx, lsem.at[1])
    done_copy.start()
    greet(z, x, y, c)

    def parts(yy, cc):
        off = pl.multiple_of(cc * 384, 128)
        yield 0, go.at[:, yy, :, pl.ds(off, 384)], pl.ds(0, 48)
        yield 1, gd.at[:, yy, :, pl.ds(off, 384)], pl.ds(240, 192)
        for j in range(4):
            col = pl.multiple_of(j * 768 + cc * 384, 128)
            yield 2 + j, gu.at[:, yy, :, pl.ds(col, 384)], pl.ds(48 + 48 * j, 48)

    swaps, loads = {}, {}
    for t, yy in enumerate((1 - y, y)):
        for i, src, rows in parts(yy, 1 - c):
            swaps[t, i] = remote(src, mate.at[:, yy, rows, :], msem.at[0, t, i], msem.at[1, t, i], near_c)
            swaps[t, i].start()
        for i, src, rows in parts(yy, c):
            loads[t, i] = pltpu.make_async_copy(src, acc.at[:, yy, rows, :], asem.at[t, i])
            loads[t, i].start()
    gb[...] = gb_in[...]

    class Reduce:
        def __init__(self, rows, held, cols, other, from_y, ys, xs_, zs):
            self.rows, self.held, self.cols, self.other, self.from_y = rows, held, cols, other, from_y
            self.ys, self.xs, self.zs = ys, xs_, zs

        def a(self, s_, yy):
            return self.held.at[s_, yy, :, self.cols]

        def y_copy(self, s_):
            return remote(self.a(s_, 1 - y), self.from_y.at[s_], self.ys.at[0, s_], self.ys.at[1, s_], near_y)

        def x_copy(self, zz):
            return remote(self.a(2 * zz + 1 - x, y), xr.at[zz, pl.ds(0, self.rows), :], self.xs.at[0, zz],
                          self.xs.at[1, zz], near_x)

        def z_copy(self, zz, slot, to):
            return remote(self.a(2 * zz + x, y), zr.at[slot, pl.ds(0, self.rows), :], self.zs.at[0, zz],
                          self.zs.at[1, slot], to)

        def total(self, s_, yy, others):
            value = self.held[s_, yy, :, self.cols].astype(F32) + self.other[s_, yy].astype(F32)
            for ref, index in others:
                value = value + ref[index, 0:self.rows, :].astype(F32)
            return value

        def keep(self, s_, yy, value):
            self.held[s_, yy, :, self.cols] = value.astype(BF)

        def y_step(self, i):
            s_ = 2 * far(i % 4) + jnp.where(i < 4, 1 - x, x)
            self.keep(s_, 1 - y, self.total(s_, 1 - y, []))
            self.y_copy(s_).start()

        def x_step(self, i):
            zz = far(i)
            s_ = 2 * zz + 1 - x
            self.y_copy(s_).wait_recv()
            self.keep(s_, y, self.total(s_, y, [(self.from_y, s_)]))
            self.x_copy(zz).start()

        def along(self, zz, up):
            s_ = 2 * zz + x
            self.y_copy(s_).wait_recv()
            self.x_copy(zz).wait_recv()
            others = [(self.from_y, s_), (xr, zz)]
            more = z > 0 if up else z < 3

            @pl.when(more)
            def _():
                self.z_copy(zz, zz, above).wait_recv()
                self.keep(s_, y, self.total(s_, y, others + [(zr, zz)]))

            @pl.when(jnp.logical_not(more))
            def _():
                self.keep(s_, y, self.total(s_, y, others))

            if up:
                self.z_copy(zz, zz, above).start()
            else:
                self.z_copy(zz, jnp.where(zz == z - 1, 4, zz), below).start()

        def z_step(self, i):
            at_slot(self.along, i)

        def finish(self):
            self.y_copy(s).wait_recv()
            self.x_copy(z).wait_recv()
            r = pl.ds(0, self.rows)
            fin[r, :] = self.total(s, y, [(self.from_y, s), (xr, z)])
            for slot, cond in ((z, z > 0), (4, z < 3)):
                @pl.when(cond)
                def _(slot=slot):
                    self.z_copy(z, slot, above).wait_recv()
                    fin[r, :] += zr[slot, r, :].astype(F32)

        def drain(self):
            def one(i, _):
                self.y_copy(i).wait_send()
                return 0

            lax.fori_loop(0, 8, one, 0)

            def two(i, _):
                self.x_copy(i).wait_send()
                pl.when(i != z)(lambda: self.z_copy(i, i, above).wait_send())
                return 0

            lax.fori_loop(0, 4, two, 0)

    rest = Reduce(REST, acc, pl.ds(0, 384), mate, yr, ysem, xsem, zsem)
    top = Reduce(TOP, ga, mine, mate2, yr2, ysem2, xsem2, zsem2)

    def dx_x(m, zz):
        return remote(dxp.at[m, 2 * zz + 1 - x], dxr.at[m, zz], dxsem.at[0, m, zz], dxsem.at[1, m, zz], near_x)

    def dx_z(m, zz, slot, to):
        return remote(dxp.at[m, 2 * zz + x], dzr.at[m, slot], dzsem.at[0, m, zz], dzsem.at[1, m, slot], to)

    def dx_along(m, zz, up):
        s_ = 2 * zz + x
        dx_x(m, zz).wait_recv()
        more = z > 0 if up else z < 3

        @pl.when(more)
        def _():
            dx_z(m, zz, zz, above).wait_recv()
            dxp[m, s_] = (dxp[m, s_].astype(F32) + dxr[m, zz].astype(F32) + dzr[m, zz].astype(F32)).astype(BF)

        @pl.when(jnp.logical_not(more))
        def _():
            dxp[m, s_] = (dxp[m, s_].astype(F32) + dxr[m, zz].astype(F32)).astype(BF)

        if up:
            dx_z(m, zz, zz, above).start()
        else:
            dx_z(m, zz, jnp.where(zz == z - 1, 4, zz), below).start()

    def dx_step(m, i):
        at_slot(functools.partial(dx_along, m), i)

    def dx_finish(m):
        dx_x(m, z).wait_recv()
        odx[m] += dxr[m, z].astype(F32)
        for slot, cond in ((z, z > 0), (4, z < 3)):
            @pl.when(cond)
            def _(slot=slot):
                dx_z(m, z, slot, above).wait_recv()
                odx[m] += dzr[m, slot].astype(F32)

    def dx_sent(m):
        def one(i, _):
            dx_x(m, i).wait_send()
            pl.when(i != z)(lambda: dx_z(m, i, i, above).wait_send())
            return 0

        lax.fori_loop(0, 4, one, 0)

    ind = block_columns()

    def pair(m, p):
        col = column(p)
        for cp in load_keys(m, p):
            cp.wait()
        dka[...] = jnp.zeros_like(dka)
        dva[...] = jnp.zeros_like(dva)
        for h in range(2):
            rows = pl.ds(h * HALF, HALF)
            qs = split_heads(q[m, rows, col])
            dos = split_heads(datt[m, rows, col])
            lane = lax.broadcasted_iota(jnp.int32, (HALF, 128), 1)

            def both(first, rows=rows, lane=lane):
                return jnp.concatenate(
                    [jnp.sum(jnp.where(lane == first + a, stats[m, rows, :], 0.0), axis=1, keepdims=True) for a in range(2)],
                    axis=0)

            log_norm, delta = both(2 * p), both(16 + 2 * p)
            qe = jnp.concatenate([qs, with_column(ind, -log_norm)], axis=1)
            doe = jnp.concatenate([dos, with_column(jnp.zeros_like(ind), -delta)], axis=1)
            dqt = jnp.zeros((128, 2 * HALF), F32)
            (wa_, wn), (ga, gn), (ra, rn) = key_rows(h)
            off = 0
            for pieces in (((wa_, 576),), ((wa_ + 576, 576),), ((ga, gn), (ra, rn))):
                n = sum(t for _, t in pieces)
                k2 = jnp.concatenate([kb[a:a + t, col] for a, t in pieces], axis=0)
                v2 = jnp.concatenate([vb[a:a + t, col] for a, t in pieces], axis=0)
                more = extra[m, h, off:off + n, :]
                pt = jnp.exp(dot_nt(jnp.concatenate([k2, more], axis=1), qe))
                ds = (pt * dot_nt(jnp.concatenate([v2, more], axis=1), doe)).astype(BF)
                dv_ = dot(pt.astype(BF), dos)
                dk_ = dot(ds, qs)
                dqt = dqt + dot(k2.T, ds)
                if off < WK:
                    a, t = pieces[0]
                    dka[a:a + t, :] += dk_
                    dva[a:a + t, :] += dv_
                else:
                    at = 0
                    for a, t in pieces:
                        kb[a:a + t, col] = dk_[at:at + t].astype(BF)
                        vb[a:a + t, col] = dv_[at:at + t].astype(BF)
                        at += t
                off += n
            q[m, rows, col] = (merge_heads(dqt.T) * 0.125).astype(BF)
        kb[0:NW, col] = dka[...].astype(BF)
        vb[0:NW, col] = dva[...].astype(BF)

    def weight(i):
        return wa[:, :, 48 * i:48 + 48 * i, :].reshape(768, 768)

    def dx_rows(m, i):
        for part in range(2):
            r = rows_at(2 * i + part, 384)
            value = dot_nt(kb[r, :], weight(1)) + dot_nt(vb[r, :], weight(2))
            xsb[r, :] = value.astype(BF)
            if part == 1:
                @pl.when(i == 0)
                def _(value=value):
                    odx[m] += value[128:384] + dot_nt(q[m], weight(0))

    def dx_piece(m, i):
        t = 2 * far(i % 4) + jnp.where(i < 4, 1 - x, x)
        row = lax.broadcasted_iota(jnp.int32, (256, 1024), 0) + 256 * t
        chosen = jnp.where(row == tgt[m], 1.0, 0.0).astype(BF)
        value = dot(chosen, xsb[NW:NS, :])
        w = t - s + 2

        @pl.when(t == s)
        def _():
            odx[m] += value

        @pl.when(t != s)
        def _():
            near = xsb[rows_at(jnp.clip(w, 0, 4), 256), :].astype(F32)
            dxp[m, t] = (value + jnp.where((w >= 0) & (w < 5), near, 0.0)).astype(BF)

        pl.when(i < 4)(lambda: dx_x(m, far(i % 4)).start())

    def weight_grads(m, i):
        cols = pl.ds(pl.multiple_of(384 * i, 128), 384)
        a = xsb[:, cols]
        chips = pl.ds(4 * i, 4)

        def keep(row, value, n):
            value = value.reshape(4, 2, 48, value.shape[1])

            @pl.when(m == 0)
            def _():
                ga[chips, :, row:row + 48, n] = value.astype(BF)

            @pl.when(m == 1)
            def _():
                ga[chips, :, row:row + 48, n] = (ga[chips, :, row:row + 48, n].astype(F32) + value).astype(BF)

        for half in range(2):
            n = slice(384 * half, 384 * half + 384)
            keep(64, dot_tn(a, kb[:, n]), n)
            keep(112, dot_tn(a, vb[:, n]), n)
        keep(16, dot_tn(a[512:768], q[m]), slice(0, 768))

    def small_grads():
        low = gb[...].astype(BF)

        def spread(i, _):
            ga[i // 2, i % 2, 0:16, :] = low
            return 0

        lax.fori_loop(0, 16, spread, 0)

    swap2 = [remote(ga.at[:, yy, :, theirs], mate2.at[:, yy], msem2.at[0, t], msem2.at[1, t], near_c)
             for t, yy in enumerate((1 - y, y))]

    def picked(g, plan):
        k = jnp.full((), 9, jnp.int32)
        for at, value in plan:
            k = jnp.where(g == at, value, k)
        return k

    def pump(g):
        k = picked(g, PLAN_Y)
        pl.when(k < 9)(lambda: rest.y_step(k))
        k2 = picked(g, PLAN_X)
        pl.when(k2 < 9)(lambda: rest.x_step(k2))
        k3 = picked(g, PLAN_D)
        pl.when(k3 < 3)(lambda: dx_step(0, k3))
        k4 = picked(g, PLAN_Z)
        pl.when(k4 < 3)(lambda: rest.z_step(k4))

        def start_top():
            swap2[0].wait_recv()
            swap2[1].wait_recv()
            lax.fori_loop(0, 8, lambda i, _: (top.y_step(i), 0)[1], 0)

        pl.when(g == PLAN_TOP)(start_top)

    for i in range(6):
        loads[0, i].wait()
        swaps[0, i].wait_recv()
    rest.y_step(0)
    done_copy.wait()
    q_copy.wait()
    extra_copy.wait()

    def load_xs(m):
        return pltpu.make_async_copy(xs_in.at[m], xsb, lsem.at[2])

    def micro(m, _):
        load_xs(m).start()

        def pairs(p, _):
            pair(m, p)

            @pl.when((m == 0) & (p == 4))
            def _():
                for i in range(6):
                    loads[1, i].wait()
                    swaps[1, i].wait_recv()
                top_copy.wait()

            pump(12 * m + p)
            return 0

        lax.fori_loop(0, 6, pairs, 0)
        load_xs(m).wait()

        def grads(i, _):
            weight_grads(m, i)
            pump(12 * m + 6 + i)
            return 0

        lax.fori_loop(0, 2, grads, 0)
        gb[0:1, :] += jnp.sum(q[m].astype(F32), axis=0, keepdims=True)

        def value_bias(i, _):
            gb[1:2, :] += jnp.sum(vb[rows_at(i, 256), :].astype(F32), axis=0, keepdims=True)
            return 0

        lax.fori_loop(0, 9, value_bias, 0)
        pump(12 * m + 8)

        @pl.when(m == 1)
        def _():
            small_grads()
            for cp in swap2:
                cp.start()

        def rows(i, _):
            dx_rows(m, i)
            pump(12 * m + 9 + i)
            return 0

        lax.fori_loop(0, 3, rows, 0)
        pl.when(m == 0)(lambda: start_keys(1))
        lax.fori_loop(0, 8, lambda i, _: (dx_piece(m, i), 0)[1], 0)
        return 0

    lax.fori_loop(0, 2, micro, 0)

    def rest_rows(cc):
        yield oo, 0, pl.multiple_of(24 * cc, 8), 24, 0
        for j in range(4):
            yield ou, 24 + 24 * j, pl.multiple_of(48 + 48 * j + 24 * cc, 8), 24, 768 * j
        yield od, 120, pl.multiple_of(240 + 96 * cc, 8), 96, 0

    def top_rows(cc):
        yield ob, 216, 0, 16, 0
        for i, ref in enumerate((oq, ok, ov)):
            yield ref, 232 + 24 * i, pl.multiple_of(16 + 48 * i + 24 * cc, 8), 24, 0

    def to_mate(rows_of, first):
        return [remote(fin.at[pl.ds(start, n), :], rcv.at[at:at + n, :], fsem.at[0, first + i], fsem.at[1, first + i], near_c)
                for i, (_, at, start, n, _) in enumerate(rows_of(1 - c))]

    def hand_over(rows_of):
        for ref, at, start, n, col in rows_of(c):
            ref[:, pl.ds(pl.multiple_of(col + c * 384, 128), 384)] = fin[pl.ds(start, n), :]

    def take_over(rows_of):
        for ref, at, start, n, col in rows_of(c):
            ref[:, pl.ds(pl.multiple_of(col + (1 - c) * 384, 128), 384)] = rcv[at:at + n, :]

    def tell(to):
        pl.semaphore_signal(ready, inc=1, device_id=to, device_id_type=MESH)

    last0 = to_mate(rest_rows, 0)

    def tail(g, _):
        def step(plan, act):
            k = picked(g, plan)
            pl.when(k < 9)(lambda: act(k))

        @pl.when(g == TAIL_B)
        def _():
            rest.finish()
            for to in (near_x, near_y, near_c):
                tell(to)
            pl.when(z > 0)(lambda: tell(below))
            pl.when(z < 3)(lambda: tell(above))
            for cp in last0:
                cp.start()
            hand_over(rest_rows)

        @pl.when(g == TAIL_W)
        def _():
            pl.semaphore_wait(ready, 3 + (z > 0).astype(jnp.int32) + (z < 3).astype(jnp.int32))

        step(TAIL_D0, lambda k: dx_step(0, k))
        pl.when(g == TAIL_D0_END)(lambda: dx_finish(0))
        step(TAIL_X, top.x_step)
        step(TAIL_D, lambda k: dx_step(1, k))
        step(TAIL_Z, top.z_step)
        return 0

    lax.fori_loop(0, TAIL, tail, 0)
    dx_finish(1)
    for cp in last0:
        cp.wait()
    take_over(rest_rows)
    top.finish()
    last1 = to_mate(top_rows, 6)
    for cp in last1:
        cp.start()
    hand_over(top_rows)
    for cp in last1:
        cp.wait()
    take_over(top_rows)
    top.drain()
    rest.drain()
    for t in range(2):
        for i in range(6):
            swaps[t, i].wait_send()
    dx_sent(0)
    dx_sent(1)
    for cp in swap2:
        cp.wait_send()


PLAN_Y = ((0, 1), (1, 2), (2, 3), (3, 4), (4, 5), (5, 6), (6, 7))
PLAN_X = ((5, 0), (6, 1), (8, 2), (11, 3))
PLAN_Z = ((13, 0), (16, 1), (19, 2))
PLAN_D = ((16, 0), (20, 1), (23, 2))
PLAN_TOP = 21
TAIL_B = 0
TAIL_W = 1
TAIL_D0 = ()
TAIL_D0_END = 1
TAIL_X = ((1, 0), (2, 1), (3, 2), (4, 3))
TAIL_D = ((1, 0), (3, 1), (5, 2))
TAIL_Z = ((4, 0), (5, 1), (6, 2))
TAIL = 7


def backward_all(datt, stats, tgt, gb, extra, q, done, k, v, xs, top, go, gu, gd):
    dma = pltpu.SemaphoreType.DMA
    sd = jax.ShapeDtypeStruct
    vm, anywhere = (pl.BlockSpec(memory_space=m) for m in (pltpu.VMEM, pl.ANY))
    mb, rows, width = q.shape
    s = pltpu.VMEM
    views = [top.reshape(8, 2, TOP, width), go.reshape(8, 2, 48, width), gu.reshape(8, 2, 48, 4 * width),
             gd.reshape(8, 2, 192, width)]
    return pl.pallas_call(
        backward_kernel,
        out_shape=[sd((24, width), F32)] * 4 + [sd((24, 4 * width), F32), sd((96, width), F32), sd((16, width), F32),
                                                sd(q.shape, F32)],
        in_specs=[vm] * 4 + [anywhere] * 10,
        out_specs=[vm] * 8,
        scratch_shapes=[
            s((NS, width), BF), s((NS, width), BF), s((NS, width), BF), s((8, 2, TOP - 16, width), BF),
            s((mb, 2, NK, 128), BF), s((NW, 128), F32), s((NW, 128), F32), s((mb, rows, width), BF),
            s((8, 2, TOP, width), BF), s((16, width), F32),
            s((8, 2, REST, 384), BF), s((8, 2, REST, 384), BF), s((8, REST, 384), BF), s((8, 2, TOP, 384), BF), s((8, TOP, 384), BF),
            s((4, REST, 384), BF),
            s((5, REST, 384), BF),
            s((mb, 8, rows, width), BF), s((mb, 4, rows, width), BF), s((mb, 5, rows, width), BF),
            s((REST, 384), F32), s((304, 384), F32),
            dma((2, 6)), dma((5,)), dma((2, 2, 6)), dma((2, 2)), dma((2, 6)),
            dma((2, 8)), dma((2, 4)), dma((2, 5)), dma((2, 8)), dma((2, 4)), dma((2, 5)),
            dma((2, mb, 4)), dma((2, mb, 5)), dma((2, 10)), pltpu.SemaphoreType.REGULAR,
        ],
        compiler_params=pltpu.CompilerParams(
            collective_id=1, has_side_effects=True, vmem_limit_bytes=62 * 2**20
        ),
    )(datt, stats, tgt, gb, extra, q, done, k, v, xs, *views)


CHUNKS = 9


def project_kernel(idx, xall, wall, bias, xs_ref, k_ref, v_ref, q_ref, xs, w, sems, wsem):
    m, i = pl.program_id(0), pl.program_id(1)

    @pl.when((m == 0) & (i == 0))
    def _():
        copy = pltpu.make_async_copy(wall.at[:, pl.ds(16, 144), :], w, wsem)
        copy.start()
        for mm in range(2):
            for cc in range(CHUNKS):
                pieces = [(0, 256)] if cc < 5 else [(0, 128), (128, 128)] if cc == 5 else [(64 * t, 64) for t in range(4)]
                base = cc if cc < 5 else 5 if cc == 5 else 7 + 4 * (cc - 6)
                for t, (off, n) in enumerate(pieces):
                    start = pl.multiple_of(idx[mm, base + t], 64)
                    pltpu.make_async_copy(xall.at[mm, pl.ds(start, n), :], xs.at[mm, cc, pl.ds(off, n), :],
                                          sems.at[mm, cc]).start()
        copy.wait()

    pltpu.make_async_copy(xall.at[0, pl.ds(0, 256), :], xs.at[m, i], sems.at[m, i]).wait()
    rows = xs[m, i]
    xs_ref[0] = rows
    k_ref[0] = dot(rows, w[:, 48:96, :].reshape(768, 768)).astype(BF)
    v_ref[0] = (dot(rows, w[:, 96:144, :].reshape(768, 768)) + bias[1:2, :]).astype(BF)

    @pl.when(i == 2)
    def _():
        q = (dot(rows, w[:, 0:48, :].reshape(768, 768)) + bias[0:1, :]).astype(BF)
        q_ref[0] = q * jnp.asarray(0.125, BF)


def project(idx, xall, wall, bias):
    mb = xall.shape[0]
    sd = jax.ShapeDtypeStruct
    chunk = pl.BlockSpec((1, 256, 768), lambda m, i, t: (m, i, 0))
    return pl.pallas_call(
        project_kernel,
        grid_spec=pltpu.PrefetchScalarGridSpec(
            num_scalar_prefetch=1,
            grid=(mb, CHUNKS),
            in_specs=[pl.BlockSpec(memory_space=pl.ANY)] * 2 + [pl.BlockSpec((16, 768), lambda m, i, t: (0, 0))],
            out_specs=[chunk, chunk, chunk, pl.BlockSpec((1, 256, 768), lambda m, i, t: (m, 0, 0))],
            scratch_shapes=[
                pltpu.VMEM((mb, CHUNKS, 256, 768), BF), pltpu.VMEM((16, 144, 768), BF),
                pltpu.SemaphoreType.DMA((mb, CHUNKS)), pltpu.SemaphoreType.DMA,
            ],
        ),
        out_shape=[sd((mb, NS, 768), BF)] * 3 + [sd((mb, 256, 768), BF)],
        compiler_params=pltpu.CompilerParams(vmem_limit_bytes=48 * 2**20),
    )(idx, xall, wall, bias)


EPS = 1e-6
G0, G1 = 0.7978845608, 0.044715


def norm(v):
    mean = jnp.mean(v, axis=-1, keepdims=True)
    centred = v - mean
    inverse = lax.rsqrt(jnp.mean(centred * centred, axis=-1, keepdims=True) + EPS)
    return centred * inverse, inverse


def norm_back(g, normed, inverse, gain):
    c = g * gain
    return inverse * (c - jnp.mean(c, axis=-1, keepdims=True)
                      - normed * jnp.mean(c * normed, axis=-1, keepdims=True))


def middle_kernel(att, x, cot, wall, bias, lse, out_ref, stats_ref, datt_ref, done_ref, go_out, gu_out, gd_out, gb_ref,
                  go_ref, gu_ref, gd_ref, gsem, w, wsem, pre, hid, mid, low, n1, r1, ffn):
    rows = x.shape[0]
    copies = [
        pltpu.make_async_copy(wall.at[:, pl.ds(0, 48), :], w.at[:, pl.ds(0, 48), :], wsem.at[0]),
        pltpu.make_async_copy(wall.at[:, pl.ds(48, 192), :], w.at[:, pl.ds(48, 192), :], wsem.at[1]),
        pltpu.make_async_copy(wall.at[:, pl.ds(240, 192), :], w.at[:, pl.ds(240, 192), :], wsem.at[2]),
    ]
    for cp in copies:
        cp.start()
    half = rows // 2
    copies[0].wait()
    w_out = w[:, 0:48, :].reshape(768, 768)
    for h in range(2):
        r = pl.ds(h * half, half)
        t = x[r, :].astype(F32) + dot(att[r, :], w_out) + bias[2:3, :]
        normed, inverse = norm(t)
        n1[r, :] = normed
        r1[r, :] = jnp.broadcast_to(inverse, (half, 128))
        value = normed * bias[4:5, :] + bias[5:6, :]
        mid[r, :] = value
        low[r, :] = value.astype(BF)
    ffn[...] = jnp.broadcast_to(bias[3:4, :], ffn.shape)
    copies[1].wait()
    copies[2].wait()

    def up_block(j):
        return w[:, pl.ds(pl.multiple_of(48 + 48 * j, 16), 48), :].reshape(768, 768)

    def down_block(j):
        return w[pl.ds(4 * j, 4), 240:432, :].reshape(768, 768)

    def forward(j, _):
        wu, wd = up_block(j), down_block(j)
        for h in range(2):
            r = pl.ds(h * half, half)
            u = dot(low[r, :], wu) + bias[pl.ds(8 + j, 1), :]
            pre[j, r, :] = u
            g = (0.5 * u * (1.0 + jnp.tanh(G0 * (u + G1 * u * u * u)))).astype(BF)
            hid[j, r, :] = g
            ffn[r, :] += dot(g, wd)
        return 0

    lax.fori_loop(0, 4, forward, 0)
    gb_ref[...] = jnp.zeros_like(gb_ref)
    for h in range(2):
        r = pl.ds(h * half, half)
        normed, inverse = norm(mid[r, :] + ffn[r, :])
        out_ref[r, :] = (normed * bias[6:7, :] + bias[7:8, :]).astype(BF)
        g = cot[r, :].astype(F32)
        gb_ref[6:7, :] += jnp.sum(g * normed, axis=0, keepdims=True)
        gb_ref[7:8, :] += jnp.sum(g, axis=0, keepdims=True)
        d_two = norm_back(g, normed, inverse, bias[6:7, :])
        mid[r, :] = d_two
        d_ffn = d_two.astype(BF)
        datt_ref[r, :] = d_ffn
        gb_ref[3:4, :] += jnp.sum(d_ffn.astype(F32), axis=0, keepdims=True)

    def sent(ref, out, j, t):
        at = pl.ds(pl.multiple_of(j * 768, 768), 768)
        return pltpu.make_async_copy(ref.at[j], out.at[at, :] if t == 0 else out.at[:, at], gsem.at[t, j])

    def backward(j, _):
        wu, wd = up_block(j), down_block(j)
        d_ffn = datt_ref[...]
        gd_ref[j] = dot_tn(hid[j], d_ffn).astype(BF)
        sent(gd_ref, gd_out, j, 0).start()
        for h in range(2):
            r = pl.ds(h * half, half)
            u = pre[j, r, :]
            th = jnp.tanh(G0 * (u + G1 * u * u * u))
            slope = 0.5 * (1.0 + th) + 0.5 * u * (1.0 - th * th) * (G0 * (1.0 + 3.0 * G1 * u * u))
            d_pre = (dot_nt(datt_ref[r, :], wd) * slope).astype(BF)
            hid[j, r, :] = d_pre
            gb_ref[pl.ds(8 + j, 1), :] += jnp.sum(d_pre.astype(F32), axis=0, keepdims=True)
            mid[r, :] += dot_nt(d_pre, wu)
        gu_ref[j] = dot_tn(low[...], hid[j]).astype(BF)
        sent(gu_ref, gu_out, j, 1).start()
        return 0

    lax.fori_loop(0, 4, backward, 0)
    for h in range(2):
        r = pl.ds(h * half, half)
        d_mid, normed = mid[r, :], n1[r, :]
        gb_ref[4:5, :] += jnp.sum(d_mid * normed, axis=0, keepdims=True)
        gb_ref[5:6, :] += jnp.sum(d_mid, axis=0, keepdims=True)
        d_one = norm_back(d_mid, normed, r1[r, 0:1], bias[4:5, :])
        done_ref[r, :] = d_one
        d_branch = d_one.astype(BF)
        low[r, :] = d_branch
        gb_ref[2:3, :] += jnp.sum(d_branch.astype(F32), axis=0, keepdims=True)
        d_att = dot_nt(d_branch, w_out).astype(BF)
        datt_ref[r, :] = d_att
        product = d_att.astype(F32) * att[r, :].astype(F32)
        lane = lax.broadcasted_iota(jnp.int32, (half, 128), 1)
        stats = lse[r, :]
        for p in range(6):
            two = product[:, 128 * p:128 * p + 128]
            stats = jnp.where(lane == 16 + 2 * p, jnp.sum(jnp.where(lane < 64, two, 0.0), axis=1, keepdims=True), stats)
            stats = jnp.where(lane == 17 + 2 * p, jnp.sum(jnp.where(lane >= 64, two, 0.0), axis=1, keepdims=True), stats)
        stats_ref[r, :] = stats
    go_ref[...] = dot_tn(att[...], low[...]).astype(BF)
    go_copy = pltpu.make_async_copy(go_ref, go_out, wsem.at[0])
    go_copy.start()
    for j in range(4):
        sent(gd_ref, gd_out, j, 0).wait()
        sent(gu_ref, gu_out, j, 1).wait()
    go_copy.wait()


def middle(att, x, cot, wall, bias, lse):
    rows = x.shape[0]
    sd = jax.ShapeDtypeStruct
    vm = pl.BlockSpec(memory_space=pltpu.VMEM)
    return pl.pallas_call(
        middle_kernel,
        in_specs=[vm, vm, vm, pl.BlockSpec(memory_space=pl.ANY), vm, vm],
        out_specs=[vm] * 4 + [pl.BlockSpec(memory_space=pl.ANY)] * 3 + [vm],
        out_shape=[sd((rows, 768), BF), sd((rows, 128), F32), sd((rows, 768), BF), sd((rows, 768), F32), sd((768, 768), BF),
                   sd((768, 3072), BF), sd((3072, 768), BF), sd((16, 768), F32)],
        scratch_shapes=[
            pltpu.VMEM((768, 768), BF), pltpu.VMEM((4, 768, 768), BF), pltpu.VMEM((4, 768, 768), BF),
            pltpu.SemaphoreType.DMA((2, 4)),
            pltpu.VMEM((16, 432, 768), BF), pltpu.SemaphoreType.DMA((3,)),
            pltpu.VMEM((4, rows, 768), F32), pltpu.VMEM((4, rows, 768), BF),
            pltpu.VMEM((rows, 768), F32), pltpu.VMEM((rows, 768), BF), pltpu.VMEM((rows, 768), F32),
            pltpu.VMEM((rows, 128), F32), pltpu.VMEM((rows, 768), F32),
        ],
        compiler_params=pltpu.CompilerParams(vmem_limit_bytes=60 * 2**20),
    )(att, x, cot, wall, bias, lse)


def back_kernel(scattered, idx, xs_ref, dk_ref, dv_ref, dq_ref, done_ref, wall, gb_in, dx_ref, own_ref, gq_ref, gk_ref, gv_ref, gb_ref,
                w, wsem, acc, aq, ak, av):
    m, i = pl.program_id(0), pl.program_id(1)

    @pl.when((m == 0) & (i == 0))
    def _():
        copy = pltpu.make_async_copy(wall.at[:, pl.ds(16, 144), :], w, wsem)
        copy.start()
        acc[...] = jnp.zeros_like(acc)
        aq[...] = jnp.zeros_like(aq)
        ak[...] = jnp.zeros_like(ak)
        av[...] = jnp.zeros_like(av)
        gb_ref[...] = gb_in[...]
        copy.wait()

    rows, dk, dv = xs_ref[0], dk_ref[0], dv_ref[0]
    ak[...] += dot_tn(rows, dk)
    av[...] += dot_tn(rows, dv)
    gb_ref[1:2, :] += jnp.sum(dv.astype(F32), axis=0, keepdims=True)
    dx = dot_nt(dk, w[:, 48:96, :].reshape(768, 768)) + dot_nt(dv, w[:, 96:144, :].reshape(768, 768))

    def add(slot, off, n):
        start = pl.multiple_of(idx[m, slot], 64)
        acc[m, pl.ds(start, n), :] += dx[off:off + n]

    if not scattered:
        dx_ref[0] = jnp.where(i == 2, jnp.zeros_like(dx), dx).astype(BF)

    @pl.when((i < 5) & (i != 2) & scattered)
    def _():
        add(jnp.minimum(i, 4), 0, 256)

    @pl.when((i == 5) & scattered)
    def _():
        add(5, 0, 128)
        add(6, 128, 128)

    @pl.when((i > 5) & scattered)
    def _():
        for t in range(4):
            add(7 + 4 * (i - 6) + t, 64 * t, 64)

    @pl.when(i == 2)
    def _():
        dq = dq_ref[0]
        aq[...] += dot_tn(rows, dq)
        gb_ref[0:1, :] += jnp.sum(dq.astype(F32), axis=0, keepdims=True)
        own_ref[0] = dx + done_ref[0] + dot_nt(dq, w[:, 0:48, :].reshape(768, 768))

    @pl.when((i == CHUNKS - 1) & scattered)
    def _():
        dx_ref[m if scattered else 0] = acc[m].astype(BF)

    @pl.when((m == 1) & (i == CHUNKS - 1))
    def _():
        gq_ref[...] = aq[...].astype(BF)
        gk_ref[...] = ak[...].astype(BF)
        gv_ref[...] = av[...].astype(BF)


def back(idx, xs, dk, dv, dq, done, wall, gb, seq_len):
    mb = xs.shape[0]
    sd = jax.ShapeDtypeStruct
    chunk = pl.BlockSpec((1, 256, 768), lambda m, i, t: (m, i, 0))
    one = pl.BlockSpec((1, 256, 768), lambda m, i, t: (m, 0, 0))
    whole = lambda *s: pl.BlockSpec(s, lambda m, i, t: (0,) * len(s))
    scattered = seq_len > 0
    held = seq_len if scattered else 256
    return pl.pallas_call(
        functools.partial(back_kernel, scattered),
        grid_spec=pltpu.PrefetchScalarGridSpec(
            num_scalar_prefetch=1,
            grid=(mb, CHUNKS),
            in_specs=[chunk, chunk, chunk, one, one, pl.BlockSpec(memory_space=pl.ANY), whole(16, 768)],
            out_specs=[whole(mb, seq_len, 768) if scattered else chunk, one, whole(768, 768), whole(768, 768), whole(768, 768), whole(16, 768)],
            scratch_shapes=[
                pltpu.VMEM((16, 144, 768), BF), pltpu.SemaphoreType.DMA, pltpu.VMEM((mb, held, 768), F32),
                pltpu.VMEM((768, 768), F32), pltpu.VMEM((768, 768), F32), pltpu.VMEM((768, 768), F32),
            ],
        ),
        out_shape=[sd((mb, seq_len if scattered else NS, 768), BF), sd((mb, 256, 768), F32), sd((768, 768), BF), sd((768, 768), BF),
                   sd((768, 768), BF), sd((16, 768), F32)],
        compiler_params=pltpu.CompilerParams(vmem_limit_bytes=60 * 2**20),
    )(idx, xs, dk, dv, dq, done, wall, gb)


def last_kernel(*refs):
    table, arrays = refs[0], refs[1:8]
    outs, vectors = refs[8:15], refs[15:]
    for src, dst in zip(arrays, outs):
        dst[...] = src[...]
    owner = lax.axis_index("seq") * 4 + lax.axis_index("batch")
    n, m = vectors[0].shape[1], vectors[8].shape[1]
    small = pltpu.roll(table[0:8, :], (768 - owner * n) % 768, axis=1)
    for i in range(8):
        vectors[i][...] = small[i:i + 1, 0:n]
    ups = jnp.broadcast_to(table[pl.ds(8 + owner // 8, 1), :], (8, 768))
    vectors[8][...] = pltpu.roll(ups, (768 - (owner % 8) * m) % 768, axis=1)[0:1, 0:m]


def last(table, arrays, n, m):
    sd = jax.ShapeDtypeStruct
    vm = pl.BlockSpec(memory_space=pltpu.VMEM)
    return pl.pallas_call(
        last_kernel,
        in_specs=[vm] * 8,
        out_specs=[vm] * 16,
        out_shape=[sd(a.shape, a.dtype) for a in arrays] + [sd((1, n), F32)] * 8 + [sd((1, m), F32)],
        compiler_params=pltpu.CompilerParams(vmem_limit_bytes=32 * 2**20),
    )(table, *arrays)

def cat_rows(ref, h):
    return jnp.concatenate([ref[0, pl.ds(a, n), :] for a, n in key_rows(h)], axis=0)


def fwd_kernel(q_ref,k_ref,v_ref,me_ref,o_ref,l_ref):
    p=pl.program_id(1)
    ind=block_columns().astype(BF)
    for h in range(2):
        me=me_ref[0,h]
        qe=jnp.concatenate([split_heads(q_ref[0,pl.ds(h*HALF,HALF),:]),ind],axis=1)
        ke=jnp.concatenate([cat_rows(k_ref, h),me],axis=1)
        s=dot_nt(qe,ke)
        top=jnp.max(s,axis=1,keepdims=True)
        e=jnp.exp(s-top).astype(BF)
        ve=jnp.concatenate([cat_rows(v_ref,h),me],axis=1)
        o=dot(e,ve)
        tot=o[:,130:131]
        o_ref[0,pl.ds(h*HALF,HALF),:]=merge_heads(o[:,:128]/tot).astype(BF)
        l_ref[0,0,pl.ds(h*256,256),:]=jnp.broadcast_to(top+jnp.log(tot),(256,128))
def attn_fwd(q,k,v,me):
    mb=q.shape[0]; npair=q.shape[2]//128
    return pl.pallas_call(fwd_kernel,grid=(mb,npair),
      in_specs=[pl.BlockSpec((1,256,128),lambda m,p:(m,0,p)),pl.BlockSpec((1,NS,128),lambda m,p:(m,0,p)),pl.BlockSpec((1,NS,128),lambda m,p:(m,0,p)),
        pl.BlockSpec((1,2,NK,128),lambda m,p:(m,0,0,0))],
      out_specs=[pl.BlockSpec((1,256,128),lambda m,p:(m,0,p)),pl.BlockSpec((1,1,512,128),lambda m,p:(m,p,0,0))],
      out_shape=[jax.ShapeDtypeStruct(q.shape,BF),jax.ShapeDtypeStruct((mb,npair,512,128),F32)],
      compiler_params=pltpu.CompilerParams(vmem_limit_bytes=56*2**20))(q,k,v,me)
def bwd_kernel(CH,q_ref,k_ref,v_ref,me_ref,o_ref,do_ref,l_ref,dq_ref,dk_ref,dv_ref,dka,dva):
    ind=block_columns()
    zero=jnp.zeros_like(ind)
    dka[...]=jnp.zeros_like(dka); dva[...]=jnp.zeros_like(dva)
    for h in range(2):
        rows=pl.ds(h*HALF,HALF)
        qs=split_heads(q_ref[0,rows,:])
        do2=do_ref[0,rows,:]
        dos=split_heads(do2)
        o2=o_ref[0,rows,:].astype(F32)
        delta=jnp.sum(dos.astype(F32)*jnp.concatenate([o2,o2],axis=0),axis=1,keepdims=True)
        lse=l_ref[0,0,pl.ds(h*256,256),0:1]
        qe=jnp.concatenate([qs,with_column(ind,-lse)],axis=1)
        doe=jnp.concatenate([dos,with_column(zero,-delta)],axis=1)
        dqt=jnp.zeros((128,256),F32)
        off=0
        for a,n in key_rows(h):
            c0=0
            while c0<n:
                c=min(CH,n-c0)
                kr=pl.ds(a+c0,c)
                k2=k_ref[0,kr,:]; v2=v_ref[0,kr,:]; me=me_ref[0,h,pl.ds(off+c0,c),:]
                st=dot_nt(jnp.concatenate([k2,me],axis=1),qe)
                pt=jnp.exp(st)
                dpt=dot_nt(jnp.concatenate([v2,me],axis=1),doe)
                ds=(pt*dpt).astype(BF)
                dva[kr,:]+=dot(pt.astype(BF),dos)
                dka[kr,:]+=dot(ds,qs)
                dqt=dqt+dot(k2.T,ds)
                c0+=c
            off+=n
        dq_ref[0,rows,:]=(merge_heads(dqt.T)*0.125).astype(BF)
    dk_ref[0]=dka[...].astype(BF); dv_ref[0]=dva[...].astype(BF)
def attn_bwd(q,k,v,me,o,do,l,CH=384):
    mb=q.shape[0]; npair=q.shape[2]//128
    qs=pl.BlockSpec((1,256,128),lambda m,p:(m,0,p)); ks=pl.BlockSpec((1,NS,128),lambda m,p:(m,0,p))
    return pl.pallas_call(functools.partial(bwd_kernel,CH),grid=(mb,npair),
      in_specs=[qs,ks,ks,pl.BlockSpec((1,2,NK,128),lambda m,p:(m,0,0,0)),qs,qs,pl.BlockSpec((1,1,512,128),lambda m,p:(m,p,0,0))],
      out_specs=[qs,ks,ks],
      out_shape=[jax.ShapeDtypeStruct(q.shape,BF),jax.ShapeDtypeStruct(k.shape,BF),jax.ShapeDtypeStruct(k.shape,BF)],
      scratch_shapes=[pltpu.VMEM((NS,128),F32)]*2,
      compiler_params=pltpu.CompilerParams(vmem_limit_bytes=56*2**20))(q,k,v,me,o,do,l)


BLK = 64
WIN = 8
RAND = 3
ALL = ("seq", "batch")


def vector_table(vectors, b_up, owner, width):
    lane = jnp.arange(width, dtype=jnp.int32)
    n, m = vectors[0].shape[0], b_up.shape[0]
    table = jnp.where(lane // n == owner, jnp.tile(jnp.stack(vectors).astype(F32), (1, width // n)), 0.0)
    flat = jnp.arange(4 * width, dtype=jnp.int32)
    ups = jnp.where(flat // m == owner, jnp.tile(b_up.astype(F32), 4 * width // m), 0.0).reshape(4, width)
    return jnp.concatenate([table, ups, jnp.zeros((4, width), F32)], axis=0)


def block_plan(lengths, randoms, device, blocks):
    ends = jnp.cumsum(lengths, axis=1)
    starts = ends - lengths

    def doc_of(block):
        at = block * BLK
        shape = (lengths.shape[0],) + (1,) * (block.ndim - 1) + (lengths.shape[1],)
        doc = jnp.sum((ends.reshape(shape) <= at[..., None]).astype(jnp.int32), axis=-1)
        doc = jnp.minimum(doc, lengths.shape[1] - 1)
        hit = jnp.arange(lengths.shape[1], dtype=jnp.int32) == doc[..., None]
        return doc, jnp.sum(jnp.where(hit, starts.reshape(shape), 0), axis=-1)

    mb = lengths.shape[0]
    half = jnp.arange(2, dtype=jnp.int32)
    query = device * 4 + 2 * half[:, None] + half[None, :]
    query = jnp.broadcast_to(query[None], (mb, 2, 2))
    q_doc, q_first = doc_of(query)
    window = device * 4 + 2 * half[:, None] - WIN + jnp.arange(2 * WIN + 2, dtype=jnp.int32)[None, :]
    window = jnp.broadcast_to(window[None], (mb, 2, 2 * WIN + 2))
    w_doc, w_first = doc_of(jnp.clip(window, 0, blocks - 1))
    w_good = (window >= 0) & (window < blocks) & (window * BLK - w_first >= 2 * BLK)
    see_window = (
        w_good[:, :, None, :]
        & (w_doc[:, :, None, :] == q_doc[..., None])
        & (jnp.abs(window[:, :, None, :] - query[..., None]) <= WIN)
    )
    see_glob = jnp.ones((mb, 2, 2, 2), bool)
    named = lax.dynamic_slice_in_dim(randoms, device * 4, 4, 1).reshape(mb, 2, 2, RAND)
    r_doc, r_first = doc_of(named)
    r_good = (
        (r_doc == q_doc[..., None])
        & (jnp.abs(named - query[..., None]) > WIN)
        & (named * BLK - r_first >= 2 * BLK)
    )
    see_random = (r_good[:, :, None] & jnp.eye(2, dtype=bool)[None, None, :, :, None]).reshape(mb, 2, 2, 2 * RAND)
    see = jnp.concatenate([see_window, see_glob, see_random], axis=3)
    chunk = jnp.clip(device + jnp.arange(-2, 3, dtype=jnp.int32), 0, blocks // 4 - 1) * (4 * BLK)
    where = jnp.concatenate(
        [jnp.broadcast_to(chunk[None], (mb, 5)), q_first[:, :, 0], named.reshape(mb, -1) * BLK], axis=1
    )
    return where, jnp.where(see, 0.0, -1e30)


def mask_columns(see):
    bias = jnp.broadcast_to(see[..., None], see.shape + (BLK,)).reshape(see.shape[:3] + (-1, 1))
    lane = jnp.arange(128, dtype=jnp.int32)
    ones = jnp.where((lane >= 2) & (lane < 5), 1.0, 0.0)
    return jnp.where(lane == 0, bias[:, :, 0], jnp.where(lane == 1, bias[:, :, 1], ones)).astype(BF)


def on_device(inputs, cotangent, doc_lengths, random_blocks, wq, wk, wv, wo, wu, wd, b_query, b_value, b_out,
              b_up, b_down, gain_attn, bias_attn, gain_ffn, bias_ffn):
    mb, _, rows, width = inputs.shape
    devices, owners = lax.axis_size("seq"), lax.axis_size("seq") * lax.axis_size("batch")
    device = lax.axis_index("seq")
    owner = device * lax.axis_size("batch") + lax.axis_index("batch")
    linked = devices == 8 and owners == 32
    seq_len = devices * rows
    x, cot = inputs[:, 0], cotangent[:, 0]
    lengths, randoms = doc_lengths[:, 0], random_blocks[:, 0]
    vectors = (b_query, b_value, b_out, b_down, gain_attn, bias_attn, gain_ffn, bias_ffn)
    flat = lambda t: t.reshape(-1, t.shape[-1])
    if linked:
        att, lse, q, xs, k, v, wall, top, bias, extra, targets = forward_all(
            lengths, randoms, x, (wq, wk, wv, wo, wu, wd), jnp.stack(vectors), b_up[None])
    else:
        where, see = block_plan(lengths, randoms, device, seq_len // BLK)
        extra, table = mask_columns(see), vector_table(vectors, b_up, owner, width)
        xall = lax.all_gather(x, "seq", axis=1, tiled=True)
        bias = lax.psum(table, ALL)
        full = [lax.all_gather(w, ALL, axis=0, tiled=True) for w in (wq, wk, wv, wo, wu, wd)]
        fold = lambda w: w.reshape(16, -1, width)
        up = full[4].reshape(16, 48, 4, width).transpose(0, 2, 1, 3).reshape(16, 192, width)
        wall = jnp.concatenate([fold(full[3]), up, fold(full[5])], axis=1)
        top = jnp.concatenate([jnp.zeros((16, 16, width), BF)] + [fold(w) for w in full[:3]], axis=1)
        xs, k, v, q = project(where, xall, top, bias)
        att, lse = attn_fwd(q, k, v, extra)
    stats = flat(lse) if linked else jnp.zeros((mb * rows, 128), F32)
    out, stats, datt, done, go, gu, gd, gb = middle(flat(att), flat(x), flat(cot), wall, bias, stats)
    datt, done = datt.reshape(att.shape), done.reshape(mb, rows, width)
    if linked:
        *grads, gb, dx = backward_all(datt, stats.reshape(mb, rows, 128), targets, gb, extra, q, done, k, v, xs, top, go, gu, gd)
    else:
        dq, dk, dv = attn_bwd(q, k, v, extra, att, datt, lse, 640)
        dxs, own, gq, gk, gv, gb = back(where, xs, dk, dv, dq, done, top, gb, 0)
        start = (where[:, :5, None] + jnp.arange(0, 256, BLK)).reshape(mb, -1)
        glob = (where[:, 5:7, None] + jnp.arange(0, 128, BLK)).reshape(mb, -1)
        to = jnp.concatenate([start, glob, where[:, 7:]], axis=1) // BLK
        parts = dxs.reshape(mb, -1, BLK, width)
        total = jnp.zeros((mb, seq_len // BLK, BLK, width), F32)
        total = jax.vmap(lambda t, i, p: t.at[i].add(p))(total, to, parts.astype(F32))
        dx = own + lax.psum_scatter(total.reshape(mb, seq_len, width), "seq", scatter_dimension=1, tiled=True)
        grads = [lax.psum_scatter(g.astype(F32), ALL, scatter_dimension=0, tiled=True) for g in (gq, gk, gv, go, gu, gd)]
        gb = lax.psum(gb, ALL)
    n, m = b_query.shape[0], b_up.shape[0]
    if linked:
        done_all = last(gb, (*grads, dx), n, m)
        grads, dx = done_all[:6], done_all[6]
        small, ups = [g.reshape(n) for g in done_all[7:15]], done_all[15].reshape(m)
    else:
        small = lax.dynamic_slice_in_dim(gb[:8], owner * n, n, 1)
        ups = lax.dynamic_slice_in_dim(gb[8:12].reshape(-1), owner * m, m, 0)
    return (
        out.reshape(inputs.shape), dx[:, None], *grads,
        small[0], small[1], small[2], ups, small[3], small[4], small[5], small[6], small[7],
    )


def solution(mesh):
    tokens = P(None, "batch", "seq", None)
    mat, vec = P(ALL, None), P(ALL)
    in_specs = (tokens, tokens, P(None, "batch", None), P(None, "batch", None, None)) + (mat,) * 6 + (vec,) * 9
    out_specs = (tokens, tokens) + (mat,) * 6 + (vec,) * 9
    return jax.shard_map(on_device, mesh=mesh, in_specs=in_specs, out_specs=out_specs, check_vma=False)
```

```python
import functools

import jax
import jax.numpy as jnp
from jax import lax
from jax.experimental import pallas as pl
from jax.experimental.pallas import tpu as pltpu
from jax.sharding import PartitionSpec as P

F32 = jnp.float32
BF = jnp.bfloat16


HALF, WK, NW, NK, NS = 128, 1152, 1280, 1664, 2304
TOP, REST = 160, 432
MESH = pl.DeviceIdType.MESH
UP, DOWN, XX, YY, CC = range(5)
WAYS = (UP, DOWN, XX, YY, CC)


def dot(a, b):
    return lax.dot_general(a, b, (((1,), (0,)), ((), ())), preferred_element_type=F32)


def dot_nt(a, b):
    return lax.dot_general(a, b, (((1,), (1,)), ((), ())), preferred_element_type=F32)


def dot_tn(a, b):
    return lax.dot_general(a, b, (((0,), (0,)), ((), ())), preferred_element_type=F32)


def place():
    s, b = lax.axis_index("seq"), lax.axis_index("batch")
    return s // 2, s % 2, b // 2, b % 2


def device(z, x, y, c):
    return (2 * z + x, 2 * y + c)


def greet(z, x, y, c):
    barrier = pltpu.get_barrier_semaphore()

    def tell(to):
        pl.semaphore_signal(barrier, inc=1, device_id=to, device_id_type=MESH)

    tell(device(z, 1 - x, y, c))
    tell(device(z, x, 1 - y, c))
    tell(device(z, x, y, 1 - c))
    pl.when(z > 0)(lambda: tell(device(z - 1, x, y, c)))
    pl.when(z < 3)(lambda: tell(device(z + 1, x, y, c)))
    pl.semaphore_wait(barrier, 3 + (z > 0).astype(jnp.int32) + (z < 3).astype(jnp.int32))


def lanes(c):
    return pl.ds(pl.multiple_of(c * 384, 128), 384)


def rows_at(i, n):
    return pl.ds(pl.multiple_of(i * n, n), n)


def remote(src, dst, send, recv, to):
    return pltpu.make_async_remote_copy(
        src_ref=src, dst_ref=dst, send_sem=send, recv_sem=recv, device_id=to, device_id_type=MESH
    )


def key_rows(h):
    return ((HALF * h, WK), (NW + HALF * h, HALF), (NW + 2 * HALF + 384 * h, 384))


def split_heads(v):
    lane = lax.broadcasted_iota(jnp.int32, v.shape, 1)
    z = jnp.zeros_like(v)
    return jnp.concatenate([jnp.where(lane < 64, v, z), jnp.where(lane >= 64, v, z)], axis=0)


def merge_heads(v):
    n = v.shape[0] // 2
    lane = lax.broadcasted_iota(jnp.int32, (n, v.shape[1]), 1)
    return jnp.where(lane < 64, v[:n], v[n:])


def block_columns():
    r = lax.broadcasted_iota(jnp.int32, (2 * HALF, 128), 0)
    lane = lax.broadcasted_iota(jnp.int32, (2 * HALF, 128), 1)
    first = (r % HALF) < 64
    return jnp.where(((lane == 0) & first) | ((lane == 1) & jnp.logical_not(first)), 1.0, 0.0)


def with_column(base, col):
    lane = lax.broadcasted_iota(jnp.int32, base.shape, 1)
    hi = col.astype(BF).astype(F32)
    rest = col - hi
    mid = rest.astype(BF).astype(F32)
    return jnp.where(lane == 2, hi, jnp.where(lane == 3, mid, jnp.where(lane == 4, rest - mid, base))).astype(BF)


def doc_of(lengths, m, block):
    at = block * 64
    doc, first, end = jnp.int32(0), jnp.int32(0), jnp.int32(0)
    for i in range(3):
        end = end + lengths[m, 0, i]
        doc = doc + (end <= at).astype(jnp.int32)
        first = jnp.where(end <= at, end, first)
    return doc, first


def write_extra(lengths, randoms, s, extra):
    lane = lax.broadcasted_iota(jnp.int32, (64, 128), 1)
    ones = jnp.where((lane >= 2) & (lane < 5), 1.0, 0.0)

    def one(i, _):
        m, h, t = i // 52, (i // 26) % 2, i % 26
        r = jnp.maximum(t - 20, 0)
        named = randoms[m, 0, 4 * s + 2 * h + r // 3, r % 3]
        block = jnp.where(t < 18, 4 * s + 2 * h - 8 + t, named)
        inside = (block >= 0) & (block < 32)
        doc, first = doc_of(lengths, m, jnp.clip(block, 0, 31))
        good = inside & (block * 64 - first >= 128)
        terms = []
        for k in range(2):
            query = 4 * s + 2 * h + k
            q_doc, _ = doc_of(lengths, m, query)
            near = jnp.abs(block - query) <= 8
            window = (t < 18) & near
            named_here = (t >= 20) & (r // 3 == k) & jnp.logical_not(near)
            seen = ((t >= 18) & (t < 20)) | (good & (doc == q_doc) & (window | named_here))
            terms.append(jnp.where(seen, 0.0, -1e30))
        value = jnp.where(lane == 0, terms[0], jnp.where(lane == 1, terms[1], ones))
        extra[m, h, rows_at(t, 64), :] = value.astype(BF)
        return 0

    lax.fori_loop(0, 104, one, 0)


def rest_block(lengths, randoms, s, m, t):
    r = jnp.maximum(t - 4, 0)
    named = randoms[m, 0, 4 * s + r // 3, r % 3]
    _, first = doc_of(lengths, m, 4 * s + 2 * jnp.minimum(t // 2, 1))
    return jnp.where(t < 4, first // 64 + t % 2, named)


def forward_kernel(lengths, randoms, x_ref, wq, wk, wv, wo, wu, wd, vectors, b_up,
                   att, lse, q_out, xs_out, k_out, v_out, wall, top_out, bias, extra, targets,
                   own, mate, merged, merged_b, xall0, xall1, xs, ks, vs, wa,
                   mate_sem, lsem, osem, asend, arecv, acrecv, bsend, brecv, bcrecv, xsend, xrecv):
    z, x, y, c = place()
    s = 2 * z + x
    to = {UP: device(z + 1, x, y, c), DOWN: device(z - 1, x, y, c), XX: device(z, 1 - x, y, c),
          YY: device(z, x, 1 - y, c), CC: device(z, x, y, 1 - c)}
    mine, theirs = lanes(c), lanes(1 - c)
    xall = (xall0, xall1)

    def guarded(way, act):
        if way == UP:
            pl.when(z < 3)(act)
        elif way == DOWN:
            pl.when(z > 0)(act)
        else:
            act()

    def x_copy(m, zz, xx, way, own_rows=False):
        i = 2 * zz + xx
        ref = xall[m].at[pl.ds(4 * i, 4)]
        return remote(x_ref.at[m] if own_rows else ref, ref, xsend.at[m, i, way], xrecv.at[m, i], to[way])

    def a_copy(zz, xx, yy, way, src=None):
        i = (2 * zz + xx) * 2 + yy
        ref = wa.at[i, :, mine]
        return remote(ref if src is None else src, ref, asend.at[i, way],
                      acrecv.at[i] if way == CC else arecv.at[i], to[way])

    def b_copy(zz, xx, yy, way, src=None):
        i = (2 * zz + xx) * 2 + yy
        ref = wall.at[i, :, mine]
        return remote(ref if src is None else src, ref, bsend.at[i, way],
                      bcrecv.at[i] if way == CC else brecv.at[i], to[way])

    greet(z, x, y, c)
    for way in (UP, DOWN, XX):
        guarded(way, lambda way=way: x_copy(0, z, x, way, True).start())
    for m in range(2):
        pltpu.make_async_copy(x_ref.at[m], xall[m].at[pl.ds(4 * s, 4)], lsem.at[m]).start()
    owner = 4 * s + 2 * y + c
    small = vectors[...].astype(F32)
    n = small.shape[1]
    own[0:8, :] = pltpu.roll(jnp.concatenate([small, jnp.zeros((8, 768 - n), F32)], axis=1), owner * n, axis=1)
    ups = b_up[...].astype(F32)
    n = ups.shape[1]
    ups = jnp.concatenate([ups, jnp.zeros((1, 768 - n), F32)], axis=1)
    ups = pltpu.roll(jnp.broadcast_to(ups, (8, 768)), (owner % 8) * n, axis=1)
    row = lax.broadcasted_iota(jnp.int32, (8, 768), 0)
    own[8:16, :] = jnp.where(row == owner // 8, ups, 0.0)
    for i, ref in enumerate((wq, wk, wv, wo)):
        own[16 + 24 * i:40 + 24 * i, :] = ref[...].astype(F32)
    for j in range(4):
        own[112 + 24 * j:136 + 24 * j, :] = wu[:, 768 * j:768 * j + 768].astype(F32)
    own[208:304, :] = wd[...].astype(F32)
    swap = remote(own.at[:, theirs], mate, mate_sem.at[0], mate_sem.at[1], to[CC])
    swap.start()
    swap.wait()

    def paired(start, n):
        here, there = own[start:start + n, mine], mate[start:start + n, :]
        return jnp.where(c == 0, jnp.concatenate([here, there], 0), jnp.concatenate([there, here], 0)).astype(BF)

    merged[0:16, :] = (own[0:16, mine] + mate[0:16, :]).astype(BF)
    for i in range(3):
        merged[16 + 48 * i:64 + 48 * i, :] = paired(16 + 24 * i, 24)
    keep_a = pltpu.make_async_copy(merged, wa.at[s * 2 + y, :, mine], lsem.at[2])
    keep_a.start()
    for way in WAYS:
        guarded(way, lambda way=way: a_copy(z, x, y, way, merged).start())
    for i in range(5):
        merged_b[48 * i:48 * i + 48, :] = paired(88 + 24 * i, 24)
    merged_b[240:432, :] = paired(208, 96)
    keep_b = pltpu.make_async_copy(merged_b, wall.at[s * 2 + y, :, mine], lsem.at[3])
    keep_b.start()
    write_extra(lengths, randoms, s, extra)

    lane = lax.broadcasted_iota(jnp.int32, (1, 1024), 1)
    for m in range(2):
        targets[m] = lax.fori_loop(
            0, 16, lambda t, v, m=m: jnp.where(
                lane // 64 == t, rest_block(lengths, randoms, s, m, t) * 64 + lane % 64, v), jnp.zeros_like(lane))

    def x_line(m, k, a=True):
        def below():
            x_copy(m, z - k, x, UP).wait_recv()
            pl.when(z < 3)(lambda: x_copy(m, z - k, x, UP).start())
            x_copy(m, z - k, x, XX).start()

        def above():
            x_copy(m, z + k, x, DOWN).wait_recv()
            pl.when(z > 0)(lambda: x_copy(m, z + k, x, DOWN).start())
            x_copy(m, z + k, x, XX).start()

        pl.when((z >= k) & (k <= 3))(below)
        pl.when(z + k <= 3)(above)

    def w_line(copy, k):
        def below():
            copy(z - k, x, y, UP).wait_recv()
            pl.when(z < 3)(lambda: copy(z - k, x, y, UP).start())
            for way in (XX, YY, CC):
                copy(z - k, x, y, way).start()

        def above():
            copy(z + k, x, y, DOWN).wait_recv()
            pl.when(z > 0)(lambda: copy(z + k, x, y, DOWN).start())
            for way in (XX, YY, CC):
                copy(z + k, x, y, way).start()

        pl.when((z >= k) & (k <= 3))(below)
        pl.when(z + k <= 3)(above)

    def at_distance(act, k):
        pl.when((k >= 0) & (k <= z))(lambda: act(z - k))
        pl.when((k > 0) & (z + k <= 3))(lambda: act(z + k))

    def w_from_x(copy, k):
        def act(zz):
            copy(zz, 1 - x, y, XX).wait_recv()
            copy(zz, 1 - x, y, YY).start()
            copy(zz, 1 - x, y, CC).start()

        at_distance(act, k)

    def w_from_y(copy, xx, k):
        def act(zz):
            copy(zz, xx, 1 - y, YY).wait_recv()
            copy(zz, xx, 1 - y, CC).start()

        at_distance(act, k)

    zfirst = c == 0

    def b_own_column(k):
        def passed(zz, way, more):
            b_copy(zz, x, y, way).wait_recv()
            pl.when(more)(lambda: b_copy(zz, x, y, way).start())
            b_copy(zz, x, y, YY).start()
            b_copy(zz, x, y, CC).start()

        pl.when((z >= k) & (k <= 3))(lambda: passed(z - k, UP, z < 3))
        pl.when(z + k <= 3)(lambda: passed(z + k, DOWN, z > 0))

    def b_to_x(k):
        def across(zz):
            b_copy(zz, x, y, XX).start()

        pl.when(zfirst)(lambda: at_distance(across, k))

    def b_other_column(k):
        def shared(zz):
            b_copy(zz, 1 - x, y, YY).start()
            b_copy(zz, 1 - x, y, CC).start()

        def crossed(zz):
            b_copy(zz, 1 - x, y, XX).wait_recv()
            shared(zz)

        def passed(zz, way, more):
            b_copy(zz, 1 - x, y, way).wait_recv()
            pl.when(more)(lambda: b_copy(zz, 1 - x, y, way).start())
            shared(zz)

        def first():
            crossed(z)
            pl.when(jnp.logical_not(zfirst) & (z < 3))(lambda: b_copy(z, 1 - x, y, UP).start())
            pl.when(jnp.logical_not(zfirst) & (z > 0))(lambda: b_copy(z, 1 - x, y, DOWN).start())

        def later():
            pl.when(zfirst)(lambda: at_distance(crossed, k))
            pl.when(jnp.logical_not(zfirst) & (z >= k))(lambda: passed(z - k, UP, z < 3))
            pl.when(jnp.logical_not(zfirst) & (z + k <= 3))(lambda: passed(z + k, DOWN, z > 0))

        pl.when(k == 0)(first)
        pl.when((k > 0) & (k <= 3))(later)

    begin = {
        "x0": lambda k: x_line(0, k),
        "x1": lambda k: x_line(1, k),
        "a": lambda k: w_line(a_copy, k),
        "ax": lambda k: w_from_x(a_copy, k),
        "ay0": lambda k: w_from_y(a_copy, x, k),
        "ay1": lambda k: w_from_y(a_copy, 1 - x, k),
        "own x1": lambda ways: [guarded(way, lambda way=way: x_copy(1, z, x, way, True).start()) for way in ways],
        "own b": lambda ways: [guarded(way, lambda way=way: b_copy(z, x, y, way, merged_b).start()) for way in ways],
    }
    for name, what in START:
        begin[name](what)
    keep_a.wait()

    def arrived(i, _):
        ref = wa.at[i, :, theirs]
        remote(ref, ref, asend.at[i, CC], acrecv.at[i], to[CC]).wait_recv()
        return 0

    lax.fori_loop(0, 16, arrived, 0)
    bias[...] = jnp.sum(wa[:, 0:16, :].astype(F32), axis=0)
    top_copy = pltpu.make_async_copy(wa, top_out, lsem.at[4])
    top_copy.start()
    lane = lax.broadcasted_iota(jnp.int32, (HALF, 128), 1)
    ind = block_columns().astype(BF)
    lse[...] = jnp.zeros_like(lse)

    def out_copy(m, t):
        src, dst = ((xs, xs_out), (ks, k_out), (vs, v_out))[t]
        return pltpu.make_async_copy(src.at[m], dst.at[m], osem.at[m, t])

    def x_here(m, k):
        def arrived_x(zz):
            x_copy(m, zz, 1 - x, XX).wait_recv()

        at_distance(arrived_x, k)

    def gather_near(m):
        x_here(m, 0)
        x_here(m, 1)
        pltpu.make_async_copy(x_ref.at[m], xall[m].at[pl.ds(4 * s, 4)], lsem.at[m]).wait()
        for t in range(5):
            chunk = xall[m][pl.ds(4 * jnp.clip(s - 2 + t, 0, 7), 4)]
            xs[m, 256 * t:256 * t + 256, :] = chunk.reshape(256, chunk.shape[-1])
        q = (dot(xs[m, 512:768, :], wa[:, 16:64, :].reshape(768, 768)) + bias[0:1, :]).astype(BF)
        q_out[m] = q * jnp.asarray(0.125, BF)

    def gather_rest(m):
        x_here(m, 2)
        x_here(m, 3)

        def named(t, _):
            xs[m, pl.ds(pl.multiple_of(NW + 64 * t, 64), 64), :] = xall[m][rest_block(lengths, randoms, s, m, t)]
            return 0

        lax.fori_loop(0, 16, named, 0)
        out_copy(m, 0).start()

    def project(m, r):
        rows = xs[m, r, :]
        ks[m, r, :] = dot(rows, wa[:, 64:112, :].reshape(768, 768)).astype(BF)
        vs[m, r, :] = (dot(rows, wa[:, 112:160, :].reshape(768, 768)) + bias[1:2, :]).astype(BF)

    def pair(m, p):
        col = pl.ds(pl.multiple_of(p * 128, 128), 128)
        for h in range(2):
            r = pl.ds(h * HALF, HALF)
            more = extra[m, h]
            keys = jnp.concatenate([ks[m, a:a + n, col] for a, n in key_rows(h)], axis=0)
            vals = jnp.concatenate([vs[m, a:a + n, col] for a, n in key_rows(h)], axis=0)
            scores = dot_nt(jnp.concatenate([split_heads(q_out[m, r, col]), ind], axis=1),
                            jnp.concatenate([keys, more], axis=1))
            top = jnp.max(scores, axis=1, keepdims=True)
            e = jnp.exp(scores - top).astype(BF)
            o = dot(e, jnp.concatenate([vals, more], axis=1))
            total = o[:, 130:131]
            att[m, r, col] = merge_heads(o[:, :128] / total).astype(BF)
            norm = top + jnp.log(total)
            lse[m, r, :] = jnp.where(lane == 2 * p, norm[:HALF], jnp.where(lane == 2 * p + 1, norm[HALF:], lse[m, r, :]))

    def picked(g, plan):
        k = jnp.full((), 9, jnp.int32)
        for at, value in plan:
            k = jnp.where(g == at, value, k)
        return k

    def pump(g):
        for name in PUMP_ORDER:
            k = picked(g, PUMPS[name])
            act = {
                "x1": lambda k: x_line(1, k), "bo": b_own_column, "bt": b_other_column, "bc": b_to_x,
                "by0": lambda k: w_from_y(b_copy, x, k), "by1": lambda k: w_from_y(b_copy, 1 - x, k),
            }[name]
            act(k)

    def step(g, _):
        m, i = g // 9, g % 9
        for mm in range(2):
            pl.when(g == 9 * mm)(lambda mm=mm: gather_near(mm))
            pl.when(g == 9 * mm + 2)(lambda mm=mm: gather_rest(mm))
        pl.when(i < 2)(lambda: project(m, rows_at(jnp.minimum(i, 1), 640)))
        pl.when(i == 2)(lambda: project(m, pl.ds(NW, NS - NW)))

        @pl.when(i == 3)
        def _():
            out_copy(m, 1).start()
            out_copy(m, 2).start()

        pl.when(i >= 3)(lambda: pair(m, i - 3))
        pump(g)
        return 0

    lax.fori_loop(0, 18, step, 0)

    lax.fori_loop(18, 24, lambda g, _: (pump(g), 0)[1], 0)

    def b_arrived(i, _):
        ref = wall.at[i, :, theirs]
        remote(ref, ref, bsend.at[i, CC], bcrecv.at[i], to[CC]).wait_recv()
        return 0

    lax.fori_loop(0, 16, b_arrived, 0)
    keep_b.wait()
    top_copy.wait()
    for m in range(2):
        for t in range(3):
            out_copy(m, t).wait()

    def sent(k, _):
        for m in range(2):
            x_copy(m, k, x, XX).wait_send()
        for copy in (a_copy, b_copy):
            for way in (YY, CC):
                copy(k, x, y, way).wait_send()
                copy(k, 1 - x, y, way).wait_send()
            copy(k, x, 1 - y, CC).wait_send()
            copy(k, 1 - x, 1 - y, CC).wait_send()
        a_copy(k, x, y, XX).wait_send()
        pl.when(zfirst | (k == z))(lambda: b_copy(k, x, y, XX).wait_send())

        def line(way):
            x_copy(0, k, x, way).wait_send()
            x_copy(1, k, x, way).wait_send()
            a_copy(k, x, y, way).wait_send()
            b_copy(k, x, y, way).wait_send()
            pl.when(jnp.logical_not(zfirst))(lambda: b_copy(k, 1 - x, y, way).wait_send())

        pl.when((k <= z) & (z < 3))(lambda: line(UP))
        pl.when((k >= z) & (z > 0))(lambda: line(DOWN))
        return 0

    lax.fori_loop(0, 4, sent, 0)


START = (
    ("x0", 1),
    ("a", 1),
    ("ay0", 0),
    ("ax", 0),
    ("a", 2),
    ("a", 3),
    ("x0", 2),
    ("own x1", (UP, DOWN,)),
    ("ax", 2),
    ("ax", 1),
    ("x0", 3),
    ("ay0", 1),
    ("ay0", 3),
    ("ay1", 2),
    ("own b", (UP, DOWN,)),
    ("ax", 3),
    ("ay1", 3),
    ("ay0", 2),
    ("ay1", 0),
    ("own b", (XX,)),
    ("own x1", (XX,)),
    ("ay1", 1),
    ("own b", (YY, CC,)),
    ("x1", 1),
)
PUMP_ORDER = ("x1", "bo", "bc", "bt", "by0", "by1")
PUMPS = {
    "x1": ((2, 2), (9, 3),),
    "bo": ((0, 1), (5, 2), (10, 3),),
    "bt": ((2, 0), (9, 1), (11, 2), (14, 3),),
    "bc": ((0, 1), (9, 2), (11, 3),),
    "by0": ((2, 0), (5, 1), (11, 2), (15, 3),),
    "by1": ((9, 0), (13, 1), (14, 2), (16, 3),),
}


def forward_all(lengths, randoms, x, weights, vectors, b_up):
    dma = pltpu.SemaphoreType.DMA
    sd = jax.ShapeDtypeStruct
    vm, anywhere, sm = (pl.BlockSpec(memory_space=m) for m in (pltpu.VMEM, pl.ANY, pltpu.SMEM))
    mb, rows, width = x.shape
    v = pltpu.VMEM
    return pl.pallas_call(
        forward_kernel,
        out_shape=[
            sd((mb, rows, width), BF), sd((mb, rows, 128), F32), sd((mb, rows, width), BF),
            sd((mb, NS, width), BF), sd((mb, NS, width), BF), sd((mb, NS, width), BF),
            sd((16, REST, width), BF), sd((16, TOP, width), BF), sd((16, width), F32),
            sd((mb, 2, NK, 128), BF), sd((mb, 1, 1024), jnp.int32),
        ],
        in_specs=[sm, sm, anywhere] + [vm] * 8,
        out_specs=[vm, vm, vm, anywhere, anywhere, anywhere, anywhere, anywhere, vm, vm, vm],
        scratch_shapes=[
            v((304, width), F32), v((304, 384), F32), v((TOP, 384), BF), v((REST, 384), BF),
            v((8 * rows // 64, 64, width), BF), v((8 * rows // 64, 64, width), BF),
            v((mb, NS, width), BF), v((mb, NS, width), BF), v((mb, NS, width), BF),
            v((16, TOP, width), BF),
            dma((2,)), dma((5,)), dma((mb, 3)),
            dma((16, 5)), dma((16,)), dma((16,)), dma((16, 5)), dma((16,)), dma((16,)),
            dma((mb, 8, 3)), dma((mb, 8)),
        ],
        compiler_params=pltpu.CompilerParams(
            collective_id=0, has_side_effects=True, vmem_limit_bytes=60 * 2**20
        ),
    )(lengths, randoms, x.reshape(mb, rows // 64, 64, width), *weights, vectors, b_up)


def backward_kernel(datt, stats, tgt, gb_in, extra_in, q_in, done, k_in, v_in, xs_in, top_in, go, gu, gd,
                    oq, ok, ov, oo, ou, od, ob, odx,
                    kb, vb, xsb, wa, extra, dka, dva, q, ga, gb,
                    acc, mate, yr, mate2, yr2, xr, zr, dxp, dxr, dzr, fin, rcv,
                    ksem, lsem, msem, msem2, asem, ysem, xsem, zsem, ysem2, xsem2, zsem2, dxsem, dzsem, fsem, ready):
    z, x, y, c = place()
    s = 2 * z + x
    mine, theirs = lanes(c), lanes(1 - c)
    near_x, near_y, near_c = device(z, 1 - x, y, c), device(z, x, 1 - y, c), device(z, x, y, 1 - c)
    above, below = device(z + 1, x, y, c), device(z - 1, x, y, c)

    def far(i):
        inner = jnp.where(i == 0, 3, jnp.where(i == 1, 0, jnp.where(i == 2, 2, 1)))
        low = jnp.where(z == 0, 3 - i, jnp.where(z == 1, inner, i))
        return jnp.where(z == 2, 3 - inner, low)

    def slot_of(i, zz):
        zt = jnp.where(zz == 0, 3 - i, jnp.where((zz == 1) & (i == 2), 2, 3))
        return zt, (zz == 0) | ((zz == 1) & (i >= 1)) | ((zz == 2) & (i == 2))

    def at_slot(act, i):
        up, sends_up = slot_of(i, z)
        down, sends_down = slot_of(i, 3 - z)
        pl.when(sends_up)(lambda: act(up, True))
        pl.when(sends_down)(lambda: act(3 - down, False))

    def column(p):
        return pl.ds(pl.multiple_of(p * 128, 128), 128)

    def load_keys(m, p):
        return (pltpu.make_async_copy(k_in.at[m, :, column(p)], kb.at[:, column(p)], ksem.at[0, p]),
                pltpu.make_async_copy(v_in.at[m, :, column(p)], vb.at[:, column(p)], ksem.at[1, p]))

    def start_keys(m):
        def one(p, _):
            for cp in load_keys(m, p):
                cp.start()
            return 0

        lax.fori_loop(0, 6, one, 0)

    start_keys(0)
    extra_copy = pltpu.make_async_copy(extra_in, extra, lsem.at[4])
    extra_copy.start()
    q_copy = pltpu.make_async_copy(q_in, q, lsem.at[3])
    q_copy.start()
    top_copy = pltpu.make_async_copy(top_in.at[:, :, pl.ds(16, 144), :], wa, lsem.at[0])
    top_copy.start()
    done_copy = pltpu.make_async_copy(done, odx, lsem.at[1])
    done_copy.start()
    greet(z, x, y, c)

    def parts(yy, cc):
        off = pl.multiple_of(cc * 384, 128)
        yield 0, go.at[:, yy, :, pl.ds(off, 384)], pl.ds(0, 48)
        yield 1, gd.at[:, yy, :, pl.ds(off, 384)], pl.ds(240, 192)
        for j in range(4):
            col = pl.multiple_of(j * 768 + cc * 384, 128)
            yield 2 + j, gu.at[:, yy, :, pl.ds(col, 384)], pl.ds(48 + 48 * j, 48)

    swaps, loads = {}, {}
    for t, yy in enumerate((1 - y, y)):
        for i, src, rows in parts(yy, 1 - c):
            swaps[t, i] = remote(src, mate.at[:, yy, rows, :], msem.at[0, t, i], msem.at[1, t, i], near_c)
            swaps[t, i].start()
        for i, src, rows in parts(yy, c):
            loads[t, i] = pltpu.make_async_copy(src, acc.at[:, yy, rows, :], asem.at[t, i])
            loads[t, i].start()
    gb[...] = gb_in[...]

    class Reduce:
        def __init__(self, rows, held, cols, other, from_y, ys, xs_, zs):
            self.rows, self.held, self.cols, self.other, self.from_y = rows, held, cols, other, from_y
            self.ys, self.xs, self.zs = ys, xs_, zs

        def a(self, s_, yy):
            return self.held.at[s_, yy, :, self.cols]

        def y_copy(self, s_):
            return remote(self.a(s_, 1 - y), self.from_y.at[s_], self.ys.at[0, s_], self.ys.at[1, s_], near_y)

        def x_copy(self, zz):
            return remote(self.a(2 * zz + 1 - x, y), xr.at[zz, pl.ds(0, self.rows), :], self.xs.at[0, zz],
                          self.xs.at[1, zz], near_x)

        def z_copy(self, zz, slot, to):
            return remote(self.a(2 * zz + x, y), zr.at[slot, pl.ds(0, self.rows), :], self.zs.at[0, zz],
                          self.zs.at[1, slot], to)

        def total(self, s_, yy, others):
            value = self.held[s_, yy, :, self.cols].astype(F32) + self.other[s_, yy].astype(F32)
            for ref, index in others:
                value = value + ref[index, 0:self.rows, :].astype(F32)
            return value

        def keep(self, s_, yy, value):
            self.held[s_, yy, :, self.cols] = value.astype(BF)

        def y_step(self, i):
            s_ = 2 * far(i % 4) + jnp.where(i < 4, 1 - x, x)
            self.keep(s_, 1 - y, self.total(s_, 1 - y, []))
            self.y_copy(s_).start()

        def x_step(self, i):
            zz = far(i)
            s_ = 2 * zz + 1 - x
            self.y_copy(s_).wait_recv()
            self.keep(s_, y, self.total(s_, y, [(self.from_y, s_)]))
            self.x_copy(zz).start()

        def along(self, zz, up):
            s_ = 2 * zz + x
            self.y_copy(s_).wait_recv()
            self.x_copy(zz).wait_recv()
            others = [(self.from_y, s_), (xr, zz)]
            more = z > 0 if up else z < 3

            @pl.when(more)
            def _():
                self.z_copy(zz, zz, above).wait_recv()
                self.keep(s_, y, self.total(s_, y, others + [(zr, zz)]))

            @pl.when(jnp.logical_not(more))
            def _():
                self.keep(s_, y, self.total(s_, y, others))

            if up:
                self.z_copy(zz, zz, above).start()
            else:
                self.z_copy(zz, jnp.where(zz == z - 1, 4, zz), below).start()

        def z_step(self, i):
            at_slot(self.along, i)

        def finish(self):
            self.y_copy(s).wait_recv()
            self.x_copy(z).wait_recv()
            r = pl.ds(0, self.rows)
            fin[r, :] = self.total(s, y, [(self.from_y, s), (xr, z)])
            for slot, cond in ((z, z > 0), (4, z < 3)):
                @pl.when(cond)
                def _(slot=slot):
                    self.z_copy(z, slot, above).wait_recv()
                    fin[r, :] += zr[slot, r, :].astype(F32)

        def drain(self):
            def one(i, _):
                self.y_copy(i).wait_send()
                return 0

            lax.fori_loop(0, 8, one, 0)

            def two(i, _):
                self.x_copy(i).wait_send()
                pl.when(i != z)(lambda: self.z_copy(i, i, above).wait_send())
                return 0

            lax.fori_loop(0, 4, two, 0)

    rest = Reduce(REST, acc, pl.ds(0, 384), mate, yr, ysem, xsem, zsem)
    top = Reduce(TOP, ga, mine, mate2, yr2, ysem2, xsem2, zsem2)

    def dx_x(m, zz):
        return remote(dxp.at[m, 2 * zz + 1 - x], dxr.at[m, zz], dxsem.at[0, m, zz], dxsem.at[1, m, zz], near_x)

    def dx_z(m, zz, slot, to):
        return remote(dxp.at[m, 2 * zz + x], dzr.at[m, slot], dzsem.at[0, m, zz], dzsem.at[1, m, slot], to)

    def dx_along(m, zz, up):
        s_ = 2 * zz + x
        dx_x(m, zz).wait_recv()
        more = z > 0 if up else z < 3

        @pl.when(more)
        def _():
            dx_z(m, zz, zz, above).wait_recv()
            dxp[m, s_] = (dxp[m, s_].astype(F32) + dxr[m, zz].astype(F32) + dzr[m, zz].astype(F32)).astype(BF)

        @pl.when(jnp.logical_not(more))
        def _():
            dxp[m, s_] = (dxp[m, s_].astype(F32) + dxr[m, zz].astype(F32)).astype(BF)

        if up:
            dx_z(m, zz, zz, above).start()
        else:
            dx_z(m, zz, jnp.where(zz == z - 1, 4, zz), below).start()

    def dx_step(m, i):
        at_slot(functools.partial(dx_along, m), i)

    def dx_finish(m):
        dx_x(m, z).wait_recv()
        odx[m] += dxr[m, z].astype(F32)
        for slot, cond in ((z, z > 0), (4, z < 3)):
            @pl.when(cond)
            def _(slot=slot):
                dx_z(m, z, slot, above).wait_recv()
                odx[m] += dzr[m, slot].astype(F32)

    def dx_sent(m):
        def one(i, _):
            dx_x(m, i).wait_send()
            pl.when(i != z)(lambda: dx_z(m, i, i, above).wait_send())
            return 0

        lax.fori_loop(0, 4, one, 0)

    ind = block_columns()

    def pair(m, p):
        col = column(p)
        for cp in load_keys(m, p):
            cp.wait()
        dka[...] = jnp.zeros_like(dka)
        dva[...] = jnp.zeros_like(dva)
        for h in range(2):
            rows = pl.ds(h * HALF, HALF)
            qs = split_heads(q[m, rows, col])
            dos = split_heads(datt[m, rows, col])
            lane = lax.broadcasted_iota(jnp.int32, (HALF, 128), 1)

            def both(first, rows=rows, lane=lane):
                return jnp.concatenate(
                    [jnp.sum(jnp.where(lane == first + a, stats[m, rows, :], 0.0), axis=1, keepdims=True) for a in range(2)],
                    axis=0)

            log_norm, delta = both(2 * p), both(16 + 2 * p)
            qe = jnp.concatenate([qs, with_column(ind, -log_norm)], axis=1)
            doe = jnp.concatenate([dos, with_column(jnp.zeros_like(ind), -delta)], axis=1)
            dqt = jnp.zeros((128, 2 * HALF), F32)
            (wa_, wn), (ga, gn), (ra, rn) = key_rows(h)
            off = 0
            for pieces in (((wa_, 576),), ((wa_ + 576, 576),), ((ga, gn), (ra, rn))):
                n = sum(t for _, t in pieces)
                k2 = jnp.concatenate([kb[a:a + t, col] for a, t in pieces], axis=0)
                v2 = jnp.concatenate([vb[a:a + t, col] for a, t in pieces], axis=0)
                more = extra[m, h, off:off + n, :]
                pt = jnp.exp(dot_nt(jnp.concatenate([k2, more], axis=1), qe))
                ds = (pt * dot_nt(jnp.concatenate([v2, more], axis=1), doe)).astype(BF)
                dv_ = dot(pt.astype(BF), dos)
                dk_ = dot(ds, qs)
                dqt = dqt + dot(k2.T, ds)
                if off < WK:
                    a, t = pieces[0]
                    dka[a:a + t, :] += dk_
                    dva[a:a + t, :] += dv_
                else:
                    at = 0
                    for a, t in pieces:
                        kb[a:a + t, col] = dk_[at:at + t].astype(BF)
                        vb[a:a + t, col] = dv_[at:at + t].astype(BF)
                        at += t
                off += n
            q[m, rows, col] = (merge_heads(dqt.T) * 0.125).astype(BF)
        kb[0:NW, col] = dka[...].astype(BF)
        vb[0:NW, col] = dva[...].astype(BF)

    def weight(i):
        return wa[:, :, 48 * i:48 + 48 * i, :].reshape(768, 768)

    def dx_rows(m, i):
        for part in range(2):
            r = rows_at(2 * i + part, 384)
            value = dot_nt(kb[r, :], weight(1)) + dot_nt(vb[r, :], weight(2))
            xsb[r, :] = value.astype(BF)
            if part == 1:
                @pl.when(i == 0)
                def _(value=value):
                    odx[m] += value[128:384] + dot_nt(q[m], weight(0))

    def dx_piece(m, i):
        t = 2 * far(i % 4) + jnp.where(i < 4, 1 - x, x)
        row = lax.broadcasted_iota(jnp.int32, (256, 1024), 0) + 256 * t
        chosen = jnp.where(row == tgt[m], 1.0, 0.0).astype(BF)
        value = dot(chosen, xsb[NW:NS, :])
        w = t - s + 2

        @pl.when(t == s)
        def _():
            odx[m] += value

        @pl.when(t != s)
        def _():
            near = xsb[rows_at(jnp.clip(w, 0, 4), 256), :].astype(F32)
            dxp[m, t] = (value + jnp.where((w >= 0) & (w < 5), near, 0.0)).astype(BF)

        pl.when(i < 4)(lambda: dx_x(m, far(i % 4)).start())

    def weight_grads(m, i):
        cols = pl.ds(pl.multiple_of(384 * i, 128), 384)
        a = xsb[:, cols]
        chips = pl.ds(4 * i, 4)

        def keep(row, value, n):
            value = value.reshape(4, 2, 48, value.shape[1])

            @pl.when(m == 0)
            def _():
                ga[chips, :, row:row + 48, n] = value.astype(BF)

            @pl.when(m == 1)
            def _():
                ga[chips, :, row:row + 48, n] = (ga[chips, :, row:row + 48, n].astype(F32) + value).astype(BF)

        for half in range(2):
            n = slice(384 * half, 384 * half + 384)
            keep(64, dot_tn(a, kb[:, n]), n)
            keep(112, dot_tn(a, vb[:, n]), n)
        keep(16, dot_tn(a[512:768], q[m]), slice(0, 768))

    def small_grads():
        low = gb[...].astype(BF)

        def spread(i, _):
            ga[i // 2, i % 2, 0:16, :] = low
            return 0

        lax.fori_loop(0, 16, spread, 0)

    swap2 = [remote(ga.at[:, yy, :, theirs], mate2.at[:, yy], msem2.at[0, t], msem2.at[1, t], near_c)
             for t, yy in enumerate((1 - y, y))]

    def rest_rows(cc):
        yield oo, 0, pl.multiple_of(24 * cc, 8), 24, 0
        for j in range(4):
            yield ou, 24 + 24 * j, pl.multiple_of(48 + 48 * j + 24 * cc, 8), 24, 768 * j
        yield od, 120, pl.multiple_of(240 + 96 * cc, 8), 96, 0

    def top_rows(cc):
        yield ob, 216, 0, 16, 0
        for i, ref in enumerate((oq, ok, ov)):
            yield ref, 232 + 24 * i, pl.multiple_of(16 + 48 * i + 24 * cc, 8), 24, 0

    def to_mate(rows_of, first):
        return [remote(fin.at[pl.ds(start, n), :], rcv.at[at:at + n, :], fsem.at[0, first + i], fsem.at[1, first + i], near_c)
                for i, (_, at, start, n, _) in enumerate(rows_of(1 - c))]

    def hand_over(rows_of):
        for ref, at, start, n, col in rows_of(c):
            ref[:, pl.ds(pl.multiple_of(col + c * 384, 128), 384)] = fin[pl.ds(start, n), :]

    def take_over(rows_of):
        for ref, at, start, n, col in rows_of(c):
            ref[:, pl.ds(pl.multiple_of(col + (1 - c) * 384, 128), 384)] = rcv[at:at + n, :]

    last0 = to_mate(rest_rows, 0)

    def picked(g, plan):
        k = jnp.full((), 9, jnp.int32)
        for at, value in plan:
            k = jnp.where(g == at, value, k)
        return k

    def start_top(_):
        swap2[0].wait_recv()
        swap2[1].wait_recv()
        lax.fori_loop(0, 8, lambda i, _: (top.y_step(i), 0)[1], 0)

    def tell(to):
        pl.semaphore_signal(ready, inc=1, device_id=to, device_id_type=MESH)

    def end_rest(_):
        rest.finish()
        for to in (near_x, near_y, near_c):
            tell(to)
        pl.when(z > 0)(lambda: tell(below))
        pl.when(z < 3)(lambda: tell(above))
        for cp in last0:
            cp.start()
        hand_over(rest_rows)

    def all_ready(_):
        pl.semaphore_wait(ready, 3 + (z > 0).astype(jnp.int32) + (z < 3).astype(jnp.int32))

    acts = {
        "Y": rest.y_step, "X": rest.x_step, "Z": rest.z_step, "BF": end_rest, "W": all_ready,
        "D0": functools.partial(dx_step, 0), "D0F": lambda _: dx_finish(0), "D1": functools.partial(dx_step, 1),
        "TY": start_top, "TX": top.x_step, "TZ": top.z_step,
    }

    def pump(g, first, last_):
        for name in STEP_ORDER:
            plan = [(at, k) for at, k in STEPS[name] if first <= at < last_]
            if plan:
                k = picked(g, plan)
                pl.when(k < 9)(lambda name=name, k=k: acts[name](k))

    for i in range(6):
        loads[0, i].wait()
        swaps[0, i].wait_recv()
    rest.y_step(0)
    done_copy.wait()
    q_copy.wait()
    extra_copy.wait()

    def load_xs(m):
        return pltpu.make_async_copy(xs_in.at[m], xsb, lsem.at[2])

    def micro(m, _):
        load_xs(m).start()

        def one(i, _):
            @pl.when(i < 6)
            def _():
                pair(m, jnp.minimum(i, 5))

            @pl.when((m == 0) & (i == MATE_AT))
            def _():
                for t in range(6):
                    loads[1, t].wait()
                    swaps[1, t].wait_recv()
                top_copy.wait()

            pl.when(i == 6)(lambda: load_xs(m).wait())
            pl.when((i >= 6) & (i < 8))(lambda: weight_grads(m, jnp.clip(i - 6, 0, 1)))

            @pl.when(i == 8)
            def _():
                gb[0:1, :] += jnp.sum(q[m].astype(F32), axis=0, keepdims=True)

                def value_bias(t, _):
                    gb[1:2, :] += jnp.sum(vb[rows_at(t, 256), :].astype(F32), axis=0, keepdims=True)
                    return 0

                lax.fori_loop(0, 9, value_bias, 0)

            pl.when(i >= 9)(lambda: dx_rows(m, jnp.clip(i - 9, 0, 2)))
            pump(12 * m + i, 0, 24)

            @pl.when((m == 1) & (i == 8))
            def _():
                small_grads()
                for cp in swap2:
                    cp.start()

            return 0

        lax.fori_loop(0, 12, one, 0)
        pl.when(m == 0)(lambda: start_keys(1))
        lax.fori_loop(0, 8, lambda i, _: (dx_piece(m, i), 0)[1], 0)
        return 0

    lax.fori_loop(0, 2, micro, 0)
    lax.fori_loop(24, 38, lambda g, _: (pump(g, 24, 38), 0)[1], 0)
    dx_finish(1)
    for cp in last0:
        cp.wait()
    take_over(rest_rows)
    top.finish()
    last1 = to_mate(top_rows, 6)
    for cp in last1:
        cp.start()
    hand_over(top_rows)
    for cp in last1:
        cp.wait()
    take_over(top_rows)
    top.drain()
    rest.drain()
    for t in range(2):
        for i in range(6):
            swaps[t, i].wait_send()
    dx_sent(0)
    dx_sent(1)
    for cp in swap2:
        cp.wait_send()


STEP_ORDER = ("X", "TY", "W", "D1", "BF", "Y", "D0", "TX", "TZ", "D0F", "Z")
STEPS = {
    "Y": ((1, 1), (2, 2), (3, 3), (5, 4), (7, 5), (9, 6), (24, 7),),
    "X": ((2, 0), (3, 1), (5, 2), (8, 3),),
    "Z": ((11, 0), (12, 1), (20, 2),),
    "D0": ((14, 0), (18, 1), (23, 2),),
    "TY": ((29, 0),),
    "BF": ((29, 0),),
    "W": ((32, 0),),
    "D0F": ((24, 0),),
    "TX": ((32, 0), (33, 1), (35, 2), (37, 3),),
    "D1": ((27, 0), (29, 1), (32, 2),),
    "TZ": ((33, 0), (35, 1), (37, 2),),
}
MATE_AT = 2


def backward_all(datt, stats, tgt, gb, extra, q, done, k, v, xs, top, go, gu, gd):
    dma = pltpu.SemaphoreType.DMA
    sd = jax.ShapeDtypeStruct
    vm, anywhere = (pl.BlockSpec(memory_space=m) for m in (pltpu.VMEM, pl.ANY))
    mb, rows, width = q.shape
    s = pltpu.VMEM
    views = [top.reshape(8, 2, TOP, width), go.reshape(8, 2, 48, width), gu.reshape(8, 2, 48, 4 * width),
             gd.reshape(8, 2, 192, width)]
    return pl.pallas_call(
        backward_kernel,
        out_shape=[sd((24, width), F32)] * 4 + [sd((24, 4 * width), F32), sd((96, width), F32), sd((16, width), F32),
                                                sd(q.shape, F32)],
        in_specs=[vm] * 4 + [anywhere] * 10,
        out_specs=[vm] * 8,
        scratch_shapes=[
            s((NS, width), BF), s((NS, width), BF), s((NS, width), BF), s((8, 2, TOP - 16, width), BF),
            s((mb, 2, NK, 128), BF), s((NW, 128), F32), s((NW, 128), F32), s((mb, rows, width), BF),
            s((8, 2, TOP, width), BF), s((16, width), F32),
            s((8, 2, REST, 384), BF), s((8, 2, REST, 384), BF), s((8, REST, 384), BF), s((8, 2, TOP, 384), BF), s((8, TOP, 384), BF),
            s((4, REST, 384), BF),
            s((5, REST, 384), BF),
            s((mb, 8, rows, width), BF), s((mb, 4, rows, width), BF), s((mb, 5, rows, width), BF),
            s((REST, 384), F32), s((304, 384), F32),
            dma((2, 6)), dma((5,)), dma((2, 2, 6)), dma((2, 2)), dma((2, 6)),
            dma((2, 8)), dma((2, 4)), dma((2, 5)), dma((2, 8)), dma((2, 4)), dma((2, 5)),
            dma((2, mb, 4)), dma((2, mb, 5)), dma((2, 10)), pltpu.SemaphoreType.REGULAR,
        ],
        compiler_params=pltpu.CompilerParams(
            collective_id=1, has_side_effects=True, vmem_limit_bytes=62 * 2**20
        ),
    )(datt, stats, tgt, gb, extra, q, done, k, v, xs, *views)


CHUNKS = 9


def project_kernel(idx, xall, wall, bias, xs_ref, k_ref, v_ref, q_ref, xs, w, sems, wsem):
    m, i = pl.program_id(0), pl.program_id(1)

    @pl.when((m == 0) & (i == 0))
    def _():
        copy = pltpu.make_async_copy(wall.at[:, pl.ds(16, 144), :], w, wsem)
        copy.start()
        for mm in range(2):
            for cc in range(CHUNKS):
                pieces = [(0, 256)] if cc < 5 else [(0, 128), (128, 128)] if cc == 5 else [(64 * t, 64) for t in range(4)]
                base = cc if cc < 5 else 5 if cc == 5 else 7 + 4 * (cc - 6)
                for t, (off, n) in enumerate(pieces):
                    start = pl.multiple_of(idx[mm, base + t], 64)
                    pltpu.make_async_copy(xall.at[mm, pl.ds(start, n), :], xs.at[mm, cc, pl.ds(off, n), :],
                                          sems.at[mm, cc]).start()
        copy.wait()

    pltpu.make_async_copy(xall.at[0, pl.ds(0, 256), :], xs.at[m, i], sems.at[m, i]).wait()
    rows = xs[m, i]
    xs_ref[0] = rows
    k_ref[0] = dot(rows, w[:, 48:96, :].reshape(768, 768)).astype(BF)
    v_ref[0] = (dot(rows, w[:, 96:144, :].reshape(768, 768)) + bias[1:2, :]).astype(BF)

    @pl.when(i == 2)
    def _():
        q = (dot(rows, w[:, 0:48, :].reshape(768, 768)) + bias[0:1, :]).astype(BF)
        q_ref[0] = q * jnp.asarray(0.125, BF)


def project(idx, xall, wall, bias):
    mb = xall.shape[0]
    sd = jax.ShapeDtypeStruct
    chunk = pl.BlockSpec((1, 256, 768), lambda m, i, t: (m, i, 0))
    return pl.pallas_call(
        project_kernel,
        grid_spec=pltpu.PrefetchScalarGridSpec(
            num_scalar_prefetch=1,
            grid=(mb, CHUNKS),
            in_specs=[pl.BlockSpec(memory_space=pl.ANY)] * 2 + [pl.BlockSpec((16, 768), lambda m, i, t: (0, 0))],
            out_specs=[chunk, chunk, chunk, pl.BlockSpec((1, 256, 768), lambda m, i, t: (m, 0, 0))],
            scratch_shapes=[
                pltpu.VMEM((mb, CHUNKS, 256, 768), BF), pltpu.VMEM((16, 144, 768), BF),
                pltpu.SemaphoreType.DMA((mb, CHUNKS)), pltpu.SemaphoreType.DMA,
            ],
        ),
        out_shape=[sd((mb, NS, 768), BF)] * 3 + [sd((mb, 256, 768), BF)],
        compiler_params=pltpu.CompilerParams(vmem_limit_bytes=48 * 2**20),
    )(idx, xall, wall, bias)


EPS = 1e-6
G0, G1 = 0.7978845608, 0.044715


def norm(v):
    mean = jnp.mean(v, axis=-1, keepdims=True)
    centred = v - mean
    inverse = lax.rsqrt(jnp.mean(centred * centred, axis=-1, keepdims=True) + EPS)
    return centred * inverse, inverse


def norm_back(g, normed, inverse, gain):
    c = g * gain
    return inverse * (c - jnp.mean(c, axis=-1, keepdims=True)
                      - normed * jnp.mean(c * normed, axis=-1, keepdims=True))


def middle_kernel(att, x, cot, wall, bias, lse, out_ref, stats_ref, datt_ref, done_ref, go_out, gu_out, gd_out, gb_ref,
                  go_ref, gu_ref, gd_ref, gsem, w, wsem, pre, hid, mid, low, n1, r1, ffn):
    rows = x.shape[0]
    copies = [
        pltpu.make_async_copy(wall.at[:, pl.ds(0, 48), :], w.at[:, pl.ds(0, 48), :], wsem.at[0]),
        pltpu.make_async_copy(wall.at[:, pl.ds(48, 192), :], w.at[:, pl.ds(48, 192), :], wsem.at[1]),
        pltpu.make_async_copy(wall.at[:, pl.ds(240, 192), :], w.at[:, pl.ds(240, 192), :], wsem.at[2]),
    ]
    for cp in copies:
        cp.start()
    half = rows // 2
    copies[0].wait()
    w_out = w[:, 0:48, :].reshape(768, 768)
    for h in range(2):
        r = pl.ds(h * half, half)
        t = x[r, :].astype(F32) + dot(att[r, :], w_out) + bias[2:3, :]
        normed, inverse = norm(t)
        n1[r, :] = normed
        r1[r, :] = jnp.broadcast_to(inverse, (half, 128))
        value = normed * bias[4:5, :] + bias[5:6, :]
        mid[r, :] = value
        low[r, :] = value.astype(BF)
    ffn[...] = jnp.broadcast_to(bias[3:4, :], ffn.shape)
    copies[1].wait()
    copies[2].wait()

    def up_block(j):
        return w[:, pl.ds(pl.multiple_of(48 + 48 * j, 16), 48), :].reshape(768, 768)

    def down_block(j):
        return w[pl.ds(4 * j, 4), 240:432, :].reshape(768, 768)

    def forward(j, _):
        wu, wd = up_block(j), down_block(j)
        for h in range(2):
            r = pl.ds(h * half, half)
            u = dot(low[r, :], wu) + bias[pl.ds(8 + j, 1), :]
            square = u * u
            th = jnp.tanh(G0 * u * (1.0 + G1 * square))
            half_u, one = 0.5 * u, 1.0 + th
            pre[j, r, :] = 0.5 * one + half_u * (one * (1.0 - th)) * (G0 + (3.0 * G0 * G1) * square)
            g = (half_u * one).astype(BF)
            hid[j, r, :] = g
            ffn[r, :] += dot(g, wd)
        return 0

    lax.fori_loop(0, 4, forward, 0)
    gb_ref[...] = jnp.zeros_like(gb_ref)
    for h in range(2):
        r = pl.ds(h * half, half)
        normed, inverse = norm(mid[r, :] + ffn[r, :])
        out_ref[r, :] = (normed * bias[6:7, :] + bias[7:8, :]).astype(BF)
        g = cot[r, :].astype(F32)
        gb_ref[6:7, :] += jnp.sum(g * normed, axis=0, keepdims=True)
        gb_ref[7:8, :] += jnp.sum(g, axis=0, keepdims=True)
        d_two = norm_back(g, normed, inverse, bias[6:7, :])
        mid[r, :] = d_two
        d_ffn = d_two.astype(BF)
        datt_ref[r, :] = d_ffn
        gb_ref[3:4, :] += jnp.sum(d_ffn.astype(F32), axis=0, keepdims=True)

    def sent(ref, out, j, t):
        at = pl.ds(pl.multiple_of(j * 768, 768), 768)
        return pltpu.make_async_copy(ref.at[j], out.at[at, :] if t == 0 else out.at[:, at], gsem.at[t, j])

    def backward(j, _):
        wu, wd = up_block(j), down_block(j)
        d_ffn = datt_ref[...]
        gd_ref[j] = dot_tn(hid[j], d_ffn).astype(BF)
        sent(gd_ref, gd_out, j, 0).start()
        for h in range(2):
            r = pl.ds(h * half, half)
            d_pre = (dot_nt(datt_ref[r, :], wd) * pre[j, r, :]).astype(BF)
            hid[j, r, :] = d_pre
            gb_ref[pl.ds(8 + j, 1), :] += jnp.sum(d_pre.astype(F32), axis=0, keepdims=True)
            mid[r, :] += dot_nt(d_pre, wu)
        gu_ref[j] = dot_tn(low[...], hid[j]).astype(BF)
        sent(gu_ref, gu_out, j, 1).start()
        return 0

    lax.fori_loop(0, 4, backward, 0)
    for h in range(2):
        r = pl.ds(h * half, half)
        d_mid, normed = mid[r, :], n1[r, :]
        gb_ref[4:5, :] += jnp.sum(d_mid * normed, axis=0, keepdims=True)
        gb_ref[5:6, :] += jnp.sum(d_mid, axis=0, keepdims=True)
        d_one = norm_back(d_mid, normed, r1[r, 0:1], bias[4:5, :])
        done_ref[r, :] = d_one
        d_branch = d_one.astype(BF)
        low[r, :] = d_branch
        gb_ref[2:3, :] += jnp.sum(d_branch.astype(F32), axis=0, keepdims=True)
        d_att = dot_nt(d_branch, w_out).astype(BF)
        datt_ref[r, :] = d_att
        product = d_att.astype(F32) * att[r, :].astype(F32)
        lane = lax.broadcasted_iota(jnp.int32, (half, 128), 1)
        stats = lse[r, :]
        for p in range(6):
            two = product[:, 128 * p:128 * p + 128]
            stats = jnp.where(lane == 16 + 2 * p, jnp.sum(jnp.where(lane < 64, two, 0.0), axis=1, keepdims=True), stats)
            stats = jnp.where(lane == 17 + 2 * p, jnp.sum(jnp.where(lane >= 64, two, 0.0), axis=1, keepdims=True), stats)
        stats_ref[r, :] = stats
    go_ref[...] = dot_tn(att[...], low[...]).astype(BF)
    go_copy = pltpu.make_async_copy(go_ref, go_out, wsem.at[0])
    go_copy.start()
    for j in range(4):
        sent(gd_ref, gd_out, j, 0).wait()
        sent(gu_ref, gu_out, j, 1).wait()
    go_copy.wait()


def middle(att, x, cot, wall, bias, lse):
    rows = x.shape[0]
    sd = jax.ShapeDtypeStruct
    vm = pl.BlockSpec(memory_space=pltpu.VMEM)
    return pl.pallas_call(
        middle_kernel,
        in_specs=[vm, vm, vm, pl.BlockSpec(memory_space=pl.ANY), vm, vm],
        out_specs=[vm] * 4 + [pl.BlockSpec(memory_space=pl.ANY)] * 3 + [vm],
        out_shape=[sd((rows, 768), BF), sd((rows, 128), F32), sd((rows, 768), BF), sd((rows, 768), F32), sd((768, 768), BF),
                   sd((768, 3072), BF), sd((3072, 768), BF), sd((16, 768), F32)],
        scratch_shapes=[
            pltpu.VMEM((768, 768), BF), pltpu.VMEM((4, 768, 768), BF), pltpu.VMEM((4, 768, 768), BF),
            pltpu.SemaphoreType.DMA((2, 4)),
            pltpu.VMEM((16, 432, 768), BF), pltpu.SemaphoreType.DMA((3,)),
            pltpu.VMEM((4, rows, 768), F32), pltpu.VMEM((4, rows, 768), BF),
            pltpu.VMEM((rows, 768), F32), pltpu.VMEM((rows, 768), BF), pltpu.VMEM((rows, 768), F32),
            pltpu.VMEM((rows, 128), F32), pltpu.VMEM((rows, 768), F32),
        ],
        compiler_params=pltpu.CompilerParams(vmem_limit_bytes=60 * 2**20),
    )(att, x, cot, wall, bias, lse)


def back_kernel(scattered, idx, xs_ref, dk_ref, dv_ref, dq_ref, done_ref, wall, gb_in, dx_ref, own_ref, gq_ref, gk_ref, gv_ref, gb_ref,
                w, wsem, acc, aq, ak, av):
    m, i = pl.program_id(0), pl.program_id(1)

    @pl.when((m == 0) & (i == 0))
    def _():
        copy = pltpu.make_async_copy(wall.at[:, pl.ds(16, 144), :], w, wsem)
        copy.start()
        acc[...] = jnp.zeros_like(acc)
        aq[...] = jnp.zeros_like(aq)
        ak[...] = jnp.zeros_like(ak)
        av[...] = jnp.zeros_like(av)
        gb_ref[...] = gb_in[...]
        copy.wait()

    rows, dk, dv = xs_ref[0], dk_ref[0], dv_ref[0]
    ak[...] += dot_tn(rows, dk)
    av[...] += dot_tn(rows, dv)
    gb_ref[1:2, :] += jnp.sum(dv.astype(F32), axis=0, keepdims=True)
    dx = dot_nt(dk, w[:, 48:96, :].reshape(768, 768)) + dot_nt(dv, w[:, 96:144, :].reshape(768, 768))

    def add(slot, off, n):
        start = pl.multiple_of(idx[m, slot], 64)
        acc[m, pl.ds(start, n), :] += dx[off:off + n]

    if not scattered:
        dx_ref[0] = jnp.where(i == 2, jnp.zeros_like(dx), dx).astype(BF)

    @pl.when((i < 5) & (i != 2) & scattered)
    def _():
        add(jnp.minimum(i, 4), 0, 256)

    @pl.when((i == 5) & scattered)
    def _():
        add(5, 0, 128)
        add(6, 128, 128)

    @pl.when((i > 5) & scattered)
    def _():
        for t in range(4):
            add(7 + 4 * (i - 6) + t, 64 * t, 64)

    @pl.when(i == 2)
    def _():
        dq = dq_ref[0]
        aq[...] += dot_tn(rows, dq)
        gb_ref[0:1, :] += jnp.sum(dq.astype(F32), axis=0, keepdims=True)
        own_ref[0] = dx + done_ref[0] + dot_nt(dq, w[:, 0:48, :].reshape(768, 768))

    @pl.when((i == CHUNKS - 1) & scattered)
    def _():
        dx_ref[m if scattered else 0] = acc[m].astype(BF)

    @pl.when((m == 1) & (i == CHUNKS - 1))
    def _():
        gq_ref[...] = aq[...].astype(BF)
        gk_ref[...] = ak[...].astype(BF)
        gv_ref[...] = av[...].astype(BF)


def back(idx, xs, dk, dv, dq, done, wall, gb, seq_len):
    mb = xs.shape[0]
    sd = jax.ShapeDtypeStruct
    chunk = pl.BlockSpec((1, 256, 768), lambda m, i, t: (m, i, 0))
    one = pl.BlockSpec((1, 256, 768), lambda m, i, t: (m, 0, 0))
    whole = lambda *s: pl.BlockSpec(s, lambda m, i, t: (0,) * len(s))
    scattered = seq_len > 0
    held = seq_len if scattered else 256
    return pl.pallas_call(
        functools.partial(back_kernel, scattered),
        grid_spec=pltpu.PrefetchScalarGridSpec(
            num_scalar_prefetch=1,
            grid=(mb, CHUNKS),
            in_specs=[chunk, chunk, chunk, one, one, pl.BlockSpec(memory_space=pl.ANY), whole(16, 768)],
            out_specs=[whole(mb, seq_len, 768) if scattered else chunk, one, whole(768, 768), whole(768, 768), whole(768, 768), whole(16, 768)],
            scratch_shapes=[
                pltpu.VMEM((16, 144, 768), BF), pltpu.SemaphoreType.DMA, pltpu.VMEM((mb, held, 768), F32),
                pltpu.VMEM((768, 768), F32), pltpu.VMEM((768, 768), F32), pltpu.VMEM((768, 768), F32),
            ],
        ),
        out_shape=[sd((mb, seq_len if scattered else NS, 768), BF), sd((mb, 256, 768), F32), sd((768, 768), BF), sd((768, 768), BF),
                   sd((768, 768), BF), sd((16, 768), F32)],
        compiler_params=pltpu.CompilerParams(vmem_limit_bytes=60 * 2**20),
    )(idx, xs, dk, dv, dq, done, wall, gb)


def last_kernel(*refs):
    table, arrays = refs[0], refs[1:8]
    outs, vectors = refs[8:15], refs[15:]
    for src, dst in zip(arrays, outs):
        dst[...] = src[...]
    owner = lax.axis_index("seq") * 4 + lax.axis_index("batch")
    n, m = vectors[0].shape[1], vectors[8].shape[1]
    small = pltpu.roll(table[0:8, :], (768 - owner * n) % 768, axis=1)
    for i in range(8):
        vectors[i][...] = small[i:i + 1, 0:n]
    ups = jnp.broadcast_to(table[pl.ds(8 + owner // 8, 1), :], (8, 768))
    vectors[8][...] = pltpu.roll(ups, (768 - (owner % 8) * m) % 768, axis=1)[0:1, 0:m]


def last(table, arrays, n, m):
    sd = jax.ShapeDtypeStruct
    vm = pl.BlockSpec(memory_space=pltpu.VMEM)
    return pl.pallas_call(
        last_kernel,
        in_specs=[vm] * 8,
        out_specs=[vm] * 16,
        out_shape=[sd(a.shape, a.dtype) for a in arrays] + [sd((1, n), F32)] * 8 + [sd((1, m), F32)],
        compiler_params=pltpu.CompilerParams(vmem_limit_bytes=60 * 2**20),
    )(table, *arrays)

def cat_rows(ref, h):
    return jnp.concatenate([ref[0, pl.ds(a, n), :] for a, n in key_rows(h)], axis=0)


def fwd_kernel(q_ref,k_ref,v_ref,me_ref,o_ref,l_ref):
    p=pl.program_id(1)
    ind=block_columns().astype(BF)
    for h in range(2):
        me=me_ref[0,h]
        qe=jnp.concatenate([split_heads(q_ref[0,pl.ds(h*HALF,HALF),:]),ind],axis=1)
        ke=jnp.concatenate([cat_rows(k_ref, h),me],axis=1)
        s=dot_nt(qe,ke)
        top=jnp.max(s,axis=1,keepdims=True)
        e=jnp.exp(s-top).astype(BF)
        ve=jnp.concatenate([cat_rows(v_ref,h),me],axis=1)
        o=dot(e,ve)
        tot=o[:,130:131]
        o_ref[0,pl.ds(h*HALF,HALF),:]=merge_heads(o[:,:128]/tot).astype(BF)
        l_ref[0,0,pl.ds(h*256,256),:]=jnp.broadcast_to(top+jnp.log(tot),(256,128))
def attn_fwd(q,k,v,me):
    mb=q.shape[0]; npair=q.shape[2]//128
    return pl.pallas_call(fwd_kernel,grid=(mb,npair),
      in_specs=[pl.BlockSpec((1,256,128),lambda m,p:(m,0,p)),pl.BlockSpec((1,NS,128),lambda m,p:(m,0,p)),pl.BlockSpec((1,NS,128),lambda m,p:(m,0,p)),
        pl.BlockSpec((1,2,NK,128),lambda m,p:(m,0,0,0))],
      out_specs=[pl.BlockSpec((1,256,128),lambda m,p:(m,0,p)),pl.BlockSpec((1,1,512,128),lambda m,p:(m,p,0,0))],
      out_shape=[jax.ShapeDtypeStruct(q.shape,BF),jax.ShapeDtypeStruct((mb,npair,512,128),F32)],
      compiler_params=pltpu.CompilerParams(vmem_limit_bytes=56*2**20))(q,k,v,me)
def bwd_kernel(CH,q_ref,k_ref,v_ref,me_ref,o_ref,do_ref,l_ref,dq_ref,dk_ref,dv_ref,dka,dva):
    ind=block_columns()
    zero=jnp.zeros_like(ind)
    dka[...]=jnp.zeros_like(dka); dva[...]=jnp.zeros_like(dva)
    for h in range(2):
        rows=pl.ds(h*HALF,HALF)
        qs=split_heads(q_ref[0,rows,:])
        do2=do_ref[0,rows,:]
        dos=split_heads(do2)
        o2=o_ref[0,rows,:].astype(F32)
        delta=jnp.sum(dos.astype(F32)*jnp.concatenate([o2,o2],axis=0),axis=1,keepdims=True)
        lse=l_ref[0,0,pl.ds(h*256,256),0:1]
        qe=jnp.concatenate([qs,with_column(ind,-lse)],axis=1)
        doe=jnp.concatenate([dos,with_column(zero,-delta)],axis=1)
        dqt=jnp.zeros((128,256),F32)
        off=0
        for a,n in key_rows(h):
            c0=0
            while c0<n:
                c=min(CH,n-c0)
                kr=pl.ds(a+c0,c)
                k2=k_ref[0,kr,:]; v2=v_ref[0,kr,:]; me=me_ref[0,h,pl.ds(off+c0,c),:]
                st=dot_nt(jnp.concatenate([k2,me],axis=1),qe)
                pt=jnp.exp(st)
                dpt=dot_nt(jnp.concatenate([v2,me],axis=1),doe)
                ds=(pt*dpt).astype(BF)
                dva[kr,:]+=dot(pt.astype(BF),dos)
                dka[kr,:]+=dot(ds,qs)
                dqt=dqt+dot(k2.T,ds)
                c0+=c
            off+=n
        dq_ref[0,rows,:]=(merge_heads(dqt.T)*0.125).astype(BF)
    dk_ref[0]=dka[...].astype(BF); dv_ref[0]=dva[...].astype(BF)
def attn_bwd(q,k,v,me,o,do,l,CH=384):
    mb=q.shape[0]; npair=q.shape[2]//128
    qs=pl.BlockSpec((1,256,128),lambda m,p:(m,0,p)); ks=pl.BlockSpec((1,NS,128),lambda m,p:(m,0,p))
    return pl.pallas_call(functools.partial(bwd_kernel,CH),grid=(mb,npair),
      in_specs=[qs,ks,ks,pl.BlockSpec((1,2,NK,128),lambda m,p:(m,0,0,0)),qs,qs,pl.BlockSpec((1,1,512,128),lambda m,p:(m,p,0,0))],
      out_specs=[qs,ks,ks],
      out_shape=[jax.ShapeDtypeStruct(q.shape,BF),jax.ShapeDtypeStruct(k.shape,BF),jax.ShapeDtypeStruct(k.shape,BF)],
      scratch_shapes=[pltpu.VMEM((NS,128),F32)]*2,
      compiler_params=pltpu.CompilerParams(vmem_limit_bytes=56*2**20))(q,k,v,me,o,do,l)


BLK = 64
WIN = 8
RAND = 3
ALL = ("seq", "batch")


def vector_table(vectors, b_up, owner, width):
    lane = jnp.arange(width, dtype=jnp.int32)
    n, m = vectors[0].shape[0], b_up.shape[0]
    table = jnp.where(lane // n == owner, jnp.tile(jnp.stack(vectors).astype(F32), (1, width // n)), 0.0)
    flat = jnp.arange(4 * width, dtype=jnp.int32)
    ups = jnp.where(flat // m == owner, jnp.tile(b_up.astype(F32), 4 * width // m), 0.0).reshape(4, width)
    return jnp.concatenate([table, ups, jnp.zeros((4, width), F32)], axis=0)


def block_plan(lengths, randoms, device, blocks):
    ends = jnp.cumsum(lengths, axis=1)
    starts = ends - lengths

    def doc_of(block):
        at = block * BLK
        shape = (lengths.shape[0],) + (1,) * (block.ndim - 1) + (lengths.shape[1],)
        doc = jnp.sum((ends.reshape(shape) <= at[..., None]).astype(jnp.int32), axis=-1)
        doc = jnp.minimum(doc, lengths.shape[1] - 1)
        hit = jnp.arange(lengths.shape[1], dtype=jnp.int32) == doc[..., None]
        return doc, jnp.sum(jnp.where(hit, starts.reshape(shape), 0), axis=-1)

    mb = lengths.shape[0]
    half = jnp.arange(2, dtype=jnp.int32)
    query = device * 4 + 2 * half[:, None] + half[None, :]
    query = jnp.broadcast_to(query[None], (mb, 2, 2))
    q_doc, q_first = doc_of(query)
    window = device * 4 + 2 * half[:, None] - WIN + jnp.arange(2 * WIN + 2, dtype=jnp.int32)[None, :]
    window = jnp.broadcast_to(window[None], (mb, 2, 2 * WIN + 2))
    w_doc, w_first = doc_of(jnp.clip(window, 0, blocks - 1))
    w_good = (window >= 0) & (window < blocks) & (window * BLK - w_first >= 2 * BLK)
    see_window = (
        w_good[:, :, None, :]
        & (w_doc[:, :, None, :] == q_doc[..., None])
        & (jnp.abs(window[:, :, None, :] - query[..., None]) <= WIN)
    )
    see_glob = jnp.ones((mb, 2, 2, 2), bool)
    named = lax.dynamic_slice_in_dim(randoms, device * 4, 4, 1).reshape(mb, 2, 2, RAND)
    r_doc, r_first = doc_of(named)
    r_good = (
        (r_doc == q_doc[..., None])
        & (jnp.abs(named - query[..., None]) > WIN)
        & (named * BLK - r_first >= 2 * BLK)
    )
    see_random = (r_good[:, :, None] & jnp.eye(2, dtype=bool)[None, None, :, :, None]).reshape(mb, 2, 2, 2 * RAND)
    see = jnp.concatenate([see_window, see_glob, see_random], axis=3)
    chunk = jnp.clip(device + jnp.arange(-2, 3, dtype=jnp.int32), 0, blocks // 4 - 1) * (4 * BLK)
    where = jnp.concatenate(
        [jnp.broadcast_to(chunk[None], (mb, 5)), q_first[:, :, 0], named.reshape(mb, -1) * BLK], axis=1
    )
    return where, jnp.where(see, 0.0, -1e30)


def mask_columns(see):
    bias = jnp.broadcast_to(see[..., None], see.shape + (BLK,)).reshape(see.shape[:3] + (-1, 1))
    lane = jnp.arange(128, dtype=jnp.int32)
    ones = jnp.where((lane >= 2) & (lane < 5), 1.0, 0.0)
    return jnp.where(lane == 0, bias[:, :, 0], jnp.where(lane == 1, bias[:, :, 1], ones)).astype(BF)


def on_device(inputs, cotangent, doc_lengths, random_blocks, wq, wk, wv, wo, wu, wd, b_query, b_value, b_out,
              b_up, b_down, gain_attn, bias_attn, gain_ffn, bias_ffn):
    mb, _, rows, width = inputs.shape
    devices, owners = lax.axis_size("seq"), lax.axis_size("seq") * lax.axis_size("batch")
    device = lax.axis_index("seq")
    owner = device * lax.axis_size("batch") + lax.axis_index("batch")
    linked = devices == 8 and owners == 32
    seq_len = devices * rows
    x, cot = inputs[:, 0], cotangent[:, 0]
    lengths, randoms = doc_lengths[:, 0], random_blocks[:, 0]
    vectors = (b_query, b_value, b_out, b_down, gain_attn, bias_attn, gain_ffn, bias_ffn)
    flat = lambda t: t.reshape(-1, t.shape[-1])
    if linked:
        att, lse, q, xs, k, v, wall, top, bias, extra, targets = forward_all(
            doc_lengths, random_blocks, x, (wq, wk, wv, wo, wu, wd), jnp.stack(vectors), b_up[None])
    else:
        where, see = block_plan(lengths, randoms, device, seq_len // BLK)
        extra, table = mask_columns(see), vector_table(vectors, b_up, owner, width)
        xall = lax.all_gather(x, "seq", axis=1, tiled=True)
        bias = lax.psum(table, ALL)
        full = [lax.all_gather(w, ALL, axis=0, tiled=True) for w in (wq, wk, wv, wo, wu, wd)]
        fold = lambda w: w.reshape(16, -1, width)
        up = full[4].reshape(16, 48, 4, width).transpose(0, 2, 1, 3).reshape(16, 192, width)
        wall = jnp.concatenate([fold(full[3]), up, fold(full[5])], axis=1)
        top = jnp.concatenate([jnp.zeros((16, 16, width), BF)] + [fold(w) for w in full[:3]], axis=1)
        xs, k, v, q = project(where, xall, top, bias)
        att, lse = attn_fwd(q, k, v, extra)
    stats = flat(lse) if linked else jnp.zeros((mb * rows, 128), F32)
    out, stats, datt, done, go, gu, gd, gb = middle(flat(att), flat(x), flat(cot), wall, bias, stats)
    datt, done = datt.reshape(att.shape), done.reshape(mb, rows, width)
    if linked:
        *grads, gb, dx = backward_all(datt, stats.reshape(mb, rows, 128), targets, gb, extra, q, done, k, v, xs, top, go, gu, gd)
    else:
        dq, dk, dv = attn_bwd(q, k, v, extra, att, datt, lse, 640)
        dxs, own, gq, gk, gv, gb = back(where, xs, dk, dv, dq, done, top, gb, 0)
        start = (where[:, :5, None] + jnp.arange(0, 256, BLK)).reshape(mb, -1)
        glob = (where[:, 5:7, None] + jnp.arange(0, 128, BLK)).reshape(mb, -1)
        to = jnp.concatenate([start, glob, where[:, 7:]], axis=1) // BLK
        parts = dxs.reshape(mb, -1, BLK, width)
        total = jnp.zeros((mb, seq_len // BLK, BLK, width), F32)
        total = jax.vmap(lambda t, i, p: t.at[i].add(p))(total, to, parts.astype(F32))
        dx = own + lax.psum_scatter(total.reshape(mb, seq_len, width), "seq", scatter_dimension=1, tiled=True)
        grads = [lax.psum_scatter(g.astype(F32), ALL, scatter_dimension=0, tiled=True) for g in (gq, gk, gv, go, gu, gd)]
        gb = lax.psum(gb, ALL)
    n, m = b_query.shape[0], b_up.shape[0]
    if linked:
        done_all = last(gb, (*grads, dx), n, m)
        grads, dx = done_all[:6], done_all[6]
        small, ups = [g.reshape(n) for g in done_all[7:15]], done_all[15].reshape(m)
    else:
        small = lax.dynamic_slice_in_dim(gb[:8], owner * n, n, 1)
        ups = lax.dynamic_slice_in_dim(gb[8:12].reshape(-1), owner * m, m, 0)
    return (
        out.reshape(inputs.shape), dx[:, None], *grads,
        small[0], small[1], small[2], ups, small[3], small[4], small[5], small[6], small[7],
    )


def solution(mesh):
    tokens = P(None, "batch", "seq", None)
    mat, vec = P(ALL, None), P(ALL)
    in_specs = (tokens, tokens, P(None, "batch", None), P(None, "batch", None, None)) + (mat,) * 6 + (vec,) * 9
    out_specs = (tokens, tokens) + (mat,) * 6 + (vec,) * 9
    return jax.shard_map(on_device, mesh=mesh, in_specs=in_specs, out_specs=out_specs, check_vma=False)
```

```python
import functools

import jax
import jax.numpy as jnp
from jax import lax
from jax.experimental import pallas as pl
from jax.experimental.pallas import tpu as pltpu
from jax.sharding import PartitionSpec as P

F32 = jnp.float32
BF = jnp.bfloat16


HALF, WK, NW, NK, NS = 128, 1152, 1280, 1664, 2304
TOP, REST = 160, 432
MESH = pl.DeviceIdType.MESH
UP, DOWN, XX, YY, CC = range(5)
WAYS = (UP, DOWN, XX, YY, CC)


def dot(a, b):
    return lax.dot_general(a, b, (((1,), (0,)), ((), ())), preferred_element_type=F32)


def dot_nt(a, b):
    return lax.dot_general(a, b, (((1,), (1,)), ((), ())), preferred_element_type=F32)


def dot_tn(a, b):
    return lax.dot_general(a, b, (((0,), (0,)), ((), ())), preferred_element_type=F32)


def place():
    s, b = lax.axis_index("seq"), lax.axis_index("batch")
    return s // 2, s % 2, b // 2, b % 2


def device(z, x, y, c):
    return (2 * z + x, 2 * y + c)


def greet(z, x, y, c):
    barrier = pltpu.get_barrier_semaphore()

    def tell(to):
        pl.semaphore_signal(barrier, inc=1, device_id=to, device_id_type=MESH)

    tell(device(z, 1 - x, y, c))
    tell(device(z, x, 1 - y, c))
    tell(device(z, x, y, 1 - c))
    pl.when(z > 0)(lambda: tell(device(z - 1, x, y, c)))
    pl.when(z < 3)(lambda: tell(device(z + 1, x, y, c)))
    pl.semaphore_wait(barrier, 3 + (z > 0).astype(jnp.int32) + (z < 3).astype(jnp.int32))


def lanes(c):
    return pl.ds(pl.multiple_of(c * 384, 128), 384)


def rows_at(i, n):
    return pl.ds(pl.multiple_of(i * n, n), n)


def remote(src, dst, send, recv, to):
    return pltpu.make_async_remote_copy(
        src_ref=src, dst_ref=dst, send_sem=send, recv_sem=recv, device_id=to, device_id_type=MESH
    )


def key_rows(h):
    return ((HALF * h, WK), (NW + HALF * h, HALF), (NW + 2 * HALF + 384 * h, 384))


def split_heads(v):
    lane = lax.broadcasted_iota(jnp.int32, v.shape, 1)
    z = jnp.zeros_like(v)
    return jnp.concatenate([jnp.where(lane < 64, v, z), jnp.where(lane >= 64, v, z)], axis=0)


def merge_heads(v):
    n = v.shape[0] // 2
    lane = lax.broadcasted_iota(jnp.int32, (n, v.shape[1]), 1)
    return jnp.where(lane < 64, v[:n], v[n:])


def block_columns():
    r = lax.broadcasted_iota(jnp.int32, (2 * HALF, 128), 0)
    lane = lax.broadcasted_iota(jnp.int32, (2 * HALF, 128), 1)
    first = (r % HALF) < 64
    return jnp.where(((lane == 0) & first) | ((lane == 1) & jnp.logical_not(first)), 1.0, 0.0)


def with_column(base, col):
    lane = lax.broadcasted_iota(jnp.int32, base.shape, 1)
    hi = col.astype(BF).astype(F32)
    rest = col - hi
    mid = rest.astype(BF).astype(F32)
    return jnp.where(lane == 2, hi, jnp.where(lane == 3, mid, jnp.where(lane == 4, rest - mid, base))).astype(BF)


def doc_of(lengths, m, block):
    at = block * 64
    doc, first, end = jnp.int32(0), jnp.int32(0), jnp.int32(0)
    for i in range(3):
        end = end + lengths[0, m, i]
        doc = doc + (end <= at).astype(jnp.int32)
        first = jnp.where(end <= at, end, first)
    return doc, first


def write_extra(lengths, randoms, s, extra):
    lane = lax.broadcasted_iota(jnp.int32, (64, 128), 1)
    ones = jnp.where((lane >= 2) & (lane < 5), 1.0, 0.0)

    def one(i, _):
        m, h, t = i // 52, (i // 26) % 2, i % 26
        r = jnp.maximum(t - 20, 0)
        named = randoms[0, m, 4 * s + 2 * h + r // 3, r % 3]
        block = jnp.where(t < 18, 4 * s + 2 * h - 8 + t, named)
        inside = (block >= 0) & (block < 32)
        doc, first = doc_of(lengths, m, jnp.clip(block, 0, 31))
        good = inside & (block * 64 - first >= 128)
        terms = []
        for k in range(2):
            query = 4 * s + 2 * h + k
            q_doc, _ = doc_of(lengths, m, query)
            near = jnp.abs(block - query) <= 8
            window = (t < 18) & near
            named_here = (t >= 20) & (r // 3 == k) & jnp.logical_not(near)
            seen = ((t >= 18) & (t < 20)) | (good & (doc == q_doc) & (window | named_here))
            terms.append(jnp.where(seen, 0.0, -1e30))
        value = jnp.where(lane == 0, terms[0], jnp.where(lane == 1, terms[1], ones))
        extra[m, h, rows_at(t, 64), :] = value.astype(BF)
        return 0

    lax.fori_loop(0, 104, one, 0)


def rest_block(lengths, randoms, s, m, t):
    r = jnp.maximum(t - 4, 0)
    named = randoms[0, m, 4 * s + r // 3, r % 3]
    _, first = doc_of(lengths, m, 4 * s + 2 * jnp.minimum(t // 2, 1))
    return jnp.where(t < 4, first // 64 + t % 2, named)


def forward_kernel(lengths, randoms, x_ref, wq_in, wk_in, wv_in, wo_in, wu_in, wd_in, v0, v1, v2, v3, v4, v5, v6, v7, b_up,
                   att_out, lse, q_end, xs_out, k_out, v_out, wall, top_out, bias, extra_out, targets,
                   wq, wk, wv, wo, wu, wd, att, q_out, extra, raw_sem, end_sem, own, mate, merged, merged_b, xall0, xall1, xs, ks, vs, wa,
                   mate_sem, lsem, osem, asend, arecv, acrecv, bsend, brecv, bcrecv, xsend, xrecv):
    z, x, y, c = place()
    s = 2 * z + x
    to = {UP: device(z + 1, x, y, c), DOWN: device(z - 1, x, y, c), XX: device(z, 1 - x, y, c),
          YY: device(z, x, 1 - y, c), CC: device(z, x, y, 1 - c)}
    mine, theirs = lanes(c), lanes(1 - c)
    xall = (xall0, xall1)

    def guarded(way, act):
        if way == UP:
            pl.when(z < 3)(act)
        elif way == DOWN:
            pl.when(z > 0)(act)
        else:
            act()

    def x_copy(m, zz, xx, way, own_rows=False):
        i = 2 * zz + xx
        ref = xall[m].at[pl.ds(4 * i, 4)]
        return remote(x_ref.at[m] if own_rows else ref, ref, xsend.at[m, i, way], xrecv.at[m, i], to[way])

    def a_copy(zz, xx, yy, way, src=None):
        i = (2 * zz + xx) * 2 + yy
        ref = wa.at[i, :, mine]
        return remote(ref if src is None else src, ref, asend.at[i, way],
                      acrecv.at[i] if way == CC else arecv.at[i], to[way])

    def b_copy(zz, xx, yy, way, src=None):
        i = (2 * zz + xx) * 2 + yy
        ref = wall.at[i, :, mine]
        return remote(ref if src is None else src, ref, bsend.at[i, way],
                      bcrecv.at[i] if way == CC else brecv.at[i], to[way])

    raw = [pltpu.make_async_copy(src, dst, raw_sem.at[i]) for i, (src, dst) in enumerate(
        zip((wq_in, wk_in, wv_in, wo_in, wu_in, wd_in), (wq, wk, wv, wo, wu, wd)))]
    for cp in raw:
        cp.start()
    greet(z, x, y, c)
    for way in (UP, DOWN, XX):
        guarded(way, lambda way=way: x_copy(0, z, x, way, True).start())
    for m in range(2):
        pltpu.make_async_copy(x_ref.at[m], xall[m].at[pl.ds(4 * s, 4)], lsem.at[m]).start()
    owner = 4 * s + 2 * y + c
    small = jnp.concatenate([v[...].astype(F32) for v in (v0, v1, v2, v3, v4, v5, v6, v7)], axis=0)
    n = small.shape[1]
    own[0:8, :] = pltpu.roll(jnp.concatenate([small, jnp.zeros((8, 768 - n), F32)], axis=1), owner * n, axis=1)
    ups = b_up[...].astype(F32)
    n = ups.shape[1]
    ups = jnp.concatenate([ups, jnp.zeros((1, 768 - n), F32)], axis=1)
    ups = pltpu.roll(jnp.broadcast_to(ups, (8, 768)), (owner % 8) * n, axis=1)
    row = lax.broadcasted_iota(jnp.int32, (8, 768), 0)
    own[8:16, :] = jnp.where(row == owner // 8, ups, 0.0)
    for cp in raw:
        cp.wait()
    for i, ref in enumerate((wq, wk, wv, wo)):
        own[16 + 24 * i:40 + 24 * i, :] = ref[...].astype(F32)
    for j in range(4):
        own[112 + 24 * j:136 + 24 * j, :] = wu[:, 768 * j:768 * j + 768].astype(F32)
    own[208:304, :] = wd[...].astype(F32)
    swap = remote(own.at[:, theirs], mate, mate_sem.at[0], mate_sem.at[1], to[CC])
    swap.start()
    swap.wait()

    def paired(start, n):
        here, there = own[start:start + n, mine], mate[start:start + n, :]
        return jnp.where(c == 0, jnp.concatenate([here, there], 0), jnp.concatenate([there, here], 0)).astype(BF)

    merged[0:16, :] = (own[0:16, mine] + mate[0:16, :]).astype(BF)
    for i in range(3):
        merged[16 + 48 * i:64 + 48 * i, :] = paired(16 + 24 * i, 24)
    keep_a = pltpu.make_async_copy(merged, wa.at[s * 2 + y, :, mine], lsem.at[2])
    keep_a.start()
    for way in WAYS:
        guarded(way, lambda way=way: a_copy(z, x, y, way, merged).start())
    for i in range(5):
        merged_b[48 * i:48 * i + 48, :] = paired(88 + 24 * i, 24)
    merged_b[240:432, :] = paired(208, 96)
    keep_b = pltpu.make_async_copy(merged_b, wall.at[s * 2 + y, :, mine], lsem.at[3])
    keep_b.start()
    write_extra(lengths, randoms, s, extra)
    extra_copy = pltpu.make_async_copy(extra, extra_out, end_sem.at[0])
    extra_copy.start()

    lane = lax.broadcasted_iota(jnp.int32, (1, 1024), 1)
    for m in range(2):
        targets[m] = lax.fori_loop(
            0, 16, lambda t, v, m=m: jnp.where(
                lane // 64 == t, rest_block(lengths, randoms, s, m, t) * 64 + lane % 64, v), jnp.zeros_like(lane))

    def x_line(m, k, a=True):
        def below():
            x_copy(m, z - k, x, UP).wait_recv()
            pl.when(z < 3)(lambda: x_copy(m, z - k, x, UP).start())
            x_copy(m, z - k, x, XX).start()

        def above():
            x_copy(m, z + k, x, DOWN).wait_recv()
            pl.when(z > 0)(lambda: x_copy(m, z + k, x, DOWN).start())
            x_copy(m, z + k, x, XX).start()

        pl.when((z >= k) & (k <= 3))(below)
        pl.when(z + k <= 3)(above)

    def w_line(copy, k):
        def below():
            copy(z - k, x, y, UP).wait_recv()
            pl.when(z < 3)(lambda: copy(z - k, x, y, UP).start())
            for way in (XX, YY, CC):
                copy(z - k, x, y, way).start()

        def above():
            copy(z + k, x, y, DOWN).wait_recv()
            pl.when(z > 0)(lambda: copy(z + k, x, y, DOWN).start())
            for way in (XX, YY, CC):
                copy(z + k, x, y, way).start()

        pl.when((z >= k) & (k <= 3))(below)
        pl.when(z + k <= 3)(above)

    def at_distance(act, k):
        pl.when((k >= 0) & (k <= z))(lambda: act(z - k))
        pl.when((k > 0) & (z + k <= 3))(lambda: act(z + k))

    def w_from_x(copy, k):
        def act(zz):
            copy(zz, 1 - x, y, XX).wait_recv()
            copy(zz, 1 - x, y, YY).start()
            copy(zz, 1 - x, y, CC).start()

        at_distance(act, k)

    def w_from_y(copy, xx, k):
        def act(zz):
            copy(zz, xx, 1 - y, YY).wait_recv()
            copy(zz, xx, 1 - y, CC).start()

        at_distance(act, k)

    zfirst = c == 0

    def b_own_column(k):
        def passed(zz, way, more):
            b_copy(zz, x, y, way).wait_recv()
            pl.when(more)(lambda: b_copy(zz, x, y, way).start())
            b_copy(zz, x, y, YY).start()
            b_copy(zz, x, y, CC).start()

        pl.when((z >= k) & (k <= 3))(lambda: passed(z - k, UP, z < 3))
        pl.when(z + k <= 3)(lambda: passed(z + k, DOWN, z > 0))

    def b_to_x(k):
        def across(zz):
            b_copy(zz, x, y, XX).start()

        pl.when(zfirst)(lambda: at_distance(across, k))

    def b_other_column(k):
        def shared(zz):
            b_copy(zz, 1 - x, y, YY).start()
            b_copy(zz, 1 - x, y, CC).start()

        def crossed(zz):
            b_copy(zz, 1 - x, y, XX).wait_recv()
            shared(zz)

        def passed(zz, way, more):
            b_copy(zz, 1 - x, y, way).wait_recv()
            pl.when(more)(lambda: b_copy(zz, 1 - x, y, way).start())
            shared(zz)

        def first():
            crossed(z)
            pl.when(jnp.logical_not(zfirst) & (z < 3))(lambda: b_copy(z, 1 - x, y, UP).start())
            pl.when(jnp.logical_not(zfirst) & (z > 0))(lambda: b_copy(z, 1 - x, y, DOWN).start())

        def later():
            pl.when(zfirst)(lambda: at_distance(crossed, k))
            pl.when(jnp.logical_not(zfirst) & (z >= k))(lambda: passed(z - k, UP, z < 3))
            pl.when(jnp.logical_not(zfirst) & (z + k <= 3))(lambda: passed(z + k, DOWN, z > 0))

        pl.when(k == 0)(first)
        pl.when((k > 0) & (k <= 3))(later)

    begin = {
        "x0": lambda k: x_line(0, k),
        "x1": lambda k: x_line(1, k),
        "a": lambda k: w_line(a_copy, k),
        "ax": lambda k: w_from_x(a_copy, k),
        "ay0": lambda k: w_from_y(a_copy, x, k),
        "ay1": lambda k: w_from_y(a_copy, 1 - x, k),
        "own x1": lambda ways: [guarded(way, lambda way=way: x_copy(1, z, x, way, True).start()) for way in ways],
        "own b": lambda ways: [guarded(way, lambda way=way: b_copy(z, x, y, way, merged_b).start()) for way in ways],
    }
    for name, what in START:
        begin[name](what)
    keep_a.wait()

    def arrived(i, _):
        ref = wa.at[i, :, theirs]
        remote(ref, ref, asend.at[i, CC], acrecv.at[i], to[CC]).wait_recv()
        return 0

    lax.fori_loop(0, 16, arrived, 0)
    bias[...] = jnp.sum(wa[:, 0:16, :].astype(F32), axis=0)
    top_copy = pltpu.make_async_copy(wa, top_out, lsem.at[4])
    top_copy.start()
    lane = lax.broadcasted_iota(jnp.int32, (HALF, 128), 1)
    ind = block_columns().astype(BF)
    lse[...] = jnp.zeros_like(lse)

    def out_copy(m, t):
        src, dst = ((xs, xs_out), (ks, k_out), (vs, v_out))[t]
        return pltpu.make_async_copy(src.at[m], dst.at[m], osem.at[m, t])

    def x_here(m, k):
        def arrived_x(zz):
            x_copy(m, zz, 1 - x, XX).wait_recv()

        at_distance(arrived_x, k)

    def q_copy(m):
        return pltpu.make_async_copy(q_out.at[m], q_end.at[m], end_sem.at[1 + m])

    def att_copy(m):
        return pltpu.make_async_copy(att.at[m], att_out.at[m], end_sem.at[3 + m])

    def gather_near(m):
        x_here(m, 0)
        x_here(m, 1)
        pltpu.make_async_copy(x_ref.at[m], xall[m].at[pl.ds(4 * s, 4)], lsem.at[m]).wait()
        for t in range(5):
            chunk = xall[m][pl.ds(4 * jnp.clip(s - 2 + t, 0, 7), 4)]
            xs[m, 256 * t:256 * t + 256, :] = chunk.reshape(256, chunk.shape[-1])
        q = (dot(xs[m, 512:768, :], wa[:, 16:64, :].reshape(768, 768)) + bias[0:1, :]).astype(BF)
        q_out[m] = q * jnp.asarray(0.125, BF)
        q_copy(m).start()

    def gather_rest(m):
        x_here(m, 2)
        x_here(m, 3)

        def named(t, _):
            xs[m, pl.ds(pl.multiple_of(NW + 64 * t, 64), 64), :] = xall[m][rest_block(lengths, randoms, s, m, t)]
            return 0

        lax.fori_loop(0, 16, named, 0)
        out_copy(m, 0).start()

    def project(m, r):
        rows = xs[m, r, :]
        ks[m, r, :] = dot(rows, wa[:, 64:112, :].reshape(768, 768)).astype(BF)
        vs[m, r, :] = (dot(rows, wa[:, 112:160, :].reshape(768, 768)) + bias[1:2, :]).astype(BF)

    def pair(m, p):
        col = pl.ds(pl.multiple_of(p * 128, 128), 128)
        for h in range(2):
            r = pl.ds(h * HALF, HALF)
            more = extra[m, h]
            keys = jnp.concatenate([ks[m, a:a + n, col] for a, n in key_rows(h)], axis=0)
            vals = jnp.concatenate([vs[m, a:a + n, col] for a, n in key_rows(h)], axis=0)
            scores = dot_nt(jnp.concatenate([split_heads(q_out[m, r, col]), ind], axis=1),
                            jnp.concatenate([keys, more], axis=1))
            top = jnp.max(scores, axis=1, keepdims=True)
            e = jnp.exp(scores - top).astype(BF)
            o = dot(e, jnp.concatenate([vals, more], axis=1))
            total = o[:, 130:131]
            att[m, r, col] = merge_heads(o[:, :128] / total).astype(BF)
            norm = top + jnp.log(total)
            lse[m, r, :] = jnp.where(lane == 2 * p, norm[:HALF], jnp.where(lane == 2 * p + 1, norm[HALF:], lse[m, r, :]))

    def picked(g, plan):
        k = jnp.full((), 9, jnp.int32)
        for at, value in plan:
            k = jnp.where(g == at, value, k)
        return k

    def pump(g):
        for name in PUMP_ORDER:
            k = picked(g, PUMPS[name])
            act = {
                "x1": lambda k: x_line(1, k), "bo": b_own_column, "bt": b_other_column, "bc": b_to_x,
                "by0": lambda k: w_from_y(b_copy, x, k), "by1": lambda k: w_from_y(b_copy, 1 - x, k),
            }[name]
            act(k)

    def step(g, _):
        m, i = g // 9, g % 9
        for mm in range(2):
            pl.when(g == 9 * mm)(lambda mm=mm: gather_near(mm))
            pl.when(g == 9 * mm + 2)(lambda mm=mm: gather_rest(mm))
        pl.when(i < 2)(lambda: project(m, rows_at(jnp.minimum(i, 1), 640)))
        pl.when(i == 2)(lambda: project(m, pl.ds(NW, NS - NW)))

        @pl.when(i == 3)
        def _():
            out_copy(m, 1).start()
            out_copy(m, 2).start()

        pl.when(i >= 3)(lambda: pair(m, i - 3))
        pl.when(i == 8)(lambda: att_copy(m).start())
        pump(g)
        return 0

    lax.fori_loop(0, 18, step, 0)

    lax.fori_loop(18, 24, lambda g, _: (pump(g), 0)[1], 0)

    def b_arrived(i, _):
        ref = wall.at[i, :, theirs]
        remote(ref, ref, bsend.at[i, CC], bcrecv.at[i], to[CC]).wait_recv()
        return 0

    lax.fori_loop(0, 16, b_arrived, 0)
    keep_b.wait()
    top_copy.wait()
    extra_copy.wait()
    for m in range(2):
        q_copy(m).wait()
        att_copy(m).wait()
        for t in range(3):
            out_copy(m, t).wait()

    def sent(k, _):
        for m in range(2):
            x_copy(m, k, x, XX).wait_send()
        for copy in (a_copy, b_copy):
            for way in (YY, CC):
                copy(k, x, y, way).wait_send()
                copy(k, 1 - x, y, way).wait_send()
            copy(k, x, 1 - y, CC).wait_send()
            copy(k, 1 - x, 1 - y, CC).wait_send()
        a_copy(k, x, y, XX).wait_send()
        pl.when(zfirst | (k == z))(lambda: b_copy(k, x, y, XX).wait_send())

        def line(way):
            x_copy(0, k, x, way).wait_send()
            x_copy(1, k, x, way).wait_send()
            a_copy(k, x, y, way).wait_send()
            b_copy(k, x, y, way).wait_send()
            pl.when(jnp.logical_not(zfirst))(lambda: b_copy(k, 1 - x, y, way).wait_send())

        pl.when((k <= z) & (z < 3))(lambda: line(UP))
        pl.when((k >= z) & (z > 0))(lambda: line(DOWN))
        return 0

    lax.fori_loop(0, 4, sent, 0)


START = (
    ("x0", 1),
    ("a", 1),
    ("ay0", 0),
    ("ax", 0),
    ("a", 2),
    ("a", 3),
    ("x0", 2),
    ("own x1", (UP, DOWN,)),
    ("ax", 2),
    ("ax", 1),
    ("x0", 3),
    ("ay0", 1),
    ("ay0", 3),
    ("ay1", 2),
    ("own b", (UP, DOWN,)),
    ("ax", 3),
    ("ay1", 3),
    ("ay0", 2),
    ("ay1", 0),
    ("own b", (XX,)),
    ("own x1", (XX,)),
    ("ay1", 1),
    ("own b", (YY, CC,)),
    ("x1", 1),
)
PUMP_ORDER = ("x1", "bo", "bc", "bt", "by0", "by1")
PUMPS = {
    "x1": ((2, 2), (9, 3),),
    "bo": ((0, 1), (5, 2), (10, 3),),
    "bt": ((2, 0), (9, 1), (11, 2), (14, 3),),
    "bc": ((0, 1), (9, 2), (11, 3),),
    "by0": ((2, 0), (5, 1), (11, 2), (15, 3),),
    "by1": ((9, 0), (13, 1), (14, 2), (16, 3),),
}


def forward_all(lengths, randoms, x, weights, vectors, b_up):
    dma = pltpu.SemaphoreType.DMA
    sd = jax.ShapeDtypeStruct
    vm, anywhere, sm = (pl.BlockSpec(memory_space=m) for m in (pltpu.VMEM, pl.ANY, pltpu.SMEM))
    mb, rows, width = x.shape
    v = pltpu.VMEM
    return pl.pallas_call(
        forward_kernel,
        out_shape=[
            sd((mb, rows, width), BF), sd((mb, rows, 128), F32), sd((mb, rows, width), BF),
            sd((mb, NS, width), BF), sd((mb, NS, width), BF), sd((mb, NS, width), BF),
            sd((16, REST, width), BF), sd((16, TOP, width), BF), sd((16, width), F32),
            sd((mb, 2, NK, 128), BF), sd((mb, 1, 1024), jnp.int32),
        ],
        in_specs=[sm, sm] + [anywhere] * 7 + [vm] * 9,
        out_specs=[anywhere, vm] + [anywhere] * 6 + [vm, anywhere, vm],
        scratch_shapes=[
            *[v(w.shape, BF) for w in weights], v((mb, rows, width), BF), v((mb, rows, width), BF),
            v((mb, 2, NK, 128), BF), dma((6,)), dma((5,)),
            v((304, width), F32), v((304, 384), F32), v((TOP, 384), BF), v((REST, 384), BF),
            v((8 * rows // 64, 64, width), BF), v((8 * rows // 64, 64, width), BF),
            v((mb, NS, width), BF), v((mb, NS, width), BF), v((mb, NS, width), BF),
            v((16, TOP, width), BF),
            dma((2,)), dma((5,)), dma((mb, 3)),
            dma((16, 5)), dma((16,)), dma((16,)), dma((16, 5)), dma((16,)), dma((16,)),
            dma((mb, 8, 3)), dma((mb, 8)),
        ],
        compiler_params=pltpu.CompilerParams(
            collective_id=0, has_side_effects=True, vmem_limit_bytes=60 * 2**20
        ),
    )(lengths, randoms, x.reshape(mb, rows // 64, 64, width), *weights, *vectors, b_up)


def backward_kernel(datt, stats, tgt, gb_in, extra_in, q_in, done, k_in, v_in, xs_in, top_in, go, gu, gd,
                    oq, ok, ov, oo, ou, od, ob, odx,
                    kb, vb, xsb, wa, extra, dka, dva, q, ga, gb,
                    acc, mate, yr, mate2, yr2, xr, zr, dxp, dxr, dzr, fin, rcv,
                    ksem, lsem, msem, msem2, asem, ysem, xsem, zsem, ysem2, xsem2, zsem2, dxsem, dzsem, fsem, ready):
    z, x, y, c = place()
    s = 2 * z + x
    mine, theirs = lanes(c), lanes(1 - c)
    near_x, near_y, near_c = device(z, 1 - x, y, c), device(z, x, 1 - y, c), device(z, x, y, 1 - c)
    above, below = device(z + 1, x, y, c), device(z - 1, x, y, c)

    def far(i):
        inner = jnp.where(i == 0, 3, jnp.where(i == 1, 0, jnp.where(i == 2, 2, 1)))
        low = jnp.where(z == 0, 3 - i, jnp.where(z == 1, inner, i))
        return jnp.where(z == 2, 3 - inner, low)

    def slot_of(i, zz):
        zt = jnp.where(zz == 0, 3 - i, jnp.where((zz == 1) & (i == 2), 2, 3))
        return zt, (zz == 0) | ((zz == 1) & (i >= 1)) | ((zz == 2) & (i == 2))

    def at_slot(act, i):
        up, sends_up = slot_of(i, z)
        down, sends_down = slot_of(i, 3 - z)
        pl.when(sends_up)(lambda: act(up, True))
        pl.when(sends_down)(lambda: act(3 - down, False))

    def column(p):
        return pl.ds(pl.multiple_of(p * 128, 128), 128)

    def load_keys(m, p):
        return (pltpu.make_async_copy(k_in.at[m, :, column(p)], kb.at[:, column(p)], ksem.at[0, p]),
                pltpu.make_async_copy(v_in.at[m, :, column(p)], vb.at[:, column(p)], ksem.at[1, p]))

    def start_keys(m):
        def one(p, _):
            for cp in load_keys(m, p):
                cp.start()
            return 0

        lax.fori_loop(0, 6, one, 0)

    start_keys(0)
    extra_copy = pltpu.make_async_copy(extra_in, extra, lsem.at[4])
    extra_copy.start()
    q_copy = pltpu.make_async_copy(q_in, q, lsem.at[3])
    q_copy.start()
    top_copy = pltpu.make_async_copy(top_in.at[:, :, pl.ds(16, 144), :], wa, lsem.at[0])
    top_copy.start()
    done_copy = pltpu.make_async_copy(done, odx, lsem.at[1])
    done_copy.start()
    greet(z, x, y, c)

    def parts(yy, cc):
        off = pl.multiple_of(cc * 384, 128)
        yield 0, go.at[:, yy, :, pl.ds(off, 384)], pl.ds(0, 48)
        yield 1, gd.at[:, yy, :, pl.ds(off, 384)], pl.ds(240, 192)
        for j in range(4):
            col = pl.multiple_of(j * 768 + cc * 384, 128)
            yield 2 + j, gu.at[:, yy, :, pl.ds(col, 384)], pl.ds(48 + 48 * j, 48)

    swaps, loads = {}, {}
    for t, yy in enumerate((1 - y, y)):
        for i, src, rows in parts(yy, 1 - c):
            swaps[t, i] = remote(src, mate.at[:, yy, rows, :], msem.at[0, t, i], msem.at[1, t, i], near_c)
            swaps[t, i].start()
        for i, src, rows in parts(yy, c):
            loads[t, i] = pltpu.make_async_copy(src, acc.at[:, yy, rows, :], asem.at[t, i])
            loads[t, i].start()
    gb[...] = gb_in[...]

    class Reduce:
        def __init__(self, rows, held, cols, other, from_y, ys, xs_, zs):
            self.rows, self.held, self.cols, self.other, self.from_y = rows, held, cols, other, from_y
            self.ys, self.xs, self.zs = ys, xs_, zs

        def a(self, s_, yy):
            return self.held.at[s_, yy, :, self.cols]

        def y_copy(self, s_):
            return remote(self.a(s_, 1 - y), self.from_y.at[s_], self.ys.at[0, s_], self.ys.at[1, s_], near_y)

        def x_copy(self, zz):
            return remote(self.a(2 * zz + 1 - x, y), xr.at[zz, pl.ds(0, self.rows), :], self.xs.at[0, zz],
                          self.xs.at[1, zz], near_x)

        def z_copy(self, zz, slot, to):
            return remote(self.a(2 * zz + x, y), zr.at[slot, pl.ds(0, self.rows), :], self.zs.at[0, zz],
                          self.zs.at[1, slot], to)

        def total(self, s_, yy, others):
            value = self.held[s_, yy, :, self.cols].astype(F32) + self.other[s_, yy].astype(F32)
            for ref, index in others:
                value = value + ref[index, 0:self.rows, :].astype(F32)
            return value

        def keep(self, s_, yy, value):
            self.held[s_, yy, :, self.cols] = value.astype(BF)

        def y_step(self, i):
            s_ = 2 * far(i % 4) + jnp.where(i < 4, 1 - x, x)
            self.keep(s_, 1 - y, self.total(s_, 1 - y, []))
            self.y_copy(s_).start()

        def x_step(self, i):
            zz = far(i)
            s_ = 2 * zz + 1 - x
            self.y_copy(s_).wait_recv()
            self.keep(s_, y, self.total(s_, y, [(self.from_y, s_)]))
            self.x_copy(zz).start()

        def along(self, zz, up):
            s_ = 2 * zz + x
            self.y_copy(s_).wait_recv()
            self.x_copy(zz).wait_recv()
            others = [(self.from_y, s_), (xr, zz)]
            more = z > 0 if up else z < 3

            @pl.when(more)
            def _():
                self.z_copy(zz, zz, above).wait_recv()
                self.keep(s_, y, self.total(s_, y, others + [(zr, zz)]))

            @pl.when(jnp.logical_not(more))
            def _():
                self.keep(s_, y, self.total(s_, y, others))

            if up:
                self.z_copy(zz, zz, above).start()
            else:
                self.z_copy(zz, jnp.where(zz == z - 1, 4, zz), below).start()

        def z_step(self, i):
            at_slot(self.along, i)

        def finish(self):
            self.y_copy(s).wait_recv()
            self.x_copy(z).wait_recv()
            r = pl.ds(0, self.rows)
            fin[r, :] = self.total(s, y, [(self.from_y, s), (xr, z)])
            for slot, cond in ((z, z > 0), (4, z < 3)):
                @pl.when(cond)
                def _(slot=slot):
                    self.z_copy(z, slot, above).wait_recv()
                    fin[r, :] += zr[slot, r, :].astype(F32)

        def drain(self):
            def one(i, _):
                self.y_copy(i).wait_send()
                return 0

            lax.fori_loop(0, 8, one, 0)

            def two(i, _):
                self.x_copy(i).wait_send()
                pl.when(i != z)(lambda: self.z_copy(i, i, above).wait_send())
                return 0

            lax.fori_loop(0, 4, two, 0)

    rest = Reduce(REST, acc, pl.ds(0, 384), mate, yr, ysem, xsem, zsem)
    top = Reduce(TOP, ga, mine, mate2, yr2, ysem2, xsem2, zsem2)

    def dx_x(m, zz):
        return remote(dxp.at[m, 2 * zz + 1 - x], dxr.at[m, zz], dxsem.at[0, m, zz], dxsem.at[1, m, zz], near_x)

    def dx_z(m, zz, slot, to):
        return remote(dxp.at[m, 2 * zz + x], dzr.at[m, slot], dzsem.at[0, m, zz], dzsem.at[1, m, slot], to)

    def dx_along(m, zz, up):
        s_ = 2 * zz + x
        dx_x(m, zz).wait_recv()
        more = z > 0 if up else z < 3

        @pl.when(more)
        def _():
            dx_z(m, zz, zz, above).wait_recv()
            dxp[m, s_] = (dxp[m, s_].astype(F32) + dxr[m, zz].astype(F32) + dzr[m, zz].astype(F32)).astype(BF)

        @pl.when(jnp.logical_not(more))
        def _():
            dxp[m, s_] = (dxp[m, s_].astype(F32) + dxr[m, zz].astype(F32)).astype(BF)

        if up:
            dx_z(m, zz, zz, above).start()
        else:
            dx_z(m, zz, jnp.where(zz == z - 1, 4, zz), below).start()

    def dx_step(m, i):
        at_slot(functools.partial(dx_along, m), i)

    def dx_finish(m):
        dx_x(m, z).wait_recv()
        odx[m] += dxr[m, z].astype(F32)
        for slot, cond in ((z, z > 0), (4, z < 3)):
            @pl.when(cond)
            def _(slot=slot):
                dx_z(m, z, slot, above).wait_recv()
                odx[m] += dzr[m, slot].astype(F32)

    def dx_sent(m):
        def one(i, _):
            dx_x(m, i).wait_send()
            pl.when(i != z)(lambda: dx_z(m, i, i, above).wait_send())
            return 0

        lax.fori_loop(0, 4, one, 0)

    ind = block_columns()

    def pair(m, p):
        col = column(p)
        for cp in load_keys(m, p):
            cp.wait()
        dka[...] = jnp.zeros_like(dka)
        dva[...] = jnp.zeros_like(dva)
        for h in range(2):
            rows = pl.ds(h * HALF, HALF)
            qs = split_heads(q[m, rows, col])
            dos = split_heads(datt[m, rows, col])
            lane = lax.broadcasted_iota(jnp.int32, (HALF, 128), 1)

            def both(first, rows=rows, lane=lane):
                return jnp.concatenate(
                    [jnp.sum(jnp.where(lane == first + a, stats[m, rows, :], 0.0), axis=1, keepdims=True) for a in range(2)],
                    axis=0)

            log_norm, delta = both(2 * p), both(16 + 2 * p)
            qe = jnp.concatenate([qs, with_column(ind, -log_norm)], axis=1)
            doe = jnp.concatenate([dos, with_column(jnp.zeros_like(ind), -delta)], axis=1)
            dqt = jnp.zeros((128, 2 * HALF), F32)
            (wa_, wn), (ga, gn), (ra, rn) = key_rows(h)
            off = 0
            for pieces in (((wa_, 576),), ((wa_ + 576, 576),), ((ga, gn), (ra, rn))):
                n = sum(t for _, t in pieces)
                k2 = jnp.concatenate([kb[a:a + t, col] for a, t in pieces], axis=0)
                v2 = jnp.concatenate([vb[a:a + t, col] for a, t in pieces], axis=0)
                more = extra[m, h, off:off + n, :]
                pt = jnp.exp(dot_nt(jnp.concatenate([k2, more], axis=1), qe))
                ds = (pt * dot_nt(jnp.concatenate([v2, more], axis=1), doe)).astype(BF)
                dv_ = dot(pt.astype(BF), dos)
                dk_ = dot(ds, qs)
                dqt = dqt + dot(k2.T, ds)
                if off < WK:
                    a, t = pieces[0]
                    dka[a:a + t, :] += dk_
                    dva[a:a + t, :] += dv_
                else:
                    at = 0
                    for a, t in pieces:
                        kb[a:a + t, col] = dk_[at:at + t].astype(BF)
                        vb[a:a + t, col] = dv_[at:at + t].astype(BF)
                        at += t
                off += n
            q[m, rows, col] = (merge_heads(dqt.T) * 0.125).astype(BF)
        kb[0:NW, col] = dka[...].astype(BF)
        vb[0:NW, col] = dva[...].astype(BF)

    def weight(i):
        return wa[:, :, 48 * i:48 + 48 * i, :].reshape(768, 768)

    def dx_rows(m, i):
        for part in range(2):
            r = rows_at(2 * i + part, 384)
            value = dot_nt(kb[r, :], weight(1)) + dot_nt(vb[r, :], weight(2))
            xsb[r, :] = value.astype(BF)
            if part == 1:
                @pl.when(i == 0)
                def _(value=value):
                    odx[m] += value[128:384] + dot_nt(q[m], weight(0))

    def dx_piece(m, i):
        t = 2 * far(i % 4) + jnp.where(i < 4, 1 - x, x)
        row = lax.broadcasted_iota(jnp.int32, (256, 1024), 0) + 256 * t
        chosen = jnp.where(row == tgt[m], 1.0, 0.0).astype(BF)
        value = dot(chosen, xsb[NW:NS, :])
        w = t - s + 2

        @pl.when(t == s)
        def _():
            odx[m] += value

        @pl.when(t != s)
        def _():
            near = xsb[rows_at(jnp.clip(w, 0, 4), 256), :].astype(F32)
            dxp[m, t] = (value + jnp.where((w >= 0) & (w < 5), near, 0.0)).astype(BF)

        pl.when(i < 4)(lambda: dx_x(m, far(i % 4)).start())

    def weight_grads(m, i):
        cols = pl.ds(pl.multiple_of(384 * i, 128), 384)
        a = xsb[:, cols]
        chips = pl.ds(4 * i, 4)

        def keep(row, value, n):
            value = value.reshape(4, 2, 48, value.shape[1])

            @pl.when(m == 0)
            def _():
                ga[chips, :, row:row + 48, n] = value.astype(BF)

            @pl.when(m == 1)
            def _():
                ga[chips, :, row:row + 48, n] = (ga[chips, :, row:row + 48, n].astype(F32) + value).astype(BF)

        for half in range(2):
            n = slice(384 * half, 384 * half + 384)
            keep(64, dot_tn(a, kb[:, n]), n)
            keep(112, dot_tn(a, vb[:, n]), n)
        keep(16, dot_tn(a[512:768], q[m]), slice(0, 768))

    def small_grads():
        low = gb[...].astype(BF)

        def spread(i, _):
            ga[i // 2, i % 2, 0:16, :] = low
            return 0

        lax.fori_loop(0, 16, spread, 0)

    swap2 = [remote(ga.at[:, yy, :, theirs], mate2.at[:, yy], msem2.at[0, t], msem2.at[1, t], near_c)
             for t, yy in enumerate((1 - y, y))]

    def rest_rows(cc):
        yield oo, 0, pl.multiple_of(24 * cc, 8), 24, 0
        for j in range(4):
            yield ou, 24 + 24 * j, pl.multiple_of(48 + 48 * j + 24 * cc, 8), 24, 768 * j
        yield od, 120, pl.multiple_of(240 + 96 * cc, 8), 96, 0

    def top_rows(cc):
        yield ob, 216, 0, 16, 0
        for i, ref in enumerate((oq, ok, ov)):
            yield ref, 232 + 24 * i, pl.multiple_of(16 + 48 * i + 24 * cc, 8), 24, 0

    def to_mate(rows_of, first):
        return [remote(fin.at[pl.ds(start, n), :], rcv.at[at:at + n, :], fsem.at[0, first + i], fsem.at[1, first + i], near_c)
                for i, (_, at, start, n, _) in enumerate(rows_of(1 - c))]

    def hand_over(rows_of):
        for ref, at, start, n, col in rows_of(c):
            ref[:, pl.ds(pl.multiple_of(col + c * 384, 128), 384)] = fin[pl.ds(start, n), :]

    def take_over(rows_of):
        for ref, at, start, n, col in rows_of(c):
            ref[:, pl.ds(pl.multiple_of(col + (1 - c) * 384, 128), 384)] = rcv[at:at + n, :]

    last0 = to_mate(rest_rows, 0)

    def picked(g, plan):
        k = jnp.full((), 9, jnp.int32)
        for at, value in plan:
            k = jnp.where(g == at, value, k)
        return k

    def start_top(_):
        swap2[0].wait_recv()
        swap2[1].wait_recv()
        lax.fori_loop(0, 8, lambda i, _: (top.y_step(i), 0)[1], 0)

    def tell(to):
        pl.semaphore_signal(ready, inc=1, device_id=to, device_id_type=MESH)

    def end_rest(_):
        rest.finish()
        for to in (near_x, near_y, near_c):
            tell(to)
        pl.when(z > 0)(lambda: tell(below))
        pl.when(z < 3)(lambda: tell(above))
        for cp in last0:
            cp.start()
        hand_over(rest_rows)

    def all_ready(_):
        pl.semaphore_wait(ready, 3 + (z > 0).astype(jnp.int32) + (z < 3).astype(jnp.int32))

    acts = {
        "Y": rest.y_step, "X": rest.x_step, "Z": rest.z_step, "BF": end_rest, "W": all_ready,
        "D0": functools.partial(dx_step, 0), "D0F": lambda _: dx_finish(0), "D1": functools.partial(dx_step, 1),
        "TY": start_top, "TX": top.x_step, "TZ": top.z_step,
    }

    def pump(g, first, last_):
        for name in STEP_ORDER:
            plan = [(at, k) for at, k in STEPS[name] if first <= at < last_]
            if plan:
                k = picked(g, plan)
                pl.when(k < 9)(lambda name=name, k=k: acts[name](k))

    for i in range(6):
        loads[0, i].wait()
        swaps[0, i].wait_recv()
    rest.y_step(0)
    done_copy.wait()
    q_copy.wait()
    extra_copy.wait()

    def load_xs(m):
        return pltpu.make_async_copy(xs_in.at[m], xsb, lsem.at[2])

    def micro(m, _):
        load_xs(m).start()

        def one(i, _):
            @pl.when(i < 6)
            def _():
                pair(m, jnp.minimum(i, 5))

            @pl.when((m == 0) & (i == MATE_AT))
            def _():
                for t in range(6):
                    loads[1, t].wait()
                    swaps[1, t].wait_recv()
                top_copy.wait()

            pl.when(i == 6)(lambda: load_xs(m).wait())
            pl.when((i >= 6) & (i < 8))(lambda: weight_grads(m, jnp.clip(i - 6, 0, 1)))

            @pl.when(i == 8)
            def _():
                gb[0:1, :] += jnp.sum(q[m].astype(F32), axis=0, keepdims=True)

                def value_bias(t, _):
                    gb[1:2, :] += jnp.sum(vb[rows_at(t, 256), :].astype(F32), axis=0, keepdims=True)
                    return 0

                lax.fori_loop(0, 9, value_bias, 0)

            pl.when(i >= 9)(lambda: dx_rows(m, jnp.clip(i - 9, 0, 2)))
            pump(12 * m + i, 0, 24)

            @pl.when((m == 1) & (i == 8))
            def _():
                small_grads()
                for cp in swap2:
                    cp.start()

            return 0

        lax.fori_loop(0, 12, one, 0)
        pl.when(m == 0)(lambda: start_keys(1))
        lax.fori_loop(0, 8, lambda i, _: (dx_piece(m, i), 0)[1], 0)
        return 0

    lax.fori_loop(0, 2, micro, 0)
    lax.fori_loop(24, 38, lambda g, _: (pump(g, 24, 38), 0)[1], 0)
    dx_finish(1)
    for cp in last0:
        cp.wait()
    take_over(rest_rows)
    top.finish()
    last1 = to_mate(top_rows, 6)
    for cp in last1:
        cp.start()
    hand_over(top_rows)
    for cp in last1:
        cp.wait()
    take_over(top_rows)
    top.drain()
    rest.drain()
    for t in range(2):
        for i in range(6):
            swaps[t, i].wait_send()
    dx_sent(0)
    dx_sent(1)
    for cp in swap2:
        cp.wait_send()


STEP_ORDER = ("Y", "BF", "W", "TY", "TX", "Z", "X", "D0F", "D1", "TZ", "D0")
STEPS = {
    "Y": ((0, 1), (4, 2), (5, 3), (6, 4), (7, 5), (9, 6), (17, 7),),
    "X": ((3, 0), (5, 1), (7, 2), (13, 3),),
    "Z": ((12, 0), (16, 1), (19, 2),),
    "D0": ((14, 0), (18, 1), (23, 2),),
    "TY": ((24, 0),),
    "BF": ((27, 0),),
    "W": ((27, 0),),
    "D0F": ((32, 0),),
    "TX": ((27, 0), (29, 1), (33, 2), (37, 3),),
    "D1": ((25, 0), (28, 1), (29, 2),),
    "TZ": ((31, 0), (33, 1), (37, 2),),
}
MATE_AT = 3


def backward_all(datt, stats, tgt, gb, extra, q, done, k, v, xs, top, go, gu, gd):
    dma = pltpu.SemaphoreType.DMA
    sd = jax.ShapeDtypeStruct
    vm, anywhere = (pl.BlockSpec(memory_space=m) for m in (pltpu.VMEM, pl.ANY))
    mb, rows, width = q.shape
    s = pltpu.VMEM
    views = [top.reshape(8, 2, TOP, width), go.reshape(8, 2, 48, width), gu.reshape(8, 2, 48, 4 * width),
             gd.reshape(8, 2, 192, width)]
    return pl.pallas_call(
        backward_kernel,
        out_shape=[sd((24, width), F32)] * 4 + [sd((24, 4 * width), F32), sd((96, width), F32), sd((16, width), F32),
                                                sd(q.shape, F32)],
        in_specs=[vm] * 4 + [anywhere] * 10,
        out_specs=[vm] * 8,
        scratch_shapes=[
            s((NS, width), BF), s((NS, width), BF), s((NS, width), BF), s((8, 2, TOP - 16, width), BF),
            s((mb, 2, NK, 128), BF), s((NW, 128), F32), s((NW, 128), F32), s((mb, rows, width), BF),
            s((8, 2, TOP, width), BF), s((16, width), F32),
            s((8, 2, REST, 384), BF), s((8, 2, REST, 384), BF), s((8, REST, 384), BF), s((8, 2, TOP, 384), BF), s((8, TOP, 384), BF),
            s((4, REST, 384), BF),
            s((5, REST, 384), BF),
            s((mb, 8, rows, width), BF), s((mb, 4, rows, width), BF), s((mb, 5, rows, width), BF),
            s((REST, 384), F32), s((304, 384), F32),
            dma((2, 6)), dma((5,)), dma((2, 2, 6)), dma((2, 2)), dma((2, 6)),
            dma((2, 8)), dma((2, 4)), dma((2, 5)), dma((2, 8)), dma((2, 4)), dma((2, 5)),
            dma((2, mb, 4)), dma((2, mb, 5)), dma((2, 10)), pltpu.SemaphoreType.REGULAR,
        ],
        compiler_params=pltpu.CompilerParams(
            collective_id=1, has_side_effects=True, vmem_limit_bytes=62 * 2**20
        ),
    )(datt, stats, tgt, gb, extra, q, done, k, v, xs, *views)


CHUNKS = 9


def project_kernel(idx, xall, wall, bias, xs_ref, k_ref, v_ref, q_ref, xs, w, sems, wsem):
    m, i = pl.program_id(0), pl.program_id(1)

    @pl.when((m == 0) & (i == 0))
    def _():
        copy = pltpu.make_async_copy(wall.at[:, pl.ds(16, 144), :], w, wsem)
        copy.start()
        for mm in range(2):
            for cc in range(CHUNKS):
                pieces = [(0, 256)] if cc < 5 else [(0, 128), (128, 128)] if cc == 5 else [(64 * t, 64) for t in range(4)]
                base = cc if cc < 5 else 5 if cc == 5 else 7 + 4 * (cc - 6)
                for t, (off, n) in enumerate(pieces):
                    start = pl.multiple_of(idx[mm, base + t], 64)
                    pltpu.make_async_copy(xall.at[mm, pl.ds(start, n), :], xs.at[mm, cc, pl.ds(off, n), :],
                                          sems.at[mm, cc]).start()
        copy.wait()

    pltpu.make_async_copy(xall.at[0, pl.ds(0, 256), :], xs.at[m, i], sems.at[m, i]).wait()
    rows = xs[m, i]
    xs_ref[0] = rows
    k_ref[0] = dot(rows, w[:, 48:96, :].reshape(768, 768)).astype(BF)
    v_ref[0] = (dot(rows, w[:, 96:144, :].reshape(768, 768)) + bias[1:2, :]).astype(BF)

    @pl.when(i == 2)
    def _():
        q = (dot(rows, w[:, 0:48, :].reshape(768, 768)) + bias[0:1, :]).astype(BF)
        q_ref[0] = q * jnp.asarray(0.125, BF)


def project(idx, xall, wall, bias):
    mb = xall.shape[0]
    sd = jax.ShapeDtypeStruct
    chunk = pl.BlockSpec((1, 256, 768), lambda m, i, t: (m, i, 0))
    return pl.pallas_call(
        project_kernel,
        grid_spec=pltpu.PrefetchScalarGridSpec(
            num_scalar_prefetch=1,
            grid=(mb, CHUNKS),
            in_specs=[pl.BlockSpec(memory_space=pl.ANY)] * 2 + [pl.BlockSpec((16, 768), lambda m, i, t: (0, 0))],
            out_specs=[chunk, chunk, chunk, pl.BlockSpec((1, 256, 768), lambda m, i, t: (m, 0, 0))],
            scratch_shapes=[
                pltpu.VMEM((mb, CHUNKS, 256, 768), BF), pltpu.VMEM((16, 144, 768), BF),
                pltpu.SemaphoreType.DMA((mb, CHUNKS)), pltpu.SemaphoreType.DMA,
            ],
        ),
        out_shape=[sd((mb, NS, 768), BF)] * 3 + [sd((mb, 256, 768), BF)],
        compiler_params=pltpu.CompilerParams(vmem_limit_bytes=48 * 2**20),
    )(idx, xall, wall, bias)


EPS = 1e-6
G0, G1 = 0.7978845608, 0.044715


def norm(v):
    mean = jnp.mean(v, axis=-1, keepdims=True)
    centred = v - mean
    inverse = lax.rsqrt(jnp.mean(centred * centred, axis=-1, keepdims=True) + EPS)
    return centred * inverse, inverse


def norm_back(g, normed, inverse, gain):
    c = g * gain
    return inverse * (c - jnp.mean(c, axis=-1, keepdims=True)
                      - normed * jnp.mean(c * normed, axis=-1, keepdims=True))


def middle_kernel(att, x_in, cot_in, wall, bias, lse_in, out_ref, stats_ref, datt_ref, done_ref, go_out, gu_out, gd_out, gb_ref,
                  x, cot, lse, isem, go_ref, gu_ref, gd_ref, gsem, w, wsem, pre, hid, mid, low, n1, r1, ffn):
    rows = att.shape[0]
    def load(j, t):
        if t == 0:
            src, dst = wall.at[:, pl.ds(0, 48), :], w.at[:, pl.ds(0, 48), :]
        elif t == 1:
            at = pl.ds(pl.multiple_of(48 + 48 * j, 16), 48)
            src, dst = wall.at[:, at, :], w.at[:, at, :]
        else:
            at = pl.ds(4 * j, 4)
            src, dst = wall.at[at, pl.ds(240, 192), :], w.at[at, pl.ds(240, 192), :]
        return pltpu.make_async_copy(src, dst, wsem.at[t, j])

    inputs = [pltpu.make_async_copy(src, dst, isem.at[i])
              for i, (src, dst) in enumerate(((x_in, x), (cot_in, cot), (lse_in, lse)))]
    load(0, 0).start()
    inputs[0].start()
    for j in range(4):
        load(j, 1).start()
        load(j, 2).start()
    inputs[1].start()
    inputs[2].start()
    half = rows // 2
    load(0, 0).wait()
    inputs[0].wait()
    w_out = w[:, 0:48, :].reshape(768, 768)
    for h in range(2):
        r = pl.ds(h * half, half)
        t = x[r, :].astype(F32) + dot(att[r, :], w_out) + bias[2:3, :]
        normed, inverse = norm(t)
        n1[r, :] = normed
        r1[r, :] = jnp.broadcast_to(inverse, (half, 128))
        value = normed * bias[4:5, :] + bias[5:6, :]
        mid[r, :] = value
        low[r, :] = value.astype(BF)
    ffn[...] = jnp.broadcast_to(bias[3:4, :], ffn.shape)

    def up_block(j):
        return w[:, pl.ds(pl.multiple_of(48 + 48 * j, 16), 48), :].reshape(768, 768)

    def down_block(j):
        return w[pl.ds(4 * j, 4), 240:432, :].reshape(768, 768)

    def forward(j, _):
        load(j, 1).wait()
        load(j, 2).wait()
        wu, wd = up_block(j), down_block(j)
        for h in range(2):
            r = pl.ds(h * half, half)
            u = dot(low[r, :], wu) + bias[pl.ds(8 + j, 1), :]
            square = u * u
            th = jnp.tanh(G0 * u * (1.0 + G1 * square))
            half_u, one = 0.5 * u, 1.0 + th
            pre[j, r, :] = 0.5 * one + half_u * (one * (1.0 - th)) * (G0 + (3.0 * G0 * G1) * square)
            g = (half_u * one).astype(BF)
            hid[j, r, :] = g
            ffn[r, :] += dot(g, wd)
        return 0

    lax.fori_loop(0, 4, forward, 0)
    gb_ref[...] = jnp.zeros_like(gb_ref)
    inputs[1].wait()
    inputs[2].wait()
    for h in range(2):
        r = pl.ds(h * half, half)
        normed, inverse = norm(mid[r, :] + ffn[r, :])
        out_ref[r, :] = (normed * bias[6:7, :] + bias[7:8, :]).astype(BF)
        g = cot[r, :].astype(F32)
        gb_ref[6:7, :] += jnp.sum(g * normed, axis=0, keepdims=True)
        gb_ref[7:8, :] += jnp.sum(g, axis=0, keepdims=True)
        d_two = norm_back(g, normed, inverse, bias[6:7, :])
        mid[r, :] = d_two
        d_ffn = d_two.astype(BF)
        datt_ref[r, :] = d_ffn
        gb_ref[3:4, :] += jnp.sum(d_ffn.astype(F32), axis=0, keepdims=True)

    def sent(ref, out, j, t):
        at = pl.ds(pl.multiple_of(j * 768, 768), 768)
        return pltpu.make_async_copy(ref.at[j], out.at[at, :] if t == 0 else out.at[:, at], gsem.at[t, j])

    def backward(j, _):
        wu, wd = up_block(j), down_block(j)
        d_ffn = datt_ref[...]
        gd_ref[j] = dot_tn(hid[j], d_ffn).astype(BF)
        sent(gd_ref, gd_out, j, 0).start()
        for h in range(2):
            r = pl.ds(h * half, half)
            d_pre = (dot_nt(datt_ref[r, :], wd) * pre[j, r, :]).astype(BF)
            hid[j, r, :] = d_pre
            gb_ref[pl.ds(8 + j, 1), :] += jnp.sum(d_pre.astype(F32), axis=0, keepdims=True)
            mid[r, :] += dot_nt(d_pre, wu)
        gu_ref[j] = dot_tn(low[...], hid[j]).astype(BF)
        sent(gu_ref, gu_out, j, 1).start()
        return 0

    lax.fori_loop(0, 4, backward, 0)
    for h in range(2):
        r = pl.ds(h * half, half)
        d_mid, normed = mid[r, :], n1[r, :]
        gb_ref[4:5, :] += jnp.sum(d_mid * normed, axis=0, keepdims=True)
        gb_ref[5:6, :] += jnp.sum(d_mid, axis=0, keepdims=True)
        d_one = norm_back(d_mid, normed, r1[r, 0:1], bias[4:5, :])
        done_ref[r, :] = d_one
        d_branch = d_one.astype(BF)
        low[r, :] = d_branch
        gb_ref[2:3, :] += jnp.sum(d_branch.astype(F32), axis=0, keepdims=True)
        d_att = dot_nt(d_branch, w_out).astype(BF)
        datt_ref[r, :] = d_att
        product = d_att.astype(F32) * att[r, :].astype(F32)
        lane = lax.broadcasted_iota(jnp.int32, (half, 128), 1)
        stats = lse[r, :]
        for p in range(6):
            two = product[:, 128 * p:128 * p + 128]
            stats = jnp.where(lane == 16 + 2 * p, jnp.sum(jnp.where(lane < 64, two, 0.0), axis=1, keepdims=True), stats)
            stats = jnp.where(lane == 17 + 2 * p, jnp.sum(jnp.where(lane >= 64, two, 0.0), axis=1, keepdims=True), stats)
        stats_ref[r, :] = stats
    go_ref[...] = dot_tn(att[...], low[...]).astype(BF)
    go_copy = pltpu.make_async_copy(go_ref, go_out, isem.at[3])
    go_copy.start()
    for j in range(4):
        sent(gd_ref, gd_out, j, 0).wait()
        sent(gu_ref, gu_out, j, 1).wait()
    go_copy.wait()


def middle(att, x, cot, wall, bias, lse):
    rows = att.shape[0]
    sd = jax.ShapeDtypeStruct
    vm, anywhere = pl.BlockSpec(memory_space=pltpu.VMEM), pl.BlockSpec(memory_space=pl.ANY)
    return pl.pallas_call(
        middle_kernel,
        in_specs=[vm, anywhere, anywhere, anywhere, vm, anywhere],
        out_specs=[vm] * 4 + [pl.BlockSpec(memory_space=pl.ANY)] * 3 + [vm],
        out_shape=[sd((rows, 768), BF), sd((rows, 128), F32), sd((rows, 768), BF), sd((rows, 768), F32), sd((768, 768), BF),
                   sd((768, 3072), BF), sd((3072, 768), BF), sd((16, 768), F32)],
        scratch_shapes=[
            pltpu.VMEM((rows, 768), BF), pltpu.VMEM((rows, 768), BF), pltpu.VMEM((rows, 128), F32),
            pltpu.SemaphoreType.DMA((4,)),
            pltpu.VMEM((768, 768), BF), pltpu.VMEM((4, 768, 768), BF), pltpu.VMEM((4, 768, 768), BF),
            pltpu.SemaphoreType.DMA((2, 4)),
            pltpu.VMEM((16, 432, 768), BF), pltpu.SemaphoreType.DMA((3, 4)),
            pltpu.VMEM((4, rows, 768), F32), pltpu.VMEM((4, rows, 768), BF),
            pltpu.VMEM((rows, 768), F32), pltpu.VMEM((rows, 768), BF), pltpu.VMEM((rows, 768), F32),
            pltpu.VMEM((rows, 128), F32), pltpu.VMEM((rows, 768), F32),
        ],
        compiler_params=pltpu.CompilerParams(vmem_limit_bytes=60 * 2**20),
    )(att, x, cot, wall, bias, lse)


def back_kernel(scattered, idx, xs_ref, dk_ref, dv_ref, dq_ref, done_ref, wall, gb_in, dx_ref, own_ref, gq_ref, gk_ref, gv_ref, gb_ref,
                w, wsem, acc, aq, ak, av):
    m, i = pl.program_id(0), pl.program_id(1)

    @pl.when((m == 0) & (i == 0))
    def _():
        copy = pltpu.make_async_copy(wall.at[:, pl.ds(16, 144), :], w, wsem)
        copy.start()
        acc[...] = jnp.zeros_like(acc)
        aq[...] = jnp.zeros_like(aq)
        ak[...] = jnp.zeros_like(ak)
        av[...] = jnp.zeros_like(av)
        gb_ref[...] = gb_in[...]
        copy.wait()

    rows, dk, dv = xs_ref[0], dk_ref[0], dv_ref[0]
    ak[...] += dot_tn(rows, dk)
    av[...] += dot_tn(rows, dv)
    gb_ref[1:2, :] += jnp.sum(dv.astype(F32), axis=0, keepdims=True)
    dx = dot_nt(dk, w[:, 48:96, :].reshape(768, 768)) + dot_nt(dv, w[:, 96:144, :].reshape(768, 768))

    def add(slot, off, n):
        start = pl.multiple_of(idx[m, slot], 64)
        acc[m, pl.ds(start, n), :] += dx[off:off + n]

    if not scattered:
        dx_ref[0] = jnp.where(i == 2, jnp.zeros_like(dx), dx).astype(BF)

    @pl.when((i < 5) & (i != 2) & scattered)
    def _():
        add(jnp.minimum(i, 4), 0, 256)

    @pl.when((i == 5) & scattered)
    def _():
        add(5, 0, 128)
        add(6, 128, 128)

    @pl.when((i > 5) & scattered)
    def _():
        for t in range(4):
            add(7 + 4 * (i - 6) + t, 64 * t, 64)

    @pl.when(i == 2)
    def _():
        dq = dq_ref[0]
        aq[...] += dot_tn(rows, dq)
        gb_ref[0:1, :] += jnp.sum(dq.astype(F32), axis=0, keepdims=True)
        own_ref[0] = dx + done_ref[0] + dot_nt(dq, w[:, 0:48, :].reshape(768, 768))

    @pl.when((i == CHUNKS - 1) & scattered)
    def _():
        dx_ref[m if scattered else 0] = acc[m].astype(BF)

    @pl.when((m == 1) & (i == CHUNKS - 1))
    def _():
        gq_ref[...] = aq[...].astype(BF)
        gk_ref[...] = ak[...].astype(BF)
        gv_ref[...] = av[...].astype(BF)


def back(idx, xs, dk, dv, dq, done, wall, gb, seq_len):
    mb = xs.shape[0]
    sd = jax.ShapeDtypeStruct
    chunk = pl.BlockSpec((1, 256, 768), lambda m, i, t: (m, i, 0))
    one = pl.BlockSpec((1, 256, 768), lambda m, i, t: (m, 0, 0))
    whole = lambda *s: pl.BlockSpec(s, lambda m, i, t: (0,) * len(s))
    scattered = seq_len > 0
    held = seq_len if scattered else 256
    return pl.pallas_call(
        functools.partial(back_kernel, scattered),
        grid_spec=pltpu.PrefetchScalarGridSpec(
            num_scalar_prefetch=1,
            grid=(mb, CHUNKS),
            in_specs=[chunk, chunk, chunk, one, one, pl.BlockSpec(memory_space=pl.ANY), whole(16, 768)],
            out_specs=[whole(mb, seq_len, 768) if scattered else chunk, one, whole(768, 768), whole(768, 768), whole(768, 768), whole(16, 768)],
            scratch_shapes=[
                pltpu.VMEM((16, 144, 768), BF), pltpu.SemaphoreType.DMA, pltpu.VMEM((mb, held, 768), F32),
                pltpu.VMEM((768, 768), F32), pltpu.VMEM((768, 768), F32), pltpu.VMEM((768, 768), F32),
            ],
        ),
        out_shape=[sd((mb, seq_len if scattered else NS, 768), BF), sd((mb, 256, 768), F32), sd((768, 768), BF), sd((768, 768), BF),
                   sd((768, 768), BF), sd((16, 768), F32)],
        compiler_params=pltpu.CompilerParams(vmem_limit_bytes=60 * 2**20),
    )(idx, xs, dk, dv, dq, done, wall, gb)


def last_kernel(*refs):
    table, arrays = refs[0], refs[1:8]
    outs, vectors = refs[8:15], refs[15:]
    for src, dst in zip(arrays, outs):
        dst[...] = src[...]
    owner = lax.axis_index("seq") * 4 + lax.axis_index("batch")
    n, m = vectors[0].shape[1], vectors[8].shape[1]
    small = pltpu.roll(table[0:8, :], (768 - owner * n) % 768, axis=1)
    for i in range(8):
        vectors[i][...] = small[i:i + 1, 0:n]
    ups = jnp.broadcast_to(table[pl.ds(8 + owner // 8, 1), :], (8, 768))
    vectors[8][...] = pltpu.roll(ups, (768 - (owner % 8) * m) % 768, axis=1)[0:1, 0:m]


def last(table, arrays, n, m):
    sd = jax.ShapeDtypeStruct
    vm = pl.BlockSpec(memory_space=pltpu.VMEM)
    return pl.pallas_call(
        last_kernel,
        in_specs=[vm] * 8,
        out_specs=[vm] * 16,
        out_shape=[sd(a.shape, a.dtype) for a in arrays] + [sd((1, n), F32)] * 8 + [sd((1, m), F32)],
        compiler_params=pltpu.CompilerParams(vmem_limit_bytes=60 * 2**20),
    )(table, *arrays)

def cat_rows(ref, h):
    return jnp.concatenate([ref[0, pl.ds(a, n), :] for a, n in key_rows(h)], axis=0)


def fwd_kernel(q_ref,k_ref,v_ref,me_ref,o_ref,l_ref):
    p=pl.program_id(1)
    ind=block_columns().astype(BF)
    for h in range(2):
        me=me_ref[0,h]
        qe=jnp.concatenate([split_heads(q_ref[0,pl.ds(h*HALF,HALF),:]),ind],axis=1)
        ke=jnp.concatenate([cat_rows(k_ref, h),me],axis=1)
        s=dot_nt(qe,ke)
        top=jnp.max(s,axis=1,keepdims=True)
        e=jnp.exp(s-top).astype(BF)
        ve=jnp.concatenate([cat_rows(v_ref,h),me],axis=1)
        o=dot(e,ve)
        tot=o[:,130:131]
        o_ref[0,pl.ds(h*HALF,HALF),:]=merge_heads(o[:,:128]/tot).astype(BF)
        l_ref[0,0,pl.ds(h*256,256),:]=jnp.broadcast_to(top+jnp.log(tot),(256,128))
def attn_fwd(q,k,v,me):
    mb=q.shape[0]; npair=q.shape[2]//128
    return pl.pallas_call(fwd_kernel,grid=(mb,npair),
      in_specs=[pl.BlockSpec((1,256,128),lambda m,p:(m,0,p)),pl.BlockSpec((1,NS,128),lambda m,p:(m,0,p)),pl.BlockSpec((1,NS,128),lambda m,p:(m,0,p)),
        pl.BlockSpec((1,2,NK,128),lambda m,p:(m,0,0,0))],
      out_specs=[pl.BlockSpec((1,256,128),lambda m,p:(m,0,p)),pl.BlockSpec((1,1,512,128),lambda m,p:(m,p,0,0))],
      out_shape=[jax.ShapeDtypeStruct(q.shape,BF),jax.ShapeDtypeStruct((mb,npair,512,128),F32)],
      compiler_params=pltpu.CompilerParams(vmem_limit_bytes=56*2**20))(q,k,v,me)
def bwd_kernel(CH,q_ref,k_ref,v_ref,me_ref,o_ref,do_ref,l_ref,dq_ref,dk_ref,dv_ref,dka,dva):
    ind=block_columns()
    zero=jnp.zeros_like(ind)
    dka[...]=jnp.zeros_like(dka); dva[...]=jnp.zeros_like(dva)
    for h in range(2):
        rows=pl.ds(h*HALF,HALF)
        qs=split_heads(q_ref[0,rows,:])
        do2=do_ref[0,rows,:]
        dos=split_heads(do2)
        o2=o_ref[0,rows,:].astype(F32)
        delta=jnp.sum(dos.astype(F32)*jnp.concatenate([o2,o2],axis=0),axis=1,keepdims=True)
        lse=l_ref[0,0,pl.ds(h*256,256),0:1]
        qe=jnp.concatenate([qs,with_column(ind,-lse)],axis=1)
        doe=jnp.concatenate([dos,with_column(zero,-delta)],axis=1)
        dqt=jnp.zeros((128,256),F32)
        off=0
        for a,n in key_rows(h):
            c0=0
            while c0<n:
                c=min(CH,n-c0)
                kr=pl.ds(a+c0,c)
                k2=k_ref[0,kr,:]; v2=v_ref[0,kr,:]; me=me_ref[0,h,pl.ds(off+c0,c),:]
                st=dot_nt(jnp.concatenate([k2,me],axis=1),qe)
                pt=jnp.exp(st)
                dpt=dot_nt(jnp.concatenate([v2,me],axis=1),doe)
                ds=(pt*dpt).astype(BF)
                dva[kr,:]+=dot(pt.astype(BF),dos)
                dka[kr,:]+=dot(ds,qs)
                dqt=dqt+dot(k2.T,ds)
                c0+=c
            off+=n
        dq_ref[0,rows,:]=(merge_heads(dqt.T)*0.125).astype(BF)
    dk_ref[0]=dka[...].astype(BF); dv_ref[0]=dva[...].astype(BF)
def attn_bwd(q,k,v,me,o,do,l,CH=384):
    mb=q.shape[0]; npair=q.shape[2]//128
    qs=pl.BlockSpec((1,256,128),lambda m,p:(m,0,p)); ks=pl.BlockSpec((1,NS,128),lambda m,p:(m,0,p))
    return pl.pallas_call(functools.partial(bwd_kernel,CH),grid=(mb,npair),
      in_specs=[qs,ks,ks,pl.BlockSpec((1,2,NK,128),lambda m,p:(m,0,0,0)),qs,qs,pl.BlockSpec((1,1,512,128),lambda m,p:(m,p,0,0))],
      out_specs=[qs,ks,ks],
      out_shape=[jax.ShapeDtypeStruct(q.shape,BF),jax.ShapeDtypeStruct(k.shape,BF),jax.ShapeDtypeStruct(k.shape,BF)],
      scratch_shapes=[pltpu.VMEM((NS,128),F32)]*2,
      compiler_params=pltpu.CompilerParams(vmem_limit_bytes=56*2**20))(q,k,v,me,o,do,l)


BLK = 64
WIN = 8
RAND = 3
ALL = ("seq", "batch")


def vector_table(vectors, b_up, owner, width):
    lane = jnp.arange(width, dtype=jnp.int32)
    n, m = vectors[0].shape[0], b_up.shape[0]
    table = jnp.where(lane // n == owner, jnp.tile(jnp.stack(vectors).astype(F32), (1, width // n)), 0.0)
    flat = jnp.arange(4 * width, dtype=jnp.int32)
    ups = jnp.where(flat // m == owner, jnp.tile(b_up.astype(F32), 4 * width // m), 0.0).reshape(4, width)
    return jnp.concatenate([table, ups, jnp.zeros((4, width), F32)], axis=0)


def block_plan(lengths, randoms, device, blocks):
    ends = jnp.cumsum(lengths, axis=1)
    starts = ends - lengths

    def doc_of(block):
        at = block * BLK
        shape = (lengths.shape[0],) + (1,) * (block.ndim - 1) + (lengths.shape[1],)
        doc = jnp.sum((ends.reshape(shape) <= at[..., None]).astype(jnp.int32), axis=-1)
        doc = jnp.minimum(doc, lengths.shape[1] - 1)
        hit = jnp.arange(lengths.shape[1], dtype=jnp.int32) == doc[..., None]
        return doc, jnp.sum(jnp.where(hit, starts.reshape(shape), 0), axis=-1)

    mb = lengths.shape[0]
    half = jnp.arange(2, dtype=jnp.int32)
    query = device * 4 + 2 * half[:, None] + half[None, :]
    query = jnp.broadcast_to(query[None], (mb, 2, 2))
    q_doc, q_first = doc_of(query)
    window = device * 4 + 2 * half[:, None] - WIN + jnp.arange(2 * WIN + 2, dtype=jnp.int32)[None, :]
    window = jnp.broadcast_to(window[None], (mb, 2, 2 * WIN + 2))
    w_doc, w_first = doc_of(jnp.clip(window, 0, blocks - 1))
    w_good = (window >= 0) & (window < blocks) & (window * BLK - w_first >= 2 * BLK)
    see_window = (
        w_good[:, :, None, :]
        & (w_doc[:, :, None, :] == q_doc[..., None])
        & (jnp.abs(window[:, :, None, :] - query[..., None]) <= WIN)
    )
    see_glob = jnp.ones((mb, 2, 2, 2), bool)
    named = lax.dynamic_slice_in_dim(randoms, device * 4, 4, 1).reshape(mb, 2, 2, RAND)
    r_doc, r_first = doc_of(named)
    r_good = (
        (r_doc == q_doc[..., None])
        & (jnp.abs(named - query[..., None]) > WIN)
        & (named * BLK - r_first >= 2 * BLK)
    )
    see_random = (r_good[:, :, None] & jnp.eye(2, dtype=bool)[None, None, :, :, None]).reshape(mb, 2, 2, 2 * RAND)
    see = jnp.concatenate([see_window, see_glob, see_random], axis=3)
    chunk = jnp.clip(device + jnp.arange(-2, 3, dtype=jnp.int32), 0, blocks // 4 - 1) * (4 * BLK)
    where = jnp.concatenate(
        [jnp.broadcast_to(chunk[None], (mb, 5)), q_first[:, :, 0], named.reshape(mb, -1) * BLK], axis=1
    )
    return where, jnp.where(see, 0.0, -1e30)


def mask_columns(see):
    bias = jnp.broadcast_to(see[..., None], see.shape + (BLK,)).reshape(see.shape[:3] + (-1, 1))
    lane = jnp.arange(128, dtype=jnp.int32)
    ones = jnp.where((lane >= 2) & (lane < 5), 1.0, 0.0)
    return jnp.where(lane == 0, bias[:, :, 0], jnp.where(lane == 1, bias[:, :, 1], ones)).astype(BF)


def on_device(inputs, cotangent, doc_lengths, random_blocks, wq, wk, wv, wo, wu, wd, b_query, b_value, b_out,
              b_up, b_down, gain_attn, bias_attn, gain_ffn, bias_ffn):
    mb, _, rows, width = inputs.shape
    devices, owners = lax.axis_size("seq"), lax.axis_size("seq") * lax.axis_size("batch")
    device = lax.axis_index("seq")
    owner = device * lax.axis_size("batch") + lax.axis_index("batch")
    linked = devices == 8 and owners == 32
    seq_len = devices * rows
    x, cot = inputs[:, 0], cotangent[:, 0]
    lengths, randoms = doc_lengths[:, 0], random_blocks[:, 0]
    vectors = (b_query, b_value, b_out, b_down, gain_attn, bias_attn, gain_ffn, bias_ffn)
    flat = lambda t: t.reshape(-1, t.shape[-1])
    if linked:
        att, lse, q, xs, k, v, wall, top, bias, extra, targets = forward_all(
            doc_lengths.transpose(1, 0, 2), random_blocks.transpose(1, 0, 2, 3), x, (wq, wk, wv, wo, wu, wd),
            [v[None] for v in vectors], b_up[None])
    else:
        where, see = block_plan(lengths, randoms, device, seq_len // BLK)
        extra, table = mask_columns(see), vector_table(vectors, b_up, owner, width)
        xall = lax.all_gather(x, "seq", axis=1, tiled=True)
        bias = lax.psum(table, ALL)
        full = [lax.all_gather(w, ALL, axis=0, tiled=True) for w in (wq, wk, wv, wo, wu, wd)]
        fold = lambda w: w.reshape(16, -1, width)
        up = full[4].reshape(16, 48, 4, width).transpose(0, 2, 1, 3).reshape(16, 192, width)
        wall = jnp.concatenate([fold(full[3]), up, fold(full[5])], axis=1)
        top = jnp.concatenate([jnp.zeros((16, 16, width), BF)] + [fold(w) for w in full[:3]], axis=1)
        xs, k, v, q = project(where, xall, top, bias)
        att, lse = attn_fwd(q, k, v, extra)
    stats = flat(lse) if linked else jnp.zeros((mb * rows, 128), F32)
    out, stats, datt, done, go, gu, gd, gb = middle(flat(att), flat(x), flat(cot), wall, bias, stats)
    datt, done = datt.reshape(att.shape), done.reshape(mb, rows, width)
    if linked:
        *grads, gb, dx = backward_all(datt, stats.reshape(mb, rows, 128), targets, gb, extra, q, done, k, v, xs, top, go, gu, gd)
    else:
        dq, dk, dv = attn_bwd(q, k, v, extra, att, datt, lse, 640)
        dxs, own, gq, gk, gv, gb = back(where, xs, dk, dv, dq, done, top, gb, 0)
        start = (where[:, :5, None] + jnp.arange(0, 256, BLK)).reshape(mb, -1)
        glob = (where[:, 5:7, None] + jnp.arange(0, 128, BLK)).reshape(mb, -1)
        to = jnp.concatenate([start, glob, where[:, 7:]], axis=1) // BLK
        parts = dxs.reshape(mb, -1, BLK, width)
        total = jnp.zeros((mb, seq_len // BLK, BLK, width), F32)
        total = jax.vmap(lambda t, i, p: t.at[i].add(p))(total, to, parts.astype(F32))
        dx = own + lax.psum_scatter(total.reshape(mb, seq_len, width), "seq", scatter_dimension=1, tiled=True)
        grads = [lax.psum_scatter(g.astype(F32), ALL, scatter_dimension=0, tiled=True) for g in (gq, gk, gv, go, gu, gd)]
        gb = lax.psum(gb, ALL)
    n, m = b_query.shape[0], b_up.shape[0]
    if linked:
        done_all = last(gb, (*grads, dx), n, m)
        grads, dx = done_all[:6], done_all[6]
        small, ups = [g.reshape(n) for g in done_all[7:15]], done_all[15].reshape(m)
    else:
        small = lax.dynamic_slice_in_dim(gb[:8], owner * n, n, 1)
        ups = lax.dynamic_slice_in_dim(gb[8:12].reshape(-1), owner * m, m, 0)
    return (
        out.reshape(inputs.shape), dx[:, None], *grads,
        small[0], small[1], small[2], ups, small[3], small[4], small[5], small[6], small[7],
    )


def solution(mesh):
    tokens = P(None, "batch", "seq", None)
    mat, vec = P(ALL, None), P(ALL)
    in_specs = (tokens, tokens, P(None, "batch", None), P(None, "batch", None, None)) + (mat,) * 6 + (vec,) * 9
    out_specs = (tokens, tokens) + (mat,) * 6 + (vec,) * 9
    return jax.shard_map(on_device, mesh=mesh, in_specs=in_specs, out_specs=out_specs, check_vma=False)
```

```python
import functools

import jax
import jax.numpy as jnp
from jax import lax
from jax.experimental import pallas as pl
from jax.experimental.pallas import tpu as pltpu
from jax.sharding import PartitionSpec as P

F32 = jnp.float32
BF = jnp.bfloat16


HALF, WK, NW, NK, NS = 128, 1152, 1280, 1664, 2304
TOP, REST = 160, 432
MESH = pl.DeviceIdType.MESH
UP, DOWN, XX, YY, CC = range(5)
WAYS = (UP, DOWN, XX, YY, CC)


def dot(a, b):
    return lax.dot_general(a, b, (((1,), (0,)), ((), ())), preferred_element_type=F32)


def dot_nt(a, b):
    return lax.dot_general(a, b, (((1,), (1,)), ((), ())), preferred_element_type=F32)


def dot_tn(a, b):
    return lax.dot_general(a, b, (((0,), (0,)), ((), ())), preferred_element_type=F32)


def place():
    s, b = lax.axis_index("seq"), lax.axis_index("batch")
    return s // 2, s % 2, b // 2, b % 2


def device(z, x, y, c):
    return (2 * z + x, 2 * y + c)


def greet(z, x, y, c):
    barrier = pltpu.get_barrier_semaphore()

    def tell(to):
        pl.semaphore_signal(barrier, inc=1, device_id=to, device_id_type=MESH)

    tell(device(z, 1 - x, y, c))
    tell(device(z, x, 1 - y, c))
    tell(device(z, x, y, 1 - c))
    pl.when(z > 0)(lambda: tell(device(z - 1, x, y, c)))
    pl.when(z < 3)(lambda: tell(device(z + 1, x, y, c)))
    pl.semaphore_wait(barrier, 3 + (z > 0).astype(jnp.int32) + (z < 3).astype(jnp.int32))


def lanes(c):
    return pl.ds(pl.multiple_of(c * 384, 128), 384)


def rows_at(i, n):
    return pl.ds(pl.multiple_of(i * n, n), n)


def remote(src, dst, send, recv, to):
    return pltpu.make_async_remote_copy(
        src_ref=src, dst_ref=dst, send_sem=send, recv_sem=recv, device_id=to, device_id_type=MESH
    )


def key_rows(h):
    return ((HALF * h, WK), (NW + HALF * h, HALF), (NW + 2 * HALF + 384 * h, 384))


def split_heads(v):
    lane = lax.broadcasted_iota(jnp.int32, v.shape, 1)
    z = jnp.zeros_like(v)
    return jnp.concatenate([jnp.where(lane < 64, v, z), jnp.where(lane >= 64, v, z)], axis=0)


def merge_heads(v):
    n = v.shape[0] // 2
    lane = lax.broadcasted_iota(jnp.int32, (n, v.shape[1]), 1)
    return jnp.where(lane < 64, v[:n], v[n:])


def block_columns():
    r = lax.broadcasted_iota(jnp.int32, (2 * HALF, 128), 0)
    lane = lax.broadcasted_iota(jnp.int32, (2 * HALF, 128), 1)
    first = (r % HALF) < 64
    return jnp.where(((lane == 0) & first) | ((lane == 1) & jnp.logical_not(first)), 1.0, 0.0)


def with_column(base, col):
    lane = lax.broadcasted_iota(jnp.int32, base.shape, 1)
    hi = col.astype(BF).astype(F32)
    rest = col - hi
    mid = rest.astype(BF).astype(F32)
    return jnp.where(lane == 2, hi, jnp.where(lane == 3, mid, jnp.where(lane == 4, rest - mid, base))).astype(BF)


def doc_of(lengths, m, block):
    at = block * 64
    doc, first, end = jnp.int32(0), jnp.int32(0), jnp.int32(0)
    for i in range(3):
        end = end + lengths[0, m, i]
        doc = doc + (end <= at).astype(jnp.int32)
        first = jnp.where(end <= at, end, first)
    return doc, first


def write_extra(lengths, randoms, s, extra):
    lane = lax.broadcasted_iota(jnp.int32, (64, 128), 1)
    ones = jnp.where((lane >= 2) & (lane < 5), 1.0, 0.0)

    def one(i, _):
        m, h, t = i // 52, (i // 26) % 2, i % 26
        r = jnp.maximum(t - 20, 0)
        named = randoms[0, m, 4 * s + 2 * h + r // 3, r % 3]
        block = jnp.where(t < 18, 4 * s + 2 * h - 8 + t, named)
        inside = (block >= 0) & (block < 32)
        doc, first = doc_of(lengths, m, jnp.clip(block, 0, 31))
        good = inside & (block * 64 - first >= 128)
        terms = []
        for k in range(2):
            query = 4 * s + 2 * h + k
            q_doc, _ = doc_of(lengths, m, query)
            near = jnp.abs(block - query) <= 8
            window = (t < 18) & near
            named_here = (t >= 20) & (r // 3 == k) & jnp.logical_not(near)
            seen = ((t >= 18) & (t < 20)) | (good & (doc == q_doc) & (window | named_here))
            terms.append(jnp.where(seen, 0.0, -1e30))
        value = jnp.where(lane == 0, terms[0], jnp.where(lane == 1, terms[1], ones))
        extra[m, h, rows_at(t, 64), :] = value.astype(BF)
        return 0

    lax.fori_loop(0, 104, one, 0)


def rest_block(lengths, randoms, s, m, t):
    r = jnp.maximum(t - 4, 0)
    named = randoms[0, m, 4 * s + r // 3, r % 3]
    _, first = doc_of(lengths, m, 4 * s + 2 * jnp.minimum(t // 2, 1))
    return jnp.where(t < 4, first // 64 + t % 2, named)


def forward_kernel(lengths, randoms, x_ref, wq_in, wk_in, wv_in, wo_in, wu_in, wd_in, v0, v1, v2, v3, v4, v5, v6, v7, b_up,
                   att_out, lse, q_end, xs_out, k_out, v_out, wall, top_out, bias, extra_out, targets,
                   wq, wk, wv, wo, wu, wd, att, q_out, extra, raw_sem, end_sem, own, mate, merged, merged_b, xall0, xall1, xs, ks, vs, wa,
                   mate_sem, lsem, osem, asend, arecv, acrecv, bsend, brecv, bcrecv, xsend, xrecv):
    z, x, y, c = place()
    s = 2 * z + x
    to = {UP: device(z + 1, x, y, c), DOWN: device(z - 1, x, y, c), XX: device(z, 1 - x, y, c),
          YY: device(z, x, 1 - y, c), CC: device(z, x, y, 1 - c)}
    mine, theirs = lanes(c), lanes(1 - c)
    xall = (xall0, xall1)

    def guarded(way, act):
        if way == UP:
            pl.when(z < 3)(act)
        elif way == DOWN:
            pl.when(z > 0)(act)
        else:
            act()

    def x_copy(m, zz, xx, way, own_rows=False):
        i = 2 * zz + xx
        ref = xall[m].at[pl.ds(4 * i, 4)]
        return remote(x_ref.at[m] if own_rows else ref, ref, xsend.at[m, i, way], xrecv.at[m, i], to[way])

    def a_copy(zz, xx, yy, way, src=None):
        i = (2 * zz + xx) * 2 + yy
        ref = wa.at[i, :, mine]
        return remote(ref if src is None else src, ref, asend.at[i, way],
                      acrecv.at[i] if way == CC else arecv.at[i], to[way])

    def b_copy(zz, xx, yy, way, src=None):
        i = (2 * zz + xx) * 2 + yy
        ref = wall.at[i, :, mine]
        return remote(ref if src is None else src, ref, bsend.at[i, way],
                      bcrecv.at[i] if way == CC else brecv.at[i], to[way])

    raw = [pltpu.make_async_copy(src, dst, raw_sem.at[i]) for i, (src, dst) in enumerate(
        zip((wq_in, wk_in, wv_in, wo_in, wu_in, wd_in), (wq, wk, wv, wo, wu, wd)))]
    for cp in raw:
        cp.start()
    greet(z, x, y, c)
    for way in (UP, DOWN, XX):
        guarded(way, lambda way=way: x_copy(0, z, x, way, True).start())
    for m in range(2):
        pltpu.make_async_copy(x_ref.at[m], xall[m].at[pl.ds(4 * s, 4)], lsem.at[m]).start()
    owner = 4 * s + 2 * y + c
    small = jnp.concatenate([v[...].astype(F32) for v in (v0, v1, v2, v3, v4, v5, v6, v7)], axis=0)
    n = small.shape[1]
    own[0:8, :] = pltpu.roll(jnp.concatenate([small, jnp.zeros((8, 768 - n), F32)], axis=1), owner * n, axis=1)
    ups = b_up[...].astype(F32)
    n = ups.shape[1]
    ups = jnp.concatenate([ups, jnp.zeros((1, 768 - n), F32)], axis=1)
    ups = pltpu.roll(jnp.broadcast_to(ups, (8, 768)), (owner % 8) * n, axis=1)
    row = lax.broadcasted_iota(jnp.int32, (8, 768), 0)
    own[8:16, :] = jnp.where(row == owner // 8, ups, 0.0)
    for cp in raw:
        cp.wait()
    for i, ref in enumerate((wq, wk, wv, wo)):
        own[16 + 24 * i:40 + 24 * i, :] = ref[...].astype(F32)
    for j in range(4):
        own[112 + 24 * j:136 + 24 * j, :] = wu[:, 768 * j:768 * j + 768].astype(F32)
    own[208:304, :] = wd[...].astype(F32)
    swap = remote(own.at[:, theirs], mate, mate_sem.at[0], mate_sem.at[1], to[CC])
    swap.start()
    swap.wait()

    def paired(start, n):
        here, there = own[start:start + n, mine], mate[start:start + n, :]
        return jnp.where(c == 0, jnp.concatenate([here, there], 0), jnp.concatenate([there, here], 0)).astype(BF)

    merged[0:16, :] = (own[0:16, mine] + mate[0:16, :]).astype(BF)
    for i in range(3):
        merged[16 + 48 * i:64 + 48 * i, :] = paired(16 + 24 * i, 24)
    keep_a = pltpu.make_async_copy(merged, wa.at[s * 2 + y, :, mine], lsem.at[2])
    keep_a.start()
    for way in WAYS:
        guarded(way, lambda way=way: a_copy(z, x, y, way, merged).start())
    for i in range(5):
        merged_b[48 * i:48 * i + 48, :] = paired(88 + 24 * i, 24)
    merged_b[240:432, :] = paired(208, 96)
    keep_b = pltpu.make_async_copy(merged_b, wall.at[s * 2 + y, :, mine], lsem.at[3])
    keep_b.start()
    write_extra(lengths, randoms, s, extra)
    extra_copy = pltpu.make_async_copy(extra, extra_out, end_sem.at[0])
    extra_copy.start()

    lane = lax.broadcasted_iota(jnp.int32, (1, 1024), 1)
    for m in range(2):
        targets[m] = lax.fori_loop(
            0, 16, lambda t, v, m=m: jnp.where(
                lane // 64 == t, rest_block(lengths, randoms, s, m, t) * 64 + lane % 64, v), jnp.zeros_like(lane))

    def x_line(m, k, a=True):
        def below():
            x_copy(m, z - k, x, UP).wait_recv()
            pl.when(z < 3)(lambda: x_copy(m, z - k, x, UP).start())
            x_copy(m, z - k, x, XX).start()

        def above():
            x_copy(m, z + k, x, DOWN).wait_recv()
            pl.when(z > 0)(lambda: x_copy(m, z + k, x, DOWN).start())
            x_copy(m, z + k, x, XX).start()

        pl.when((z >= k) & (k <= 3))(below)
        pl.when(z + k <= 3)(above)

    def w_line(copy, k):
        def below():
            copy(z - k, x, y, UP).wait_recv()
            pl.when(z < 3)(lambda: copy(z - k, x, y, UP).start())
            for way in (XX, YY, CC):
                copy(z - k, x, y, way).start()

        def above():
            copy(z + k, x, y, DOWN).wait_recv()
            pl.when(z > 0)(lambda: copy(z + k, x, y, DOWN).start())
            for way in (XX, YY, CC):
                copy(z + k, x, y, way).start()

        pl.when((z >= k) & (k <= 3))(below)
        pl.when(z + k <= 3)(above)

    def at_distance(act, k):
        pl.when((k >= 0) & (k <= z))(lambda: act(z - k))
        pl.when((k > 0) & (z + k <= 3))(lambda: act(z + k))

    def w_from_x(copy, k):
        def act(zz):
            copy(zz, 1 - x, y, XX).wait_recv()
            copy(zz, 1 - x, y, YY).start()
            copy(zz, 1 - x, y, CC).start()

        at_distance(act, k)

    def w_from_y(copy, xx, k):
        def act(zz):
            copy(zz, xx, 1 - y, YY).wait_recv()
            copy(zz, xx, 1 - y, CC).start()

        at_distance(act, k)

    zfirst = c == 0

    def b_own_column(k):
        def passed(zz, way, more):
            b_copy(zz, x, y, way).wait_recv()
            pl.when(more)(lambda: b_copy(zz, x, y, way).start())
            b_copy(zz, x, y, YY).start()
            b_copy(zz, x, y, CC).start()

        pl.when((z >= k) & (k <= 3))(lambda: passed(z - k, UP, z < 3))
        pl.when(z + k <= 3)(lambda: passed(z + k, DOWN, z > 0))

    def b_to_x(k):
        def across(zz):
            b_copy(zz, x, y, XX).start()

        pl.when(zfirst)(lambda: at_distance(across, k))

    def b_other_column(k):
        def shared(zz):
            b_copy(zz, 1 - x, y, YY).start()
            b_copy(zz, 1 - x, y, CC).start()

        def crossed(zz):
            b_copy(zz, 1 - x, y, XX).wait_recv()
            shared(zz)

        def passed(zz, way, more):
            b_copy(zz, 1 - x, y, way).wait_recv()
            pl.when(more)(lambda: b_copy(zz, 1 - x, y, way).start())
            shared(zz)

        def first():
            crossed(z)
            pl.when(jnp.logical_not(zfirst) & (z < 3))(lambda: b_copy(z, 1 - x, y, UP).start())
            pl.when(jnp.logical_not(zfirst) & (z > 0))(lambda: b_copy(z, 1 - x, y, DOWN).start())

        def later():
            pl.when(zfirst)(lambda: at_distance(crossed, k))
            pl.when(jnp.logical_not(zfirst) & (z >= k))(lambda: passed(z - k, UP, z < 3))
            pl.when(jnp.logical_not(zfirst) & (z + k <= 3))(lambda: passed(z + k, DOWN, z > 0))

        pl.when(k == 0)(first)
        pl.when((k > 0) & (k <= 3))(later)

    begin = {
        "x0": lambda k: x_line(0, k),
        "x1": lambda k: x_line(1, k),
        "a": lambda k: w_line(a_copy, k),
        "ax": lambda k: w_from_x(a_copy, k),
        "ay0": lambda k: w_from_y(a_copy, x, k),
        "ay1": lambda k: w_from_y(a_copy, 1 - x, k),
        "own x1": lambda ways: [guarded(way, lambda way=way: x_copy(1, z, x, way, True).start()) for way in ways],
        "own b": lambda ways: [guarded(way, lambda way=way: b_copy(z, x, y, way, merged_b).start()) for way in ways],
    }
    for name, what in START:
        begin[name](what)
    keep_a.wait()

    def arrived(i, _):
        ref = wa.at[i, :, theirs]
        remote(ref, ref, asend.at[i, CC], acrecv.at[i], to[CC]).wait_recv()
        return 0

    lax.fori_loop(0, 16, arrived, 0)
    bias[...] = jnp.sum(wa[:, 0:16, :].astype(F32), axis=0)
    top_copy = pltpu.make_async_copy(wa, top_out, lsem.at[4])
    top_copy.start()
    lane = lax.broadcasted_iota(jnp.int32, (HALF, 128), 1)
    ind = block_columns().astype(BF)
    lse[...] = jnp.zeros_like(lse)

    def out_copy(m, t):
        src, dst = ((xs, xs_out), (ks, k_out), (vs, v_out))[t]
        return pltpu.make_async_copy(src.at[m], dst.at[m], osem.at[m, t])

    def x_here(m, k):
        def arrived_x(zz):
            x_copy(m, zz, 1 - x, XX).wait_recv()

        at_distance(arrived_x, k)

    def q_copy(m):
        return pltpu.make_async_copy(q_out.at[m], q_end.at[m], end_sem.at[1 + m])

    def att_copy(m):
        return pltpu.make_async_copy(att.at[m], att_out.at[m], end_sem.at[3 + m])

    def gather_near(m):
        x_here(m, 0)
        x_here(m, 1)
        pltpu.make_async_copy(x_ref.at[m], xall[m].at[pl.ds(4 * s, 4)], lsem.at[m]).wait()
        for t in range(5):
            chunk = xall[m][pl.ds(4 * jnp.clip(s - 2 + t, 0, 7), 4)]
            xs[m, 256 * t:256 * t + 256, :] = chunk.reshape(256, chunk.shape[-1])
        q = (dot(xs[m, 512:768, :], wa[:, 16:64, :].reshape(768, 768)) + bias[0:1, :]).astype(BF)
        q_out[m] = q * jnp.asarray(0.125, BF)
        q_copy(m).start()

    def gather_rest(m):
        x_here(m, 2)
        x_here(m, 3)

        def named(t, _):
            xs[m, pl.ds(pl.multiple_of(NW + 64 * t, 64), 64), :] = xall[m][rest_block(lengths, randoms, s, m, t)]
            return 0

        lax.fori_loop(0, 16, named, 0)
        out_copy(m, 0).start()

    def project(m, r):
        rows = xs[m, r, :]
        ks[m, r, :] = dot(rows, wa[:, 64:112, :].reshape(768, 768)).astype(BF)
        vs[m, r, :] = (dot(rows, wa[:, 112:160, :].reshape(768, 768)) + bias[1:2, :]).astype(BF)

    def pair(m, p):
        col = pl.ds(pl.multiple_of(p * 128, 128), 128)
        for h in range(2):
            r = pl.ds(h * HALF, HALF)
            more = extra[m, h]
            keys = jnp.concatenate([ks[m, a:a + n, col] for a, n in key_rows(h)], axis=0)
            vals = jnp.concatenate([vs[m, a:a + n, col] for a, n in key_rows(h)], axis=0)
            scores = dot_nt(jnp.concatenate([split_heads(q_out[m, r, col]), ind], axis=1),
                            jnp.concatenate([keys, more], axis=1))
            top = jnp.max(scores, axis=1, keepdims=True)
            e = jnp.exp(scores - top).astype(BF)
            o = dot(e, jnp.concatenate([vals, more], axis=1))
            total = o[:, 130:131]
            att[m, r, col] = merge_heads(o[:, :128] / total).astype(BF)
            norm = top + jnp.log(total)
            lse[m, r, :] = jnp.where(lane == 2 * p, norm[:HALF], jnp.where(lane == 2 * p + 1, norm[HALF:], lse[m, r, :]))

    def picked(g, plan):
        k = jnp.full((), 9, jnp.int32)
        for at, value in plan:
            k = jnp.where(g == at, value, k)
        return k

    def pump(g):
        for name in PUMP_ORDER:
            k = picked(g, PUMPS[name])
            act = {
                "x1": lambda k: x_line(1, k), "bo": b_own_column, "bt": b_other_column, "bc": b_to_x,
                "by0": lambda k: w_from_y(b_copy, x, k), "by1": lambda k: w_from_y(b_copy, 1 - x, k),
            }[name]
            act(k)

    def step(g, _):
        m, i = g // 9, g % 9
        for mm in range(2):
            pl.when(g == 9 * mm)(lambda mm=mm: gather_near(mm))
            pl.when(g == 9 * mm + 2)(lambda mm=mm: gather_rest(mm))
        pl.when(i < 2)(lambda: project(m, rows_at(jnp.minimum(i, 1), 640)))
        pl.when(i == 2)(lambda: project(m, pl.ds(NW, NS - NW)))

        @pl.when(i == 3)
        def _():
            out_copy(m, 1).start()
            out_copy(m, 2).start()

        pl.when(i >= 3)(lambda: pair(m, i - 3))
        pl.when(i == 8)(lambda: att_copy(m).start())
        pump(g)
        return 0

    lax.fori_loop(0, 18, step, 0)

    lax.fori_loop(18, 24, lambda g, _: (pump(g), 0)[1], 0)

    def b_arrived(i, _):
        ref = wall.at[i, :, theirs]
        remote(ref, ref, bsend.at[i, CC], bcrecv.at[i], to[CC]).wait_recv()
        return 0

    lax.fori_loop(0, 16, b_arrived, 0)
    keep_b.wait()
    top_copy.wait()
    extra_copy.wait()
    for m in range(2):
        q_copy(m).wait()
        att_copy(m).wait()
        for t in range(3):
            out_copy(m, t).wait()

    def sent(k, _):
        for m in range(2):
            x_copy(m, k, x, XX).wait_send()
        for copy in (a_copy, b_copy):
            for way in (YY, CC):
                copy(k, x, y, way).wait_send()
                copy(k, 1 - x, y, way).wait_send()
            copy(k, x, 1 - y, CC).wait_send()
            copy(k, 1 - x, 1 - y, CC).wait_send()
        a_copy(k, x, y, XX).wait_send()
        pl.when(zfirst | (k == z))(lambda: b_copy(k, x, y, XX).wait_send())

        def line(way):
            x_copy(0, k, x, way).wait_send()
            x_copy(1, k, x, way).wait_send()
            a_copy(k, x, y, way).wait_send()
            b_copy(k, x, y, way).wait_send()
            pl.when(jnp.logical_not(zfirst))(lambda: b_copy(k, 1 - x, y, way).wait_send())

        pl.when((k <= z) & (z < 3))(lambda: line(UP))
        pl.when((k >= z) & (z > 0))(lambda: line(DOWN))
        return 0

    lax.fori_loop(0, 4, sent, 0)


START = (
    ("x0", 1),
    ("a", 1),
    ("ay0", 0),
    ("ax", 0),
    ("a", 2),
    ("a", 3),
    ("x0", 2),
    ("own x1", (UP, DOWN,)),
    ("ax", 2),
    ("ax", 1),
    ("x0", 3),
    ("ay0", 1),
    ("ay0", 3),
    ("ay1", 2),
    ("own b", (UP, DOWN,)),
    ("ax", 3),
    ("ay1", 3),
    ("ay0", 2),
    ("ay1", 0),
    ("own b", (XX,)),
    ("own x1", (XX,)),
    ("ay1", 1),
    ("own b", (YY, CC,)),
    ("x1", 1),
)
PUMP_ORDER = ("x1", "bo", "bc", "bt", "by0", "by1")
PUMPS = {
    "x1": ((2, 2), (9, 3),),
    "bo": ((0, 1), (5, 2), (10, 3),),
    "bt": ((2, 0), (9, 1), (11, 2), (14, 3),),
    "bc": ((0, 1), (9, 2), (11, 3),),
    "by0": ((2, 0), (5, 1), (11, 2), (15, 3),),
    "by1": ((9, 0), (13, 1), (14, 2), (16, 3),),
}


def forward_all(lengths, randoms, x, weights, vectors, b_up):
    dma = pltpu.SemaphoreType.DMA
    sd = jax.ShapeDtypeStruct
    vm, anywhere, sm = (pl.BlockSpec(memory_space=m) for m in (pltpu.VMEM, pl.ANY, pltpu.SMEM))
    mb, rows, width = x.shape
    v = pltpu.VMEM
    return pl.pallas_call(
        forward_kernel,
        out_shape=[
            sd((mb, rows, width), BF), sd((mb, rows, 128), F32), sd((mb, rows, width), BF),
            sd((mb, NS, width), BF), sd((mb, NS, width), BF), sd((mb, NS, width), BF),
            sd((16, REST, width), BF), sd((16, TOP, width), BF), sd((16, width), F32),
            sd((mb, 2, NK, 128), BF), sd((mb, 1, 1024), jnp.int32),
        ],
        in_specs=[sm, sm] + [anywhere] * 7 + [vm] * 9,
        out_specs=[anywhere, vm] + [anywhere] * 6 + [vm, anywhere, vm],
        scratch_shapes=[
            *[v(w.shape, BF) for w in weights], v((mb, rows, width), BF), v((mb, rows, width), BF),
            v((mb, 2, NK, 128), BF), dma((6,)), dma((5,)),
            v((304, width), F32), v((304, 384), F32), v((TOP, 384), BF), v((REST, 384), BF),
            v((8 * rows // 64, 64, width), BF), v((8 * rows // 64, 64, width), BF),
            v((mb, NS, width), BF), v((mb, NS, width), BF), v((mb, NS, width), BF),
            v((16, TOP, width), BF),
            dma((2,)), dma((5,)), dma((mb, 3)),
            dma((16, 5)), dma((16,)), dma((16,)), dma((16, 5)), dma((16,)), dma((16,)),
            dma((mb, 8, 3)), dma((mb, 8)),
        ],
        compiler_params=pltpu.CompilerParams(
            collective_id=0, has_side_effects=True, vmem_limit_bytes=60 * 2**20
        ),
    )(lengths, randoms, x.reshape(mb, rows // 64, 64, width), *weights, *vectors, b_up)


def backward_kernel(datt, stats, tgt, gb_in, extra_in, q_in, done, k_in, v_in, xs_in, top_in, go, gu, gd,
                    oq, ok, ov, oo, ou, od, ob, odx,
                    kb, vb, xsb, wa, extra, dka, dva, q, ga, gb,
                    acc, mate, yr, mate2, yr2, xr, zr, dxp, dxr, dzr, fin, rcv,
                    ksem, lsem, msem, msem2, asem, ysem, xsem, zsem, ysem2, xsem2, zsem2, dxsem, dzsem, fsem, ready):
    z, x, y, c = place()
    s = 2 * z + x
    mine, theirs = lanes(c), lanes(1 - c)
    near_x, near_y, near_c = device(z, 1 - x, y, c), device(z, x, 1 - y, c), device(z, x, y, 1 - c)
    above, below = device(z + 1, x, y, c), device(z - 1, x, y, c)

    def far(i):
        inner = jnp.where(i == 0, 3, jnp.where(i == 1, 0, jnp.where(i == 2, 2, 1)))
        low = jnp.where(z == 0, 3 - i, jnp.where(z == 1, inner, i))
        return jnp.where(z == 2, 3 - inner, low)

    def slot_of(i, zz):
        zt = jnp.where(zz == 0, 3 - i, jnp.where((zz == 1) & (i == 2), 2, 3))
        return zt, (zz == 0) | ((zz == 1) & (i >= 1)) | ((zz == 2) & (i == 2))

    def at_slot(act, i):
        up, sends_up = slot_of(i, z)
        down, sends_down = slot_of(i, 3 - z)
        pl.when(sends_up)(lambda: act(up, True))
        pl.when(sends_down)(lambda: act(3 - down, False))

    def column(p):
        return pl.ds(pl.multiple_of(p * 128, 128), 128)

    def load_keys(m, p):
        return (pltpu.make_async_copy(k_in.at[m, :, column(p)], kb.at[:, column(p)], ksem.at[0, p]),
                pltpu.make_async_copy(v_in.at[m, :, column(p)], vb.at[:, column(p)], ksem.at[1, p]))

    def start_keys(m):
        def one(p, _):
            for cp in load_keys(m, p):
                cp.start()
            return 0

        lax.fori_loop(0, 6, one, 0)

    start_keys(0)
    extra_copy = pltpu.make_async_copy(extra_in, extra, lsem.at[4])
    extra_copy.start()
    q_copy = pltpu.make_async_copy(q_in, q, lsem.at[3])
    q_copy.start()
    top_copy = pltpu.make_async_copy(top_in.at[:, :, pl.ds(16, 144), :], wa, lsem.at[0])
    top_copy.start()
    done_copy = pltpu.make_async_copy(done, odx, lsem.at[1])
    done_copy.start()
    greet(z, x, y, c)

    def parts(yy, cc):
        off = pl.multiple_of(cc * 384, 128)
        yield 0, go.at[:, yy, :, pl.ds(off, 384)], pl.ds(0, 48)
        yield 1, gd.at[:, yy, :, pl.ds(off, 384)], pl.ds(240, 192)
        for j in range(4):
            col = pl.multiple_of(j * 768 + cc * 384, 128)
            yield 2 + j, gu.at[:, yy, :, pl.ds(col, 384)], pl.ds(48 + 48 * j, 48)

    swaps, loads = {}, {}
    for t, yy in enumerate((1 - y, y)):
        for i, src, rows in parts(yy, 1 - c):
            swaps[t, i] = remote(src, mate.at[:, yy, rows, :], msem.at[0, t, i], msem.at[1, t, i], near_c)
            swaps[t, i].start()
        for i, src, rows in parts(yy, c):
            loads[t, i] = pltpu.make_async_copy(src, acc.at[:, yy, rows, :], asem.at[t, i])
            loads[t, i].start()
    gb[...] = gb_in[...]

    class Reduce:
        def __init__(self, rows, held, cols, other, from_y, ys, xs_, zs):
            self.rows, self.held, self.cols, self.other, self.from_y = rows, held, cols, other, from_y
            self.ys, self.xs, self.zs = ys, xs_, zs

        def a(self, s_, yy):
            return self.held.at[s_, yy, :, self.cols]

        def y_copy(self, s_):
            return remote(self.a(s_, 1 - y), self.from_y.at[s_], self.ys.at[0, s_], self.ys.at[1, s_], near_y)

        def x_copy(self, zz):
            return remote(self.a(2 * zz + 1 - x, y), xr.at[zz, pl.ds(0, self.rows), :], self.xs.at[0, zz],
                          self.xs.at[1, zz], near_x)

        def z_copy(self, zz, slot, to):
            return remote(self.a(2 * zz + x, y), zr.at[slot, pl.ds(0, self.rows), :], self.zs.at[0, zz],
                          self.zs.at[1, slot], to)

        def total(self, s_, yy, others):
            value = self.held[s_, yy, :, self.cols].astype(F32) + self.other[s_, yy].astype(F32)
            for ref, index in others:
                value = value + ref[index, 0:self.rows, :].astype(F32)
            return value

        def keep(self, s_, yy, value):
            self.held[s_, yy, :, self.cols] = value.astype(BF)

        def y_step(self, i):
            s_ = 2 * far(i % 4) + jnp.where(i < 4, 1 - x, x)
            self.keep(s_, 1 - y, self.total(s_, 1 - y, []))
            self.y_copy(s_).start()

        def x_step(self, i):
            zz = far(i)
            s_ = 2 * zz + 1 - x
            self.y_copy(s_).wait_recv()
            self.keep(s_, y, self.total(s_, y, [(self.from_y, s_)]))
            self.x_copy(zz).start()

        def along(self, zz, up):
            s_ = 2 * zz + x
            self.y_copy(s_).wait_recv()
            self.x_copy(zz).wait_recv()
            others = [(self.from_y, s_), (xr, zz)]
            more = z > 0 if up else z < 3

            @pl.when(more)
            def _():
                self.z_copy(zz, zz, above).wait_recv()
                self.keep(s_, y, self.total(s_, y, others + [(zr, zz)]))

            @pl.when(jnp.logical_not(more))
            def _():
                self.keep(s_, y, self.total(s_, y, others))

            if up:
                self.z_copy(zz, zz, above).start()
            else:
                self.z_copy(zz, jnp.where(zz == z - 1, 4, zz), below).start()

        def z_step(self, i):
            at_slot(self.along, i)

        def finish(self):
            self.y_copy(s).wait_recv()
            self.x_copy(z).wait_recv()
            r = pl.ds(0, self.rows)
            fin[r, :] = self.total(s, y, [(self.from_y, s), (xr, z)])
            for slot, cond in ((z, z > 0), (4, z < 3)):
                @pl.when(cond)
                def _(slot=slot):
                    self.z_copy(z, slot, above).wait_recv()
                    fin[r, :] += zr[slot, r, :].astype(F32)

        def drain(self):
            def one(i, _):
                self.y_copy(i).wait_send()
                return 0

            lax.fori_loop(0, 8, one, 0)

            def two(i, _):
                self.x_copy(i).wait_send()
                pl.when(i != z)(lambda: self.z_copy(i, i, above).wait_send())
                return 0

            lax.fori_loop(0, 4, two, 0)

    rest = Reduce(REST, acc, pl.ds(0, 384), mate, yr, ysem, xsem, zsem)
    top = Reduce(TOP, ga, mine, mate2, yr2, ysem2, xsem2, zsem2)

    def dx_x(m, zz):
        return remote(dxp.at[m, 2 * zz + 1 - x], dxr.at[m, zz], dxsem.at[0, m, zz], dxsem.at[1, m, zz], near_x)

    def dx_z(m, zz, slot, to):
        return remote(dxp.at[m, 2 * zz + x], dzr.at[m, slot], dzsem.at[0, m, zz], dzsem.at[1, m, slot], to)

    def dx_along(m, zz, up):
        s_ = 2 * zz + x
        dx_x(m, zz).wait_recv()
        more = z > 0 if up else z < 3

        @pl.when(more)
        def _():
            dx_z(m, zz, zz, above).wait_recv()
            dxp[m, s_] = (dxp[m, s_].astype(F32) + dxr[m, zz].astype(F32) + dzr[m, zz].astype(F32)).astype(BF)

        @pl.when(jnp.logical_not(more))
        def _():
            dxp[m, s_] = (dxp[m, s_].astype(F32) + dxr[m, zz].astype(F32)).astype(BF)

        if up:
            dx_z(m, zz, zz, above).start()
        else:
            dx_z(m, zz, jnp.where(zz == z - 1, 4, zz), below).start()

    def dx_step(m, i):
        at_slot(functools.partial(dx_along, m), i)

    def dx_finish(m):
        dx_x(m, z).wait_recv()
        odx[m] += dxr[m, z].astype(F32)
        for slot, cond in ((z, z > 0), (4, z < 3)):
            @pl.when(cond)
            def _(slot=slot):
                dx_z(m, z, slot, above).wait_recv()
                odx[m] += dzr[m, slot].astype(F32)

    def dx_sent(m):
        def one(i, _):
            dx_x(m, i).wait_send()
            pl.when(i != z)(lambda: dx_z(m, i, i, above).wait_send())
            return 0

        lax.fori_loop(0, 4, one, 0)

    ind = block_columns()

    def pair(m, p):
        col = column(p)
        for cp in load_keys(m, p):
            cp.wait()
        dka[...] = jnp.zeros_like(dka)
        dva[...] = jnp.zeros_like(dva)
        for h in range(2):
            rows = pl.ds(h * HALF, HALF)
            qs = split_heads(q[m, rows, col])
            dos = split_heads(datt[m, rows, col])
            lane = lax.broadcasted_iota(jnp.int32, (HALF, 128), 1)

            def both(first, rows=rows, lane=lane):
                return jnp.concatenate(
                    [jnp.sum(jnp.where(lane == first + a, stats[m, rows, :], 0.0), axis=1, keepdims=True) for a in range(2)],
                    axis=0)

            log_norm, delta = both(2 * p), both(16 + 2 * p)
            qe = jnp.concatenate([qs, with_column(ind, -log_norm)], axis=1)
            doe = jnp.concatenate([dos, with_column(jnp.zeros_like(ind), -delta)], axis=1)
            dqt = jnp.zeros((128, 2 * HALF), F32)
            (wa_, wn), (ga, gn), (ra, rn) = key_rows(h)
            off = 0
            for pieces in (((wa_, 576),), ((wa_ + 576, 576),), ((ga, gn), (ra, rn))):
                n = sum(t for _, t in pieces)
                k2 = jnp.concatenate([kb[a:a + t, col] for a, t in pieces], axis=0)
                v2 = jnp.concatenate([vb[a:a + t, col] for a, t in pieces], axis=0)
                more = extra[m, h, off:off + n, :]
                pt = jnp.exp(dot_nt(jnp.concatenate([k2, more], axis=1), qe))
                ds = (pt * dot_nt(jnp.concatenate([v2, more], axis=1), doe)).astype(BF)
                dv_ = dot(pt.astype(BF), dos)
                dk_ = dot(ds, qs)
                dqt = dqt + dot(k2.T, ds)
                if off < WK:
                    a, t = pieces[0]
                    dka[a:a + t, :] += dk_
                    dva[a:a + t, :] += dv_
                else:
                    at = 0
                    for a, t in pieces:
                        kb[a:a + t, col] = dk_[at:at + t].astype(BF)
                        vb[a:a + t, col] = dv_[at:at + t].astype(BF)
                        at += t
                off += n
            q[m, rows, col] = (merge_heads(dqt.T) * 0.125).astype(BF)
        kb[0:NW, col] = dka[...].astype(BF)
        vb[0:NW, col] = dva[...].astype(BF)

    def weight(i):
        return wa[:, :, 48 * i:48 + 48 * i, :].reshape(768, 768)

    def dx_rows(m, i):
        for part in range(2):
            r = rows_at(2 * i + part, 384)
            value = dot_nt(kb[r, :], weight(1)) + dot_nt(vb[r, :], weight(2))
            xsb[r, :] = value.astype(BF)
            if part == 1:
                @pl.when(i == 0)
                def _(value=value):
                    odx[m] += value[128:384] + dot_nt(q[m], weight(0))

    def dx_piece(m, i):
        t = 2 * far(i % 4) + jnp.where(i < 4, 1 - x, x)
        row = lax.broadcasted_iota(jnp.int32, (256, 1024), 0) + 256 * t
        chosen = jnp.where(row == tgt[m], 1.0, 0.0).astype(BF)
        value = dot(chosen, xsb[NW:NS, :])
        w = t - s + 2

        @pl.when(t == s)
        def _():
            odx[m] += value

        @pl.when(t != s)
        def _():
            near = xsb[rows_at(jnp.clip(w, 0, 4), 256), :].astype(F32)
            dxp[m, t] = (value + jnp.where((w >= 0) & (w < 5), near, 0.0)).astype(BF)

        pl.when(i < 4)(lambda: dx_x(m, far(i % 4)).start())

    def weight_grads(m, i):
        cols = pl.ds(pl.multiple_of(384 * i, 128), 384)
        a = xsb[:, cols]
        chips = pl.ds(4 * i, 4)

        def keep(row, value, n):
            value = value.reshape(4, 2, 48, value.shape[1])

            @pl.when(m == 0)
            def _():
                ga[chips, :, row:row + 48, n] = value.astype(BF)

            @pl.when(m == 1)
            def _():
                ga[chips, :, row:row + 48, n] = (ga[chips, :, row:row + 48, n].astype(F32) + value).astype(BF)

        for half in range(2):
            n = slice(384 * half, 384 * half + 384)
            keep(64, dot_tn(a, kb[:, n]), n)
            keep(112, dot_tn(a, vb[:, n]), n)
        keep(16, dot_tn(a[512:768], q[m]), slice(0, 768))

    def small_grads():
        low = gb[...].astype(BF)

        def spread(i, _):
            ga[i // 2, i % 2, 0:16, :] = low
            return 0

        lax.fori_loop(0, 16, spread, 0)

    swap2 = [remote(ga.at[:, yy, :, theirs], mate2.at[:, yy], msem2.at[0, t], msem2.at[1, t], near_c)
             for t, yy in enumerate((1 - y, y))]

    def rest_rows(cc):
        yield oo, 0, pl.multiple_of(24 * cc, 8), 24, 0
        for j in range(4):
            yield ou, 24 + 24 * j, pl.multiple_of(48 + 48 * j + 24 * cc, 8), 24, 768 * j
        yield od, 120, pl.multiple_of(240 + 96 * cc, 8), 96, 0

    def top_rows(cc):
        yield ob, 216, 0, 16, 0
        for i, ref in enumerate((oq, ok, ov)):
            yield ref, 232 + 24 * i, pl.multiple_of(16 + 48 * i + 24 * cc, 8), 24, 0

    def to_mate(rows_of, first):
        return [remote(fin.at[pl.ds(start, n), :], rcv.at[at:at + n, :], fsem.at[0, first + i], fsem.at[1, first + i], near_c)
                for i, (_, at, start, n, _) in enumerate(rows_of(1 - c))]

    def hand_over(rows_of):
        for ref, at, start, n, col in rows_of(c):
            ref[:, pl.ds(pl.multiple_of(col + c * 384, 128), 384)] = fin[pl.ds(start, n), :]

    def take_over(rows_of):
        for ref, at, start, n, col in rows_of(c):
            ref[:, pl.ds(pl.multiple_of(col + (1 - c) * 384, 128), 384)] = rcv[at:at + n, :]

    last0 = to_mate(rest_rows, 0)

    def picked(g, plan):
        k = jnp.full((), 9, jnp.int32)
        for at, value in plan:
            k = jnp.where(g == at, value, k)
        return k

    def start_top(_):
        swap2[0].wait_recv()
        swap2[1].wait_recv()
        lax.fori_loop(0, 8, lambda i, _: (top.y_step(i), 0)[1], 0)

    def tell(to):
        pl.semaphore_signal(ready, inc=1, device_id=to, device_id_type=MESH)

    def end_rest(_):
        rest.finish()
        for to in (near_x, near_y, near_c):
            tell(to)
        pl.when(z > 0)(lambda: tell(below))
        pl.when(z < 3)(lambda: tell(above))
        for cp in last0:
            cp.start()
        hand_over(rest_rows)

    def all_ready(_):
        pl.semaphore_wait(ready, 3 + (z > 0).astype(jnp.int32) + (z < 3).astype(jnp.int32))

    acts = {
        "Y": rest.y_step, "X": rest.x_step, "Z": rest.z_step, "BF": end_rest, "W": all_ready,
        "D0": functools.partial(dx_step, 0), "D0F": lambda _: dx_finish(0), "D1": functools.partial(dx_step, 1),
        "TY": start_top, "TX": top.x_step, "TZ": top.z_step,
    }

    def pump(g, first, last_):
        for name in STEP_ORDER:
            plan = [(at, k) for at, k in STEPS[name] if first <= at < last_]
            if plan:
                k = picked(g, plan)
                pl.when(k < 9)(lambda name=name, k=k: acts[name](k))

    for i in range(6):
        loads[0, i].wait()
        swaps[0, i].wait_recv()
    rest.y_step(0)
    done_copy.wait()
    q_copy.wait()
    extra_copy.wait()

    def load_xs(m):
        return pltpu.make_async_copy(xs_in.at[m], xsb, lsem.at[2])

    def micro(m, _):
        load_xs(m).start()

        def one(i, _):
            @pl.when(i < 6)
            def _():
                pair(m, jnp.minimum(i, 5))

            @pl.when((m == 0) & (i == MATE_AT))
            def _():
                for t in range(6):
                    loads[1, t].wait()
                    swaps[1, t].wait_recv()
                top_copy.wait()

            pl.when(i == 6)(lambda: load_xs(m).wait())
            pl.when((i >= 6) & (i < 8))(lambda: weight_grads(m, jnp.clip(i - 6, 0, 1)))

            @pl.when(i == 8)
            def _():
                gb[0:1, :] += jnp.sum(q[m].astype(F32), axis=0, keepdims=True)

                def value_bias(t, _):
                    gb[1:2, :] += jnp.sum(vb[rows_at(t, 256), :].astype(F32), axis=0, keepdims=True)
                    return 0

                lax.fori_loop(0, 9, value_bias, 0)

            pl.when(i >= 9)(lambda: dx_rows(m, jnp.clip(i - 9, 0, 2)))
            pump(12 * m + i, 0, 24)

            @pl.when((m == 1) & (i == 8))
            def _():
                small_grads()
                for cp in swap2:
                    cp.start()

            return 0

        lax.fori_loop(0, 12, one, 0)
        pl.when(m == 0)(lambda: start_keys(1))
        lax.fori_loop(0, 8, lambda i, _: (dx_piece(m, i), 0)[1], 0)
        return 0

    lax.fori_loop(0, 2, micro, 0)
    lax.fori_loop(24, 38, lambda g, _: (pump(g, 24, 38), 0)[1], 0)
    dx_finish(1)
    for cp in last0:
        cp.wait()
    take_over(rest_rows)
    top.finish()
    last1 = to_mate(top_rows, 6)
    for cp in last1:
        cp.start()
    hand_over(top_rows)
    for cp in last1:
        cp.wait()
    take_over(top_rows)
    top.drain()
    rest.drain()
    for t in range(2):
        for i in range(6):
            swaps[t, i].wait_send()
    dx_sent(0)
    dx_sent(1)
    for cp in swap2:
        cp.wait_send()


STEP_ORDER = ("Y", "BF", "W", "TY", "TX", "Z", "X", "D0F", "D1", "TZ", "D0")
STEPS = {
    "Y": ((0, 1), (4, 2), (5, 3), (6, 4), (7, 5), (9, 6), (17, 7),),
    "X": ((3, 0), (5, 1), (7, 2), (13, 3),),
    "Z": ((12, 0), (16, 1), (19, 2),),
    "D0": ((14, 0), (18, 1), (23, 2),),
    "TY": ((24, 0),),
    "BF": ((27, 0),),
    "W": ((27, 0),),
    "D0F": ((32, 0),),
    "TX": ((27, 0), (29, 1), (33, 2), (37, 3),),
    "D1": ((25, 0), (28, 1), (29, 2),),
    "TZ": ((31, 0), (33, 1), (37, 2),),
}
MATE_AT = 3


def backward_all(datt, stats, tgt, gb, extra, q, done, k, v, xs, top, go, gu, gd):
    dma = pltpu.SemaphoreType.DMA
    sd = jax.ShapeDtypeStruct
    vm, anywhere = (pl.BlockSpec(memory_space=m) for m in (pltpu.VMEM, pl.ANY))
    mb, rows, width = q.shape
    s = pltpu.VMEM
    views = [top.reshape(8, 2, TOP, width), go.reshape(8, 2, 48, width), gu.reshape(8, 2, 48, 4 * width),
             gd.reshape(8, 2, 192, width)]
    return pl.pallas_call(
        backward_kernel,
        out_shape=[sd((24, width), F32)] * 4 + [sd((24, 4 * width), F32), sd((96, width), F32), sd((16, width), F32),
                                                sd(q.shape, F32)],
        in_specs=[vm] * 4 + [anywhere] * 10,
        out_specs=[vm] * 8,
        scratch_shapes=[
            s((NS, width), BF), s((NS, width), BF), s((NS, width), BF), s((8, 2, TOP - 16, width), BF),
            s((mb, 2, NK, 128), BF), s((NW, 128), F32), s((NW, 128), F32), s((mb, rows, width), BF),
            s((8, 2, TOP, width), BF), s((16, width), F32),
            s((8, 2, REST, 384), BF), s((8, 2, REST, 384), BF), s((8, REST, 384), BF), s((8, 2, TOP, 384), BF), s((8, TOP, 384), BF),
            s((4, REST, 384), BF),
            s((5, REST, 384), BF),
            s((mb, 8, rows, width), BF), s((mb, 4, rows, width), BF), s((mb, 5, rows, width), BF),
            s((REST, 384), F32), s((304, 384), F32),
            dma((2, 6)), dma((5,)), dma((2, 2, 6)), dma((2, 2)), dma((2, 6)),
            dma((2, 8)), dma((2, 4)), dma((2, 5)), dma((2, 8)), dma((2, 4)), dma((2, 5)),
            dma((2, mb, 4)), dma((2, mb, 5)), dma((2, 10)), pltpu.SemaphoreType.REGULAR,
        ],
        compiler_params=pltpu.CompilerParams(
            collective_id=1, has_side_effects=True, vmem_limit_bytes=62 * 2**20
        ),
    )(datt, stats, tgt, gb, extra, q, done, k, v, xs, *views)


CHUNKS = 9


def project_kernel(idx, xall, wall, bias, xs_ref, k_ref, v_ref, q_ref, xs, w, sems, wsem):
    m, i = pl.program_id(0), pl.program_id(1)

    @pl.when((m == 0) & (i == 0))
    def _():
        copy = pltpu.make_async_copy(wall.at[:, pl.ds(16, 144), :], w, wsem)
        copy.start()
        for mm in range(2):
            for cc in range(CHUNKS):
                pieces = [(0, 256)] if cc < 5 else [(0, 128), (128, 128)] if cc == 5 else [(64 * t, 64) for t in range(4)]
                base = cc if cc < 5 else 5 if cc == 5 else 7 + 4 * (cc - 6)
                for t, (off, n) in enumerate(pieces):
                    start = pl.multiple_of(idx[mm, base + t], 64)
                    pltpu.make_async_copy(xall.at[mm, pl.ds(start, n), :], xs.at[mm, cc, pl.ds(off, n), :],
                                          sems.at[mm, cc]).start()
        copy.wait()

    pltpu.make_async_copy(xall.at[0, pl.ds(0, 256), :], xs.at[m, i], sems.at[m, i]).wait()
    rows = xs[m, i]
    xs_ref[0] = rows
    k_ref[0] = dot(rows, w[:, 48:96, :].reshape(768, 768)).astype(BF)
    v_ref[0] = (dot(rows, w[:, 96:144, :].reshape(768, 768)) + bias[1:2, :]).astype(BF)

    @pl.when(i == 2)
    def _():
        q = (dot(rows, w[:, 0:48, :].reshape(768, 768)) + bias[0:1, :]).astype(BF)
        q_ref[0] = q * jnp.asarray(0.125, BF)


def project(idx, xall, wall, bias):
    mb = xall.shape[0]
    sd = jax.ShapeDtypeStruct
    chunk = pl.BlockSpec((1, 256, 768), lambda m, i, t: (m, i, 0))
    return pl.pallas_call(
        project_kernel,
        grid_spec=pltpu.PrefetchScalarGridSpec(
            num_scalar_prefetch=1,
            grid=(mb, CHUNKS),
            in_specs=[pl.BlockSpec(memory_space=pl.ANY)] * 2 + [pl.BlockSpec((16, 768), lambda m, i, t: (0, 0))],
            out_specs=[chunk, chunk, chunk, pl.BlockSpec((1, 256, 768), lambda m, i, t: (m, 0, 0))],
            scratch_shapes=[
                pltpu.VMEM((mb, CHUNKS, 256, 768), BF), pltpu.VMEM((16, 144, 768), BF),
                pltpu.SemaphoreType.DMA((mb, CHUNKS)), pltpu.SemaphoreType.DMA,
            ],
        ),
        out_shape=[sd((mb, NS, 768), BF)] * 3 + [sd((mb, 256, 768), BF)],
        compiler_params=pltpu.CompilerParams(vmem_limit_bytes=48 * 2**20),
    )(idx, xall, wall, bias)


EPS = 1e-6
G0, G1 = 0.7978845608, 0.044715


def norm(v):
    mean = jnp.mean(v, axis=-1, keepdims=True)
    centred = v - mean
    inverse = lax.rsqrt(jnp.mean(centred * centred, axis=-1, keepdims=True) + EPS)
    return centred * inverse, inverse


def norm_back(g, normed, inverse, gain):
    c = g * gain
    return inverse * (c - jnp.mean(c, axis=-1, keepdims=True)
                      - normed * jnp.mean(c * normed, axis=-1, keepdims=True))


def middle_kernel(att, x_in, cot_in, wall, bias, lse_in, out_ref, stats_ref, datt_ref, done_ref, go_out, gu_out, gd_out, gb_ref,
                  x, cot, lse, isem, go_ref, gu_ref, gd_ref, gsem, w, wsem, pre, hid, mid, low, n1, r1, ffn):
    rows = att.shape[0]
    def load(j, t):
        if t == 0:
            src, dst = wall.at[:, pl.ds(0, 48), :], w.at[:, pl.ds(0, 48), :]
        elif t == 1:
            at = pl.ds(pl.multiple_of(48 + 48 * j, 16), 48)
            src, dst = wall.at[:, at, :], w.at[:, at, :]
        else:
            at = pl.ds(4 * j, 4)
            src, dst = wall.at[at, pl.ds(240, 192), :], w.at[at, pl.ds(240, 192), :]
        return pltpu.make_async_copy(src, dst, wsem.at[t, j])

    inputs = [pltpu.make_async_copy(src, dst, isem.at[i])
              for i, (src, dst) in enumerate(((x_in, x), (cot_in, cot), (lse_in, lse)))]
    load(0, 0).start()
    inputs[0].start()
    for j in range(4):
        load(j, 1).start()
        load(j, 2).start()
    inputs[1].start()
    inputs[2].start()
    half = rows
    load(0, 0).wait()
    inputs[0].wait()
    w_out = w[:, 0:48, :].reshape(768, 768)
    for h in range(1):
        r = pl.ds(h * half, half)
        t = x[r, :].astype(F32) + dot(att[r, :], w_out) + bias[2:3, :]
        normed, inverse = norm(t)
        n1[r, :] = normed
        r1[r, :] = jnp.broadcast_to(inverse, (half, 128))
        value = normed * bias[4:5, :] + bias[5:6, :]
        mid[r, :] = value
        low[r, :] = value.astype(BF)
    ffn[...] = jnp.broadcast_to(bias[3:4, :], ffn.shape)

    def up_block(j):
        return w[:, pl.ds(pl.multiple_of(48 + 48 * j, 16), 48), :].reshape(768, 768)

    def down_block(j):
        return w[pl.ds(4 * j, 4), 240:432, :].reshape(768, 768)

    def forward(j, _):
        load(j, 1).wait()
        load(j, 2).wait()
        wu, wd = up_block(j), down_block(j)
        for h in range(1):
            r = pl.ds(h * half, half)
            u = dot(low[r, :], wu) + bias[pl.ds(8 + j, 1), :]
            square = u * u
            th = jnp.tanh(G0 * u * (1.0 + G1 * square))
            half_u, one = 0.5 * u, 1.0 + th
            pre[j, r, :] = 0.5 * one + half_u * (one * (1.0 - th)) * (G0 + (3.0 * G0 * G1) * square)
            g = (half_u * one).astype(BF)
            hid[j, r, :] = g
            ffn[r, :] += dot(g, wd)
        return 0

    lax.fori_loop(0, 4, forward, 0)
    gb_ref[...] = jnp.zeros_like(gb_ref)
    inputs[1].wait()
    inputs[2].wait()
    for h in range(1):
        r = pl.ds(h * half, half)
        normed, inverse = norm(mid[r, :] + ffn[r, :])
        out_ref[r, :] = (normed * bias[6:7, :] + bias[7:8, :]).astype(BF)
        g = cot[r, :].astype(F32)
        gb_ref[6:7, :] += jnp.sum(g * normed, axis=0, keepdims=True)
        gb_ref[7:8, :] += jnp.sum(g, axis=0, keepdims=True)
        d_two = norm_back(g, normed, inverse, bias[6:7, :])
        mid[r, :] = d_two
        d_ffn = d_two.astype(BF)
        datt_ref[r, :] = d_ffn
        gb_ref[3:4, :] += jnp.sum(d_ffn.astype(F32), axis=0, keepdims=True)

    def sent(ref, out, j, t):
        at = pl.ds(pl.multiple_of(j * 768, 768), 768)
        return pltpu.make_async_copy(ref.at[j], out.at[at, :] if t == 0 else out.at[:, at], gsem.at[t, j])

    def backward(j, _):
        wu, wd = up_block(j), down_block(j)
        d_ffn = datt_ref[...]
        gd_ref[j] = dot_tn(hid[j], d_ffn).astype(BF)
        sent(gd_ref, gd_out, j, 0).start()
        for h in range(1):
            r = pl.ds(h * half, half)
            d_pre = (dot_nt(datt_ref[r, :], wd) * pre[j, r, :]).astype(BF)
            hid[j, r, :] = d_pre
            gb_ref[pl.ds(8 + j, 1), :] += jnp.sum(d_pre.astype(F32), axis=0, keepdims=True)
            mid[r, :] += dot_nt(d_pre, wu)
        gu_ref[j] = dot_tn(low[...], hid[j]).astype(BF)
        sent(gu_ref, gu_out, j, 1).start()
        return 0

    lax.fori_loop(0, 4, backward, 0)
    for h in range(1):
        r = pl.ds(h * half, half)
        d_mid, normed = mid[r, :], n1[r, :]
        gb_ref[4:5, :] += jnp.sum(d_mid * normed, axis=0, keepdims=True)
        gb_ref[5:6, :] += jnp.sum(d_mid, axis=0, keepdims=True)
        d_one = norm_back(d_mid, normed, r1[r, 0:1], bias[4:5, :])
        done_ref[r, :] = d_one
        d_branch = d_one.astype(BF)
        low[r, :] = d_branch
        gb_ref[2:3, :] += jnp.sum(d_branch.astype(F32), axis=0, keepdims=True)
        d_att = dot_nt(d_branch, w_out).astype(BF)
        datt_ref[r, :] = d_att
        product = d_att.astype(F32) * att[r, :].astype(F32)
        lane = lax.broadcasted_iota(jnp.int32, (half, 128), 1)
        stats = lse[r, :]
        for p in range(6):
            two = product[:, 128 * p:128 * p + 128]
            stats = jnp.where(lane == 16 + 2 * p, jnp.sum(jnp.where(lane < 64, two, 0.0), axis=1, keepdims=True), stats)
            stats = jnp.where(lane == 17 + 2 * p, jnp.sum(jnp.where(lane >= 64, two, 0.0), axis=1, keepdims=True), stats)
        stats_ref[r, :] = stats
    go_ref[...] = dot_tn(att[...], low[...]).astype(BF)
    go_copy = pltpu.make_async_copy(go_ref, go_out, isem.at[3])
    go_copy.start()
    for j in range(4):
        sent(gd_ref, gd_out, j, 0).wait()
        sent(gu_ref, gu_out, j, 1).wait()
    go_copy.wait()


def middle(att, x, cot, wall, bias, lse):
    rows = att.shape[0]
    sd = jax.ShapeDtypeStruct
    vm, anywhere = pl.BlockSpec(memory_space=pltpu.VMEM), pl.BlockSpec(memory_space=pl.ANY)
    return pl.pallas_call(
        middle_kernel,
        in_specs=[vm, anywhere, anywhere, anywhere, vm, anywhere],
        out_specs=[vm] * 4 + [pl.BlockSpec(memory_space=pl.ANY)] * 3 + [vm],
        out_shape=[sd((rows, 768), BF), sd((rows, 128), F32), sd((rows, 768), BF), sd((rows, 768), F32), sd((768, 768), BF),
                   sd((768, 3072), BF), sd((3072, 768), BF), sd((16, 768), F32)],
        scratch_shapes=[
            pltpu.VMEM((rows, 768), BF), pltpu.VMEM((rows, 768), BF), pltpu.VMEM((rows, 128), F32),
            pltpu.SemaphoreType.DMA((4,)),
            pltpu.VMEM((768, 768), BF), pltpu.VMEM((4, 768, 768), BF), pltpu.VMEM((4, 768, 768), BF),
            pltpu.SemaphoreType.DMA((2, 4)),
            pltpu.VMEM((16, 432, 768), BF), pltpu.SemaphoreType.DMA((3, 4)),
            pltpu.VMEM((4, rows, 768), F32), pltpu.VMEM((4, rows, 768), BF),
            pltpu.VMEM((rows, 768), F32), pltpu.VMEM((rows, 768), BF), pltpu.VMEM((rows, 768), F32),
            pltpu.VMEM((rows, 128), F32), pltpu.VMEM((rows, 768), F32),
        ],
        compiler_params=pltpu.CompilerParams(vmem_limit_bytes=60 * 2**20),
    )(att, x, cot, wall, bias, lse)


def back_kernel(scattered, idx, xs_ref, dk_ref, dv_ref, dq_ref, done_ref, wall, gb_in, dx_ref, own_ref, gq_ref, gk_ref, gv_ref, gb_ref,
                w, wsem, acc, aq, ak, av):
    m, i = pl.program_id(0), pl.program_id(1)

    @pl.when((m == 0) & (i == 0))
    def _():
        copy = pltpu.make_async_copy(wall.at[:, pl.ds(16, 144), :], w, wsem)
        copy.start()
        acc[...] = jnp.zeros_like(acc)
        aq[...] = jnp.zeros_like(aq)
        ak[...] = jnp.zeros_like(ak)
        av[...] = jnp.zeros_like(av)
        gb_ref[...] = gb_in[...]
        copy.wait()

    rows, dk, dv = xs_ref[0], dk_ref[0], dv_ref[0]
    ak[...] += dot_tn(rows, dk)
    av[...] += dot_tn(rows, dv)
    gb_ref[1:2, :] += jnp.sum(dv.astype(F32), axis=0, keepdims=True)
    dx = dot_nt(dk, w[:, 48:96, :].reshape(768, 768)) + dot_nt(dv, w[:, 96:144, :].reshape(768, 768))

    def add(slot, off, n):
        start = pl.multiple_of(idx[m, slot], 64)
        acc[m, pl.ds(start, n), :] += dx[off:off + n]

    if not scattered:
        dx_ref[0] = jnp.where(i == 2, jnp.zeros_like(dx), dx).astype(BF)

    @pl.when((i < 5) & (i != 2) & scattered)
    def _():
        add(jnp.minimum(i, 4), 0, 256)

    @pl.when((i == 5) & scattered)
    def _():
        add(5, 0, 128)
        add(6, 128, 128)

    @pl.when((i > 5) & scattered)
    def _():
        for t in range(4):
            add(7 + 4 * (i - 6) + t, 64 * t, 64)

    @pl.when(i == 2)
    def _():
        dq = dq_ref[0]
        aq[...] += dot_tn(rows, dq)
        gb_ref[0:1, :] += jnp.sum(dq.astype(F32), axis=0, keepdims=True)
        own_ref[0] = dx + done_ref[0] + dot_nt(dq, w[:, 0:48, :].reshape(768, 768))

    @pl.when((i == CHUNKS - 1) & scattered)
    def _():
        dx_ref[m if scattered else 0] = acc[m].astype(BF)

    @pl.when((m == 1) & (i == CHUNKS - 1))
    def _():
        gq_ref[...] = aq[...].astype(BF)
        gk_ref[...] = ak[...].astype(BF)
        gv_ref[...] = av[...].astype(BF)


def back(idx, xs, dk, dv, dq, done, wall, gb, seq_len):
    mb = xs.shape[0]
    sd = jax.ShapeDtypeStruct
    chunk = pl.BlockSpec((1, 256, 768), lambda m, i, t: (m, i, 0))
    one = pl.BlockSpec((1, 256, 768), lambda m, i, t: (m, 0, 0))
    whole = lambda *s: pl.BlockSpec(s, lambda m, i, t: (0,) * len(s))
    scattered = seq_len > 0
    held = seq_len if scattered else 256
    return pl.pallas_call(
        functools.partial(back_kernel, scattered),
        grid_spec=pltpu.PrefetchScalarGridSpec(
            num_scalar_prefetch=1,
            grid=(mb, CHUNKS),
            in_specs=[chunk, chunk, chunk, one, one, pl.BlockSpec(memory_space=pl.ANY), whole(16, 768)],
            out_specs=[whole(mb, seq_len, 768) if scattered else chunk, one, whole(768, 768), whole(768, 768), whole(768, 768), whole(16, 768)],
            scratch_shapes=[
                pltpu.VMEM((16, 144, 768), BF), pltpu.SemaphoreType.DMA, pltpu.VMEM((mb, held, 768), F32),
                pltpu.VMEM((768, 768), F32), pltpu.VMEM((768, 768), F32), pltpu.VMEM((768, 768), F32),
            ],
        ),
        out_shape=[sd((mb, seq_len if scattered else NS, 768), BF), sd((mb, 256, 768), F32), sd((768, 768), BF), sd((768, 768), BF),
                   sd((768, 768), BF), sd((16, 768), F32)],
        compiler_params=pltpu.CompilerParams(vmem_limit_bytes=60 * 2**20),
    )(idx, xs, dk, dv, dq, done, wall, gb)


def last_kernel(*refs):
    table, arrays = refs[0], refs[1:8]
    outs, vectors = refs[8:15], refs[15:]
    for src, dst in zip(arrays, outs):
        dst[...] = src[...]
    owner = lax.axis_index("seq") * 4 + lax.axis_index("batch")
    n, m = vectors[0].shape[1], vectors[8].shape[1]
    small = pltpu.roll(table[0:8, :], (768 - owner * n) % 768, axis=1)
    for i in range(8):
        vectors[i][...] = small[i:i + 1, 0:n]
    ups = jnp.broadcast_to(table[pl.ds(8 + owner // 8, 1), :], (8, 768))
    vectors[8][...] = pltpu.roll(ups, (768 - (owner % 8) * m) % 768, axis=1)[0:1, 0:m]


def last(table, arrays, n, m):
    sd = jax.ShapeDtypeStruct
    vm = pl.BlockSpec(memory_space=pltpu.VMEM)
    return pl.pallas_call(
        last_kernel,
        in_specs=[vm] * 8,
        out_specs=[vm] * 16,
        out_shape=[sd(a.shape, a.dtype) for a in arrays] + [sd((1, n), F32)] * 8 + [sd((1, m), F32)],
        compiler_params=pltpu.CompilerParams(vmem_limit_bytes=60 * 2**20),
    )(table, *arrays)

def cat_rows(ref, h):
    return jnp.concatenate([ref[0, pl.ds(a, n), :] for a, n in key_rows(h)], axis=0)


def fwd_kernel(q_ref,k_ref,v_ref,me_ref,o_ref,l_ref):
    p=pl.program_id(1)
    ind=block_columns().astype(BF)
    for h in range(2):
        me=me_ref[0,h]
        qe=jnp.concatenate([split_heads(q_ref[0,pl.ds(h*HALF,HALF),:]),ind],axis=1)
        ke=jnp.concatenate([cat_rows(k_ref, h),me],axis=1)
        s=dot_nt(qe,ke)
        top=jnp.max(s,axis=1,keepdims=True)
        e=jnp.exp(s-top).astype(BF)
        ve=jnp.concatenate([cat_rows(v_ref,h),me],axis=1)
        o=dot(e,ve)
        tot=o[:,130:131]
        o_ref[0,pl.ds(h*HALF,HALF),:]=merge_heads(o[:,:128]/tot).astype(BF)
        l_ref[0,0,pl.ds(h*256,256),:]=jnp.broadcast_to(top+jnp.log(tot),(256,128))
def attn_fwd(q,k,v,me):
    mb=q.shape[0]; npair=q.shape[2]//128
    return pl.pallas_call(fwd_kernel,grid=(mb,npair),
      in_specs=[pl.BlockSpec((1,256,128),lambda m,p:(m,0,p)),pl.BlockSpec((1,NS,128),lambda m,p:(m,0,p)),pl.BlockSpec((1,NS,128),lambda m,p:(m,0,p)),
        pl.BlockSpec((1,2,NK,128),lambda m,p:(m,0,0,0))],
      out_specs=[pl.BlockSpec((1,256,128),lambda m,p:(m,0,p)),pl.BlockSpec((1,1,512,128),lambda m,p:(m,p,0,0))],
      out_shape=[jax.ShapeDtypeStruct(q.shape,BF),jax.ShapeDtypeStruct((mb,npair,512,128),F32)],
      compiler_params=pltpu.CompilerParams(vmem_limit_bytes=56*2**20))(q,k,v,me)
def bwd_kernel(CH,q_ref,k_ref,v_ref,me_ref,o_ref,do_ref,l_ref,dq_ref,dk_ref,dv_ref,dka,dva):
    ind=block_columns()
    zero=jnp.zeros_like(ind)
    dka[...]=jnp.zeros_like(dka); dva[...]=jnp.zeros_like(dva)
    for h in range(2):
        rows=pl.ds(h*HALF,HALF)
        qs=split_heads(q_ref[0,rows,:])
        do2=do_ref[0,rows,:]
        dos=split_heads(do2)
        o2=o_ref[0,rows,:].astype(F32)
        delta=jnp.sum(dos.astype(F32)*jnp.concatenate([o2,o2],axis=0),axis=1,keepdims=True)
        lse=l_ref[0,0,pl.ds(h*256,256),0:1]
        qe=jnp.concatenate([qs,with_column(ind,-lse)],axis=1)
        doe=jnp.concatenate([dos,with_column(zero,-delta)],axis=1)
        dqt=jnp.zeros((128,256),F32)
        off=0
        for a,n in key_rows(h):
            c0=0
            while c0<n:
                c=min(CH,n-c0)
                kr=pl.ds(a+c0,c)
                k2=k_ref[0,kr,:]; v2=v_ref[0,kr,:]; me=me_ref[0,h,pl.ds(off+c0,c),:]
                st=dot_nt(jnp.concatenate([k2,me],axis=1),qe)
                pt=jnp.exp(st)
                dpt=dot_nt(jnp.concatenate([v2,me],axis=1),doe)
                ds=(pt*dpt).astype(BF)
                dva[kr,:]+=dot(pt.astype(BF),dos)
                dka[kr,:]+=dot(ds,qs)
                dqt=dqt+dot(k2.T,ds)
                c0+=c
            off+=n
        dq_ref[0,rows,:]=(merge_heads(dqt.T)*0.125).astype(BF)
    dk_ref[0]=dka[...].astype(BF); dv_ref[0]=dva[...].astype(BF)
def attn_bwd(q,k,v,me,o,do,l,CH=384):
    mb=q.shape[0]; npair=q.shape[2]//128
    qs=pl.BlockSpec((1,256,128),lambda m,p:(m,0,p)); ks=pl.BlockSpec((1,NS,128),lambda m,p:(m,0,p))
    return pl.pallas_call(functools.partial(bwd_kernel,CH),grid=(mb,npair),
      in_specs=[qs,ks,ks,pl.BlockSpec((1,2,NK,128),lambda m,p:(m,0,0,0)),qs,qs,pl.BlockSpec((1,1,512,128),lambda m,p:(m,p,0,0))],
      out_specs=[qs,ks,ks],
      out_shape=[jax.ShapeDtypeStruct(q.shape,BF),jax.ShapeDtypeStruct(k.shape,BF),jax.ShapeDtypeStruct(k.shape,BF)],
      scratch_shapes=[pltpu.VMEM((NS,128),F32)]*2,
      compiler_params=pltpu.CompilerParams(vmem_limit_bytes=56*2**20))(q,k,v,me,o,do,l)


BLK = 64
WIN = 8
RAND = 3
ALL = ("seq", "batch")


def vector_table(vectors, b_up, owner, width):
    lane = jnp.arange(width, dtype=jnp.int32)
    n, m = vectors[0].shape[0], b_up.shape[0]
    table = jnp.where(lane // n == owner, jnp.tile(jnp.stack(vectors).astype(F32), (1, width // n)), 0.0)
    flat = jnp.arange(4 * width, dtype=jnp.int32)
    ups = jnp.where(flat // m == owner, jnp.tile(b_up.astype(F32), 4 * width // m), 0.0).reshape(4, width)
    return jnp.concatenate([table, ups, jnp.zeros((4, width), F32)], axis=0)


def block_plan(lengths, randoms, device, blocks):
    ends = jnp.cumsum(lengths, axis=1)
    starts = ends - lengths

    def doc_of(block):
        at = block * BLK
        shape = (lengths.shape[0],) + (1,) * (block.ndim - 1) + (lengths.shape[1],)
        doc = jnp.sum((ends.reshape(shape) <= at[..., None]).astype(jnp.int32), axis=-1)
        doc = jnp.minimum(doc, lengths.shape[1] - 1)
        hit = jnp.arange(lengths.shape[1], dtype=jnp.int32) == doc[..., None]
        return doc, jnp.sum(jnp.where(hit, starts.reshape(shape), 0), axis=-1)

    mb = lengths.shape[0]
    half = jnp.arange(2, dtype=jnp.int32)
    query = device * 4 + 2 * half[:, None] + half[None, :]
    query = jnp.broadcast_to(query[None], (mb, 2, 2))
    q_doc, q_first = doc_of(query)
    window = device * 4 + 2 * half[:, None] - WIN + jnp.arange(2 * WIN + 2, dtype=jnp.int32)[None, :]
    window = jnp.broadcast_to(window[None], (mb, 2, 2 * WIN + 2))
    w_doc, w_first = doc_of(jnp.clip(window, 0, blocks - 1))
    w_good = (window >= 0) & (window < blocks) & (window * BLK - w_first >= 2 * BLK)
    see_window = (
        w_good[:, :, None, :]
        & (w_doc[:, :, None, :] == q_doc[..., None])
        & (jnp.abs(window[:, :, None, :] - query[..., None]) <= WIN)
    )
    see_glob = jnp.ones((mb, 2, 2, 2), bool)
    named = lax.dynamic_slice_in_dim(randoms, device * 4, 4, 1).reshape(mb, 2, 2, RAND)
    r_doc, r_first = doc_of(named)
    r_good = (
        (r_doc == q_doc[..., None])
        & (jnp.abs(named - query[..., None]) > WIN)
        & (named * BLK - r_first >= 2 * BLK)
    )
    see_random = (r_good[:, :, None] & jnp.eye(2, dtype=bool)[None, None, :, :, None]).reshape(mb, 2, 2, 2 * RAND)
    see = jnp.concatenate([see_window, see_glob, see_random], axis=3)
    chunk = jnp.clip(device + jnp.arange(-2, 3, dtype=jnp.int32), 0, blocks // 4 - 1) * (4 * BLK)
    where = jnp.concatenate(
        [jnp.broadcast_to(chunk[None], (mb, 5)), q_first[:, :, 0], named.reshape(mb, -1) * BLK], axis=1
    )
    return where, jnp.where(see, 0.0, -1e30)


def mask_columns(see):
    bias = jnp.broadcast_to(see[..., None], see.shape + (BLK,)).reshape(see.shape[:3] + (-1, 1))
    lane = jnp.arange(128, dtype=jnp.int32)
    ones = jnp.where((lane >= 2) & (lane < 5), 1.0, 0.0)
    return jnp.where(lane == 0, bias[:, :, 0], jnp.where(lane == 1, bias[:, :, 1], ones)).astype(BF)


def on_device(inputs, cotangent, doc_lengths, random_blocks, wq, wk, wv, wo, wu, wd, b_query, b_value, b_out,
              b_up, b_down, gain_attn, bias_attn, gain_ffn, bias_ffn):
    mb, _, rows, width = inputs.shape
    devices, owners = lax.axis_size("seq"), lax.axis_size("seq") * lax.axis_size("batch")
    device = lax.axis_index("seq")
    owner = device * lax.axis_size("batch") + lax.axis_index("batch")
    linked = devices == 8 and owners == 32
    seq_len = devices * rows
    x, cot = inputs[:, 0], cotangent[:, 0]
    lengths, randoms = doc_lengths[:, 0], random_blocks[:, 0]
    vectors = (b_query, b_value, b_out, b_down, gain_attn, bias_attn, gain_ffn, bias_ffn)
    flat = lambda t: t.reshape(-1, t.shape[-1])
    if linked:
        att, lse, q, xs, k, v, wall, top, bias, extra, targets = forward_all(
            doc_lengths.transpose(1, 0, 2), random_blocks.transpose(1, 0, 2, 3), x, (wq, wk, wv, wo, wu, wd),
            [v[None] for v in vectors], b_up[None])
    else:
        where, see = block_plan(lengths, randoms, device, seq_len // BLK)
        extra, table = mask_columns(see), vector_table(vectors, b_up, owner, width)
        xall = lax.all_gather(x, "seq", axis=1, tiled=True)
        bias = lax.psum(table, ALL)
        full = [lax.all_gather(w, ALL, axis=0, tiled=True) for w in (wq, wk, wv, wo, wu, wd)]
        fold = lambda w: w.reshape(16, -1, width)
        up = full[4].reshape(16, 48, 4, width).transpose(0, 2, 1, 3).reshape(16, 192, width)
        wall = jnp.concatenate([fold(full[3]), up, fold(full[5])], axis=1)
        top = jnp.concatenate([jnp.zeros((16, 16, width), BF)] + [fold(w) for w in full[:3]], axis=1)
        xs, k, v, q = project(where, xall, top, bias)
        att, lse = attn_fwd(q, k, v, extra)
    stats = flat(lse) if linked else jnp.zeros((mb * rows, 128), F32)
    out, stats, datt, done, go, gu, gd, gb = middle(flat(att), flat(x), flat(cot), wall, bias, stats)
    datt, done = datt.reshape(att.shape), done.reshape(mb, rows, width)
    if linked:
        *grads, gb, dx = backward_all(datt, stats.reshape(mb, rows, 128), targets, gb, extra, q, done, k, v, xs, top, go, gu, gd)
    else:
        dq, dk, dv = attn_bwd(q, k, v, extra, att, datt, lse, 640)
        dxs, own, gq, gk, gv, gb = back(where, xs, dk, dv, dq, done, top, gb, 0)
        start = (where[:, :5, None] + jnp.arange(0, 256, BLK)).reshape(mb, -1)
        glob = (where[:, 5:7, None] + jnp.arange(0, 128, BLK)).reshape(mb, -1)
        to = jnp.concatenate([start, glob, where[:, 7:]], axis=1) // BLK
        parts = dxs.reshape(mb, -1, BLK, width)
        total = jnp.zeros((mb, seq_len // BLK, BLK, width), F32)
        total = jax.vmap(lambda t, i, p: t.at[i].add(p))(total, to, parts.astype(F32))
        dx = own + lax.psum_scatter(total.reshape(mb, seq_len, width), "seq", scatter_dimension=1, tiled=True)
        grads = [lax.psum_scatter(g.astype(F32), ALL, scatter_dimension=0, tiled=True) for g in (gq, gk, gv, go, gu, gd)]
        gb = lax.psum(gb, ALL)
    n, m = b_query.shape[0], b_up.shape[0]
    if linked:
        done_all = last(gb, (*grads, dx), n, m)
        grads, dx = done_all[:6], done_all[6]
        small, ups = [g.reshape(n) for g in done_all[7:15]], done_all[15].reshape(m)
    else:
        small = lax.dynamic_slice_in_dim(gb[:8], owner * n, n, 1)
        ups = lax.dynamic_slice_in_dim(gb[8:12].reshape(-1), owner * m, m, 0)
    return (
        out.reshape(inputs.shape), dx[:, None], *grads,
        small[0], small[1], small[2], ups, small[3], small[4], small[5], small[6], small[7],
    )


def solution(mesh):
    tokens = P(None, "batch", "seq", None)
    mat, vec = P(ALL, None), P(ALL)
    in_specs = (tokens, tokens, P(None, "batch", None), P(None, "batch", None, None)) + (mat,) * 6 + (vec,) * 9
    out_specs = (tokens, tokens) + (mat,) * 6 + (vec,) * 9
    return jax.shard_map(on_device, mesh=mesh, in_specs=in_specs, out_specs=out_specs, check_vma=False)
```
